128 devices in a mesh: grp: 4 (over y_hi, core), tp: 32 (over z, y_lo, x).
Axes of the slice: x: 4, y: 4 (y_hi: 2, y_lo: 2; y = y_hi * 2 + y_lo), z: 4, core: 2. Of those that a mesh axis runs over, the one named last changes fastest.
Arguments:
- main_inputs: bfloat16 [128, 2, 8192], P(('grp', 'tp')), parts along dimension 0, may hold values from -6 to 6
- cont_inputs: bfloat16 [128, 8, 2, 8192], P(('grp', 'tp')), parts along dimension 0, may hold values from -6 to 6
- prefix_cache: bfloat16 [128, 256, 2048], P(('grp', 'tp')), parts along dimension 0, may hold values from -4 to 40.5
- prefix_len: int32 [128], P(('grp', 'tp')), parts along dimension 0, may hold values from 1 to 254, as said below
- boundary: int32 [128], P(('grp', 'tp')), parts along dimension 0, may hold values from 1 to 2
- rms_gain: float32 [8192], replicated, may hold values from 0.1 to 1.9
- qkv_bias: float32 [10240], replicated, may hold values from -2 to 64
- w_qkv: bfloat16 [32, 2048, 1280], P('tp'), may hold values from -0.0625 to 0.0625
- w_out: bfloat16 [32, 2048, 1024], P('tp'), may hold values from -0.0625 to 0.0625
- value_head: float32 [8192], replicated, may hold values from -0.0625 to 0.0625
Outputs:
- main_out: bfloat16 [128, 2, 8192], P(('grp', 'tp')), parts along dimension 0
- values: float32 [128], P(('grp', 'tp')), parts along dimension 0
The draws below stay inside these ranges and needn't reach their ends.
There are 4 independent parts, one for each index of `grp`. The reference program is written for one: setup_inputs(seed, part) draws one part's arguments, and reference() takes and returns one part's arrays. A program takes and returns all parts, laid end to end along the dimension named above; an argument that names none is the same for every part. Nothing has to cross between parts.
Inputs may be any that keep to these rules, and one draw needn't show every extreme that they name: prefix_len + 2 fits in 256; some row reaches the most.
All inputs are finite; a program needn't handle non-finite values.
Results may differ from the reference program's by a relative error of at most 0.0065.
Values may be sent and summed in bfloat16 or wider, within the bound.
No kernel may reach another device: no remote copies, remote signals or barrier semaphores. Data moves between devices by JAX's collectives and lax.ppermute only.
A program may use at most 128 MiB of HBM per device.

```python
import math
import jax
import jax.numpy as jnp
from jax import lax

D = 8192
KVH = 8
HD = 128
NR = 4
LMAX = 256
MAIN = 2
CONTS = 8
CSTEPS = 2
QKV = 10240
NC = 8
ROWS = 32
N_TP = 32


def draw_prefix_cache(key, part):
    key = jax.random.fold_in(key, 11)
    base_key = jax.random.fold_in(key, 0)
    shape = (ROWS, LMAX, 2 * KVH, HD)
    cache = jnp.clip(jax.random.normal(base_key, shape, jnp.float32), -4.0, 4.0)
    return cache.reshape(ROWS, LMAX, 2 * KVH * HD).astype(jnp.bfloat16)


def draw_qkv_bias(key, part):
    key = jax.random.fold_in(key, 23)
    base_key = jax.random.fold_in(key, 0)
    total = D + 2 * KVH * HD
    bias = 0.5 * jnp.clip(jax.random.normal(base_key, (total,), jnp.float32), -4.0, 4.0)
    return bias


def draw_prefix_len(key, part):
    key = jax.random.fold_in(key, 37)
    len_key, pick_key = jax.random.split(key, 2)
    lengths = jax.random.randint(len_key, (ROWS,), 1, LMAX - MAIN + 1)
    chosen = jax.random.randint(pick_key, (), 0, ROWS)
    return jnp.where(jnp.arange(ROWS) == chosen, LMAX - MAIN, lengths).astype(jnp.int32)


def with_ends(values, rng, least, largest):
    longest = values.shape.index(max(values.shape))
    spots = []
    for shift in (0, 1):
        where = [jax.random.randint(jax.random.fold_in(rng, axis), (), 0, length) for axis, length in enumerate(values.shape)]
        where[longest] = (where[longest] + shift) % values.shape[longest]
        spots.append(tuple(where))
    return values.at[spots[0]].set(least).at[spots[1]].set(largest)


def steps_of(stream_key, dims, cuts, low, top_value):
    factor_of = 1.0
    for dim, shards_of in cuts:
        draws = jax.random.uniform(jax.random.fold_in(jax.random.fold_in(stream_key, 6), dim), (shards_of,), jnp.float32, low / len(cuts), top_value / len(cuts))
        factor_of = factor_of * jnp.repeat(jnp.exp(draws), dims[dim] // shards_of).reshape((-1,) + (1,) * (len(dims) - 1 - dim))
    return factor_of


def bell_draw(stream_key, dims, scale, bound, cuts=(), kind=jnp.bfloat16):
    drawn = scale * jax.random.normal(stream_key, dims, jnp.float32)
    if cuts:
        drawn = drawn * steps_of(stream_key, dims, cuts, -0.22, 0.18)
    return jnp.clip(drawn, -bound, bound).astype(kind)


def setup_inputs(seed: int = 0, part: int = 0) -> dict:
    key_of = jax.random.split(jax.random.key(seed), 11)
    own_keys = jax.random.split(jax.random.fold_in(key_of[10], part), 11)
    main_inputs = bell_draw(own_keys[0], (ROWS, MAIN, D), 1.0, 6.0, ((0, 32),))
    cont_inputs = bell_draw(own_keys[1], (ROWS, CONTS, CSTEPS, D), 1.0, 6.0, ((0, 32),))
    prefix_cache = draw_prefix_cache(jax.random.fold_in(jax.random.fold_in(key_of[10], part), 71), part)
    prefix_len = draw_prefix_len(jax.random.fold_in(jax.random.fold_in(key_of[10], part), 71), part)
    boundary = with_ends(jax.random.randint(own_keys[4], (ROWS,), 1, MAIN + 1), jax.random.fold_in(own_keys[4], 1), 1, MAIN).astype(jnp.int32)
    rms_gain = jnp.clip(1.0 + 0.18 * jax.random.normal(key_of[5], (D,), jnp.float32), 0.1, 1.9)
    qkv_bias = draw_qkv_bias(jax.random.fold_in(key_of[10], 71), part)
    w_qkv = bell_draw(key_of[7], (N_TP, D // NR, QKV // NC), D ** -0.5, 0.0625, ((0, 32),))
    w_out = bell_draw(key_of[8], (N_TP, D // NR, D // NC), D ** -0.5, 0.0625, ((0, 32),))
    value_head = bell_draw(key_of[9], (D,), D ** -0.5, 0.0625, (), jnp.float32)
    return dict(main_inputs=main_inputs, cont_inputs=cont_inputs, prefix_cache=prefix_cache, prefix_len=prefix_len, boundary=boundary, rms_gain=rms_gain, qkv_bias=qkv_bias, w_qkv=w_qkv, w_out=w_out, value_head=value_head)


THETA = 1000000.0
EPS = 1e-06
MASKED_SCORE = -1e+30

def rms_normed(hidden, gain_row):
    wide_rows = hidden.astype(jnp.float32)
    inv_scale = lax.rsqrt(lax.optimization_barrier(jnp.mean(wide_rows * wide_rows, axis=-1, keepdims=True)) + EPS)
    return (wide_rows * inv_scale * gain_row).astype(jnp.bfloat16)

def rotate(vectors, positions, head_width):
    half_width = head_width // 2
    frequency = THETA ** (-(jnp.arange(half_width, dtype=jnp.float32) * 2.0) / head_width)
    angles = positions.astype(jnp.float32)[:, None] * frequency[None, :]
    cosine = jnp.cos(angles)[:, None, :]
    sine_part = jnp.sin(angles)[:, None, :]
    shaped = vectors.reshape(vectors.shape[0], -1, head_width)
    front_half = shaped[..., :half_width]
    back_half = shaped[..., half_width:]
    turned = jnp.concatenate([front_half * cosine - back_half * sine_part, back_half * cosine + front_half * sine_part], axis=-1)
    return turned.reshape(vectors.shape)

def attend(query_rows, segments, kv_heads, head_width):
    row_count = query_rows.shape[0]
    group_size = query_rows.shape[1] // head_width // kv_heads
    kv_width = kv_heads * head_width
    query_grid = query_rows.astype(jnp.float32).reshape(row_count, kv_heads, group_size, head_width)
    inv_root = 1.0 / math.sqrt(head_width)
    logit_list = []
    value_list = []
    for kv_cache, visible_len in segments:
        slot_count = kv_cache.shape[1]
        key_tiles = kv_cache[:, :, :kv_width].astype(jnp.float32).reshape(row_count, slot_count, kv_heads, head_width)
        value_list.append(kv_cache[:, :, kv_width:].astype(jnp.float32).reshape(row_count, slot_count, kv_heads, head_width))
        logits = jnp.einsum('bkgd,blkd->bkgl', query_grid, key_tiles) * inv_root
        visible = (jnp.arange(slot_count, dtype=jnp.int32)[None, :] < visible_len[:, None])[:, None, None, :]
        logit_list.append(jnp.where(visible, logits, MASKED_SCORE))
    highest = reduce_max([lax.optimization_barrier(jnp.max(entry, axis=-1, keepdims=True)) for entry in logit_list])
    expos = [jnp.exp(entry - highest) for entry in logit_list]
    total_mass = expos[0].sum(axis=-1, keepdims=True)
    for entry in expos[1:]:
        total_mass = total_mass + entry.sum(axis=-1, keepdims=True)
    attended = jnp.zeros(query_grid.shape, jnp.float32)
    for entry, value_tiles in zip(expos, value_list):
        weights_bf = (entry / total_mass).astype(jnp.bfloat16)
        attended = attended + jnp.einsum('bkgl,blkd->bkgd', weights_bf.astype(jnp.float32), value_tiles)
    return attended.reshape(row_count, -1).astype(jnp.bfloat16)

def reduce_max(entries):
    result = entries[0]
    for entry in entries[1:]:
        result = jnp.maximum(result, entry)
    return result

def assemble(blocks):
    members, part_rows, part_cols = blocks.shape
    col_blocks = members // NR
    grid = blocks.reshape(NR, col_blocks, part_rows, part_cols).transpose(0, 2, 1, 3)
    return grid.reshape(NR * part_rows, col_blocks * part_cols)

def layer_steps(inputs, kv_cache, cache_len, gain_row, bias_row, w_qkv_full, w_out_full):
    row_count, step_count, width_model = inputs.shape
    kv_width = KVH * HD
    new_kv = jnp.zeros((row_count, step_count, 2 * kv_width), jnp.bfloat16)
    outputs = []
    for step_index in range(step_count):
        hidden = inputs[:, step_index]
        projected = jnp.dot(rms_normed(hidden, gain_row), w_qkv_full, preferred_element_type=jnp.float32) + bias_row
        positions = cache_len + step_index
        query_rows = rotate(projected[:, :width_model], positions, HD).astype(jnp.bfloat16)
        key_rows = rotate(projected[:, width_model:width_model + kv_width], positions, HD).astype(jnp.bfloat16)
        value_rows = projected[:, width_model + kv_width:].astype(jnp.bfloat16)
        new_kv = new_kv.at[:, step_index].set(jnp.concatenate([key_rows, value_rows], axis=1))
        seen = jnp.full((row_count,), step_index + 1, jnp.int32)
        attended = attend(query_rows, [(kv_cache, cache_len), (new_kv, seen)], KVH, HD)
        mixed_out = jnp.dot(attended, w_out_full, preferred_element_type=jnp.float32)
        outputs.append((hidden.astype(jnp.float32) + mixed_out).astype(jnp.bfloat16))
    return (jnp.stack(outputs, axis=1), new_kv)

def extend_state(prefix_cache, prefix_len, main_kv, boundary):
    slot_index = jnp.arange(prefix_cache.shape[1], dtype=jnp.int32)[None, :]
    state_cache = prefix_cache
    for step_index in range(main_kv.shape[1]):
        landing = (slot_index == (prefix_len + step_index)[:, None]) & (step_index < boundary)[:, None]
        state_cache = jnp.where(landing[:, :, None], main_kv[:, step_index][:, None, :], state_cache)
    return state_cache

def reference(main_inputs, cont_inputs, prefix_cache, prefix_len, boundary, rms_gain, qkv_bias, w_qkv, w_out, value_head):
    w_qkv_full = assemble(w_qkv)
    w_out_full = assemble(w_out)
    main_out, main_kv = layer_steps(main_inputs, prefix_cache, prefix_len, rms_gain, qkv_bias, w_qkv_full, w_out_full)
    state_cache = extend_state(prefix_cache, prefix_len, main_kv, boundary)
    state_len = prefix_len + boundary

    def continue_one(feed):
        outputs, unused = layer_steps(feed, state_cache, state_len, rms_gain, qkv_bias, w_qkv_full, w_out_full)
        scores = jnp.dot(outputs.reshape(-1, D).astype(jnp.float32), value_head, precision=lax.Precision.HIGHEST)
        return lax.optimization_barrier(jnp.sum(scores.reshape(outputs.shape[0], outputs.shape[1]), axis=1))
    returns = lax.map(continue_one, jnp.moveaxis(cont_inputs, 1, 0))
    return (main_out, lax.optimization_barrier(jnp.sum(returns, axis=0)) / CONTS)
```

```python
import functools
import math

import jax
import jax.numpy as jnp
from jax import lax
from jax.experimental import pallas as pl
from jax.experimental.pallas import tpu as pltpu
from jax.sharding import PartitionSpec as P

KVH = 8
HD = 128
D = 8192
QKV = 10240
ROW_BLOCKS = 4
COL_BLOCKS = 8
MEMBERS = ROW_BLOCKS * COL_BLOCKS
FEATURES = D // ROW_BLOCKS
CONTS = 8
STEPS = 2
ROWS = 8
TILE = 256

THETA = 1000000.0
EPS = 1e-06
MASKED_SCORE = -1e30

VMEM_LIMIT = 24 * 1024 * 1024
VMEM = pl.BlockSpec(memory_space=pltpu.VMEM)
SMEM = pl.BlockSpec(memory_space=pltpu.SMEM)


def cost(flops, moved):
    return pl.CostEstimate(flops=flops, bytes_accessed=moved, transcendentals=0)


def kernel_params():
    return pltpu.CompilerParams(vmem_limit_bytes=VMEM_LIMIT)


PIECE = FEATURES // 4
QKV_PIECE = 384
OUT_PIECE = D // COL_BLOCKS // 4


def store_copies(out_ref, r, lanes, rows):
    for c in range(COL_BLOCKS):
        out_ref[r * COL_BLOCKS + c, :, lanes] = rows


def norm_kernel(main_ref, cont_ref, gain_ref, first_ref, second_ref, piece_ref):
    def normed(rows):
        wide = rows.astype(jnp.float32)
        inv = lax.rsqrt(jnp.mean(wide * wide, axis=-1, keepdims=True) + EPS)
        return wide * inv * gain_ref[...]

    cont = normed(cont_ref[...])
    main = normed(main_ref[...])
    for r in range(ROW_BLOCKS):
        lanes = slice(r * FEATURES, (r + 1) * FEATURES)
        store_copies(first_ref, r, slice(0, FEATURES), cont[:ROWS, lanes].astype(jnp.bfloat16))
        store_copies(second_ref, r, slice(0, FEATURES), cont[ROWS:, lanes].astype(jnp.bfloat16))
        for j in range(4):
            at = r * FEATURES + j * PIECE
            for s in range(STEPS):
                piece_ref[s * 4 + j : s * 4 + j + 1, :] = main[s : s + 1, at : at + PIECE]
        store_copies(first_ref, r, slice(FEATURES, FEATURES + PIECE), piece_ref[...].astype(jnp.bfloat16))


def norm_rows(main, cont, gain):
    return pl.pallas_call(
        norm_kernel,
        out_shape=(
            jax.ShapeDtypeStruct((MEMBERS, ROWS, FEATURES + PIECE), jnp.bfloat16),
            jax.ShapeDtypeStruct((MEMBERS, ROWS, FEATURES), jnp.bfloat16),
        ),
        in_specs=[VMEM] * 3,
        out_specs=(VMEM, VMEM),
        scratch_shapes=[pltpu.VMEM((8, PIECE), jnp.float32)],
        compiler_params=kernel_params(),
        cost_estimate=cost(10**6, 4 * 10**6),
        name="norm_rows",
    )(main, cont, gain)


def product_kernel(tiles, piece, x_ref, w_ref, out_ref, rows_ref, wide_ref):
    n = pl.program_id(0)
    members = x_ref.shape[0]
    count = members * ROWS

    @pl.when(n == 0)
    def _():
        flat = x_ref[:, :, :FEATURES].astype(jnp.float32).reshape(count, FEATURES)
        rows_ref[:count, :] = flat.astype(jnp.bfloat16)
        if piece:
            packed = x_ref[:, :, FEATURES:].astype(jnp.float32).reshape(count, PIECE)
            for k in range(PIECE // 128):
                wide_ref[k] = packed[:, k * 128 : (k + 1) * 128]
                for j in range(4):
                    rows = wide_ref[k, pl.ds(j, members * STEPS, stride=4), :]
                    lane = j * PIECE + k * 128
                    rows_ref[count:, lane : lane + 128] = rows.astype(jnp.bfloat16)

    weight = w_ref[0, :, pl.ds(pl.multiple_of(n * TILE, TILE), TILE)]
    prod = jnp.dot(rows_ref[...], weight, preferred_element_type=jnp.float32)
    cont = prod[:count].reshape(members, ROWS, TILE).astype(out_ref.dtype)
    out_ref[:, :, pl.ds(pl.multiple_of(n * TILE, TILE), TILE)] = cont
    if piece:
        for tile in range(tiles):

            @pl.when(n == tile)
            def _():
                for h in range(TILE // 128):
                    j, k = divmod(tile * (TILE // 128) + h, piece // 128)
                    wide_ref[k, pl.ds(j, members * STEPS, stride=4), :] = prod[count:, h * 128 : (h + 1) * 128]

        @pl.when(n == tiles - 1)
        def _():
            for k in range(piece // 128):
                lane = tiles * TILE + k * 128
                packed = wide_ref[k].reshape(members, ROWS, 128)
                out_ref[:, :, lane : lane + 128] = packed.astype(out_ref.dtype)


def block_product(rows, blocks, piece, kind):
    tiles = blocks.shape[2] // TILE
    count = MEMBERS * ROWS + (MEMBERS * STEPS if piece else 0)
    return pl.pallas_call(
        functools.partial(product_kernel, tiles, piece),
        out_shape=jax.ShapeDtypeStruct((MEMBERS, ROWS, tiles * TILE + piece), kind),
        grid=(tiles,),
        in_specs=[VMEM, VMEM],
        out_specs=VMEM,
        scratch_shapes=[
            pltpu.VMEM((count, FEATURES), jnp.bfloat16),
            pltpu.VMEM((4, MEMBERS * ROWS, 128), jnp.float32),
        ],
        compiler_params=kernel_params(),
        cost_estimate=cost(2 * count * FEATURES * tiles * TILE, 12 * 10**6),
        name="block_product",
    )(rows, blocks)


def summed_block(parts_ref, c):
    total = parts_ref[c].astype(jnp.float32)
    for r in range(1, ROW_BLOCKS):
        total = total + parts_ref[r * COL_BLOCKS + c].astype(jnp.float32)
    return total


def attend_kernel(first, len_ref, bound_ref, parts_ref, bias_ref, cos_ref, sin_ref, cache_ref, *refs):
    if first:
        out_ref, main_kv_ref, qkv_ref, piece_ref = refs
    else:
        main_kv_ref, out_ref, qkv_ref = refs
    rows = qkv_ref.shape[0]
    prefix_len = len_ref[0]
    boundary = bound_ref[0]
    cols = QKV // COL_BLOCKS
    kv_width = KVH * HD
    if first:
        qkv_ref[ROWS:, :] = jnp.zeros((rows - ROWS, QKV), jnp.float32)
    for c in range(COL_BLOCKS):
        total = summed_block(parts_ref, c)
        qkv_ref[:ROWS, c * cols : (c + 1) * cols] = total[:, :cols]
        if first:
            for m in range(cols // 128):
                j, k = divmod(m, QKV_PIECE // 128)
                lane = cols + k * 128
                at = c * cols + m * 128
                for s in range(STEPS):
                    qkv_ref[ROWS + s : ROWS + s + 1, at : at + 128] = total[s * 4 + j : s * 4 + j + 1, lane : lane + 128]
    cosine = cos_ref[:rows, :]
    sine = sin_ref[:rows, :]

    def plain(start):
        return qkv_ref[:, start : start + HD] + bias_ref[:, start : start + HD]

    def rotated(start):
        head = plain(start)
        return head * cosine + pltpu.roll(head, HD // 2, 1) * sine

    def fresh(values, lane):
        if first:
            main_kv_ref[:, lane : lane + HD] = values[ROWS:]
            parts = [values]
        else:
            parts = [values, main_kv_ref[:, lane : lane + HD]]
        parts.append(jnp.zeros((128 - 2 * ROWS, HD), jnp.float32))
        return jnp.concatenate(parts, axis=0).astype(jnp.bfloat16)

    slots = cache_ref.shape[0]
    group = D // HD // KVH
    seen = lax.broadcasted_iota(jnp.int32, (1, slots), 1) < prefix_len
    row = lax.broadcasted_iota(jnp.int32, (rows, 128), 0)
    col = lax.broadcasted_iota(jnp.int32, (rows, 128), 1)
    own = (row // STEPS == col // STEPS) & (col <= row)
    main = (row < ROWS) & (col >= ROWS) & (col < ROWS + boundary)
    fresh_seen = jnp.concatenate([(own | main).astype(jnp.int32)] * group, axis=0) > 0
    inv_root = 1.0 / math.sqrt(HD)
    contract = (((1,), (1,)), ((), ()))
    for g in range(KVH):
        query = jnp.concatenate([rotated((g * group + h) * HD) for h in range(group)], axis=0).astype(jnp.bfloat16)
        fresh_key = fresh(rotated(D + g * HD), g * HD)
        fresh_value = fresh(plain(D + kv_width + g * HD), kv_width + g * HD)
        key = cache_ref[:, g * HD : (g + 1) * HD]
        value = cache_ref[:, kv_width + g * HD : kv_width + (g + 1) * HD]
        old = lax.dot_general(query, key, contract, preferred_element_type=jnp.float32) * inv_root
        new = lax.dot_general(query, fresh_key, contract, preferred_element_type=jnp.float32) * inv_root
        old = jnp.where(seen, old, MASKED_SCORE)
        new = jnp.where(fresh_seen, new, MASKED_SCORE)
        highest = jnp.maximum(jnp.max(old, axis=-1, keepdims=True), jnp.max(new, axis=-1, keepdims=True))
        old = jnp.exp(old - highest)
        new = jnp.exp(new - highest)
        mass = jnp.sum(old, axis=-1, keepdims=True) + jnp.sum(new, axis=-1, keepdims=True)
        inv_mass = 1.0 / mass
        mixed = jnp.dot((old * inv_mass).astype(jnp.bfloat16), value, preferred_element_type=jnp.float32)
        mixed = mixed + jnp.dot((new * inv_mass).astype(jnp.bfloat16), fresh_value, preferred_element_type=jnp.float32)
        for h in range(group):
            r, place = divmod(g * group + h, FEATURES // HD)
            top = h * rows
            cont = mixed[top : top + ROWS].astype(jnp.bfloat16)
            store_copies(out_ref, r, slice(place * HD, (place + 1) * HD), cont)
            if first:
                j, k = divmod(place, PIECE // HD)
                for s in range(STEPS):
                    at = s * 4 + j
                    line = top + ROWS + s
                    piece_ref[r, at : at + 1, k * HD : (k + 1) * HD] = mixed[line : line + 1]
    if first:
        for r in range(ROW_BLOCKS):
            store_copies(out_ref, r, slice(FEATURES, FEATURES + PIECE), piece_ref[r].astype(jnp.bfloat16))


def attend_first(*args):
    return pl.pallas_call(
        functools.partial(attend_kernel, True),
        out_shape=(
            jax.ShapeDtypeStruct((MEMBERS, ROWS, FEATURES + PIECE), jnp.bfloat16),
            jax.ShapeDtypeStruct((ROWS, 2 * KVH * HD), jnp.float32),
        ),
        in_specs=[SMEM, SMEM] + [VMEM] * 5,
        out_specs=(VMEM, VMEM),
        scratch_shapes=[
            pltpu.VMEM((2 * ROWS, QKV), jnp.float32),
            pltpu.VMEM((ROW_BLOCKS, 8, PIECE), jnp.float32),
        ],
        compiler_params=kernel_params(),
        cost_estimate=cost(2 * 10**8, 8 * 10**6),
        name="attend_first",
    )(*args)


def attend_second(*args):
    return pl.pallas_call(
        functools.partial(attend_kernel, False),
        out_shape=jax.ShapeDtypeStruct((MEMBERS, ROWS, FEATURES), jnp.bfloat16),
        in_specs=[SMEM, SMEM] + [VMEM] * 6,
        out_specs=VMEM,
        scratch_shapes=[pltpu.VMEM((ROWS, QKV), jnp.float32)],
        compiler_params=kernel_params(),
        cost_estimate=cost(2 * 10**8, 8 * 10**6),
        name="attend_second",
    )(*args)


def finish_kernel(first_ref, second_ref, main_ref, cont_ref, head_ref, out_ref, score_ref, wide_ref):
    cols = D // COL_BLOCKS
    total_score = jnp.zeros((ROWS, 128), jnp.float32)
    for c in range(COL_BLOCKS):
        lanes = slice(c * cols, (c + 1) * cols)
        total = summed_block(first_ref, c)
        mixed = jnp.concatenate([total[:, :cols], summed_block(second_ref, c)], axis=0)
        output = (cont_ref[:, lanes].astype(jnp.float32) + mixed).astype(jnp.bfloat16)
        weighted = output.astype(jnp.float32) * head_ref[:, lanes]
        weighted = weighted[:ROWS] + weighted[ROWS:]
        for k in range(cols // 128):
            total_score = total_score + weighted[:, k * 128 : (k + 1) * 128]
        for j in range(4):
            at = slice(c * cols + j * OUT_PIECE, c * cols + (j + 1) * OUT_PIECE)
            for s in range(STEPS):
                wide_ref[s : s + 1, at] = total[s * 4 + j : s * 4 + j + 1, cols:]
    out_ref[...] = (main_ref[...].astype(jnp.float32) + wide_ref[:STEPS, :]).astype(jnp.bfloat16)
    summed = jnp.sum(jnp.sum(total_score, axis=1, keepdims=True), axis=0, keepdims=True)
    score_ref[...] = jnp.broadcast_to(summed / CONTS, (8, 128))


def finish(first, second, main, cont, value_head):
    return pl.pallas_call(
        finish_kernel,
        out_shape=(
            jax.ShapeDtypeStruct((STEPS, D), jnp.bfloat16),
            jax.ShapeDtypeStruct((8, 128), jnp.float32),
        ),
        in_specs=[VMEM] * 5,
        out_specs=(VMEM, VMEM),
        scratch_shapes=[pltpu.VMEM((8, D), jnp.float32)],
        compiler_params=kernel_params(),
        cost_estimate=cost(10**6, 4 * 10**6),
        name="finish",
    )(first, second, main, cont, value_head)


def rope_tables(prefix_len, boundary):
    half = HD // 2
    frequency = THETA ** (-(jnp.arange(half, dtype=jnp.float32) * 2.0) / HD)
    index = jnp.arange(2 * ROWS, dtype=jnp.int32)
    positions = prefix_len + jnp.where(index < ROWS, boundary, 0) + index % STEPS
    angles = positions.astype(jnp.float32)[:, None] * frequency[None, :]
    cosine = jnp.cos(angles)
    sine = jnp.sin(angles)
    return jnp.concatenate([cosine, cosine], axis=1), jnp.concatenate([-sine, sine], axis=1)


def exchange(rows):
    return lax.all_to_all(rows, "tp", split_axis=0, concat_axis=0, tiled=True)


def on_device(
    main_inputs, cont_inputs, prefix_cache, prefix_len, boundary, rms_gain, qkv_bias, w_qkv, w_out, value_head
):
    main = main_inputs.reshape(STEPS, D)
    cont = cont_inputs.reshape(2 * ROWS, D)
    cosine, sine = rope_tables(prefix_len, boundary)
    first, second = norm_rows(main, cont, rms_gain[None, :])
    first = exchange(first)
    second = exchange(second)
    first = exchange(block_product(first, w_qkv, QKV_PIECE, jnp.float32))
    second = exchange(block_product(second, w_qkv, 0, jnp.float32))
    shared = (qkv_bias[None, :], cosine, sine, prefix_cache[0])
    first, main_kv = attend_first(prefix_len, boundary, first, *shared)
    second = attend_second(prefix_len, boundary, second, *shared, main_kv)
    first = exchange(first)
    second = exchange(second)
    first = exchange(block_product(first, w_out, OUT_PIECE, jnp.bfloat16))
    second = exchange(block_product(second, w_out, 0, jnp.bfloat16))
    main_out, score = finish(first, second, main, cont, value_head[None, :])
    return main_out[None], score[0, :1]


def solution(mesh):
    return jax.shard_map(
        on_device,
        mesh=mesh,
        in_specs=(
            P(("grp", "tp"), None, None),
            P(("grp", "tp"), None, None, None),
            P(("grp", "tp"), None, None),
            P(("grp", "tp")),
            P(("grp", "tp")),
            P(),
            P(),
            P("tp", None, None),
            P("tp", None, None),
            P(),
        ),
        out_specs=(P(("grp", "tp"), None, None), P(("grp", "tp"))),
        check_vma=False,
    )
```

```python
import functools
import math

import jax
import jax.numpy as jnp
from jax import lax
from jax.experimental import pallas as pl
from jax.experimental.pallas import tpu as pltpu
from jax.sharding import PartitionSpec as P

KVH = 8
HD = 128
D = 8192
QKV = 10240
ROW_BLOCKS = 4
COL_BLOCKS = 8
FEATURES = D // ROW_BLOCKS
CONTS = 8
STEPS = 2
CTOK = CONTS * STEPS
TILE = 256

THETA = 1000000.0
EPS = 1e-06
MASKED_SCORE = -1e30

VMEM_LIMIT = 48 * 1024 * 1024
VMEM = pl.BlockSpec(memory_space=pltpu.VMEM)
SMEM = pl.BlockSpec(memory_space=pltpu.SMEM)


def cost(flops, moved):
    return pl.CostEstimate(flops=flops, bytes_accessed=moved, transcendentals=0)


def kernel_params():
    return pltpu.CompilerParams(vmem_limit_bytes=VMEM_LIMIT)


def norm_kernel(main_ref, cont_ref, gain_ref, out_ref, piece_ref):
    def normed(rows):
        wide = rows.astype(jnp.float32)
        inv = lax.rsqrt(jnp.mean(wide * wide, axis=-1, keepdims=True) + EPS)
        return wide * inv * gain_ref[...]

    cont = normed(cont_ref[...]).astype(jnp.bfloat16)
    main = normed(main_ref[...])
    for r in range(ROW_BLOCKS):
        for j in range(FEATURES // TILE):
            lanes = slice(r * FEATURES + j * TILE, r * FEATURES + (j + 1) * TILE)
            for s in range(STEPS):
                piece_ref[r, s * 8 + j : s * 8 + j + 1, :] = main[s : s + 1, lanes]
    for r in range(ROW_BLOCKS):
        piece = piece_ref[r].astype(jnp.bfloat16)
        for c in range(COL_BLOCKS):
            out_ref[r * COL_BLOCKS + c, :, :FEATURES] = cont[:, r * FEATURES : (r + 1) * FEATURES]
            out_ref[r * COL_BLOCKS + c, :, FEATURES:] = piece


def norm_rows(main, cont, gain):
    return pl.pallas_call(
        norm_kernel,
        out_shape=jax.ShapeDtypeStruct((32, CTOK, FEATURES + TILE), jnp.bfloat16),
        in_specs=[VMEM] * 3,
        out_specs=VMEM,
        scratch_shapes=[pltpu.VMEM((ROW_BLOCKS, 16, TILE), jnp.float32)],
        compiler_params=kernel_params(),
        cost_estimate=cost(10**6, 4 * 10**6),
        name="norm_rows",
    )(main, cont, gain)


REST = 768


def rest_tile(block):
    return jnp.where(block == 6, 2, 0)


def product_kernel(tiles, rest, x_ref, w_ref, out_ref, rows_ref, wide_ref):
    n = pl.program_id(0)
    members = x_ref.shape[0]
    count = members * CTOK
    lines = members * STEPS
    halves = TILE // 128

    @pl.when(n == 0)
    def _():
        rows_ref[:count, :] = x_ref[:, :, :FEATURES].reshape(count, FEATURES)
        packed = x_ref[:, :, FEATURES:].reshape(members * 16, TILE).astype(jnp.float32)
        for k in range(halves):
            wide_ref[k] = packed[:, k * 128 : (k + 1) * 128]
            for j in range(FEATURES // TILE):
                lane = j * TILE + k * 128
                rows_ref[count:, lane : lane + 128] = wide_ref[k, pl.ds(j, lines, stride=8), :].astype(jnp.bfloat16)

    prod = jnp.dot(rows_ref[...], w_ref[0], preferred_element_type=jnp.float32)
    high = prod.astype(jnp.bfloat16)
    out_ref[:, :, pl.ds(pl.multiple_of(n * TILE, TILE), TILE)] = high[:count].reshape(members, CTOK, TILE)
    for k in range(halves):
        wide_ref[k, pl.ds(n, lines, stride=8), :] = prod[count:, k * 128 : (k + 1) * 128]
    width = tiles * TILE
    if rest:
        start = rest_tile(lax.rem(lax.axis_index("tp"), COL_BLOCKS))

        @pl.when((n >= start) & (n < start + rest // TILE))
        def _():
            low = prod - high.astype(jnp.float32)
            place = n - start
            lane = pl.multiple_of(width + place * TILE, TILE)
            out_ref[:, :, pl.ds(lane, TILE)] = low[:count].astype(jnp.bfloat16).reshape(members, CTOK, TILE)
            for k in range(halves):
                wide_ref[k, pl.ds(tiles + place, lines, stride=8), :] = low[count:, k * 128 : (k + 1) * 128]

    @pl.when(n == tiles - 1)
    def _():
        for k in range(halves):
            lane = width + rest + k * 128
            out_ref[:, :, lane : lane + 128] = wide_ref[k].astype(jnp.bfloat16).reshape(members, 16, 128)


def block_product(rows, blocks, rest):
    members = rows.shape[0]
    tiles = blocks.shape[2] // TILE
    return pl.pallas_call(
        functools.partial(product_kernel, tiles, rest),
        out_shape=jax.ShapeDtypeStruct((members, CTOK, (tiles + 1) * TILE + rest), jnp.bfloat16),
        grid=(tiles,),
        in_specs=[
            VMEM,
            pl.BlockSpec((1, FEATURES, TILE), lambda n: (0, 0, n)),
        ],
        out_specs=VMEM,
        scratch_shapes=[
            pltpu.VMEM((members * (CTOK + STEPS), FEATURES), jnp.bfloat16),
            pltpu.VMEM((TILE // 128, members * 16, 128), jnp.float32),
        ],
        compiler_params=kernel_params(),
        cost_estimate=cost(2 * members * (CTOK + STEPS) * FEATURES * tiles * TILE, 12 * 10**6),
        name="block_product",
    )(rows, blocks)


def summed_block(parts_ref, c, lanes):
    total = parts_ref[c, :, lanes].astype(jnp.float32)
    for r in range(1, ROW_BLOCKS):
        total = total + parts_ref[r * COL_BLOCKS + c, :, lanes].astype(jnp.float32)
    return total


def head_attention(query, key, value, fresh_key, fresh_value, seen, fresh_seen):
    inv_root = 1.0 / math.sqrt(HD)
    contract = (((1,), (1,)), ((), ()))
    old = lax.dot_general(query, key, contract, preferred_element_type=jnp.float32) * inv_root
    new = lax.dot_general(query, fresh_key, contract, preferred_element_type=jnp.float32) * inv_root
    old = jnp.where(seen, old, MASKED_SCORE)
    new = jnp.where(fresh_seen, new, MASKED_SCORE)
    highest = jnp.maximum(jnp.max(old, axis=-1, keepdims=True), jnp.max(new, axis=-1, keepdims=True))
    old = jnp.exp(old - highest)
    new = jnp.exp(new - highest)
    mass = jnp.sum(old, axis=-1, keepdims=True) + jnp.sum(new, axis=-1, keepdims=True)
    inv_mass = 1.0 / mass
    mixed = jnp.dot((old * inv_mass).astype(jnp.bfloat16), value, preferred_element_type=jnp.float32)
    return mixed + jnp.dot((new * inv_mass).astype(jnp.bfloat16), fresh_value, preferred_element_type=jnp.float32)


def load_qkv(main, parts_ref, qkv_ref):
    cols = QKV // COL_BLOCKS
    for c in range(COL_BLOCKS):
        first = 2 if c == 6 else 0
        if main:
            total = summed_block(parts_ref, c, slice(cols + REST, cols + REST + TILE))
        else:
            total = summed_block(parts_ref, c, slice(0, cols + REST))
        for j in range(cols // TILE):
            lanes = slice(c * cols + j * TILE, c * cols + (j + 1) * TILE)
            rest = j - first
            has_rest = 0 <= rest < REST // TILE
            if main:
                for s in range(STEPS):
                    line = total[s * 8 + j : s * 8 + j + 1]
                    if has_rest:
                        at = s * 8 + cols // TILE + rest
                        line = line + total[at : at + 1]
                    qkv_ref[s : s + 1, lanes] = line
            else:
                value = total[:, j * TILE : (j + 1) * TILE]
                if has_rest:
                    value = value + total[:, cols + rest * TILE : cols + (rest + 1) * TILE]
                qkv_ref[:, lanes] = value


def head_readers(qkv_ref, bias_ref, cos_ref, sin_ref):
    cosine = cos_ref[...]
    sine = sin_ref[...]

    def plain(start):
        return qkv_ref[:, start : start + HD] + bias_ref[:, start : start + HD]

    def rotated(start):
        head = plain(start)
        return head * cosine + pltpu.roll(head, HD // 2, 1) * sine

    return plain, rotated


def fresh_block(pieces):
    rows = sum(piece.shape[0] for piece in pieces)
    pad = jnp.zeros((128 - rows, HD), jnp.float32)
    return jnp.concatenate(list(pieces) + [pad], axis=0).astype(jnp.bfloat16)


GROUP = D // HD // KVH
KV_WIDTH = KVH * HD


def attend_main_kernel(len_ref, parts_ref, bias_ref, cos_ref, sin_ref, cache_ref, out_ref, kv_ref, qkv_ref, piece_ref):
    rows = qkv_ref.shape[0]
    qkv_ref[...] = jnp.zeros(qkv_ref.shape, jnp.float32)
    load_qkv(True, parts_ref, qkv_ref)
    plain, rotated = head_readers(qkv_ref, bias_ref, cos_ref, sin_ref)
    seen = lax.broadcasted_iota(jnp.int32, (1, cache_ref.shape[0]), 1) < len_ref[0]
    row = lax.broadcasted_iota(jnp.int32, (rows, 128), 0)
    col = lax.broadcasted_iota(jnp.int32, (rows, 128), 1)
    own = ((col <= row) & (col < STEPS)).astype(jnp.int32)
    fresh_seen = jnp.concatenate([own] * GROUP, axis=0) > 0
    for g in range(KVH):
        query = jnp.concatenate([rotated((g * GROUP + h) * HD) for h in range(GROUP)], axis=0).astype(jnp.bfloat16)
        fresh_key = rotated(D + g * HD)
        fresh_value = plain(D + KV_WIDTH + g * HD)
        kv_ref[:, g * HD : (g + 1) * HD] = fresh_key
        kv_ref[:, KV_WIDTH + g * HD : KV_WIDTH + (g + 1) * HD] = fresh_value
        key = cache_ref[:, g * HD : (g + 1) * HD]
        value = cache_ref[:, KV_WIDTH + g * HD : KV_WIDTH + (g + 1) * HD]
        mixed = head_attention(
            query, key, value, fresh_block([fresh_key]), fresh_block([fresh_value]), seen, fresh_seen
        )
        for h in range(GROUP):
            r, place = divmod(g * GROUP + h, FEATURES // HD)
            j, lane = place // 2, (place % 2) * HD
            for s in range(STEPS):
                at = s * 8 + j
                piece_ref[r, at : at + 1, lane : lane + HD] = mixed[h * rows + s : h * rows + s + 1]
    for r in range(ROW_BLOCKS):
        piece = piece_ref[r].astype(jnp.bfloat16)
        for c in range(COL_BLOCKS):
            out_ref[r * COL_BLOCKS + c] = piece


def attend_main(prefix_len, parts, bias, cosine, sine, cache):
    return pl.pallas_call(
        attend_main_kernel,
        out_shape=(
            jax.ShapeDtypeStruct((32, 16, TILE), jnp.bfloat16),
            jax.ShapeDtypeStruct((8, 2 * KV_WIDTH), jnp.float32),
        ),
        in_specs=[SMEM] + [VMEM] * 5,
        out_specs=(VMEM, VMEM),
        scratch_shapes=[
            pltpu.VMEM((8, QKV), jnp.float32),
            pltpu.VMEM((ROW_BLOCKS, 16, TILE), jnp.float32),
        ],
        compiler_params=kernel_params(),
        cost_estimate=cost(2 * 10**8, 6 * 10**6),
        name="attend_main",
    )(prefix_len, parts, bias, cosine, sine, cache)


def attend_cont_kernel(
    len_ref, bound_ref, parts_ref, bias_ref, cos_ref, sin_ref, cache_ref, kv_ref, cont_ref, head_ref, read_ref,
    score_ref, qkv_ref, weight_ref,
):
    rows = qkv_ref.shape[0]
    load_qkv(False, parts_ref, qkv_ref)
    plain, rotated = head_readers(qkv_ref, bias_ref, cos_ref, sin_ref)
    for r in range(ROW_BLOCKS):
        block = read_ref[r * COL_BLOCKS : (r + 1) * COL_BLOCKS, :]
        weight_ref[:, r * FEATURES : (r + 1) * FEATURES] = jnp.sum(block, axis=0, keepdims=True)
    seen = lax.broadcasted_iota(jnp.int32, (1, cache_ref.shape[0]), 1) < len_ref[0]
    row = lax.broadcasted_iota(jnp.int32, (rows, 128), 0)
    col = lax.broadcasted_iota(jnp.int32, (rows, 128), 1)
    own = (row // STEPS == col // STEPS) & (col <= row)
    main = (col >= rows) & (col < rows + bound_ref[0])
    fresh_seen = jnp.concatenate([(own | main).astype(jnp.int32)] * GROUP, axis=0) > 0
    total = jnp.zeros((rows, HD), jnp.float32)
    for k in range(D // HD):
        lanes = slice(k * HD, (k + 1) * HD)
        total = total + cont_ref[:, lanes].astype(jnp.float32) * head_ref[:, lanes]
    for g in range(KVH):
        query = jnp.concatenate([rotated((g * GROUP + h) * HD) for h in range(GROUP)], axis=0).astype(jnp.bfloat16)
        at_key = slice(g * HD, (g + 1) * HD)
        at_value = slice(KV_WIDTH + g * HD, KV_WIDTH + (g + 1) * HD)
        fresh_key = fresh_block([rotated(D + g * HD), kv_ref[:, at_key]])
        fresh_value = fresh_block([plain(D + KV_WIDTH + g * HD), kv_ref[:, at_value]])
        mixed = head_attention(
            query, cache_ref[:, at_key], cache_ref[:, at_value], fresh_key, fresh_value, seen, fresh_seen
        )
        mixed = mixed.astype(jnp.bfloat16).astype(jnp.float32)
        for h in range(GROUP):
            lanes = slice((g * GROUP + h) * HD, (g * GROUP + h + 1) * HD)
            total = total + mixed[h * rows : (h + 1) * rows] * weight_ref[:, lanes]
    summed = jnp.sum(jnp.sum(total, axis=1, keepdims=True), axis=0, keepdims=True)
    score_ref[...] = jnp.broadcast_to(summed / CONTS, (8, 128))


def attend_cont(*args):
    return pl.pallas_call(
        attend_cont_kernel,
        out_shape=jax.ShapeDtypeStruct((8, 128), jnp.float32),
        in_specs=[SMEM, SMEM] + [VMEM] * 9,
        out_specs=VMEM,
        scratch_shapes=[pltpu.VMEM((CTOK, QKV), jnp.float32), pltpu.VMEM((1, D), jnp.float32)],
        compiler_params=kernel_params(),
        cost_estimate=cost(4 * 10**8, 8 * 10**6),
        name="attend_cont",
    )(*args)


def readout_kernel(head_ref, w_ref, out_ref):
    row = head_ref[pl.ds(lax.rem(lax.axis_index("tp"), COL_BLOCKS), 1), :]
    high = row.astype(jnp.bfloat16).astype(jnp.float32)
    middle = (row - high).astype(jnp.bfloat16).astype(jnp.float32)
    low = row - high - middle
    pieces = jnp.concatenate([high, middle, low, jnp.zeros((13, row.shape[1]), jnp.float32)], axis=0)
    prod = lax.dot_general(
        pieces.astype(jnp.bfloat16), w_ref[0], (((1,), (1,)), ((), ())), preferred_element_type=jnp.float32
    )
    out_ref[...] = prod[0:1] + prod[1:2] + prod[2:3]


def readout(value_head, blocks):
    return pl.pallas_call(
        readout_kernel,
        out_shape=jax.ShapeDtypeStruct((1, FEATURES), jnp.float32),
        in_specs=[VMEM, VMEM],
        out_specs=VMEM,
        compiler_params=kernel_params(),
        cost_estimate=cost(2 * 10**8, 5 * 10**6),
        name="readout",
    )(value_head, blocks)


def out_kernel(tiles, x_ref, w_ref, out_ref, rows_ref, wide_ref):
    n = pl.program_id(0)
    members = x_ref.shape[0]
    lines = members * STEPS
    halves = TILE // 128

    @pl.when(n == 0)
    def _():
        packed = x_ref[...].reshape(members * 16, TILE).astype(jnp.float32)
        for k in range(halves):
            wide_ref[k] = packed[:, k * 128 : (k + 1) * 128]
            for j in range(FEATURES // TILE):
                lane = j * TILE + k * 128
                rows_ref[:, lane : lane + 128] = wide_ref[k, pl.ds(j, lines, stride=8), :].astype(jnp.bfloat16)

    prod = jnp.dot(rows_ref[...], w_ref[0], preferred_element_type=jnp.float32)
    for k in range(halves):
        wide_ref[k, pl.ds(n, lines, stride=4), :] = prod[:, k * 128 : (k + 1) * 128]

    @pl.when(n == tiles - 1)
    def _():
        for k in range(halves):
            packed = wide_ref[k, : members * 8, :].reshape(members, 8, 128)
            out_ref[:, :, k * 128 : (k + 1) * 128] = packed


def out_product(rows, blocks):
    members = rows.shape[0]
    tiles = blocks.shape[2] // TILE
    return pl.pallas_call(
        functools.partial(out_kernel, tiles),
        out_shape=jax.ShapeDtypeStruct((members, 8, TILE), jnp.float32),
        grid=(tiles,),
        in_specs=[
            VMEM,
            pl.BlockSpec((1, FEATURES, TILE), lambda n: (0, 0, n)),
        ],
        out_specs=VMEM,
        scratch_shapes=[
            pltpu.VMEM((members * STEPS, FEATURES), jnp.bfloat16),
            pltpu.VMEM((TILE // 128, members * 16, 128), jnp.float32),
        ],
        compiler_params=kernel_params(),
        cost_estimate=cost(3 * 10**8, 5 * 10**6),
        name="out_product",
    )(rows, blocks)


def finish_kernel(parts_ref, main_ref, out_ref, wide_ref):
    cols = D // COL_BLOCKS
    for c in range(COL_BLOCKS):
        total = summed_block(parts_ref, c, slice(0, TILE))
        for j in range(cols // TILE):
            at = slice(c * cols + j * TILE, c * cols + (j + 1) * TILE)
            for s in range(STEPS):
                wide_ref[s : s + 1, at] = total[s * 4 + j : s * 4 + j + 1]
    out_ref[...] = (main_ref[...].astype(jnp.float32) + wide_ref[:STEPS, :]).astype(jnp.bfloat16)


def finish(parts, main):
    return pl.pallas_call(
        finish_kernel,
        out_shape=jax.ShapeDtypeStruct((STEPS, D), jnp.bfloat16),
        in_specs=[VMEM] * 2,
        out_specs=VMEM,
        scratch_shapes=[pltpu.VMEM((8, D), jnp.float32)],
        compiler_params=kernel_params(),
        cost_estimate=cost(10**6, 2 * 10**6),
        name="finish",
    )(parts, main)


def rope_tables(positions):
    half = HD // 2
    frequency = THETA ** (-(jnp.arange(half, dtype=jnp.float32) * 2.0) / HD)
    angles = positions.astype(jnp.float32)[:, None] * frequency[None, :]
    cosine = jnp.cos(angles)
    sine = jnp.sin(angles)
    return jnp.concatenate([cosine, cosine], axis=1), jnp.concatenate([-sine, sine], axis=1)


def exchange(rows):
    return lax.all_to_all(rows, "tp", split_axis=0, concat_axis=0, tiled=True)


def on_device(
    main_inputs, cont_inputs, prefix_cache, prefix_len, boundary, rms_gain, qkv_bias, w_qkv, w_out, value_head
):
    main = main_inputs.reshape(STEPS, D)
    cont = cont_inputs.reshape(CTOK, D)
    bias = qkv_bias[None, :]
    cache = prefix_cache[0]
    head = value_head[None, :]
    step = jnp.arange(CTOK, dtype=jnp.int32) % STEPS
    main_tables = rope_tables(prefix_len + step[:8])
    cont_tables = rope_tables(prefix_len + boundary + step)
    read = lax.all_gather(readout(value_head.reshape(COL_BLOCKS, D // COL_BLOCKS), w_out), "tp", axis=0, tiled=True)
    sent = exchange(norm_rows(main, cont, rms_gain[None, :]))
    parts = exchange(block_product(sent, w_qkv, REST))
    mixed, main_kv = attend_main(prefix_len, parts, bias, *main_tables, cache)
    mixed = exchange(mixed)
    score = attend_cont(prefix_len, boundary, parts, bias, *cont_tables, cache, main_kv, cont, head, read)
    main_out = finish(exchange(out_product(mixed, w_out)), main)
    return main_out[None], score[0, :1]


def solution(mesh):
    return jax.shard_map(
        on_device,
        mesh=mesh,
        in_specs=(
            P(("grp", "tp"), None, None),
            P(("grp", "tp"), None, None, None),
            P(("grp", "tp"), None, None),
            P(("grp", "tp")),
            P(("grp", "tp")),
            P(),
            P(),
            P("tp", None, None),
            P("tp", None, None),
            P(),
        ),
        out_specs=(P(("grp", "tp"), None, None), P(("grp", "tp"))),
        check_vma=False,
    )
```

```python
import functools
import math

import jax
import jax.numpy as jnp
from jax import lax
from jax.experimental import pallas as pl
from jax.experimental.pallas import tpu as pltpu
from jax.sharding import PartitionSpec as P

KVH = 8
HD = 128
D = 8192
QKV = 10240
ROW_BLOCKS = 4
COL_BLOCKS = 8
FEATURES = D // ROW_BLOCKS
CONTS = 8
STEPS = 2
CTOK = CONTS * STEPS
TILE = 256

THETA = 1000000.0
EPS = 1e-06
MASKED_SCORE = -1e30

VMEM_LIMIT = 48 * 1024 * 1024
VMEM = pl.BlockSpec(memory_space=pltpu.VMEM)
SMEM = pl.BlockSpec(memory_space=pltpu.SMEM)
HBM = pl.BlockSpec(memory_space=pltpu.HBM)


def whole(shape):
    return pl.BlockSpec(shape, lambda *_: (0,) * len(shape))


def cost(flops, moved):
    return pl.CostEstimate(flops=flops, bytes_accessed=moved, transcendentals=0)


def kernel_params():
    return pltpu.CompilerParams(vmem_limit_bytes=VMEM_LIMIT)


def norm_kernel(main_hbm, cont_hbm, gain_hbm, out_ref, main_ref, cont_ref, gain_ref, rows_ref, piece_ref, sems):
    pairs = ((main_hbm, main_ref), (cont_hbm, cont_ref), (gain_hbm, gain_ref))
    copies = [pltpu.make_async_copy(src, dst, sems.at[i]) for i, (src, dst) in enumerate(pairs)]
    for copy in copies:
        copy.start()
    for copy in copies:
        copy.wait()

    def normed(wide):
        inv = lax.rsqrt(jnp.mean(wide * wide, axis=-1, keepdims=True) + EPS)
        return wide * inv * gain_ref[...]

    for c in range(CONTS):
        rows_ref[c * STEPS : (c + 1) * STEPS, :] = cont_ref[c].astype(jnp.float32)
    cont = normed(rows_ref[...]).astype(jnp.bfloat16)
    main = normed(main_ref[...].astype(jnp.float32))
    for r in range(ROW_BLOCKS):
        for j in range(FEATURES // TILE):
            lanes = slice(r * FEATURES + j * TILE, r * FEATURES + (j + 1) * TILE)
            for s in range(STEPS):
                piece_ref[r, s * 8 + j : s * 8 + j + 1, :] = main[s : s + 1, lanes]
    for r in range(ROW_BLOCKS):
        piece = piece_ref[r].astype(jnp.bfloat16)
        for c in range(COL_BLOCKS):
            out_ref[r * COL_BLOCKS + c, :, :FEATURES] = cont[:, r * FEATURES : (r + 1) * FEATURES]
            out_ref[r * COL_BLOCKS + c, :, FEATURES:] = piece


def norm_rows(main, cont, gain):
    return pl.pallas_call(
        norm_kernel,
        out_shape=jax.ShapeDtypeStruct((32, CTOK, FEATURES + TILE), jnp.bfloat16),
        in_specs=[HBM] * 3,
        out_specs=VMEM,
        scratch_shapes=[
            pltpu.VMEM((STEPS, D), jnp.bfloat16),
            pltpu.VMEM((CONTS, STEPS, D), jnp.bfloat16),
            pltpu.VMEM((1, D), jnp.float32),
            pltpu.VMEM((CTOK, D), jnp.float32),
            pltpu.VMEM((ROW_BLOCKS, 16, TILE), jnp.float32),
            pltpu.SemaphoreType.DMA((3,)),
        ],
        compiler_params=kernel_params(),
        cost_estimate=cost(10**6, 4 * 10**6),
        name="norm_rows",
    )(main, cont, gain)


def weight_tile(n, tiles, w_hbm, w_ref, sems):
    def copy(i):
        lanes = pl.ds(pl.multiple_of(i * TILE, TILE), TILE)
        return pltpu.make_async_copy(w_hbm.at[0, :, lanes], w_ref.at[i], sems.at[i])

    @pl.when(n == 0)
    def _():
        for i in range(tiles):
            copy(i).start()

    return copy(n)


REST = 768


def rest_tile(block):
    return jnp.where(block == 6, 2, 0)


def product_kernel(tiles, rest, x_ref, w_hbm, out_ref, rows_ref, wide_ref, w_ref, sems):
    n = pl.program_id(0)
    members = x_ref.shape[0]
    count = members * CTOK
    lines = members * STEPS
    halves = TILE // 128
    tile = weight_tile(n, tiles, w_hbm, w_ref, sems)

    @pl.when(n == 0)
    def _():
        rows_ref[:count, :] = x_ref[:, :, :FEATURES].reshape(count, FEATURES)
        packed = x_ref[:, :, FEATURES:].reshape(members * 16, TILE).astype(jnp.float32)
        for k in range(halves):
            wide_ref[k] = packed[:, k * 128 : (k + 1) * 128]
            for j in range(FEATURES // TILE):
                lane = j * TILE + k * 128
                rows_ref[count:, lane : lane + 128] = wide_ref[k, pl.ds(j, lines, stride=8), :].astype(jnp.bfloat16)

    tile.wait()
    prod = jnp.dot(rows_ref[...], w_ref[n], preferred_element_type=jnp.float32)
    high = prod.astype(jnp.bfloat16)
    out_ref[:, :, pl.ds(pl.multiple_of(n * TILE, TILE), TILE)] = high[:count].reshape(members, CTOK, TILE)
    for k in range(halves):
        wide_ref[k, pl.ds(n, lines, stride=8), :] = prod[count:, k * 128 : (k + 1) * 128]
    width = tiles * TILE
    if rest:
        start = rest_tile(lax.rem(lax.axis_index("tp"), COL_BLOCKS))

        @pl.when((n >= start) & (n < start + rest // TILE))
        def _():
            low = prod - high.astype(jnp.float32)
            place = n - start
            lane = pl.multiple_of(width + place * TILE, TILE)
            out_ref[:, :, pl.ds(lane, TILE)] = low[:count].astype(jnp.bfloat16).reshape(members, CTOK, TILE)
            for k in range(halves):
                wide_ref[k, pl.ds(tiles + place, lines, stride=8), :] = low[count:, k * 128 : (k + 1) * 128]

    @pl.when(n == tiles - 1)
    def _():
        for k in range(halves):
            lane = width + rest + k * 128
            out_ref[:, :, lane : lane + 128] = wide_ref[k].astype(jnp.bfloat16).reshape(members, 16, 128)


def block_product(rows, blocks, rest):
    members = rows.shape[0]
    tiles = blocks.shape[2] // TILE
    return pl.pallas_call(
        functools.partial(product_kernel, tiles, rest),
        out_shape=jax.ShapeDtypeStruct((members, CTOK, (tiles + 1) * TILE + rest), jnp.bfloat16),
        grid=(tiles,),
        in_specs=[VMEM, HBM],
        out_specs=whole((members, CTOK, (tiles + 1) * TILE + rest)),
        scratch_shapes=[
            pltpu.VMEM((members * (CTOK + STEPS), FEATURES), jnp.bfloat16),
            pltpu.VMEM((TILE // 128, members * 16, 128), jnp.float32),
            pltpu.VMEM((tiles, FEATURES, TILE), jnp.bfloat16),
            pltpu.SemaphoreType.DMA((tiles,)),
        ],
        compiler_params=kernel_params(),
        cost_estimate=cost(2 * members * (CTOK + STEPS) * FEATURES * tiles * TILE, 12 * 10**6),
        name="block_product",
    )(rows, blocks)


def summed_block(parts_ref, c, lanes):
    total = parts_ref[c, :, lanes].astype(jnp.float32)
    for r in range(1, ROW_BLOCKS):
        total = total + parts_ref[r * COL_BLOCKS + c, :, lanes].astype(jnp.float32)
    return total


def head_attention(query, key, value, fresh_key, fresh_value, seen, fresh_seen):
    inv_root = 1.0 / math.sqrt(HD)
    contract = (((1,), (1,)), ((), ()))
    old = lax.dot_general(query, key, contract, preferred_element_type=jnp.float32) * inv_root
    new = lax.dot_general(query, fresh_key, contract, preferred_element_type=jnp.float32) * inv_root
    old = jnp.where(seen, old, MASKED_SCORE)
    new = jnp.where(fresh_seen, new, MASKED_SCORE)
    highest = jnp.maximum(jnp.max(old, axis=-1, keepdims=True), jnp.max(new, axis=-1, keepdims=True))
    old = jnp.exp(old - highest)
    new = jnp.exp(new - highest)
    mass = jnp.sum(old, axis=-1, keepdims=True) + jnp.sum(new, axis=-1, keepdims=True)
    inv_mass = 1.0 / mass
    mixed = jnp.dot((old * inv_mass).astype(jnp.bfloat16), value, preferred_element_type=jnp.float32)
    return mixed + jnp.dot((new * inv_mass).astype(jnp.bfloat16), fresh_value, preferred_element_type=jnp.float32)


def load_qkv(main, parts_ref, qkv_ref):
    cols = QKV // COL_BLOCKS
    for c in range(COL_BLOCKS):
        first = 2 if c == 6 else 0
        if main:
            total = summed_block(parts_ref, c, slice(cols + REST, cols + REST + TILE))
        else:
            total = summed_block(parts_ref, c, slice(0, cols + REST))
        for j in range(cols // TILE):
            lanes = slice(c * cols + j * TILE, c * cols + (j + 1) * TILE)
            rest = j - first
            has_rest = 0 <= rest < REST // TILE
            if main:
                for s in range(STEPS):
                    line = total[s * 8 + j : s * 8 + j + 1]
                    if has_rest:
                        at = s * 8 + cols // TILE + rest
                        line = line + total[at : at + 1]
                    qkv_ref[s : s + 1, lanes] = line
            else:
                value = total[:, j * TILE : (j + 1) * TILE]
                if has_rest:
                    value = value + total[:, cols + rest * TILE : cols + (rest + 1) * TILE]
                qkv_ref[:, lanes] = value


def head_readers(qkv_ref, bias_ref, cos_ref, sin_ref):
    cosine = cos_ref[...]
    sine = sin_ref[...]

    def plain(start):
        return qkv_ref[:, start : start + HD] + bias_ref[:, start : start + HD]

    def rotated(start):
        head = plain(start)
        return head * cosine + pltpu.roll(head, HD // 2, 1) * sine

    return plain, rotated


def fresh_block(pieces):
    rows = sum(piece.shape[0] for piece in pieces)
    pad = jnp.zeros((128 - rows, HD), jnp.float32)
    return jnp.concatenate(list(pieces) + [pad], axis=0).astype(jnp.bfloat16)


GROUP = D // HD // KVH
KV_WIDTH = KVH * HD


def attend_main_kernel(len_ref, parts_ref, bias_ref, cos_ref, sin_ref, cache_ref, out_ref, kv_ref, qkv_ref, piece_ref):
    rows = qkv_ref.shape[0]
    qkv_ref[...] = jnp.zeros(qkv_ref.shape, jnp.float32)
    load_qkv(True, parts_ref, qkv_ref)
    plain, rotated = head_readers(qkv_ref, bias_ref, cos_ref, sin_ref)
    seen = lax.broadcasted_iota(jnp.int32, (1, cache_ref.shape[0]), 1) < len_ref[0]
    row = lax.broadcasted_iota(jnp.int32, (rows, 128), 0)
    col = lax.broadcasted_iota(jnp.int32, (rows, 128), 1)
    own = ((col <= row) & (col < STEPS)).astype(jnp.int32)
    fresh_seen = jnp.concatenate([own] * GROUP, axis=0) > 0
    for g in range(KVH):
        query = jnp.concatenate([rotated((g * GROUP + h) * HD) for h in range(GROUP)], axis=0).astype(jnp.bfloat16)
        fresh_key = rotated(D + g * HD)
        fresh_value = plain(D + KV_WIDTH + g * HD)
        kv_ref[:, g * HD : (g + 1) * HD] = fresh_key
        kv_ref[:, KV_WIDTH + g * HD : KV_WIDTH + (g + 1) * HD] = fresh_value
        key = cache_ref[:, g * HD : (g + 1) * HD]
        value = cache_ref[:, KV_WIDTH + g * HD : KV_WIDTH + (g + 1) * HD]
        mixed = head_attention(
            query, key, value, fresh_block([fresh_key]), fresh_block([fresh_value]), seen, fresh_seen
        )
        for h in range(GROUP):
            r, place = divmod(g * GROUP + h, FEATURES // HD)
            j, lane = place // 2, (place % 2) * HD
            for s in range(STEPS):
                at = s * 8 + j
                piece_ref[r, at : at + 1, lane : lane + HD] = mixed[h * rows + s : h * rows + s + 1]
    for r in range(ROW_BLOCKS):
        piece = piece_ref[r].astype(jnp.bfloat16)
        for c in range(COL_BLOCKS):
            out_ref[r * COL_BLOCKS + c] = piece


def attend_main(prefix_len, parts, bias, cosine, sine, cache):
    return pl.pallas_call(
        attend_main_kernel,
        out_shape=(
            jax.ShapeDtypeStruct((32, 16, TILE), jnp.bfloat16),
            jax.ShapeDtypeStruct((8, 2 * KV_WIDTH), jnp.float32),
        ),
        in_specs=[SMEM] + [VMEM] * 5,
        out_specs=(whole((32, 16, TILE)), whole((8, 2 * KV_WIDTH))),
        scratch_shapes=[
            pltpu.VMEM((8, QKV), jnp.float32),
            pltpu.VMEM((ROW_BLOCKS, 16, TILE), jnp.float32),
        ],
        compiler_params=kernel_params(),
        cost_estimate=cost(2 * 10**8, 6 * 10**6),
        name="attend_main",
    )(prefix_len, parts, bias, cosine, sine, cache)


def attend_cont_kernel(
    len_ref, bound_ref, parts_ref, bias_ref, cos_ref, sin_ref, cache_ref, kv_ref, out_ref, qkv_ref
):
    rows = qkv_ref.shape[0]
    load_qkv(False, parts_ref, qkv_ref)
    plain, rotated = head_readers(qkv_ref, bias_ref, cos_ref, sin_ref)
    seen = lax.broadcasted_iota(jnp.int32, (1, cache_ref.shape[0]), 1) < len_ref[0]
    row = lax.broadcasted_iota(jnp.int32, (rows, 128), 0)
    col = lax.broadcasted_iota(jnp.int32, (rows, 128), 1)
    own = (row // STEPS == col // STEPS) & (col <= row)
    main = (col >= rows) & (col < rows + bound_ref[0])
    fresh_seen = jnp.concatenate([(own | main).astype(jnp.int32)] * GROUP, axis=0) > 0
    for g in range(KVH):
        query = jnp.concatenate([rotated((g * GROUP + h) * HD) for h in range(GROUP)], axis=0).astype(jnp.bfloat16)
        at_key = slice(g * HD, (g + 1) * HD)
        at_value = slice(KV_WIDTH + g * HD, KV_WIDTH + (g + 1) * HD)
        fresh_key = fresh_block([rotated(D + g * HD), kv_ref[:, at_key]])
        fresh_value = fresh_block([plain(D + KV_WIDTH + g * HD), kv_ref[:, at_value]])
        mixed = head_attention(
            query, cache_ref[:, at_key], cache_ref[:, at_value], fresh_key, fresh_value, seen, fresh_seen
        )
        mixed = mixed.astype(jnp.bfloat16)
        for h in range(GROUP):
            out_ref[:, (g * GROUP + h) * HD : (g * GROUP + h + 1) * HD] = mixed[h * rows : (h + 1) * rows]


def attend_cont(*args):
    return pl.pallas_call(
        attend_cont_kernel,
        out_shape=jax.ShapeDtypeStruct((CTOK, D), jnp.bfloat16),
        in_specs=[SMEM, SMEM] + [VMEM] * 5 + [whole((8, 2 * KV_WIDTH))],
        out_specs=whole((CTOK, D)),
        scratch_shapes=[pltpu.VMEM((CTOK, QKV), jnp.float32)],
        compiler_params=kernel_params(),
        cost_estimate=cost(4 * 10**8, 8 * 10**6),
        name="attend_cont",
    )(*args)


def readout_kernel(head_ref, w_hbm, out_ref, w_ref, sem):
    copy = pltpu.make_async_copy(w_hbm.at[0], w_ref, sem)
    copy.start()
    row = head_ref[pl.ds(lax.rem(lax.axis_index("tp"), COL_BLOCKS), 1), :]
    high = row.astype(jnp.bfloat16).astype(jnp.float32)
    middle = (row - high).astype(jnp.bfloat16).astype(jnp.float32)
    low = row - high - middle
    pieces = jnp.concatenate([high, middle, low, jnp.zeros((13, row.shape[1]), jnp.float32)], axis=0)
    copy.wait()
    prod = lax.dot_general(
        pieces.astype(jnp.bfloat16), w_ref[...], (((1,), (1,)), ((), ())), preferred_element_type=jnp.float32
    )
    out_ref[...] = prod[0:1] + prod[1:2] + prod[2:3]


def readout(value_head, blocks):
    return pl.pallas_call(
        readout_kernel,
        out_shape=jax.ShapeDtypeStruct((1, FEATURES), jnp.float32),
        in_specs=[whole(value_head.shape), HBM],
        out_specs=whole((1, FEATURES)),
        scratch_shapes=[pltpu.VMEM((FEATURES, D // COL_BLOCKS), jnp.bfloat16), pltpu.SemaphoreType.DMA],
        compiler_params=kernel_params(),
        cost_estimate=cost(2 * 10**8, 5 * 10**6),
        name="readout",
    )(value_head, blocks)


def out_kernel(tiles, x_ref, read_ref, w_hbm, out_ref, rows_ref, wide_ref, read8_ref, w_ref, sems):
    n = pl.program_id(0)
    members = x_ref.shape[0]
    lines = members * STEPS
    halves = TILE // 128
    tile = weight_tile(n, tiles, w_hbm, w_ref, sems)

    @pl.when(n == 0)
    def _():
        for j in range(FEATURES // TILE):
            read8_ref[j : j + 1, :] = read_ref[:, j * TILE : (j + 1) * TILE]
        out_ref[:, 8:, :] = jnp.broadcast_to(read8_ref[...][None], (members, 8, TILE))
        packed = x_ref[...].reshape(members * 16, TILE).astype(jnp.float32)
        for k in range(halves):
            wide_ref[k] = packed[:, k * 128 : (k + 1) * 128]
            for j in range(FEATURES // TILE):
                lane = j * TILE + k * 128
                rows_ref[:, lane : lane + 128] = wide_ref[k, pl.ds(j, lines, stride=8), :].astype(jnp.bfloat16)

    tile.wait()
    prod = jnp.dot(rows_ref[...], w_ref[n], preferred_element_type=jnp.float32)
    for k in range(halves):
        wide_ref[k, pl.ds(n, lines, stride=4), :] = prod[:, k * 128 : (k + 1) * 128]

    @pl.when(n == tiles - 1)
    def _():
        for k in range(halves):
            packed = wide_ref[k, : members * 8, :].reshape(members, 8, 128)
            out_ref[:, :8, k * 128 : (k + 1) * 128] = packed


def out_product(rows, read, blocks):
    members = rows.shape[0]
    tiles = blocks.shape[2] // TILE
    return pl.pallas_call(
        functools.partial(out_kernel, tiles),
        out_shape=jax.ShapeDtypeStruct((members, 16, TILE), jnp.float32),
        grid=(tiles,),
        in_specs=[whole(rows.shape), whole(read.shape), HBM],
        out_specs=whole((members, 16, TILE)),
        scratch_shapes=[
            pltpu.VMEM((members * STEPS, FEATURES), jnp.bfloat16),
            pltpu.VMEM((TILE // 128, members * 16, 128), jnp.float32),
            pltpu.VMEM((8, TILE), jnp.float32),
            pltpu.VMEM((tiles, FEATURES, TILE), jnp.bfloat16),
            pltpu.SemaphoreType.DMA((tiles,)),
        ],
        compiler_params=kernel_params(),
        cost_estimate=cost(3 * 10**8, 5 * 10**6),
        name="out_product",
    )(rows, read, blocks)


def finish_kernel(parts_ref, main_ref, cont_ref, head_ref, mixed_ref, out_ref, score_ref, wide_ref):
    cols = D // COL_BLOCKS
    for c in range(COL_BLOCKS):
        total = summed_block(parts_ref, c, slice(0, TILE))
        for j in range(cols // TILE):
            at = slice(c * cols + j * TILE, c * cols + (j + 1) * TILE)
            for s in range(STEPS):
                wide_ref[s : s + 1, at] = total[s * 4 + j : s * 4 + j + 1]
    out_ref[...] = (main_ref[...].astype(jnp.float32) + wide_ref[:STEPS, :]).astype(jnp.bfloat16)
    score = jnp.zeros((CTOK, TILE), jnp.float32)
    direct = jnp.zeros((STEPS, TILE), jnp.float32)
    for r in range(ROW_BLOCKS):
        read = parts_ref[r * COL_BLOCKS, 8:, :]
        for c in range(1, COL_BLOCKS):
            read = read + parts_ref[r * COL_BLOCKS + c, 8:, :]
        for j in range(FEATURES // TILE):
            lanes = slice(r * FEATURES + j * TILE, r * FEATURES + (j + 1) * TILE)
            score = score + mixed_ref[:, lanes].astype(jnp.float32) * read[j : j + 1, :]
            for c in range(CONTS):
                direct = direct + cont_ref[c, :, lanes].astype(jnp.float32) * head_ref[:, lanes]
    total = jnp.sum(score, axis=0, keepdims=True) + jnp.sum(direct, axis=0, keepdims=True)
    score_ref[...] = jnp.broadcast_to(jnp.sum(total, axis=1, keepdims=True) / CONTS, (8, 128))


def finish(parts, main, cont, head, mixed):
    return pl.pallas_call(
        finish_kernel,
        out_shape=(
            jax.ShapeDtypeStruct((STEPS, D), jnp.bfloat16),
            jax.ShapeDtypeStruct((8, 128), jnp.float32),
        ),
        in_specs=[whole(parts.shape), VMEM, VMEM, VMEM, whole(mixed.shape)],
        out_specs=(whole((STEPS, D)), whole((8, 128))),
        scratch_shapes=[pltpu.VMEM((8, D), jnp.float32)],
        compiler_params=kernel_params(),
        cost_estimate=cost(10**6, 2 * 10**6),
        name="finish",
    )(parts, main, cont, head, mixed)


def rope_tables(positions):
    half = HD // 2
    frequency = THETA ** (-(jnp.arange(half, dtype=jnp.float32) * 2.0) / HD)
    angles = positions.astype(jnp.float32)[:, None] * frequency[None, :]
    cosine = jnp.cos(angles)
    sine = jnp.sin(angles)
    return jnp.concatenate([cosine, cosine], axis=1), jnp.concatenate([-sine, sine], axis=1)


def exchange(rows):
    return lax.all_to_all(rows, "tp", split_axis=0, concat_axis=0, tiled=True)


def on_device(
    main_inputs, cont_inputs, prefix_cache, prefix_len, boundary, rms_gain, qkv_bias, w_qkv, w_out, value_head
):
    main = main_inputs.reshape(STEPS, D)
    cont = cont_inputs.reshape(CONTS, STEPS, D)
    bias = qkv_bias[None, :]
    cache = prefix_cache[0]
    head = value_head[None, :]
    step = jnp.arange(CTOK, dtype=jnp.int32) % STEPS
    main_tables = rope_tables(prefix_len + step[:8])
    cont_tables = rope_tables(prefix_len + boundary + step)
    read = readout(value_head.reshape(COL_BLOCKS, D // COL_BLOCKS), w_out)
    sent = exchange(norm_rows(main, cont, rms_gain[None, :]))
    parts = exchange(block_product(sent, w_qkv, REST))
    mixed, main_kv = attend_main(prefix_len, parts, bias, *main_tables, cache)
    mixed = exchange(mixed)
    cont_mixed = attend_cont(prefix_len, boundary, parts, bias, *cont_tables, cache, main_kv)
    parts = exchange(out_product(mixed, read, w_out))
    main_out, score = finish(parts, main, cont, head, cont_mixed)
    return main_out[None], score[0, :1]


def solution(mesh):
    return jax.shard_map(
        on_device,
        mesh=mesh,
        in_specs=(
            P(("grp", "tp"), None, None),
            P(("grp", "tp"), None, None, None),
            P(("grp", "tp"), None, None),
            P(("grp", "tp")),
            P(("grp", "tp")),
            P(),
            P(),
            P("tp", None, None),
            P("tp", None, None),
            P(),
        ),
        out_specs=(P(("grp", "tp"), None, None), P(("grp", "tp"))),
        check_vma=False,
    )
```

```python
import functools
import math

import jax
import jax.numpy as jnp
from jax import lax
from jax.experimental import pallas as pl
from jax.experimental.pallas import tpu as pltpu
from jax.sharding import PartitionSpec as P

KVH = 8
HD = 128
D = 8192
QKV = 10240
ROW_BLOCKS = 4
COL_BLOCKS = 8
MEMBERS = ROW_BLOCKS * COL_BLOCKS
FEATURES = D // ROW_BLOCKS
CONTS = 8
STEPS = 2
CTOK = CONTS * STEPS
TILE = 256

THETA = 1000000.0
EPS = 1e-06
MASKED_SCORE = -1e30

VMEM_LIMIT = 48 * 1024 * 1024
VMEM_MOST = 60 * 1024 * 1024
VMEM_LESS = 32 * 1024 * 1024
VMEM = pl.BlockSpec(memory_space=pltpu.VMEM)
SMEM = pl.BlockSpec(memory_space=pltpu.SMEM)
HBM = pl.BlockSpec(memory_space=pltpu.HBM)


def whole(shape):
    return pl.BlockSpec(shape, lambda *_: (0,) * len(shape))


def cost(flops, moved):
    return pl.CostEstimate(flops=flops, bytes_accessed=moved, transcendentals=0)


def kernel_params(limit=VMEM_LIMIT):
    return pltpu.CompilerParams(vmem_limit_bytes=limit)


def norm_kernel(main_hbm, cont_hbm, gain_hbm, out_ref, main_ref, cont_ref, gain_ref, rows_ref, piece_ref, sems):
    pairs = ((main_hbm, main_ref), (cont_hbm, cont_ref), (gain_hbm, gain_ref))
    copies = [pltpu.make_async_copy(src, dst, sems.at[i]) for i, (src, dst) in enumerate(pairs)]
    for copy in copies:
        copy.start()
    for copy in copies:
        copy.wait()

    def normed(wide):
        inv = lax.rsqrt(jnp.mean(wide * wide, axis=-1, keepdims=True) + EPS)
        return wide * inv * gain_ref[...]

    for c in range(CONTS):
        rows_ref[c * STEPS : (c + 1) * STEPS, :] = cont_ref[c].astype(jnp.float32)
    cont = normed(rows_ref[...]).astype(jnp.bfloat16)
    main = normed(main_ref[...].astype(jnp.float32))
    for r in range(ROW_BLOCKS):
        for j in range(FEATURES // TILE):
            lanes = slice(r * FEATURES + j * TILE, r * FEATURES + (j + 1) * TILE)
            for s in range(STEPS):
                piece_ref[r, s * 8 + j : s * 8 + j + 1, :] = main[s : s + 1, lanes]
    for r in range(ROW_BLOCKS):
        piece = piece_ref[r].astype(jnp.bfloat16)
        out_ref[r, :, :FEATURES] = cont[:, r * FEATURES : (r + 1) * FEATURES]
        out_ref[r, :, FEATURES:] = piece


def norm_rows(main, cont, gain):
    return pl.pallas_call(
        norm_kernel,
        out_shape=jax.ShapeDtypeStruct((ROW_BLOCKS, CTOK, FEATURES + TILE), jnp.bfloat16),
        in_specs=[HBM] * 3,
        out_specs=VMEM,
        scratch_shapes=[
            pltpu.VMEM((STEPS, D), jnp.bfloat16),
            pltpu.VMEM((CONTS, STEPS, D), jnp.bfloat16),
            pltpu.VMEM((1, D), jnp.float32),
            pltpu.VMEM((CTOK, D), jnp.float32),
            pltpu.VMEM((ROW_BLOCKS, 16, TILE), jnp.float32),
            pltpu.SemaphoreType.DMA((3,)),
        ],
        compiler_params=kernel_params(),
        cost_estimate=cost(10**6, 4 * 10**6),
        name="norm_rows",
    )(main, cont, gain)


def weight_tile(n, tiles, w_hbm, w_ref, sems):
    def copy(i):
        lanes = pl.ds(pl.multiple_of(i * TILE, TILE), TILE)
        return pltpu.make_async_copy(w_hbm.at[0, :, lanes], w_ref.at[i], sems.at[i])

    @pl.when(n == 0)
    def _():
        for i in range(tiles):
            copy(i).start()

    return copy(n)


REST = 768


def rest_tile(block):
    return jnp.where(block == 6, 2, 0)


def product_kernel(tiles, counts, places, *refs):
    x_refs = refs[: len(counts)]
    refs = refs[len(counts) :]
    if places:
        earlier_ref, w_hbm, out_ref, rows_ref, wide_ref, w_ref, sems, part_ref = refs
    else:
        w_hbm, part_ref, rows_ref, wide_ref, w_ref, sems = refs
    n = pl.program_id(0)
    members = sum(counts)
    count = members * CTOK
    lines = members * STEPS
    halves = TILE // 128
    width = tiles * TILE
    tile = weight_tile(n, tiles, w_hbm, w_ref, sems)

    @pl.when(n == 0)
    def _():
        at = 0
        for x_ref, size in zip(x_refs, counts):
            rows = slice(at * CTOK, (at + size) * CTOK)
            rows_ref[rows, :] = x_ref[:, :, :FEATURES].reshape(size * CTOK, FEATURES)
            packed = x_ref[:, :, FEATURES:].reshape(size * CTOK, TILE).astype(jnp.float32)
            for k in range(halves):
                wide_ref[k, rows, :] = packed[:, k * 128 : (k + 1) * 128]
            at += size
        for k in range(halves):
            for j in range(FEATURES // TILE):
                lane = j * TILE + k * 128
                rows_ref[count:, lane : lane + 128] = wide_ref[k, pl.ds(j, lines, stride=8), :].astype(jnp.bfloat16)

    tile.wait()
    prod = jnp.dot(rows_ref[...], w_ref[n], preferred_element_type=jnp.float32)
    high = prod.astype(jnp.bfloat16)
    part_ref[:, :, pl.ds(pl.multiple_of(n * TILE, TILE), TILE)] = high[:count].reshape(members, CTOK, TILE)
    for k in range(halves):
        wide_ref[k, pl.ds(n, lines, stride=8), :] = prod[count:, k * 128 : (k + 1) * 128]
    start = rest_tile(lax.rem(lax.axis_index("tp"), COL_BLOCKS))

    @pl.when((n >= start) & (n < start + REST // TILE))
    def _():
        low = prod - high.astype(jnp.float32)
        place = n - start
        lane = pl.multiple_of(width + place * TILE, TILE)
        part_ref[:, :, pl.ds(lane, TILE)] = low[:count].astype(jnp.bfloat16).reshape(members, CTOK, TILE)
        for k in range(halves):
            wide_ref[k, pl.ds(tiles + place, lines, stride=8), :] = low[count:, k * 128 : (k + 1) * 128]

    @pl.when(n == tiles - 1)
    def _():
        for k in range(halves):
            lane = width + REST + k * 128
            part_ref[:, :, lane : lane + 128] = wide_ref[k].astype(jnp.bfloat16).reshape(members, CTOK, 128)
        if places:
            me = lax.rem(lax.axis_index("tp"), COL_BLOCKS)
            y, x = me // 4, lax.rem(me, 4)
            done = earlier_ref.shape[0] // ROW_BLOCKS
            for i, (dy, dx) in enumerate(places):
                column = lax.rem(y + dy, 2) * 4 + lax.rem(x + dx, 4)
                for z in range(ROW_BLOCKS):
                    if i < done:
                        message = earlier_ref[i * ROW_BLOCKS + z]
                    else:
                        message = part_ref[(i - done) * ROW_BLOCKS + z]
                    out_ref[z * COL_BLOCKS + column] = message


def block_product(messages, blocks, earlier=None, places=()):
    tiles = blocks.shape[2] // TILE
    lanes = (tiles + 1) * TILE + REST
    counts = tuple(rows.shape[0] for rows in messages)
    members = sum(counts)
    part = (members, CTOK, lanes)
    scratch = [
        pltpu.VMEM((members * (CTOK + STEPS), FEATURES), jnp.bfloat16),
        pltpu.VMEM((TILE // 128, members * CTOK, 128), jnp.float32),
        pltpu.VMEM((tiles, FEATURES, TILE), jnp.bfloat16),
        pltpu.SemaphoreType.DMA((tiles,)),
    ]
    operands = list(messages)
    out = part
    if places:
        operands.append(earlier)
        out = (MEMBERS, CTOK, lanes)
        scratch.append(pltpu.VMEM(part, jnp.bfloat16))
    return pl.pallas_call(
        functools.partial(product_kernel, tiles, counts, places),
        out_shape=jax.ShapeDtypeStruct(out, jnp.bfloat16),
        grid=(tiles,),
        in_specs=[VMEM] * len(operands) + [HBM],
        out_specs=whole(out) if places else VMEM,
        scratch_shapes=scratch,
        compiler_params=kernel_params(VMEM_LESS),
        cost_estimate=cost(2 * members * (CTOK + STEPS) * FEATURES * tiles * TILE, 12 * 10**6),
        name="block_product",
    )(*operands, blocks)


def summed_block(parts_ref, c, lanes):
    total = parts_ref[c, :, lanes].astype(jnp.float32)
    for r in range(1, ROW_BLOCKS):
        total = total + parts_ref[r * COL_BLOCKS + c, :, lanes].astype(jnp.float32)
    return total


def head_attention(query, key, value, fresh_key, fresh_value, seen, fresh_seen):
    inv_root = 1.0 / math.sqrt(HD)
    contract = (((1,), (1,)), ((), ()))
    old = lax.dot_general(query, key, contract, preferred_element_type=jnp.float32) * inv_root
    new = lax.dot_general(query, fresh_key, contract, preferred_element_type=jnp.float32) * inv_root
    old = jnp.where(seen, old, MASKED_SCORE)
    new = jnp.where(fresh_seen, new, MASKED_SCORE)
    highest = jnp.maximum(jnp.max(old, axis=-1, keepdims=True), jnp.max(new, axis=-1, keepdims=True))
    old = jnp.exp(old - highest)
    new = jnp.exp(new - highest)
    mass = jnp.sum(old, axis=-1, keepdims=True) + jnp.sum(new, axis=-1, keepdims=True)
    inv_mass = 1.0 / mass
    mixed = jnp.dot((old * inv_mass).astype(jnp.bfloat16), value, preferred_element_type=jnp.float32)
    return mixed + jnp.dot((new * inv_mass).astype(jnp.bfloat16), fresh_value, preferred_element_type=jnp.float32)


def load_qkv(main, parts_ref, qkv_ref):
    cols = QKV // COL_BLOCKS
    for c in range(COL_BLOCKS):
        first = 2 if c == 6 else 0
        if main:
            total = summed_block(parts_ref, c, slice(cols + REST, cols + REST + TILE))
        else:
            total = summed_block(parts_ref, c, slice(0, cols + REST))
        for j in range(cols // TILE):
            lanes = slice(c * cols + j * TILE, c * cols + (j + 1) * TILE)
            rest = j - first
            has_rest = 0 <= rest < REST // TILE
            if main:
                for s in range(STEPS):
                    line = total[s * 8 + j : s * 8 + j + 1]
                    if has_rest:
                        at = s * 8 + cols // TILE + rest
                        line = line + total[at : at + 1]
                    qkv_ref[s : s + 1, lanes] = line
            else:
                value = total[:, j * TILE : (j + 1) * TILE]
                if has_rest:
                    value = value + total[:, cols + rest * TILE : cols + (rest + 1) * TILE]
                qkv_ref[:, lanes] = value


def head_readers(qkv_ref, bias_ref, cos_ref, sin_ref):
    cosine = cos_ref[...]
    sine = sin_ref[...]

    def plain(start):
        return qkv_ref[:, start : start + HD] + bias_ref[:, start : start + HD]

    def rotated(start):
        head = plain(start)
        return head * cosine + pltpu.roll(head, HD // 2, 1) * sine

    return plain, rotated


def fresh_block(pieces):
    rows = sum(piece.shape[0] for piece in pieces)
    pad = jnp.zeros((128 - rows, HD), jnp.float32)
    return jnp.concatenate(list(pieces) + [pad], axis=0).astype(jnp.bfloat16)


GROUP = D // HD // KVH
KV_WIDTH = KVH * HD


def attend_main_kernel(len_ref, parts_ref, bias_ref, cos_ref, sin_ref, cache_ref, out_ref, kv_ref, qkv_ref, piece_ref):
    rows = qkv_ref.shape[0]
    qkv_ref[...] = jnp.zeros(qkv_ref.shape, jnp.float32)
    load_qkv(True, parts_ref, qkv_ref)
    plain, rotated = head_readers(qkv_ref, bias_ref, cos_ref, sin_ref)
    seen = lax.broadcasted_iota(jnp.int32, (1, cache_ref.shape[0]), 1) < len_ref[0]
    row = lax.broadcasted_iota(jnp.int32, (rows, 128), 0)
    col = lax.broadcasted_iota(jnp.int32, (rows, 128), 1)
    own = ((col <= row) & (col < STEPS)).astype(jnp.int32)
    fresh_seen = jnp.concatenate([own] * GROUP, axis=0) > 0
    for g in range(KVH):
        query = jnp.concatenate([rotated((g * GROUP + h) * HD) for h in range(GROUP)], axis=0).astype(jnp.bfloat16)
        fresh_key = rotated(D + g * HD)
        fresh_value = plain(D + KV_WIDTH + g * HD)
        kv_ref[:, g * HD : (g + 1) * HD] = fresh_key
        kv_ref[:, KV_WIDTH + g * HD : KV_WIDTH + (g + 1) * HD] = fresh_value
        key = cache_ref[:, g * HD : (g + 1) * HD]
        value = cache_ref[:, KV_WIDTH + g * HD : KV_WIDTH + (g + 1) * HD]
        mixed = head_attention(
            query, key, value, fresh_block([fresh_key]), fresh_block([fresh_value]), seen, fresh_seen
        )
        for h in range(GROUP):
            r, place = divmod(g * GROUP + h, FEATURES // HD)
            j, lane = place // 2, (place % 2) * HD
            for s in range(STEPS):
                at = s * 8 + j
                piece_ref[r, at : at + 1, lane : lane + HD] = mixed[h * rows + s : h * rows + s + 1]
    for r in range(ROW_BLOCKS):
        piece = piece_ref[r].astype(jnp.bfloat16)
        for c in range(COL_BLOCKS):
            out_ref[r * COL_BLOCKS + c] = piece


def attend_main(prefix_len, parts, bias, cosine, sine, cache):
    return pl.pallas_call(
        attend_main_kernel,
        out_shape=(
            jax.ShapeDtypeStruct((32, 16, TILE), jnp.bfloat16),
            jax.ShapeDtypeStruct((8, 2 * KV_WIDTH), jnp.float32),
        ),
        in_specs=[SMEM] + [VMEM] * 5,
        out_specs=(whole((32, 16, TILE)), whole((8, 2 * KV_WIDTH))),
        scratch_shapes=[
            pltpu.VMEM((8, QKV), jnp.float32),
            pltpu.VMEM((ROW_BLOCKS, 16, TILE), jnp.float32),
        ],
        compiler_params=kernel_params(),
        cost_estimate=cost(2 * 10**8, 6 * 10**6),
        name="attend_main",
    )(prefix_len, parts, bias, cosine, sine, cache)


def attend_cont_kernel(
    len_ref, bound_ref, parts_ref, bias_ref, cos_ref, sin_ref, cache_ref, kv_ref, out_ref, qkv_ref
):
    rows = qkv_ref.shape[0]
    load_qkv(False, parts_ref, qkv_ref)
    plain, rotated = head_readers(qkv_ref, bias_ref, cos_ref, sin_ref)
    seen = lax.broadcasted_iota(jnp.int32, (1, cache_ref.shape[0]), 1) < len_ref[0]
    row = lax.broadcasted_iota(jnp.int32, (rows, 128), 0)
    col = lax.broadcasted_iota(jnp.int32, (rows, 128), 1)
    own = (row // STEPS == col // STEPS) & (col <= row)
    main = (col >= rows) & (col < rows + bound_ref[0])
    fresh_seen = jnp.concatenate([(own | main).astype(jnp.int32)] * GROUP, axis=0) > 0
    for g in range(KVH):
        query = jnp.concatenate([rotated((g * GROUP + h) * HD) for h in range(GROUP)], axis=0).astype(jnp.bfloat16)
        at_key = slice(g * HD, (g + 1) * HD)
        at_value = slice(KV_WIDTH + g * HD, KV_WIDTH + (g + 1) * HD)
        fresh_key = fresh_block([rotated(D + g * HD), kv_ref[:, at_key]])
        fresh_value = fresh_block([plain(D + KV_WIDTH + g * HD), kv_ref[:, at_value]])
        mixed = head_attention(
            query, cache_ref[:, at_key], cache_ref[:, at_value], fresh_key, fresh_value, seen, fresh_seen
        )
        mixed = mixed.astype(jnp.bfloat16)
        for h in range(GROUP):
            out_ref[:, (g * GROUP + h) * HD : (g * GROUP + h + 1) * HD] = mixed[h * rows : (h + 1) * rows]


def attend_cont(*args):
    return pl.pallas_call(
        attend_cont_kernel,
        out_shape=jax.ShapeDtypeStruct((CTOK, D), jnp.bfloat16),
        in_specs=[SMEM, SMEM] + [VMEM] * 5 + [whole((8, 2 * KV_WIDTH))],
        out_specs=whole((CTOK, D)),
        scratch_shapes=[pltpu.VMEM((CTOK, QKV), jnp.float32)],
        compiler_params=kernel_params(),
        cost_estimate=cost(4 * 10**8, 8 * 10**6),
        name="attend_cont",
    )(*args)


def readout_kernel(head_ref, w_hbm, out_ref, w_ref, sem):
    copy = pltpu.make_async_copy(w_hbm.at[0], w_ref, sem)
    copy.start()
    row = head_ref[pl.ds(lax.rem(lax.axis_index("tp"), COL_BLOCKS), 1), :]
    high = row.astype(jnp.bfloat16).astype(jnp.float32)
    middle = (row - high).astype(jnp.bfloat16).astype(jnp.float32)
    low = row - high - middle
    pieces = jnp.concatenate([high, middle, low, jnp.zeros((13, row.shape[1]), jnp.float32)], axis=0)
    copy.wait()
    prod = lax.dot_general(
        pieces.astype(jnp.bfloat16), w_ref[...], (((1,), (1,)), ((), ())), preferred_element_type=jnp.float32
    )
    out_ref[...] = prod[0:1] + prod[1:2] + prod[2:3]


def readout(value_head, blocks):
    return pl.pallas_call(
        readout_kernel,
        out_shape=jax.ShapeDtypeStruct((1, FEATURES), jnp.float32),
        in_specs=[whole(value_head.shape), HBM],
        out_specs=whole((1, FEATURES)),
        scratch_shapes=[pltpu.VMEM((FEATURES, D // COL_BLOCKS), jnp.bfloat16), pltpu.SemaphoreType.DMA],
        compiler_params=kernel_params(),
        cost_estimate=cost(2 * 10**8, 5 * 10**6),
        name="readout",
    )(value_head, blocks)


def out_kernel(tiles, x_ref, read_ref, w_hbm, out_ref, rows_ref, wide_ref, read8_ref, w_ref, sems):
    n = pl.program_id(0)
    members = x_ref.shape[0]
    lines = members * STEPS
    halves = TILE // 128
    tile = weight_tile(n, tiles, w_hbm, w_ref, sems)

    @pl.when(n == 0)
    def _():
        for j in range(FEATURES // TILE):
            read8_ref[j : j + 1, :] = read_ref[:, j * TILE : (j + 1) * TILE]
        out_ref[:, 8:, :] = jnp.broadcast_to(read8_ref[...][None], (members, 8, TILE))
        packed = x_ref[...].reshape(members * 16, TILE).astype(jnp.float32)
        for k in range(halves):
            wide_ref[k] = packed[:, k * 128 : (k + 1) * 128]
            for j in range(FEATURES // TILE):
                lane = j * TILE + k * 128
                rows_ref[:, lane : lane + 128] = wide_ref[k, pl.ds(j, lines, stride=8), :].astype(jnp.bfloat16)

    tile.wait()
    prod = jnp.dot(rows_ref[...], w_ref[n], preferred_element_type=jnp.float32)
    for k in range(halves):
        wide_ref[k, pl.ds(n, lines, stride=4), :] = prod[:, k * 128 : (k + 1) * 128]

    @pl.when(n == tiles - 1)
    def _():
        for k in range(halves):
            packed = wide_ref[k, : members * 8, :].reshape(members, 8, 128)
            out_ref[:, :8, k * 128 : (k + 1) * 128] = packed


def out_product(rows, read, blocks):
    members = rows.shape[0]
    tiles = blocks.shape[2] // TILE
    return pl.pallas_call(
        functools.partial(out_kernel, tiles),
        out_shape=jax.ShapeDtypeStruct((members, 16, TILE), jnp.float32),
        grid=(tiles,),
        in_specs=[whole(rows.shape), whole(read.shape), HBM],
        out_specs=whole((members, 16, TILE)),
        scratch_shapes=[
            pltpu.VMEM((members * STEPS, FEATURES), jnp.bfloat16),
            pltpu.VMEM((TILE // 128, members * 16, 128), jnp.float32),
            pltpu.VMEM((8, TILE), jnp.float32),
            pltpu.VMEM((tiles, FEATURES, TILE), jnp.bfloat16),
            pltpu.SemaphoreType.DMA((tiles,)),
        ],
        compiler_params=kernel_params(VMEM_MOST),
        cost_estimate=cost(3 * 10**8, 5 * 10**6),
        name="out_product",
    )(rows, read, blocks)


def finish_kernel(parts_ref, main_ref, cont_ref, head_ref, mixed_ref, out_ref, score_ref, wide_ref):
    cols = D // COL_BLOCKS
    for c in range(COL_BLOCKS):
        total = summed_block(parts_ref, c, slice(0, TILE))
        for j in range(cols // TILE):
            at = slice(c * cols + j * TILE, c * cols + (j + 1) * TILE)
            for s in range(STEPS):
                wide_ref[s : s + 1, at] = total[s * 4 + j : s * 4 + j + 1]
    out_ref[...] = (main_ref[...].astype(jnp.float32) + wide_ref[:STEPS, :]).astype(jnp.bfloat16)
    score = jnp.zeros((CTOK, TILE), jnp.float32)
    direct = jnp.zeros((STEPS, TILE), jnp.float32)
    for r in range(ROW_BLOCKS):
        read = parts_ref[r * COL_BLOCKS, 8:, :]
        for c in range(1, COL_BLOCKS):
            read = read + parts_ref[r * COL_BLOCKS + c, 8:, :]
        for j in range(FEATURES // TILE):
            lanes = slice(r * FEATURES + j * TILE, r * FEATURES + (j + 1) * TILE)
            score = score + mixed_ref[:, lanes].astype(jnp.float32) * read[j : j + 1, :]
            for c in range(CONTS):
                direct = direct + cont_ref[c, :, lanes].astype(jnp.float32) * head_ref[:, lanes]
    total = jnp.sum(score, axis=0, keepdims=True) + jnp.sum(direct, axis=0, keepdims=True)
    score_ref[...] = jnp.broadcast_to(jnp.sum(total, axis=1, keepdims=True) / CONTS, (8, 128))


def finish(parts, main, cont, head, mixed):
    return pl.pallas_call(
        finish_kernel,
        out_shape=(
            jax.ShapeDtypeStruct((STEPS, D), jnp.bfloat16),
            jax.ShapeDtypeStruct((8, 128), jnp.float32),
        ),
        in_specs=[whole(parts.shape), whole(main.shape), whole(cont.shape), whole(head.shape), whole(mixed.shape)],
        out_specs=(whole((STEPS, D)), whole((8, 128))),
        scratch_shapes=[pltpu.VMEM((8, D), jnp.float32)],
        compiler_params=kernel_params(VMEM_MOST),
        cost_estimate=cost(10**6, 2 * 10**6),
        name="finish",
    )(parts, main, cont, head, mixed)


def rope_tables(positions):
    half = HD // 2
    frequency = THETA ** (-(jnp.arange(half, dtype=jnp.float32) * 2.0) / HD)
    angles = positions.astype(jnp.float32)[:, None] * frequency[None, :]
    cosine = jnp.cos(angles)
    sine = jnp.sin(angles)
    return jnp.concatenate([cosine, cosine], axis=1), jnp.concatenate([-sine, sine], axis=1)


def exchange(rows):
    return lax.all_to_all(rows, "tp", split_axis=0, concat_axis=0, tiled=True)


ALONG = [[z * COL_BLOCKS + c for z in range(ROW_BLOCKS)] for c in range(COL_BLOCKS)]


def from_side(rows, dy, dx):
    route = []
    for to in range(MEMBERS):
        z, y, x = to // 8, to // 4 % 2, to % 4
        route.append((z * 8 + (y + dy) % 2 * 4 + (x + dx) % 4, to))
    return lax.ppermute(rows, "tp", route)


def forward_product(rows, blocks):
    near = lax.all_to_all(rows, "tp", split_axis=0, concat_axis=0, tiled=True, axis_index_groups=ALONG)
    half = ROW_BLOCKS // 2
    over = from_side(near, 1, 0)
    here, far, places = [], [], []
    for dy, mine in ((0, near), (1, over)):
        after = from_side(mine, 0, 1)
        before = from_side(mine, 0, 3)
        far += [from_side(before[:half], 0, 3), from_side(after[half:], 0, 1)]
        here += [mine, after, before]
        places += [(dy, 0), (dy, 1), (dy, 3)]
    earlier = block_product(here, blocks)
    return block_product(far, blocks, earlier, tuple(places) + ((0, 2), (1, 2)))


def on_device(
    main_inputs, cont_inputs, prefix_cache, prefix_len, boundary, rms_gain, qkv_bias, w_qkv, w_out, value_head
):
    main = main_inputs.reshape(STEPS, D)
    cont = cont_inputs.reshape(CONTS, STEPS, D)
    bias = qkv_bias[None, :]
    cache = prefix_cache[0]
    head = value_head[None, :]
    step = jnp.arange(CTOK, dtype=jnp.int32) % STEPS
    main_tables = rope_tables(prefix_len + step[:8])
    cont_tables = rope_tables(prefix_len + boundary + step)
    read = readout(value_head.reshape(COL_BLOCKS, D // COL_BLOCKS), w_out)
    parts = exchange(forward_product(norm_rows(main, cont, rms_gain[None, :]), w_qkv))
    mixed, main_kv = attend_main(prefix_len, parts, bias, *main_tables, cache)
    mixed = exchange(mixed)
    cont_mixed = attend_cont(prefix_len, boundary, parts, bias, *cont_tables, cache, main_kv)
    mixed, cont_mixed, read = lax.optimization_barrier((mixed, cont_mixed, read))
    parts = exchange(out_product(mixed, read, w_out))
    main_out, score = finish(parts, main, cont, head, cont_mixed)
    return main_out[None], score[0, :1]


def solution(mesh):
    return jax.shard_map(
        on_device,
        mesh=mesh,
        in_specs=(
            P(("grp", "tp"), None, None),
            P(("grp", "tp"), None, None, None),
            P(("grp", "tp"), None, None),
            P(("grp", "tp")),
            P(("grp", "tp")),
            P(),
            P(),
            P("tp", None, None),
            P("tp", None, None),
            P(),
        ),
        out_specs=(P(("grp", "tp"), None, None), P(("grp", "tp"))),
        check_vma=False,
    )
```

```python
import functools
import math

import jax
import jax.numpy as jnp
from jax import lax
from jax.experimental import pallas as pl
from jax.experimental.pallas import tpu as pltpu
from jax.sharding import PartitionSpec as P

KVH = 8
HD = 128
D = 8192
QKV = 10240
ROW_BLOCKS = 4
COL_BLOCKS = 8
MEMBERS = ROW_BLOCKS * COL_BLOCKS
FEATURES = D // ROW_BLOCKS
CONTS = 8
STEPS = 2
CTOK = CONTS * STEPS
TILE = 256

THETA = 1000000.0
EPS = 1e-06
MASKED_SCORE = -1e30

VMEM_LIMIT = 32 * 1024 * 1024
VMEM = pl.BlockSpec(memory_space=pltpu.VMEM)
SMEM = pl.BlockSpec(memory_space=pltpu.SMEM)
HBM = pl.BlockSpec(memory_space=pltpu.HBM)


def whole(shape):
    return pl.BlockSpec(shape, lambda *_: (0,) * len(shape))


def cost(flops, moved):
    return pl.CostEstimate(flops=flops, bytes_accessed=moved, transcendentals=0)


def in_hbm(array):
    return pltpu.with_memory_space_constraint(array, pltpu.HBM)


def kernel_params():
    return pltpu.CompilerParams(vmem_limit_bytes=VMEM_LIMIT)


def norm_kernel(main_hbm, cont_hbm, gain_hbm, out_ref, main_ref, cont_ref, gain_ref, rows_ref, piece_ref, sems):
    pairs = ((main_hbm, main_ref), (cont_hbm, cont_ref), (gain_hbm, gain_ref))
    copies = [pltpu.make_async_copy(src, dst, sems.at[i]) for i, (src, dst) in enumerate(pairs)]
    for copy in copies:
        copy.start()
    for copy in copies:
        copy.wait()

    def normed(wide):
        inv = lax.rsqrt(jnp.mean(wide * wide, axis=-1, keepdims=True) + EPS)
        return wide * inv * gain_ref[...]

    for c in range(CONTS):
        rows_ref[c * STEPS : (c + 1) * STEPS, :] = cont_ref[c].astype(jnp.float32)
    cont = normed(rows_ref[...]).astype(jnp.bfloat16)
    main = normed(main_ref[...].astype(jnp.float32))
    for r in range(ROW_BLOCKS):
        for j in range(FEATURES // TILE):
            lanes = slice(r * FEATURES + j * TILE, r * FEATURES + (j + 1) * TILE)
            for s in range(STEPS):
                piece_ref[r, s * 8 + j : s * 8 + j + 1, :] = main[s : s + 1, lanes]
    for r in range(ROW_BLOCKS):
        piece = piece_ref[r].astype(jnp.bfloat16)
        out_ref[r, :, :FEATURES] = cont[:, r * FEATURES : (r + 1) * FEATURES]
        out_ref[r, :, FEATURES:] = piece


def norm_rows(main, cont, gain):
    return pl.pallas_call(
        norm_kernel,
        out_shape=jax.ShapeDtypeStruct((ROW_BLOCKS, CTOK, FEATURES + TILE), jnp.bfloat16),
        in_specs=[HBM] * 3,
        out_specs=VMEM,
        scratch_shapes=[
            pltpu.VMEM((STEPS, D), jnp.bfloat16),
            pltpu.VMEM((CONTS, STEPS, D), jnp.bfloat16),
            pltpu.VMEM((1, D), jnp.float32),
            pltpu.VMEM((CTOK, D), jnp.float32),
            pltpu.VMEM((ROW_BLOCKS, 16, TILE), jnp.float32),
            pltpu.SemaphoreType.DMA((3,)),
        ],
        compiler_params=kernel_params(),
        cost_estimate=cost(10**6, 4 * 10**6),
        name="norm_rows",
    )(in_hbm(main), in_hbm(cont), in_hbm(gain))


def weight_tile(n, tiles, w_hbm, w_ref, sems):
    def copy(i):
        lanes = pl.ds(pl.multiple_of(i * TILE, TILE), TILE)
        return pltpu.make_async_copy(w_hbm.at[0, :, lanes], w_ref.at[i], sems.at[i])

    @pl.when(n == 0)
    def _():
        for i in range(tiles):
            copy(i).start()

    return copy(n)


REST = 768


def rest_tile(block):
    return jnp.where(block == 6, 2, 0)


def plane_place():
    column = lax.rem(lax.axis_index("tp"), COL_BLOCKS)
    return column // 4, lax.rem(column, 4)


def product_kernel(tiles, counts, *refs):
    x_refs = refs[: len(counts)]
    w_hbm, *out_refs = refs[len(counts) : len(counts) + 1 + ROW_BLOCKS]
    rows_ref, wide_ref, w_ref, sems, part_ref = refs[len(counts) + 1 + ROW_BLOCKS :]
    n = pl.program_id(0)
    members = sum(counts)
    count = members * CTOK
    lines = members * STEPS
    halves = TILE // 128
    width = tiles * TILE
    tile = weight_tile(n, tiles, w_hbm, w_ref, sems)

    @pl.when(n == 0)
    def _():
        at = 0
        for x_ref, size in zip(x_refs, counts):
            rows = slice(at * CTOK, (at + size) * CTOK)
            rows_ref[rows, :] = x_ref[:, :, :FEATURES].reshape(size * CTOK, FEATURES)
            packed = x_ref[:, :, FEATURES:].reshape(size * CTOK, TILE).astype(jnp.float32)
            for k in range(halves):
                wide_ref[k, rows, :] = packed[:, k * 128 : (k + 1) * 128]
            at += size
        for k in range(halves):
            for j in range(FEATURES // TILE):
                lane = j * TILE + k * 128
                rows_ref[count:, lane : lane + 128] = wide_ref[k, pl.ds(j, lines, stride=8), :].astype(jnp.bfloat16)

    tile.wait()
    prod = jnp.dot(rows_ref[...], w_ref[n], preferred_element_type=jnp.float32)
    high = prod.astype(jnp.bfloat16)
    part_ref[:, :, pl.ds(pl.multiple_of(n * TILE, TILE), TILE)] = high[:count].reshape(members, CTOK, TILE)
    for k in range(halves):
        wide_ref[k, pl.ds(n, lines, stride=8), :] = prod[count:, k * 128 : (k + 1) * 128]
    start = rest_tile(lax.rem(lax.axis_index("tp"), COL_BLOCKS))

    @pl.when((n >= start) & (n < start + REST // TILE))
    def _():
        low = prod - high.astype(jnp.float32)
        place = n - start
        lane = pl.multiple_of(width + place * TILE, TILE)
        part_ref[:, :, pl.ds(lane, TILE)] = low[:count].astype(jnp.bfloat16).reshape(members, CTOK, TILE)
        for k in range(halves):
            wide_ref[k, pl.ds(tiles + place, lines, stride=8), :] = low[count:, k * 128 : (k + 1) * 128]

    @pl.when(n == tiles - 1)
    def _():
        for k in range(halves):
            lane = width + REST + k * 128
            part_ref[:, :, lane : lane + 128] = wide_ref[k].astype(jnp.bfloat16).reshape(members, CTOK, 128)
        z = lax.axis_index("tp") // COL_BLOCKS
        for k, out_ref in enumerate(out_refs):
            to = lax.rem(z + k, ROW_BLOCKS)
            for g in range(members // ROW_BLOCKS):
                out_ref[g] = part_ref[g * ROW_BLOCKS + to]


def block_product(messages, blocks):
    tiles = blocks.shape[2] // TILE
    lanes = (tiles + 1) * TILE + REST
    counts = tuple(rows.shape[0] for rows in messages)
    members = sum(counts)
    return pl.pallas_call(
        functools.partial(product_kernel, tiles, counts),
        out_shape=[jax.ShapeDtypeStruct((members // ROW_BLOCKS, CTOK, lanes), jnp.bfloat16)] * ROW_BLOCKS,
        grid=(tiles,),
        in_specs=[VMEM] * len(counts) + [HBM],
        out_specs=[VMEM] * ROW_BLOCKS,
        scratch_shapes=[
            pltpu.VMEM((members * (CTOK + STEPS), FEATURES), jnp.bfloat16),
            pltpu.VMEM((TILE // 128, members * CTOK, 128), jnp.float32),
            pltpu.VMEM((tiles, FEATURES, TILE), jnp.bfloat16),
            pltpu.SemaphoreType.DMA((tiles,)),
            pltpu.VMEM((members, CTOK, lanes), jnp.bfloat16),
        ],
        compiler_params=kernel_params(),
        cost_estimate=cost(2 * members * (CTOK + STEPS) * FEATURES * tiles * TILE, 12 * 10**6),
        name="block_product",
    )(*messages, in_hbm(blocks))


def sum_kernel(bias_ref, *refs):
    part_refs, out_refs = refs[:ROW_BLOCKS], refs[ROW_BLOCKS:]
    column = lax.rem(lax.axis_index("tp"), COL_BLOCKS)
    late = column == 6
    last = (column == COL_BLOCKS - 1).astype(jnp.float32)
    cols = QKV // COL_BLOCKS
    tiles = cols // TILE
    kept = REST // TILE
    zero = jnp.zeros((CTOK, TILE), jnp.float32)

    def value_bias(j):
        if j == 0:
            return jnp.zeros((1, TILE), jnp.float32)
        at = QKV - cols + j * TILE
        return bias_ref[:, at : at + TILE] * last

    main_bias = jnp.concatenate([value_bias(j) for j in range(tiles)], axis=0)
    for g, out_ref in enumerate(out_refs):

        def total(lane):
            value = part_refs[0][g, :, lane : lane + TILE].astype(jnp.float32)
            for ref in part_refs[1:]:
                value = value + ref[g, :, lane : lane + TILE].astype(jnp.float32)
            return value

        rest = [total(cols + i * TILE) for i in range(kept)] + [zero] * (tiles - kept)
        lows = []
        for j in range(tiles):
            shifted = rest[j - tiles + kept] if j >= tiles - kept else zero
            value = total(j * TILE) + jnp.where(late, shifted, rest[j]) + value_bias(j)
            high = value.astype(jnp.bfloat16)
            out_ref[:, j * TILE : (j + 1) * TILE] = high
            lows.append(value - high.astype(jnp.float32))
        for i in range(kept):
            low = jnp.where(late, lows[i + tiles - kept], lows[i])
            out_ref[:, cols + i * TILE : cols + (i + 1) * TILE] = low.astype(jnp.bfloat16)
        main = total(cols + REST)
        pad = jnp.zeros((tiles - kept, TILE), jnp.float32)
        pieces = []
        for s in range(STEPS):
            low = main[s * 8 + tiles : (s + 1) * 8]
            both = jnp.where(late, jnp.concatenate([pad, low], axis=0), jnp.concatenate([low, pad], axis=0))
            value = main[s * 8 : s * 8 + tiles] + both + main_bias
            high = value.astype(jnp.bfloat16).astype(jnp.float32)
            low = value - high
            pieces += [high, jnp.where(late, low[tiles - kept :], low[:kept])]
        out_ref[:, cols + REST :] = jnp.concatenate(pieces, axis=0).astype(jnp.bfloat16)


def sum_parts(bias, parts):
    groups, rows, lanes = parts[0].shape
    return pl.pallas_call(
        sum_kernel,
        out_shape=[jax.ShapeDtypeStruct((rows, lanes), jnp.bfloat16)] * groups,
        in_specs=[VMEM] * (1 + len(parts)),
        out_specs=[VMEM] * groups,
        compiler_params=kernel_params(),
        cost_estimate=cost(10**6, 3 * 10**6),
        name="sum_parts",
    )(bias, *parts)


def load_parts(part_refs, parts_ref):
    y, x = plane_place()
    for ref, (dy, dx) in zip(part_refs, HOMES):
        column = lax.rem(y + dy, 2) * 4 + lax.rem(x + 4 - dx, 4)
        parts_ref[column] = ref[...]


def summed_block(parts_ref, c, lanes):
    total = parts_ref[c, :, lanes].astype(jnp.float32)
    for r in range(1, ROW_BLOCKS):
        total = total + parts_ref[r * COL_BLOCKS + c, :, lanes].astype(jnp.float32)
    return total


def head_attention(query, key, value, fresh_key, fresh_value, seen, fresh_seen):
    inv_root = 1.0 / math.sqrt(HD)
    contract = (((1,), (1,)), ((), ()))
    old = lax.dot_general(query, key, contract, preferred_element_type=jnp.float32) * inv_root
    new = lax.dot_general(query, fresh_key, contract, preferred_element_type=jnp.float32) * inv_root
    old = jnp.where(seen, old, MASKED_SCORE)
    new = jnp.where(fresh_seen, new, MASKED_SCORE)
    highest = jnp.maximum(jnp.max(old, axis=-1, keepdims=True), jnp.max(new, axis=-1, keepdims=True))
    old = jnp.exp(old - highest)
    new = jnp.exp(new - highest)
    mass = jnp.sum(old, axis=-1, keepdims=True) + jnp.sum(new, axis=-1, keepdims=True)
    inv_mass = 1.0 / mass
    mixed = jnp.dot((old * inv_mass).astype(jnp.bfloat16), value, preferred_element_type=jnp.float32)
    return mixed + jnp.dot((new * inv_mass).astype(jnp.bfloat16), fresh_value, preferred_element_type=jnp.float32)


def load_qkv(main, parts_ref, qkv_ref):
    cols = QKV // COL_BLOCKS
    for c in range(COL_BLOCKS):
        first = 2 if c == 6 else 0
        if main:
            total = parts_ref[c, :, cols + REST :].astype(jnp.float32)
        else:
            total = parts_ref[c, :, : cols + REST].astype(jnp.float32)
        for j in range(cols // TILE):
            lanes = slice(c * cols + j * TILE, c * cols + (j + 1) * TILE)
            rest = j - first
            has_rest = 0 <= rest < REST // TILE
            if main:
                for s in range(STEPS):
                    line = total[s * 8 + j : s * 8 + j + 1]
                    if has_rest:
                        at = s * 8 + cols // TILE + rest
                        line = line + total[at : at + 1]
                    qkv_ref[s : s + 1, lanes] = line
            else:
                value = total[:, j * TILE : (j + 1) * TILE]
                if has_rest:
                    value = value + total[:, cols + rest * TILE : cols + (rest + 1) * TILE]
                qkv_ref[:, lanes] = value


def head_readers(qkv_ref, bias_ref, cos_ref, sin_ref):
    cosine = cos_ref[...]
    sine = sin_ref[...]

    def plain(start):
        return qkv_ref[:, start : start + HD]

    def rotated(start):
        head = plain(start) + bias_ref[:, start : start + HD]
        return head * cosine + pltpu.roll(head, HD // 2, 1) * sine

    return plain, rotated


def fresh_block(pieces):
    rows = sum(piece.shape[0] for piece in pieces)
    pad = jnp.zeros((128 - rows, HD), jnp.float32)
    return jnp.concatenate(list(pieces) + [pad], axis=0).astype(jnp.bfloat16)


GROUP = D // HD // KVH
KV_WIDTH = KVH * HD


def attend_main_kernel(len_ref, bias_ref, cos_ref, sin_ref, cache_ref, *refs):
    part_refs = refs[:COL_BLOCKS]
    out_ref, kv_ref, qkv_ref, piece_ref, parts_ref = refs[COL_BLOCKS:]
    rows = qkv_ref.shape[0]
    load_parts(part_refs, parts_ref)
    qkv_ref[...] = jnp.zeros(qkv_ref.shape, jnp.float32)
    load_qkv(True, parts_ref, qkv_ref)
    plain, rotated = head_readers(qkv_ref, bias_ref, cos_ref, sin_ref)
    seen = lax.broadcasted_iota(jnp.int32, (1, cache_ref.shape[0]), 1) < len_ref[0]
    row = lax.broadcasted_iota(jnp.int32, (rows, 128), 0)
    col = lax.broadcasted_iota(jnp.int32, (rows, 128), 1)
    own = ((col <= row) & (col < STEPS)).astype(jnp.int32)
    fresh_seen = jnp.concatenate([own] * GROUP, axis=0) > 0
    for g in range(KVH):
        query = jnp.concatenate([rotated((g * GROUP + h) * HD) for h in range(GROUP)], axis=0).astype(jnp.bfloat16)
        fresh_key = rotated(D + g * HD)
        fresh_value = plain(D + KV_WIDTH + g * HD)
        kv_ref[:, g * HD : (g + 1) * HD] = fresh_key
        kv_ref[:, KV_WIDTH + g * HD : KV_WIDTH + (g + 1) * HD] = fresh_value
        key = cache_ref[:, g * HD : (g + 1) * HD]
        value = cache_ref[:, KV_WIDTH + g * HD : KV_WIDTH + (g + 1) * HD]
        mixed = head_attention(
            query, key, value, fresh_block([fresh_key]), fresh_block([fresh_value]), seen, fresh_seen
        )
        for h in range(GROUP):
            r, place = divmod(g * GROUP + h, FEATURES // HD)
            j, lane = place // 2, (place % 2) * HD
            for s in range(STEPS):
                at = s * 8 + j
                piece_ref[r, at : at + 1, lane : lane + HD] = mixed[h * rows + s : h * rows + s + 1]
    for r in range(ROW_BLOCKS):
        piece = piece_ref[r].astype(jnp.bfloat16)
        for c in range(COL_BLOCKS):
            out_ref[r * COL_BLOCKS + c] = piece


def attend_main(prefix_len, bias, cosine, sine, cache, parts):
    return pl.pallas_call(
        attend_main_kernel,
        out_shape=(
            jax.ShapeDtypeStruct((32, 16, TILE), jnp.bfloat16),
            jax.ShapeDtypeStruct((8, 2 * KV_WIDTH), jnp.float32),
        ),
        in_specs=[SMEM] + [VMEM] * (4 + COL_BLOCKS),
        out_specs=(whole((32, 16, TILE)), whole((8, 2 * KV_WIDTH))),
        scratch_shapes=[
            pltpu.VMEM((8, QKV), jnp.float32),
            pltpu.VMEM((ROW_BLOCKS, 16, TILE), jnp.float32),
            pltpu.VMEM((COL_BLOCKS,) + parts[0].shape, jnp.bfloat16),
        ],
        compiler_params=kernel_params(),
        cost_estimate=cost(2 * 10**8, 6 * 10**6),
        name="attend_main",
    )(prefix_len, bias, cosine, sine, cache, *parts)


def attend_cont_kernel(len_ref, bound_ref, bias_ref, cos_ref, sin_ref, cache_ref, kv_ref, *refs):
    part_refs = refs[:COL_BLOCKS]
    out_ref, qkv_ref, parts_ref = refs[COL_BLOCKS:]
    load_parts(part_refs, parts_ref)
    rows = qkv_ref.shape[0]
    load_qkv(False, parts_ref, qkv_ref)
    plain, rotated = head_readers(qkv_ref, bias_ref, cos_ref, sin_ref)
    seen = lax.broadcasted_iota(jnp.int32, (1, cache_ref.shape[0]), 1) < len_ref[0]
    row = lax.broadcasted_iota(jnp.int32, (rows, 128), 0)
    col = lax.broadcasted_iota(jnp.int32, (rows, 128), 1)
    own = (row // STEPS == col // STEPS) & (col <= row)
    main = (col >= rows) & (col < rows + bound_ref[0])
    fresh_seen = jnp.concatenate([(own | main).astype(jnp.int32)] * GROUP, axis=0) > 0
    for g in range(KVH):
        query = jnp.concatenate([rotated((g * GROUP + h) * HD) for h in range(GROUP)], axis=0).astype(jnp.bfloat16)
        at_key = slice(g * HD, (g + 1) * HD)
        at_value = slice(KV_WIDTH + g * HD, KV_WIDTH + (g + 1) * HD)
        fresh_key = fresh_block([rotated(D + g * HD), kv_ref[:, at_key]])
        fresh_value = fresh_block([plain(D + KV_WIDTH + g * HD), kv_ref[:, at_value]])
        mixed = head_attention(
            query, cache_ref[:, at_key], cache_ref[:, at_value], fresh_key, fresh_value, seen, fresh_seen
        )
        mixed = mixed.astype(jnp.bfloat16)
        for h in range(GROUP):
            out_ref[:, (g * GROUP + h) * HD : (g * GROUP + h + 1) * HD] = mixed[h * rows : (h + 1) * rows]


def attend_cont(*args):
    return pl.pallas_call(
        attend_cont_kernel,
        out_shape=jax.ShapeDtypeStruct((CTOK, D), jnp.bfloat16),
        in_specs=[SMEM, SMEM] + [VMEM] * 4 + [whole((8, 2 * KV_WIDTH))] + [VMEM] * COL_BLOCKS,
        out_specs=whole((CTOK, D)),
        scratch_shapes=[
            pltpu.VMEM((CTOK, QKV), jnp.float32),
            pltpu.VMEM((COL_BLOCKS,) + args[-1].shape, jnp.bfloat16),
        ],
        compiler_params=kernel_params(),
        cost_estimate=cost(4 * 10**8, 8 * 10**6),
        name="attend_cont",
    )(*args)


def readout_kernel(head_ref, w_hbm, out_ref, w_ref, sem):
    copy = pltpu.make_async_copy(w_hbm.at[0], w_ref, sem)
    copy.start()
    row = head_ref[pl.ds(lax.rem(lax.axis_index("tp"), COL_BLOCKS), 1), :]
    high = row.astype(jnp.bfloat16).astype(jnp.float32)
    middle = (row - high).astype(jnp.bfloat16).astype(jnp.float32)
    low = row - high - middle
    pieces = jnp.concatenate([high, middle, low, jnp.zeros((13, row.shape[1]), jnp.float32)], axis=0)
    copy.wait()
    prod = lax.dot_general(
        pieces.astype(jnp.bfloat16), w_ref[...], (((1,), (1,)), ((), ())), preferred_element_type=jnp.float32
    )
    out_ref[...] = prod[0:1] + prod[1:2] + prod[2:3]


def readout(value_head, blocks):
    return pl.pallas_call(
        readout_kernel,
        out_shape=jax.ShapeDtypeStruct((1, FEATURES), jnp.float32),
        in_specs=[whole(value_head.shape), HBM],
        out_specs=whole((1, FEATURES)),
        scratch_shapes=[pltpu.VMEM((FEATURES, D // COL_BLOCKS), jnp.bfloat16), pltpu.SemaphoreType.DMA],
        compiler_params=kernel_params(),
        cost_estimate=cost(2 * 10**8, 5 * 10**6),
        name="readout",
    )(value_head, in_hbm(blocks))


def out_kernel(tiles, x_ref, read_ref, w_hbm, out_ref, rows_ref, wide_ref, read8_ref, w_ref, sems):
    n = pl.program_id(0)
    members = x_ref.shape[0]
    lines = members * STEPS
    halves = TILE // 128
    tile = weight_tile(n, tiles, w_hbm, w_ref, sems)

    @pl.when(n == 0)
    def _():
        for j in range(FEATURES // TILE):
            read8_ref[j : j + 1, :] = read_ref[:, j * TILE : (j + 1) * TILE]
        out_ref[:, 8:, :] = jnp.broadcast_to(read8_ref[...][None], (members, 8, TILE))
        packed = x_ref[...].reshape(members * 16, TILE).astype(jnp.float32)
        for k in range(halves):
            wide_ref[k] = packed[:, k * 128 : (k + 1) * 128]
            for j in range(FEATURES // TILE):
                lane = j * TILE + k * 128
                rows_ref[:, lane : lane + 128] = wide_ref[k, pl.ds(j, lines, stride=8), :].astype(jnp.bfloat16)

    tile.wait()
    prod = jnp.dot(rows_ref[...], w_ref[n], preferred_element_type=jnp.float32)
    for k in range(halves):
        wide_ref[k, pl.ds(n, lines, stride=4), :] = prod[:, k * 128 : (k + 1) * 128]

    @pl.when(n == tiles - 1)
    def _():
        for k in range(halves):
            packed = wide_ref[k, : members * 8, :].reshape(members, 8, 128)
            out_ref[:, :8, k * 128 : (k + 1) * 128] = packed


def out_product(rows, read, blocks):
    members = rows.shape[0]
    tiles = blocks.shape[2] // TILE
    return pl.pallas_call(
        functools.partial(out_kernel, tiles),
        out_shape=jax.ShapeDtypeStruct((members, 16, TILE), jnp.float32),
        grid=(tiles,),
        in_specs=[whole(rows.shape), whole(read.shape), HBM],
        out_specs=whole((members, 16, TILE)),
        scratch_shapes=[
            pltpu.VMEM((members * STEPS, FEATURES), jnp.bfloat16),
            pltpu.VMEM((TILE // 128, members * 16, 128), jnp.float32),
            pltpu.VMEM((8, TILE), jnp.float32),
            pltpu.VMEM((tiles, FEATURES, TILE), jnp.bfloat16),
            pltpu.SemaphoreType.DMA((tiles,)),
        ],
        compiler_params=kernel_params(),
        cost_estimate=cost(3 * 10**8, 5 * 10**6),
        name="out_product",
    )(rows, read, in_hbm(blocks))


def finish_kernel(parts_ref, main_ref, cont_ref, head_ref, mixed_ref, out_ref, score_ref, wide_ref):
    cols = D // COL_BLOCKS
    for c in range(COL_BLOCKS):
        total = summed_block(parts_ref, c, slice(0, TILE))
        for j in range(cols // TILE):
            at = slice(c * cols + j * TILE, c * cols + (j + 1) * TILE)
            for s in range(STEPS):
                wide_ref[s : s + 1, at] = total[s * 4 + j : s * 4 + j + 1]
    out_ref[...] = (main_ref[...].astype(jnp.float32) + wide_ref[:STEPS, :]).astype(jnp.bfloat16)
    score = jnp.zeros((CTOK, TILE), jnp.float32)
    direct = jnp.zeros((STEPS, TILE), jnp.float32)
    for r in range(ROW_BLOCKS):
        read = parts_ref[r * COL_BLOCKS, 8:, :]
        for c in range(1, COL_BLOCKS):
            read = read + parts_ref[r * COL_BLOCKS + c, 8:, :]
        for j in range(FEATURES // TILE):
            lanes = slice(r * FEATURES + j * TILE, r * FEATURES + (j + 1) * TILE)
            score = score + mixed_ref[:, lanes].astype(jnp.float32) * read[j : j + 1, :]
            for c in range(CONTS):
                direct = direct + cont_ref[c, :, lanes].astype(jnp.float32) * head_ref[:, lanes]
    total = jnp.sum(score, axis=0, keepdims=True) + jnp.sum(direct, axis=0, keepdims=True)
    score_ref[...] = jnp.broadcast_to(jnp.sum(total, axis=1, keepdims=True) / CONTS, (8, 128))


def finish(parts, main, cont, head, mixed):
    return pl.pallas_call(
        finish_kernel,
        out_shape=(
            jax.ShapeDtypeStruct((STEPS, D), jnp.bfloat16),
            jax.ShapeDtypeStruct((8, 128), jnp.float32),
        ),
        in_specs=[whole(parts.shape), whole(main.shape), whole(cont.shape), whole(head.shape), whole(mixed.shape)],
        out_specs=(whole((STEPS, D)), whole((8, 128))),
        scratch_shapes=[pltpu.VMEM((8, D), jnp.float32)],
        compiler_params=kernel_params(),
        cost_estimate=cost(10**6, 2 * 10**6),
        name="finish",
    )(parts, main, cont, head, mixed)


def rope_tables(positions):
    half = HD // 2
    frequency = THETA ** (-(jnp.arange(half, dtype=jnp.float32) * 2.0) / HD)
    angles = positions.astype(jnp.float32)[:, None] * frequency[None, :]
    cosine = jnp.cos(angles)
    sine = jnp.sin(angles)
    return jnp.concatenate([cosine, cosine], axis=1), jnp.concatenate([-sine, sine], axis=1)


def exchange(rows):
    return lax.all_to_all(rows, "tp", split_axis=0, concat_axis=0, tiled=True)


ALONG = [[z * COL_BLOCKS + c for z in range(ROW_BLOCKS)] for c in range(COL_BLOCKS)]


def from_side(rows, dy, dx):
    route = []
    for to in range(MEMBERS):
        z, y, x = to // 8, to // 4 % 2, to % 4
        route.append((z * 8 + (y + dy) % 2 * 4 + (x + dx) % 4, to))
    return lax.ppermute(rows, "tp", route)


def from_along(rows, dz):
    route = [((to + dz * COL_BLOCKS) % MEMBERS, to) for to in range(MEMBERS)]
    return lax.ppermute(rows, "tp", route)


FIRST_HOMES = ((0, 0), (1, 0), (0, 1), (0, 3))
SECOND_HOMES = ((1, 1), (1, 3), (0, 2), (1, 2))
HOMES = FIRST_HOMES + SECOND_HOMES


def project(rows, blocks, bias):
    near = lax.all_to_all(rows, "tp", split_axis=0, concat_axis=0, tiled=True, axis_index_groups=ALONG)
    half = ROW_BLOCKS // 2
    over = from_side(near, 1, 0)
    sides, far = [], []
    for mine in (near, over):
        after = from_side(mine, 0, 1)
        before = from_side(mine, 0, 3)
        far += [from_side(before[:half], 0, 3), from_side(after[half:], 0, 1)]
        sides.append([after, before])
    received = []
    for homes, messages in ((FIRST_HOMES, [near, over] + sides[0]), (SECOND_HOMES, sides[1] + far)):
        parts = block_product(messages, blocks)
        parts = [parts[0]] + [from_along(parts[k], -k) for k in range(1, ROW_BLOCKS)]
        for (dy, dx), summed in zip(homes, sum_parts(bias, parts)):
            received.append(from_side(summed, -dy, -dx) if dy or dx else summed)
    return received


def on_device(
    main_inputs, cont_inputs, prefix_cache, prefix_len, boundary, rms_gain, qkv_bias, w_qkv, w_out, value_head
):
    main = main_inputs.reshape(STEPS, D)
    cont = cont_inputs.reshape(CONTS, STEPS, D)
    bias = qkv_bias[None, :]
    cache = prefix_cache[0]
    head = value_head[None, :]
    step = jnp.arange(CTOK, dtype=jnp.int32) % STEPS
    main_tables = rope_tables(prefix_len + step[:8])
    cont_tables = rope_tables(prefix_len + boundary + step)
    read = readout(value_head.reshape(COL_BLOCKS, D // COL_BLOCKS), w_out)
    parts = project(norm_rows(main, cont, rms_gain[None, :]), w_qkv, bias)
    mixed, main_kv = attend_main(prefix_len, bias, *main_tables, cache, parts)
    mixed = exchange(mixed)
    cont_mixed = attend_cont(prefix_len, boundary, bias, *cont_tables, cache, main_kv, *parts)
    mixed, cont_mixed, read = lax.optimization_barrier((mixed, cont_mixed, read))
    parts = exchange(out_product(mixed, read, w_out))
    main_out, score = finish(parts, main, cont, head, cont_mixed)
    return main_out[None], score[0, :1]


def solution(mesh):
    return jax.shard_map(
        on_device,
        mesh=mesh,
        in_specs=(
            P(("grp", "tp"), None, None),
            P(("grp", "tp"), None, None, None),
            P(("grp", "tp"), None, None),
            P(("grp", "tp")),
            P(("grp", "tp")),
            P(),
            P(),
            P("tp", None, None),
            P("tp", None, None),
            P(),
        ),
        out_specs=(P(("grp", "tp"), None, None), P(("grp", "tp"))),
        check_vma=False,
    )
```

```python
import functools
import math

import jax
import jax.numpy as jnp
from jax import lax
from jax.experimental import pallas as pl
from jax.experimental.pallas import tpu as pltpu
from jax.sharding import PartitionSpec as P

KVH = 8
HD = 128
D = 8192
QKV = 10240
ROW_BLOCKS = 4
COL_BLOCKS = 8
MEMBERS = ROW_BLOCKS * COL_BLOCKS
FEATURES = D // ROW_BLOCKS
CONTS = 8
STEPS = 2
CTOK = CONTS * STEPS
TILE = 256

THETA = 1000000.0
EPS = 1e-06
MASKED_SCORE = -1e30

VMEM_LIMIT = 32 * 1024 * 1024
VMEM = pl.BlockSpec(memory_space=pltpu.VMEM)
SMEM = pl.BlockSpec(memory_space=pltpu.SMEM)
HBM = pl.BlockSpec(memory_space=pltpu.HBM)


def whole(shape):
    return pl.BlockSpec(shape, lambda *_: (0,) * len(shape))


def cost(flops, moved):
    return pl.CostEstimate(flops=flops, bytes_accessed=moved, transcendentals=0)


def in_hbm(array):
    return pltpu.with_memory_space_constraint(array, pltpu.HBM)


def kernel_params():
    return pltpu.CompilerParams(vmem_limit_bytes=VMEM_LIMIT)


def norm_kernel(main_hbm, cont_hbm, gain_hbm, out_ref, main_ref, cont_ref, gain_ref, rows_ref, piece_ref, sems):
    pairs = ((main_hbm, main_ref), (cont_hbm, cont_ref), (gain_hbm, gain_ref))
    copies = [pltpu.make_async_copy(src, dst, sems.at[i]) for i, (src, dst) in enumerate(pairs)]
    for copy in copies:
        copy.start()
    for copy in copies:
        copy.wait()

    def normed(wide):
        inv = lax.rsqrt(jnp.mean(wide * wide, axis=-1, keepdims=True) + EPS)
        return wide * inv * gain_ref[...]

    for c in range(CONTS):
        rows_ref[c * STEPS : (c + 1) * STEPS, :] = cont_ref[c].astype(jnp.float32)
    cont = normed(rows_ref[...]).astype(jnp.bfloat16)
    main = normed(main_ref[...].astype(jnp.float32))
    for r in range(ROW_BLOCKS):
        for j in range(FEATURES // TILE):
            lanes = slice(r * FEATURES + j * TILE, r * FEATURES + (j + 1) * TILE)
            for s in range(STEPS):
                piece_ref[r, s * 8 + j : s * 8 + j + 1, :] = main[s : s + 1, lanes]
    for r in range(ROW_BLOCKS):
        piece = piece_ref[r].astype(jnp.bfloat16)
        out_ref[r, :, :FEATURES] = cont[:, r * FEATURES : (r + 1) * FEATURES]
        out_ref[r, :, FEATURES:] = piece


def norm_rows(main, cont, gain):
    return pl.pallas_call(
        norm_kernel,
        out_shape=jax.ShapeDtypeStruct((ROW_BLOCKS, CTOK, FEATURES + TILE), jnp.bfloat16),
        in_specs=[HBM] * 3,
        out_specs=VMEM,
        scratch_shapes=[
            pltpu.VMEM((STEPS, D), jnp.bfloat16),
            pltpu.VMEM((CONTS, STEPS, D), jnp.bfloat16),
            pltpu.VMEM((1, D), jnp.float32),
            pltpu.VMEM((CTOK, D), jnp.float32),
            pltpu.VMEM((ROW_BLOCKS, 16, TILE), jnp.float32),
            pltpu.SemaphoreType.DMA((3,)),
        ],
        compiler_params=kernel_params(),
        cost_estimate=cost(10**6, 4 * 10**6),
        name="norm_rows",
    )(in_hbm(main), in_hbm(cont), in_hbm(gain))


def weight_tile(n, tiles, w_hbm, w_ref, sems):
    def copy(i):
        lanes = pl.ds(pl.multiple_of(i * TILE, TILE), TILE)
        return pltpu.make_async_copy(w_hbm.at[0, :, lanes], w_ref.at[i], sems.at[i])

    @pl.when(n == 0)
    def _():
        for i in range(tiles):
            copy(i).start()

    return copy(n)


REST = 768


def rest_tile(block):
    return jnp.where(block == 6, 2, 0)


def plane_place():
    column = lax.rem(lax.axis_index("tp"), COL_BLOCKS)
    return column // 4, lax.rem(column, 4)


def product_kernel(tiles, counts, *refs):
    x_refs = refs[: len(counts)]
    w_hbm, *out_refs = refs[len(counts) : len(counts) + 1 + ROW_BLOCKS]
    rows_ref, wide_ref, w_ref, sems, part_ref = refs[len(counts) + 1 + ROW_BLOCKS :]
    n = pl.program_id(0)
    members = sum(counts)
    count = members * CTOK
    lines = members * STEPS
    halves = TILE // 128
    width = tiles * TILE
    tile = weight_tile(n, tiles, w_hbm, w_ref, sems)

    @pl.when(n == 0)
    def _():
        at = 0
        for x_ref, size in zip(x_refs, counts):
            rows = slice(at * CTOK, (at + size) * CTOK)
            rows_ref[rows, :] = x_ref[:, :, :FEATURES].reshape(size * CTOK, FEATURES)
            packed = x_ref[:, :, FEATURES:].reshape(size * CTOK, TILE).astype(jnp.float32)
            for k in range(halves):
                wide_ref[k, rows, :] = packed[:, k * 128 : (k + 1) * 128]
            at += size
        for k in range(halves):
            for j in range(FEATURES // TILE):
                lane = j * TILE + k * 128
                rows_ref[count:, lane : lane + 128] = wide_ref[k, pl.ds(j, lines, stride=8), :].astype(jnp.bfloat16)

    tile.wait()
    prod = jnp.dot(rows_ref[...], w_ref[n], preferred_element_type=jnp.float32)
    high = prod.astype(jnp.bfloat16)
    part_ref[:, :, pl.ds(pl.multiple_of(n * TILE, TILE), TILE)] = high[:count].reshape(members, CTOK, TILE)
    for k in range(halves):
        wide_ref[k, pl.ds(n, lines, stride=8), :] = prod[count:, k * 128 : (k + 1) * 128]
    start = rest_tile(lax.rem(lax.axis_index("tp"), COL_BLOCKS))

    @pl.when((n >= start) & (n < start + REST // TILE))
    def _():
        low = prod - high.astype(jnp.float32)
        place = n - start
        lane = pl.multiple_of(width + place * TILE, TILE)
        part_ref[:, :, pl.ds(lane, TILE)] = low[:count].astype(jnp.bfloat16).reshape(members, CTOK, TILE)
        for k in range(halves):
            wide_ref[k, pl.ds(tiles + place, lines, stride=8), :] = low[count:, k * 128 : (k + 1) * 128]

    @pl.when(n == tiles - 1)
    def _():
        for k in range(halves):
            lane = width + REST + k * 128
            part_ref[:, :, lane : lane + 128] = wide_ref[k].astype(jnp.bfloat16).reshape(members, CTOK, 128)
        z = lax.axis_index("tp") // COL_BLOCKS
        for k, out_ref in enumerate(out_refs):
            to = lax.rem(z + k, ROW_BLOCKS)
            for g in range(members // ROW_BLOCKS):
                out_ref[g] = part_ref[g * ROW_BLOCKS + to]


def block_product(messages, blocks):
    tiles = blocks.shape[2] // TILE
    lanes = (tiles + 1) * TILE + REST
    counts = tuple(rows.shape[0] for rows in messages)
    members = sum(counts)
    return pl.pallas_call(
        functools.partial(product_kernel, tiles, counts),
        out_shape=[jax.ShapeDtypeStruct((members // ROW_BLOCKS, CTOK, lanes), jnp.bfloat16)] * ROW_BLOCKS,
        grid=(tiles,),
        in_specs=[VMEM] * len(counts) + [HBM],
        out_specs=[VMEM] * ROW_BLOCKS,
        scratch_shapes=[
            pltpu.VMEM((members * (CTOK + STEPS), FEATURES), jnp.bfloat16),
            pltpu.VMEM((TILE // 128, members * CTOK, 128), jnp.float32),
            pltpu.VMEM((tiles, FEATURES, TILE), jnp.bfloat16),
            pltpu.SemaphoreType.DMA((tiles,)),
            pltpu.VMEM((members, CTOK, lanes), jnp.bfloat16),
        ],
        compiler_params=kernel_params(),
        cost_estimate=cost(2 * members * (CTOK + STEPS) * FEATURES * tiles * TILE, 12 * 10**6),
        name="block_product",
    )(*messages, in_hbm(blocks))


def sum_kernel(bias_ref, *refs):
    part_refs, out_refs = refs[:ROW_BLOCKS], refs[ROW_BLOCKS:]
    column = lax.rem(lax.axis_index("tp"), COL_BLOCKS)
    late = column == 6
    last = (column == COL_BLOCKS - 1).astype(jnp.float32)
    cols = QKV // COL_BLOCKS
    tiles = cols // TILE
    kept = REST // TILE
    zero = jnp.zeros((CTOK, TILE), jnp.float32)

    def value_bias(j):
        if j == 0:
            return jnp.zeros((1, TILE), jnp.float32)
        at = QKV - cols + j * TILE
        return bias_ref[:, at : at + TILE] * last

    main_bias = jnp.concatenate([value_bias(j) for j in range(tiles)], axis=0)
    for g, out_ref in enumerate(out_refs):

        def total(lane):
            value = part_refs[0][g, :, lane : lane + TILE].astype(jnp.float32)
            for ref in part_refs[1:]:
                value = value + ref[g, :, lane : lane + TILE].astype(jnp.float32)
            return value

        rest = [total(cols + i * TILE) for i in range(kept)] + [zero] * (tiles - kept)
        lows = []
        for j in range(tiles):
            shifted = rest[j - tiles + kept] if j >= tiles - kept else zero
            value = total(j * TILE) + jnp.where(late, shifted, rest[j]) + value_bias(j)
            high = value.astype(jnp.bfloat16)
            out_ref[:, j * TILE : (j + 1) * TILE] = high
            lows.append(value - high.astype(jnp.float32))
        for i in range(kept):
            low = jnp.where(late, lows[i + tiles - kept], lows[i])
            out_ref[:, cols + i * TILE : cols + (i + 1) * TILE] = low.astype(jnp.bfloat16)
        main = total(cols + REST)
        pad = jnp.zeros((tiles - kept, TILE), jnp.float32)
        pieces = []
        for s in range(STEPS):
            low = main[s * 8 + tiles : (s + 1) * 8]
            both = jnp.where(late, jnp.concatenate([pad, low], axis=0), jnp.concatenate([low, pad], axis=0))
            value = main[s * 8 : s * 8 + tiles] + both + main_bias
            high = value.astype(jnp.bfloat16).astype(jnp.float32)
            low = value - high
            pieces += [high, jnp.where(late, low[tiles - kept :], low[:kept])]
        out_ref[:, cols + REST :] = jnp.concatenate(pieces, axis=0).astype(jnp.bfloat16)


def sum_parts(bias, parts):
    groups, rows, lanes = parts[0].shape
    return pl.pallas_call(
        sum_kernel,
        out_shape=[jax.ShapeDtypeStruct((rows, lanes), jnp.bfloat16)] * groups,
        in_specs=[VMEM] * (1 + len(parts)),
        out_specs=[VMEM] * groups,
        compiler_params=kernel_params(),
        cost_estimate=cost(10**6, 3 * 10**6),
        name="sum_parts",
    )(bias, *parts)


def load_parts(part_refs, parts_ref):
    y, x = plane_place()
    for ref, (dy, dx) in zip(part_refs, HOMES):
        column = lax.rem(y + dy, 2) * 4 + lax.rem(x + 4 - dx, 4)
        parts_ref[column] = ref[...]


def summed_block(parts_ref, c, lanes):
    total = parts_ref[c, :, lanes].astype(jnp.float32)
    for r in range(1, ROW_BLOCKS):
        total = total + parts_ref[r * COL_BLOCKS + c, :, lanes].astype(jnp.float32)
    return total


def head_attention(query, key, value, fresh_key, fresh_value, seen, fresh_seen):
    inv_root = 1.0 / math.sqrt(HD)
    contract = (((1,), (1,)), ((), ()))
    old = lax.dot_general(query, key, contract, preferred_element_type=jnp.float32) * inv_root
    new = lax.dot_general(query, fresh_key, contract, preferred_element_type=jnp.float32) * inv_root
    old = jnp.where(seen, old, MASKED_SCORE)
    new = jnp.where(fresh_seen, new, MASKED_SCORE)
    highest = jnp.maximum(jnp.max(old, axis=-1, keepdims=True), jnp.max(new, axis=-1, keepdims=True))
    old = jnp.exp(old - highest)
    new = jnp.exp(new - highest)
    mass = jnp.sum(old, axis=-1, keepdims=True) + jnp.sum(new, axis=-1, keepdims=True)
    inv_mass = 1.0 / mass
    mixed = jnp.dot((old * inv_mass).astype(jnp.bfloat16), value, preferred_element_type=jnp.float32)
    return mixed + jnp.dot((new * inv_mass).astype(jnp.bfloat16), fresh_value, preferred_element_type=jnp.float32)


def load_qkv(main, parts_ref, qkv_ref):
    cols = QKV // COL_BLOCKS
    for c in range(COL_BLOCKS):
        first = 2 if c == 6 else 0
        if main:
            total = parts_ref[c, :, cols + REST :].astype(jnp.float32)
        else:
            total = parts_ref[c, :, : cols + REST].astype(jnp.float32)
        for j in range(cols // TILE):
            lanes = slice(c * cols + j * TILE, c * cols + (j + 1) * TILE)
            rest = j - first
            has_rest = 0 <= rest < REST // TILE
            if main:
                for s in range(STEPS):
                    line = total[s * 8 + j : s * 8 + j + 1]
                    if has_rest:
                        at = s * 8 + cols // TILE + rest
                        line = line + total[at : at + 1]
                    qkv_ref[s : s + 1, lanes] = line
            else:
                value = total[:, j * TILE : (j + 1) * TILE]
                if has_rest:
                    value = value + total[:, cols + rest * TILE : cols + (rest + 1) * TILE]
                qkv_ref[:, lanes] = value


def head_readers(qkv_ref, bias_ref, cos_ref, sin_ref):
    cosine = cos_ref[...]
    sine = sin_ref[...]

    def plain(start):
        return qkv_ref[:, start : start + HD]

    def rotated(start):
        head = plain(start) + bias_ref[:, start : start + HD]
        return head * cosine + pltpu.roll(head, HD // 2, 1) * sine

    return plain, rotated


def fresh_block(pieces):
    rows = sum(piece.shape[0] for piece in pieces)
    pad = jnp.zeros((128 - rows, HD), jnp.float32)
    return jnp.concatenate(list(pieces) + [pad], axis=0).astype(jnp.bfloat16)


GROUP = D // HD // KVH
KV_WIDTH = KVH * HD


def attend_main_kernel(len_ref, bias_ref, cos_ref, sin_ref, cache_ref, *refs):
    part_refs = refs[:COL_BLOCKS]
    out_ref, kv_ref, qkv_ref, piece_ref, parts_ref = refs[COL_BLOCKS:]
    rows = qkv_ref.shape[0]
    load_parts(part_refs, parts_ref)
    qkv_ref[...] = jnp.zeros(qkv_ref.shape, jnp.float32)
    load_qkv(True, parts_ref, qkv_ref)
    plain, rotated = head_readers(qkv_ref, bias_ref, cos_ref, sin_ref)
    seen = lax.broadcasted_iota(jnp.int32, (1, cache_ref.shape[0]), 1) < len_ref[0]
    row = lax.broadcasted_iota(jnp.int32, (rows, 128), 0)
    col = lax.broadcasted_iota(jnp.int32, (rows, 128), 1)
    own = ((col <= row) & (col < STEPS)).astype(jnp.int32)
    fresh_seen = jnp.concatenate([own] * GROUP, axis=0) > 0
    for g in range(KVH):
        query = jnp.concatenate([rotated((g * GROUP + h) * HD) for h in range(GROUP)], axis=0).astype(jnp.bfloat16)
        fresh_key = rotated(D + g * HD)
        fresh_value = plain(D + KV_WIDTH + g * HD)
        kv_ref[:, g * HD : (g + 1) * HD] = fresh_key
        kv_ref[:, KV_WIDTH + g * HD : KV_WIDTH + (g + 1) * HD] = fresh_value
        key = cache_ref[:, g * HD : (g + 1) * HD]
        value = cache_ref[:, KV_WIDTH + g * HD : KV_WIDTH + (g + 1) * HD]
        mixed = head_attention(
            query, key, value, fresh_block([fresh_key]), fresh_block([fresh_value]), seen, fresh_seen
        )
        for h in range(GROUP):
            r, place = divmod(g * GROUP + h, FEATURES // HD)
            j, lane = place // 2, (place % 2) * HD
            for s in range(STEPS):
                at = s * 8 + j
                piece_ref[r, at : at + 1, lane : lane + HD] = mixed[h * rows + s : h * rows + s + 1]
    for r in range(ROW_BLOCKS):
        piece = piece_ref[r].astype(jnp.bfloat16)
        for c in range(COL_BLOCKS):
            out_ref[r * COL_BLOCKS + c] = piece


def attend_main(prefix_len, bias, cosine, sine, cache, parts):
    return pl.pallas_call(
        attend_main_kernel,
        out_shape=(
            jax.ShapeDtypeStruct((32, 16, TILE), jnp.bfloat16),
            jax.ShapeDtypeStruct((8, 2 * KV_WIDTH), jnp.float32),
        ),
        in_specs=[SMEM] + [VMEM] * (4 + COL_BLOCKS),
        out_specs=(whole((32, 16, TILE)), whole((8, 2 * KV_WIDTH))),
        scratch_shapes=[
            pltpu.VMEM((8, QKV), jnp.float32),
            pltpu.VMEM((ROW_BLOCKS, 16, TILE), jnp.float32),
            pltpu.VMEM((COL_BLOCKS,) + parts[0].shape, jnp.bfloat16),
        ],
        compiler_params=kernel_params(),
        cost_estimate=cost(2 * 10**8, 6 * 10**6),
        name="attend_main",
    )(prefix_len, bias, cosine, sine, cache, *parts)


def attend_cont_kernel(len_ref, bound_ref, bias_ref, cos_ref, sin_ref, cache_ref, kv_ref, *refs):
    part_refs = refs[:COL_BLOCKS]
    out_ref, qkv_ref, parts_ref = refs[COL_BLOCKS:]
    load_parts(part_refs, parts_ref)
    rows = qkv_ref.shape[0]
    load_qkv(False, parts_ref, qkv_ref)
    plain, rotated = head_readers(qkv_ref, bias_ref, cos_ref, sin_ref)
    seen = lax.broadcasted_iota(jnp.int32, (1, cache_ref.shape[0]), 1) < len_ref[0]
    row = lax.broadcasted_iota(jnp.int32, (rows, 128), 0)
    col = lax.broadcasted_iota(jnp.int32, (rows, 128), 1)
    own = (row // STEPS == col // STEPS) & (col <= row)
    main = (col >= rows) & (col < rows + bound_ref[0])
    fresh_seen = jnp.concatenate([(own | main).astype(jnp.int32)] * GROUP, axis=0) > 0
    for g in range(KVH):
        query = jnp.concatenate([rotated((g * GROUP + h) * HD) for h in range(GROUP)], axis=0).astype(jnp.bfloat16)
        at_key = slice(g * HD, (g + 1) * HD)
        at_value = slice(KV_WIDTH + g * HD, KV_WIDTH + (g + 1) * HD)
        fresh_key = fresh_block([rotated(D + g * HD), kv_ref[:, at_key]])
        fresh_value = fresh_block([plain(D + KV_WIDTH + g * HD), kv_ref[:, at_value]])
        mixed = head_attention(
            query, cache_ref[:, at_key], cache_ref[:, at_value], fresh_key, fresh_value, seen, fresh_seen
        )
        mixed = mixed.astype(jnp.bfloat16)
        for h in range(GROUP):
            out_ref[:, (g * GROUP + h) * HD : (g * GROUP + h + 1) * HD] = mixed[h * rows : (h + 1) * rows]


def attend_cont(*args):
    return pl.pallas_call(
        attend_cont_kernel,
        out_shape=jax.ShapeDtypeStruct((CTOK, D), jnp.bfloat16),
        in_specs=[SMEM, SMEM] + [VMEM] * 4 + [whole((8, 2 * KV_WIDTH))] + [VMEM] * COL_BLOCKS,
        out_specs=whole((CTOK, D)),
        scratch_shapes=[
            pltpu.VMEM((CTOK, QKV), jnp.float32),
            pltpu.VMEM((COL_BLOCKS,) + args[-1].shape, jnp.bfloat16),
        ],
        compiler_params=kernel_params(),
        cost_estimate=cost(4 * 10**8, 8 * 10**6),
        name="attend_cont",
    )(*args)


def readout_kernel(head_ref, w_hbm, out_ref, w_ref, sem):
    copy = pltpu.make_async_copy(w_hbm.at[0], w_ref, sem)
    copy.start()
    row = head_ref[pl.ds(lax.rem(lax.axis_index("tp"), COL_BLOCKS), 1), :]
    high = row.astype(jnp.bfloat16).astype(jnp.float32)
    middle = (row - high).astype(jnp.bfloat16).astype(jnp.float32)
    low = row - high - middle
    pieces = jnp.concatenate([high, middle, low, jnp.zeros((13, row.shape[1]), jnp.float32)], axis=0)
    copy.wait()
    prod = lax.dot_general(
        pieces.astype(jnp.bfloat16), w_ref[...], (((1,), (1,)), ((), ())), preferred_element_type=jnp.float32
    )
    out_ref[...] = prod[0:1] + prod[1:2] + prod[2:3]


def readout(value_head, blocks):
    return pl.pallas_call(
        readout_kernel,
        out_shape=jax.ShapeDtypeStruct((1, FEATURES), jnp.float32),
        in_specs=[whole(value_head.shape), HBM],
        out_specs=whole((1, FEATURES)),
        scratch_shapes=[pltpu.VMEM((FEATURES, D // COL_BLOCKS), jnp.bfloat16), pltpu.SemaphoreType.DMA],
        compiler_params=kernel_params(),
        cost_estimate=cost(2 * 10**8, 5 * 10**6),
        name="readout",
    )(value_head, in_hbm(blocks))


def out_kernel(tiles, x_ref, read_ref, w_hbm, out_ref, rows_ref, wide_ref, read8_ref, w_ref, sems):
    n = pl.program_id(0)
    members = x_ref.shape[0]
    lines = members * STEPS
    halves = TILE // 128
    tile = weight_tile(n, tiles, w_hbm, w_ref, sems)

    @pl.when(n == 0)
    def _():
        for j in range(FEATURES // TILE):
            read8_ref[j : j + 1, :] = read_ref[:, j * TILE : (j + 1) * TILE]
        out_ref[:, 8:, :] = jnp.broadcast_to(read8_ref[...][None], (members, 8, TILE))
        packed = x_ref[...].reshape(members * 16, TILE).astype(jnp.float32)
        for k in range(halves):
            wide_ref[k] = packed[:, k * 128 : (k + 1) * 128]
            for j in range(FEATURES // TILE):
                lane = j * TILE + k * 128
                rows_ref[:, lane : lane + 128] = wide_ref[k, pl.ds(j, lines, stride=8), :].astype(jnp.bfloat16)

    tile.wait()
    prod = jnp.dot(rows_ref[...], w_ref[n], preferred_element_type=jnp.float32)
    for k in range(halves):
        wide_ref[k, pl.ds(n, lines, stride=4), :] = prod[:, k * 128 : (k + 1) * 128]

    @pl.when(n == tiles - 1)
    def _():
        for k in range(halves):
            packed = wide_ref[k, : members * 8, :].reshape(members, 8, 128)
            out_ref[:, :8, k * 128 : (k + 1) * 128] = packed


def out_product(rows, read, blocks):
    members = rows.shape[0]
    tiles = blocks.shape[2] // TILE
    return pl.pallas_call(
        functools.partial(out_kernel, tiles),
        out_shape=jax.ShapeDtypeStruct((members, 16, TILE), jnp.float32),
        grid=(tiles,),
        in_specs=[whole(rows.shape), whole(read.shape), HBM],
        out_specs=whole((members, 16, TILE)),
        scratch_shapes=[
            pltpu.VMEM((members * STEPS, FEATURES), jnp.bfloat16),
            pltpu.VMEM((TILE // 128, members * 16, 128), jnp.float32),
            pltpu.VMEM((8, TILE), jnp.float32),
            pltpu.VMEM((tiles, FEATURES, TILE), jnp.bfloat16),
            pltpu.SemaphoreType.DMA((tiles,)),
        ],
        compiler_params=kernel_params(),
        cost_estimate=cost(3 * 10**8, 5 * 10**6),
        name="out_product",
    )(rows, read, in_hbm(blocks))


def finish_kernel(parts_ref, main_ref, cont_ref, head_ref, mixed_ref, out_ref, score_ref, wide_ref):
    cols = D // COL_BLOCKS
    for c in range(COL_BLOCKS):
        total = summed_block(parts_ref, c, slice(0, TILE))
        for j in range(cols // TILE):
            at = slice(c * cols + j * TILE, c * cols + (j + 1) * TILE)
            for s in range(STEPS):
                wide_ref[s : s + 1, at] = total[s * 4 + j : s * 4 + j + 1]
    out_ref[...] = (main_ref[...].astype(jnp.float32) + wide_ref[:STEPS, :]).astype(jnp.bfloat16)
    score = jnp.zeros((CTOK, TILE), jnp.float32)
    direct = jnp.zeros((STEPS, TILE), jnp.float32)
    for r in range(ROW_BLOCKS):
        read = parts_ref[r * COL_BLOCKS, 8:, :]
        for c in range(1, COL_BLOCKS):
            read = read + parts_ref[r * COL_BLOCKS + c, 8:, :]
        for j in range(FEATURES // TILE):
            lanes = slice(r * FEATURES + j * TILE, r * FEATURES + (j + 1) * TILE)
            score = score + mixed_ref[:, lanes].astype(jnp.float32) * read[j : j + 1, :]
            for c in range(CONTS):
                direct = direct + cont_ref[c, :, lanes].astype(jnp.float32) * head_ref[:, lanes]
    total = jnp.sum(score, axis=0, keepdims=True) + jnp.sum(direct, axis=0, keepdims=True)
    score_ref[...] = jnp.broadcast_to(jnp.sum(total, axis=1, keepdims=True) / CONTS, (8, 128))


def finish(parts, main, cont, head, mixed):
    return pl.pallas_call(
        finish_kernel,
        out_shape=(
            jax.ShapeDtypeStruct((STEPS, D), jnp.bfloat16),
            jax.ShapeDtypeStruct((8, 128), jnp.float32),
        ),
        in_specs=[whole(parts.shape), whole(main.shape), whole(cont.shape), whole(head.shape), whole(mixed.shape)],
        out_specs=(whole((STEPS, D)), whole((8, 128))),
        scratch_shapes=[pltpu.VMEM((8, D), jnp.float32)],
        compiler_params=kernel_params(),
        cost_estimate=cost(10**6, 2 * 10**6),
        name="finish",
    )(parts, main, cont, head, mixed)


def rope_tables(positions):
    half = HD // 2
    frequency = THETA ** (-(jnp.arange(half, dtype=jnp.float32) * 2.0) / HD)
    angles = positions.astype(jnp.float32)[:, None] * frequency[None, :]
    cosine = jnp.cos(angles)
    sine = jnp.sin(angles)
    return jnp.concatenate([cosine, cosine], axis=1), jnp.concatenate([-sine, sine], axis=1)


def exchange(rows):
    return lax.all_to_all(rows, "tp", split_axis=0, concat_axis=0, tiled=True)


ALONG = [[z * COL_BLOCKS + c for z in range(ROW_BLOCKS)] for c in range(COL_BLOCKS)]


def from_side(rows, dy, dx):
    route = []
    for to in range(MEMBERS):
        z, y, x = to // 8, to // 4 % 2, to % 4
        route.append((z * 8 + (y + dy) % 2 * 4 + (x + dx) % 4, to))
    return lax.ppermute(rows, "tp", route)


def from_along(rows, dz):
    route = [((to + dz * COL_BLOCKS) % MEMBERS, to) for to in range(MEMBERS)]
    return lax.ppermute(rows, "tp", route)


NEAR_HOMES = ((0, 0), (1, 0))
SIDE_HOMES = ((0, 1), (0, 3), (1, 1), (1, 3))
FAR_HOMES = ((0, 2), (1, 2))
HOMES = NEAR_HOMES + SIDE_HOMES + FAR_HOMES


def project(rows, blocks, bias):
    near = lax.all_to_all(rows, "tp", split_axis=0, concat_axis=0, tiled=True, axis_index_groups=ALONG)
    half = ROW_BLOCKS // 2
    over = from_side(near, 1, 0)
    side, far = [], []
    for mine in (near, over):
        after = from_side(mine, 0, 1)
        before = from_side(mine, 0, 3)
        far += [from_side(before[:half], 0, 3), from_side(after[half:], 0, 1)]
        side += [after, before]
    received = []
    for homes, messages in ((NEAR_HOMES, [near, over]), (SIDE_HOMES, side), (FAR_HOMES, far)):
        parts = block_product(messages, blocks)
        parts = [parts[0]] + [from_along(parts[k], -k) for k in range(1, ROW_BLOCKS)]
        for (dy, dx), summed in zip(homes, sum_parts(bias, parts)):
            received.append(from_side(summed, -dy, -dx) if dy or dx else summed)
    return received


def on_device(
    main_inputs, cont_inputs, prefix_cache, prefix_len, boundary, rms_gain, qkv_bias, w_qkv, w_out, value_head
):
    main = main_inputs.reshape(STEPS, D)
    cont = cont_inputs.reshape(CONTS, STEPS, D)
    bias = qkv_bias[None, :]
    cache = prefix_cache[0]
    head = value_head[None, :]
    step = jnp.arange(CTOK, dtype=jnp.int32) % STEPS
    main_tables = rope_tables(prefix_len + step[:8])
    cont_tables = rope_tables(prefix_len + boundary + step)
    read = readout(value_head.reshape(COL_BLOCKS, D // COL_BLOCKS), w_out)
    parts = project(norm_rows(main, cont, rms_gain[None, :]), w_qkv, bias)
    mixed, main_kv = attend_main(prefix_len, bias, *main_tables, cache, parts)
    mixed = exchange(mixed)
    cont_mixed = attend_cont(prefix_len, boundary, bias, *cont_tables, cache, main_kv, *parts)
    mixed, cont_mixed, read = lax.optimization_barrier((mixed, cont_mixed, read))
    parts = exchange(out_product(mixed, read, w_out))
    main_out, score = finish(parts, main, cont, head, cont_mixed)
    return main_out[None], score[0, :1]


def solution(mesh):
    return jax.shard_map(
        on_device,
        mesh=mesh,
        in_specs=(
            P(("grp", "tp"), None, None),
            P(("grp", "tp"), None, None, None),
            P(("grp", "tp"), None, None),
            P(("grp", "tp")),
            P(("grp", "tp")),
            P(),
            P(),
            P("tp", None, None),
            P("tp", None, None),
            P(),
        ),
        out_specs=(P(("grp", "tp"), None, None), P(("grp", "tp"))),
        check_vma=False,
    )
```

```python
import functools
import math

import jax
import jax.numpy as jnp
from jax import lax
from jax.experimental import pallas as pl
from jax.experimental.pallas import tpu as pltpu
from jax.sharding import PartitionSpec as P

KVH = 8
HD = 128
D = 8192
QKV = 10240
ROW_BLOCKS = 4
COL_BLOCKS = 8
MEMBERS = ROW_BLOCKS * COL_BLOCKS
FEATURES = D // ROW_BLOCKS
CONTS = 8
STEPS = 2
CTOK = CONTS * STEPS
TILE = 256

THETA = 1000000.0
EPS = 1e-06
MASKED_SCORE = -1e30

VMEM_LIMIT = 32 * 1024 * 1024
VMEM = pl.BlockSpec(memory_space=pltpu.VMEM)
SMEM = pl.BlockSpec(memory_space=pltpu.SMEM)
HBM = pl.BlockSpec(memory_space=pltpu.HBM)


def whole(shape):
    return pl.BlockSpec(shape, lambda *_: (0,) * len(shape))


def cost(flops, moved):
    return pl.CostEstimate(flops=flops, bytes_accessed=moved, transcendentals=0)


def in_hbm(array):
    return pltpu.with_memory_space_constraint(array, pltpu.HBM)


def kernel_params():
    return pltpu.CompilerParams(vmem_limit_bytes=VMEM_LIMIT)


def norm_kernel(main_hbm, cont_hbm, gain_hbm, out_ref, main_ref, cont_ref, gain_ref, rows_ref, piece_ref, sems):
    pairs = ((main_hbm, main_ref), (cont_hbm, cont_ref), (gain_hbm, gain_ref))
    copies = [pltpu.make_async_copy(src, dst, sems.at[i]) for i, (src, dst) in enumerate(pairs)]
    for copy in copies:
        copy.start()
    for copy in copies:
        copy.wait()

    def normed(wide):
        inv = lax.rsqrt(jnp.mean(wide * wide, axis=-1, keepdims=True) + EPS)
        return wide * inv * gain_ref[...]

    for c in range(CONTS):
        rows_ref[c * STEPS : (c + 1) * STEPS, :] = cont_ref[c].astype(jnp.float32)
    cont = normed(rows_ref[...]).astype(jnp.bfloat16)
    main = normed(main_ref[...].astype(jnp.float32))
    for r in range(ROW_BLOCKS):
        for j in range(FEATURES // TILE):
            lanes = slice(r * FEATURES + j * TILE, r * FEATURES + (j + 1) * TILE)
            for s in range(STEPS):
                piece_ref[r, s * 8 + j : s * 8 + j + 1, :] = main[s : s + 1, lanes]
    for r in range(ROW_BLOCKS):
        piece = piece_ref[r].astype(jnp.bfloat16)
        out_ref[r, :, :FEATURES] = cont[:, r * FEATURES : (r + 1) * FEATURES]
        out_ref[r, :, FEATURES:] = piece


def norm_rows(main, cont, gain):
    return pl.pallas_call(
        norm_kernel,
        out_shape=jax.ShapeDtypeStruct((ROW_BLOCKS, CTOK, FEATURES + TILE), jnp.bfloat16),
        in_specs=[HBM] * 3,
        out_specs=VMEM,
        scratch_shapes=[
            pltpu.VMEM((STEPS, D), jnp.bfloat16),
            pltpu.VMEM((CONTS, STEPS, D), jnp.bfloat16),
            pltpu.VMEM((1, D), jnp.float32),
            pltpu.VMEM((CTOK, D), jnp.float32),
            pltpu.VMEM((ROW_BLOCKS, 16, TILE), jnp.float32),
            pltpu.SemaphoreType.DMA((3,)),
        ],
        compiler_params=kernel_params(),
        cost_estimate=cost(10**6, 4 * 10**6),
        name="norm_rows",
    )(in_hbm(main), in_hbm(cont), in_hbm(gain))


def weight_tile(n, tiles, w_hbm, w_ref, sems):
    def copy(i):
        lanes = pl.ds(pl.multiple_of(i * TILE, TILE), TILE)
        return pltpu.make_async_copy(w_hbm.at[0, :, lanes], w_ref.at[i], sems.at[i])

    @pl.when(n == 0)
    def _():
        for i in range(tiles):
            copy(i).start()

    return copy(n)


REST = 768


def rest_tile(block):
    return jnp.where(block == 6, 2, 0)


def plane_place():
    column = lax.rem(lax.axis_index("tp"), COL_BLOCKS)
    return column // 4, lax.rem(column, 4)


def product_kernel(tiles, counts, places, *refs):
    x_refs, refs = refs[: len(counts)], refs[len(counts) :]
    if places:
        earlier_ref, refs = refs[0], refs[1:]
    w_hbm, *out_refs = refs[: 1 + ROW_BLOCKS]
    main_ref, rows_ref, wide_ref, w_ref, sems, part_ref = refs[1 + ROW_BLOCKS :]
    n = pl.program_id(0)
    members = sum(counts)
    count = members * CTOK
    lines = members * STEPS
    halves = TILE // 128
    width = tiles * TILE
    tile = weight_tile(n, tiles, w_hbm, w_ref, sems)

    @pl.when(n == 0)
    def _():
        at = 0
        for x_ref, size in zip(x_refs, counts):
            rows = slice(at * CTOK, (at + size) * CTOK)
            rows_ref[rows, :] = x_ref[:, :, :FEATURES].reshape(size * CTOK, FEATURES)
            packed = x_ref[:, :, FEATURES:].reshape(size * CTOK, TILE).astype(jnp.float32)
            for k in range(halves):
                wide_ref[k, rows, :] = packed[:, k * 128 : (k + 1) * 128]
            at += size
        for k in range(halves):
            for j in range(FEATURES // TILE):
                lane = j * TILE + k * 128
                rows_ref[count:, lane : lane + 128] = wide_ref[k, pl.ds(j, lines, stride=8), :].astype(jnp.bfloat16)

    tile.wait()
    prod = jnp.dot(rows_ref[...], w_ref[n], preferred_element_type=jnp.float32)
    high = prod.astype(jnp.bfloat16)
    part_ref[:, :, pl.ds(pl.multiple_of(n * TILE, TILE), TILE)] = high[:count].reshape(members, CTOK, TILE)
    for k in range(halves):
        wide_ref[k, pl.ds(n, lines, stride=8), :] = prod[count:, k * 128 : (k + 1) * 128]
    start = rest_tile(lax.rem(lax.axis_index("tp"), COL_BLOCKS))

    @pl.when((n >= start) & (n < start + REST // TILE))
    def _():
        low = prod - high.astype(jnp.float32)
        place = n - start
        lane = pl.multiple_of(width + place * TILE, TILE)
        part_ref[:, :, pl.ds(lane, TILE)] = low[:count].astype(jnp.bfloat16).reshape(members, CTOK, TILE)
        for k in range(halves):
            wide_ref[k, pl.ds(tiles + place, lines, stride=8), :] = low[count:, k * 128 : (k + 1) * 128]

    @pl.when(n == tiles - 1)
    def _():
        z = lax.axis_index("tp") // COL_BLOCKS
        done = earlier_ref.shape[0] // ROW_BLOCKS if places else 0
        for k in range(halves):
            lanes = slice(k * 128, (k + 1) * 128)
            packed = wide_ref[k].astype(jnp.bfloat16).reshape(members, CTOK, 128)
            if not places:
                main_ref[:, :, lanes] = packed
            for i, (dy, dx) in enumerate(places):
                y, x = plane_place()
                column = lax.rem(y + dy, 2) * 4 + lax.rem(x + dx, 4)
                for r in range(ROW_BLOCKS):
                    if i < done:
                        message = earlier_ref[i * ROW_BLOCKS + r, :, lanes]
                    else:
                        message = packed[(i - done) * ROW_BLOCKS + r]
                    main_ref[r * COL_BLOCKS + column, :, lanes] = message
        for k, out_ref in enumerate(out_refs):
            to = lax.rem(z + k, ROW_BLOCKS)
            for g in range(members // ROW_BLOCKS):
                out_ref[g] = part_ref[g * ROW_BLOCKS + to]


def block_product(messages, blocks, earlier=(), places=()):
    tiles = blocks.shape[2] // TILE
    lanes = tiles * TILE + REST
    counts = tuple(rows.shape[0] for rows in messages)
    members = sum(counts)
    return pl.pallas_call(
        functools.partial(product_kernel, tiles, counts, places),
        out_shape=[jax.ShapeDtypeStruct((members // ROW_BLOCKS, CTOK, lanes), jnp.bfloat16)] * ROW_BLOCKS
        + [jax.ShapeDtypeStruct((MEMBERS if places else members, CTOK, TILE), jnp.bfloat16)],
        grid=(tiles,),
        in_specs=[VMEM] * (len(counts) + len(earlier)) + [HBM],
        out_specs=[VMEM] * (1 + ROW_BLOCKS),
        scratch_shapes=[
            pltpu.VMEM((members * (CTOK + STEPS), FEATURES), jnp.bfloat16),
            pltpu.VMEM((TILE // 128, members * CTOK, 128), jnp.float32),
            pltpu.VMEM((tiles, FEATURES, TILE), jnp.bfloat16),
            pltpu.SemaphoreType.DMA((tiles,)),
            pltpu.VMEM((members, CTOK, lanes), jnp.bfloat16),
        ],
        compiler_params=kernel_params(),
        cost_estimate=cost(2 * members * (CTOK + STEPS) * FEATURES * tiles * TILE, 12 * 10**6),
        name="block_product",
    )(*messages, *earlier, in_hbm(blocks))


def sum_kernel(bias_ref, *refs):
    part_refs, out_refs = refs[:ROW_BLOCKS], refs[ROW_BLOCKS:]
    column = lax.rem(lax.axis_index("tp"), COL_BLOCKS)
    late = column == 6
    last = (column == COL_BLOCKS - 1).astype(jnp.float32)
    cols = QKV // COL_BLOCKS
    tiles = cols // TILE
    kept = REST // TILE
    zero = jnp.zeros((CTOK, TILE), jnp.float32)

    def value_bias(j):
        if j == 0:
            return jnp.zeros((1, TILE), jnp.float32)
        at = QKV - cols + j * TILE
        return bias_ref[:, at : at + TILE] * last

    for g, out_ref in enumerate(out_refs):

        def total(lane):
            value = part_refs[0][g, :, lane : lane + TILE].astype(jnp.float32)
            for ref in part_refs[1:]:
                value = value + ref[g, :, lane : lane + TILE].astype(jnp.float32)
            return value

        rest = [total(cols + i * TILE) for i in range(kept)] + [zero] * (tiles - kept)
        lows = []
        for j in range(tiles):
            shifted = rest[j - tiles + kept] if j >= tiles - kept else zero
            value = total(j * TILE) + jnp.where(late, shifted, rest[j]) + value_bias(j)
            high = value.astype(jnp.bfloat16)
            out_ref[:, j * TILE : (j + 1) * TILE] = high
            lows.append(value - high.astype(jnp.float32))
        for i in range(kept):
            low = jnp.where(late, lows[i + tiles - kept], lows[i])
            out_ref[:, cols + i * TILE : cols + (i + 1) * TILE] = low.astype(jnp.bfloat16)


def sum_parts(bias, parts):
    groups, rows, lanes = parts[0].shape
    return pl.pallas_call(
        sum_kernel,
        out_shape=[jax.ShapeDtypeStruct((rows, lanes), jnp.bfloat16)] * groups,
        in_specs=[VMEM] * (1 + len(parts)),
        out_specs=[VMEM] * groups,
        compiler_params=kernel_params(),
        cost_estimate=cost(10**6, 3 * 10**6),
        name="sum_parts",
    )(bias, *parts)


def load_parts(part_refs, parts_ref):
    y, x = plane_place()
    for ref, (dy, dx) in zip(part_refs, HOMES):
        column = lax.rem(y + dy, 2) * 4 + lax.rem(x + 4 - dx, 4)
        parts_ref[column] = ref[...]


def summed_block(parts_ref, c, lanes):
    total = parts_ref[c, :, lanes].astype(jnp.float32)
    for r in range(1, ROW_BLOCKS):
        total = total + parts_ref[r * COL_BLOCKS + c, :, lanes].astype(jnp.float32)
    return total


def head_attention(query, key, value, fresh_key, fresh_value, seen, fresh_seen):
    inv_root = 1.0 / math.sqrt(HD)
    contract = (((1,), (1,)), ((), ()))
    old = lax.dot_general(query, key, contract, preferred_element_type=jnp.float32) * inv_root
    new = lax.dot_general(query, fresh_key, contract, preferred_element_type=jnp.float32) * inv_root
    old = jnp.where(seen, old, MASKED_SCORE)
    new = jnp.where(fresh_seen, new, MASKED_SCORE)
    highest = jnp.maximum(jnp.max(old, axis=-1, keepdims=True), jnp.max(new, axis=-1, keepdims=True))
    old = jnp.exp(old - highest)
    new = jnp.exp(new - highest)
    mass = jnp.sum(old, axis=-1, keepdims=True) + jnp.sum(new, axis=-1, keepdims=True)
    inv_mass = 1.0 / mass
    mixed = jnp.dot((old * inv_mass).astype(jnp.bfloat16), value, preferred_element_type=jnp.float32)
    return mixed + jnp.dot((new * inv_mass).astype(jnp.bfloat16), fresh_value, preferred_element_type=jnp.float32)


def load_qkv(main, parts_ref, qkv_ref):
    cols = QKV // COL_BLOCKS
    for c in range(COL_BLOCKS):
        first = 2 if c == 6 else 0
        total = summed_block(parts_ref, c, slice(0, TILE)) if main else parts_ref[c].astype(jnp.float32)
        for j in range(cols // TILE):
            lanes = slice(c * cols + j * TILE, c * cols + (j + 1) * TILE)
            rest = j - first
            has_rest = 0 <= rest < REST // TILE
            if main:
                for s in range(STEPS):
                    line = total[s * 8 + j : s * 8 + j + 1]
                    if has_rest:
                        at = s * 8 + cols // TILE + rest
                        line = line + total[at : at + 1]
                    qkv_ref[s : s + 1, lanes] = line
            else:
                value = total[:, j * TILE : (j + 1) * TILE]
                if has_rest:
                    value = value + total[:, cols + rest * TILE : cols + (rest + 1) * TILE]
                qkv_ref[:, lanes] = value


def head_readers(qkv_ref, bias_ref, cos_ref, sin_ref):
    cosine = cos_ref[...]
    sine = sin_ref[...]

    def plain(start):
        return qkv_ref[:, start : start + HD]

    def rotated(start):
        head = plain(start) + bias_ref[:, start : start + HD]
        return head * cosine + pltpu.roll(head, HD // 2, 1) * sine

    return plain, rotated


def fresh_block(pieces):
    rows = sum(piece.shape[0] for piece in pieces)
    pad = jnp.zeros((128 - rows, HD), jnp.float32)
    return jnp.concatenate(list(pieces) + [pad], axis=0).astype(jnp.bfloat16)


GROUP = D // HD // KVH
KV_WIDTH = KVH * HD


def attend_main_kernel(
    len_ref, bias_ref, cos_ref, sin_ref, cache_ref, parts_ref, out_ref, kv_ref, qkv_ref, piece_ref
):
    rows = qkv_ref.shape[0]
    qkv_ref[...] = jnp.zeros(qkv_ref.shape, jnp.float32)
    load_qkv(True, parts_ref, qkv_ref)
    qkv_ref[:, D + KV_WIDTH :] = qkv_ref[:, D + KV_WIDTH :] + bias_ref[:, D + KV_WIDTH :]
    plain, rotated = head_readers(qkv_ref, bias_ref, cos_ref, sin_ref)
    seen = lax.broadcasted_iota(jnp.int32, (1, cache_ref.shape[0]), 1) < len_ref[0]
    row = lax.broadcasted_iota(jnp.int32, (rows, 128), 0)
    col = lax.broadcasted_iota(jnp.int32, (rows, 128), 1)
    own = ((col <= row) & (col < STEPS)).astype(jnp.int32)
    fresh_seen = jnp.concatenate([own] * GROUP, axis=0) > 0
    for g in range(KVH):
        query = jnp.concatenate([rotated((g * GROUP + h) * HD) for h in range(GROUP)], axis=0).astype(jnp.bfloat16)
        fresh_key = rotated(D + g * HD)
        fresh_value = plain(D + KV_WIDTH + g * HD)
        kv_ref[:, g * HD : (g + 1) * HD] = fresh_key
        kv_ref[:, KV_WIDTH + g * HD : KV_WIDTH + (g + 1) * HD] = fresh_value
        key = cache_ref[:, g * HD : (g + 1) * HD]
        value = cache_ref[:, KV_WIDTH + g * HD : KV_WIDTH + (g + 1) * HD]
        mixed = head_attention(
            query, key, value, fresh_block([fresh_key]), fresh_block([fresh_value]), seen, fresh_seen
        )
        for h in range(GROUP):
            r, place = divmod(g * GROUP + h, FEATURES // HD)
            j, lane = place // 2, (place % 2) * HD
            for s in range(STEPS):
                at = s * 8 + j
                piece_ref[r, at : at + 1, lane : lane + HD] = mixed[h * rows + s : h * rows + s + 1]
    for r in range(ROW_BLOCKS):
        piece = piece_ref[r].astype(jnp.bfloat16)
        for c in range(COL_BLOCKS):
            out_ref[r * COL_BLOCKS + c] = piece


def attend_main(prefix_len, bias, cosine, sine, cache, parts):
    return pl.pallas_call(
        attend_main_kernel,
        out_shape=(
            jax.ShapeDtypeStruct((32, 16, TILE), jnp.bfloat16),
            jax.ShapeDtypeStruct((8, 2 * KV_WIDTH), jnp.float32),
        ),
        in_specs=[SMEM] + [VMEM] * 5,
        out_specs=(whole((32, 16, TILE)), whole((8, 2 * KV_WIDTH))),
        scratch_shapes=[
            pltpu.VMEM((8, QKV), jnp.float32),
            pltpu.VMEM((ROW_BLOCKS, 16, TILE), jnp.float32),
        ],
        compiler_params=kernel_params(),
        cost_estimate=cost(2 * 10**8, 6 * 10**6),
        name="attend_main",
    )(prefix_len, bias, cosine, sine, cache, parts)


def attend_cont_kernel(len_ref, bound_ref, bias_ref, cos_ref, sin_ref, cache_ref, kv_ref, *refs):
    part_refs = refs[:COL_BLOCKS]
    out_ref, qkv_ref, parts_ref = refs[COL_BLOCKS:]
    load_parts(part_refs, parts_ref)
    rows = qkv_ref.shape[0]
    load_qkv(False, parts_ref, qkv_ref)
    plain, rotated = head_readers(qkv_ref, bias_ref, cos_ref, sin_ref)
    seen = lax.broadcasted_iota(jnp.int32, (1, cache_ref.shape[0]), 1) < len_ref[0]
    row = lax.broadcasted_iota(jnp.int32, (rows, 128), 0)
    col = lax.broadcasted_iota(jnp.int32, (rows, 128), 1)
    own = (row // STEPS == col // STEPS) & (col <= row)
    main = (col >= rows) & (col < rows + bound_ref[0])
    fresh_seen = jnp.concatenate([(own | main).astype(jnp.int32)] * GROUP, axis=0) > 0
    for g in range(KVH):
        query = jnp.concatenate([rotated((g * GROUP + h) * HD) for h in range(GROUP)], axis=0).astype(jnp.bfloat16)
        at_key = slice(g * HD, (g + 1) * HD)
        at_value = slice(KV_WIDTH + g * HD, KV_WIDTH + (g + 1) * HD)
        fresh_key = fresh_block([rotated(D + g * HD), kv_ref[:, at_key]])
        fresh_value = fresh_block([plain(D + KV_WIDTH + g * HD), kv_ref[:, at_value]])
        mixed = head_attention(
            query, cache_ref[:, at_key], cache_ref[:, at_value], fresh_key, fresh_value, seen, fresh_seen
        )
        mixed = mixed.astype(jnp.bfloat16)
        for h in range(GROUP):
            out_ref[:, (g * GROUP + h) * HD : (g * GROUP + h + 1) * HD] = mixed[h * rows : (h + 1) * rows]


def attend_cont(*args):
    return pl.pallas_call(
        attend_cont_kernel,
        out_shape=jax.ShapeDtypeStruct((CTOK, D), jnp.bfloat16),
        in_specs=[SMEM, SMEM] + [VMEM] * 4 + [whole((8, 2 * KV_WIDTH))] + [VMEM] * COL_BLOCKS,
        out_specs=whole((CTOK, D)),
        scratch_shapes=[
            pltpu.VMEM((CTOK, QKV), jnp.float32),
            pltpu.VMEM((COL_BLOCKS,) + args[-1].shape, jnp.bfloat16),
        ],
        compiler_params=kernel_params(),
        cost_estimate=cost(4 * 10**8, 8 * 10**6),
        name="attend_cont",
    )(*args)


def readout_kernel(head_ref, w_hbm, out_ref, w_ref, sem):
    copy = pltpu.make_async_copy(w_hbm.at[0], w_ref, sem)
    copy.start()
    row = head_ref[pl.ds(lax.rem(lax.axis_index("tp"), COL_BLOCKS), 1), :]
    high = row.astype(jnp.bfloat16).astype(jnp.float32)
    middle = (row - high).astype(jnp.bfloat16).astype(jnp.float32)
    low = row - high - middle
    pieces = jnp.concatenate([high, middle, low, jnp.zeros((13, row.shape[1]), jnp.float32)], axis=0)
    copy.wait()
    prod = lax.dot_general(
        pieces.astype(jnp.bfloat16), w_ref[...], (((1,), (1,)), ((), ())), preferred_element_type=jnp.float32
    )
    out_ref[...] = prod[0:1] + prod[1:2] + prod[2:3]


def readout(value_head, blocks):
    return pl.pallas_call(
        readout_kernel,
        out_shape=jax.ShapeDtypeStruct((1, FEATURES), jnp.float32),
        in_specs=[whole(value_head.shape), HBM],
        out_specs=whole((1, FEATURES)),
        scratch_shapes=[pltpu.VMEM((FEATURES, D // COL_BLOCKS), jnp.bfloat16), pltpu.SemaphoreType.DMA],
        compiler_params=kernel_params(),
        cost_estimate=cost(2 * 10**8, 5 * 10**6),
        name="readout",
    )(value_head, in_hbm(blocks))


def out_kernel(tiles, x_ref, read_ref, w_hbm, out_ref, rows_ref, wide_ref, read8_ref, w_ref, sems):
    n = pl.program_id(0)
    members = x_ref.shape[0]
    lines = members * STEPS
    halves = TILE // 128
    tile = weight_tile(n, tiles, w_hbm, w_ref, sems)

    @pl.when(n == 0)
    def _():
        for j in range(FEATURES // TILE):
            read8_ref[j : j + 1, :] = read_ref[:, j * TILE : (j + 1) * TILE]
        out_ref[:, 8:, :] = jnp.broadcast_to(read8_ref[...][None], (members, 8, TILE))
        packed = x_ref[...].reshape(members * 16, TILE).astype(jnp.float32)
        for k in range(halves):
            wide_ref[k] = packed[:, k * 128 : (k + 1) * 128]
            for j in range(FEATURES // TILE):
                lane = j * TILE + k * 128
                rows_ref[:, lane : lane + 128] = wide_ref[k, pl.ds(j, lines, stride=8), :].astype(jnp.bfloat16)

    tile.wait()
    prod = jnp.dot(rows_ref[...], w_ref[n], preferred_element_type=jnp.float32)
    for k in range(halves):
        wide_ref[k, pl.ds(n, lines, stride=4), :] = prod[:, k * 128 : (k + 1) * 128]

    @pl.when(n == tiles - 1)
    def _():
        for k in range(halves):
            packed = wide_ref[k, : members * 8, :].reshape(members, 8, 128)
            out_ref[:, :8, k * 128 : (k + 1) * 128] = packed


def out_product(rows, read, blocks):
    members = rows.shape[0]
    tiles = blocks.shape[2] // TILE
    return pl.pallas_call(
        functools.partial(out_kernel, tiles),
        out_shape=jax.ShapeDtypeStruct((members, 16, TILE), jnp.float32),
        grid=(tiles,),
        in_specs=[whole(rows.shape), whole(read.shape), HBM],
        out_specs=whole((members, 16, TILE)),
        scratch_shapes=[
            pltpu.VMEM((members * STEPS, FEATURES), jnp.bfloat16),
            pltpu.VMEM((TILE // 128, members * 16, 128), jnp.float32),
            pltpu.VMEM((8, TILE), jnp.float32),
            pltpu.VMEM((tiles, FEATURES, TILE), jnp.bfloat16),
            pltpu.SemaphoreType.DMA((tiles,)),
        ],
        compiler_params=kernel_params(),
        cost_estimate=cost(3 * 10**8, 5 * 10**6),
        name="out_product",
    )(rows, read, in_hbm(blocks))


def finish_kernel(parts_ref, main_ref, cont_ref, head_ref, mixed_ref, out_ref, score_ref, wide_ref):
    cols = D // COL_BLOCKS
    for c in range(COL_BLOCKS):
        total = summed_block(parts_ref, c, slice(0, TILE))
        for j in range(cols // TILE):
            at = slice(c * cols + j * TILE, c * cols + (j + 1) * TILE)
            for s in range(STEPS):
                wide_ref[s : s + 1, at] = total[s * 4 + j : s * 4 + j + 1]
    out_ref[...] = (main_ref[...].astype(jnp.float32) + wide_ref[:STEPS, :]).astype(jnp.bfloat16)
    score = jnp.zeros((CTOK, TILE), jnp.float32)
    direct = jnp.zeros((STEPS, TILE), jnp.float32)
    for r in range(ROW_BLOCKS):
        read = parts_ref[r * COL_BLOCKS, 8:, :]
        for c in range(1, COL_BLOCKS):
            read = read + parts_ref[r * COL_BLOCKS + c, 8:, :]
        for j in range(FEATURES // TILE):
            lanes = slice(r * FEATURES + j * TILE, r * FEATURES + (j + 1) * TILE)
            score = score + mixed_ref[:, lanes].astype(jnp.float32) * read[j : j + 1, :]
            for c in range(CONTS):
                direct = direct + cont_ref[c, :, lanes].astype(jnp.float32) * head_ref[:, lanes]
    total = jnp.sum(score, axis=0, keepdims=True) + jnp.sum(direct, axis=0, keepdims=True)
    score_ref[...] = jnp.broadcast_to(jnp.sum(total, axis=1, keepdims=True) / CONTS, (8, 128))


def finish(parts, main, cont, head, mixed):
    return pl.pallas_call(
        finish_kernel,
        out_shape=(
            jax.ShapeDtypeStruct((STEPS, D), jnp.bfloat16),
            jax.ShapeDtypeStruct((8, 128), jnp.float32),
        ),
        in_specs=[whole(parts.shape), whole(main.shape), whole(cont.shape), whole(head.shape), whole(mixed.shape)],
        out_specs=(whole((STEPS, D)), whole((8, 128))),
        scratch_shapes=[pltpu.VMEM((8, D), jnp.float32)],
        compiler_params=kernel_params(),
        cost_estimate=cost(10**6, 2 * 10**6),
        name="finish",
    )(parts, main, cont, head, mixed)


def rope_tables(positions):
    half = HD // 2
    frequency = THETA ** (-(jnp.arange(half, dtype=jnp.float32) * 2.0) / HD)
    angles = positions.astype(jnp.float32)[:, None] * frequency[None, :]
    cosine = jnp.cos(angles)
    sine = jnp.sin(angles)
    return jnp.concatenate([cosine, cosine], axis=1), jnp.concatenate([-sine, sine], axis=1)


def exchange(rows):
    return lax.all_to_all(rows, "tp", split_axis=0, concat_axis=0, tiled=True)


ALONG = [[z * COL_BLOCKS + c for z in range(ROW_BLOCKS)] for c in range(COL_BLOCKS)]


def from_side(rows, dy, dx):
    route = []
    for to in range(MEMBERS):
        z, y, x = to // 8, to // 4 % 2, to % 4
        route.append((z * 8 + (y + dy) % 2 * 4 + (x + dx) % 4, to))
    return lax.ppermute(rows, "tp", route)


def from_along(rows, dz):
    route = [((to + dz * COL_BLOCKS) % MEMBERS, to) for to in range(MEMBERS)]
    return lax.ppermute(rows, "tp", route)


FIRST_HOMES = ((0, 0), (1, 0), (0, 1), (0, 3))
SECOND_HOMES = ((1, 1), (1, 3), (0, 2), (1, 2))
HOMES = FIRST_HOMES + SECOND_HOMES


def project(rows, blocks, bias):
    near = lax.all_to_all(rows, "tp", split_axis=0, concat_axis=0, tiled=True, axis_index_groups=ALONG)
    half = ROW_BLOCKS // 2
    over = from_side(near, 1, 0)
    sides, far = [], []
    for mine in (near, over):
        after = from_side(mine, 0, 1)
        before = from_side(mine, 0, 3)
        far += [from_side(before[:half], 0, 3), from_side(after[half:], 0, 1)]
        sides.append([after, before])
    *first, main = block_product([near, over] + sides[0], blocks)
    *second, main = block_product(sides[1] + far, blocks, (main,), HOMES)
    received = []
    for homes, parts in ((FIRST_HOMES, first), (SECOND_HOMES, second)):
        parts = [parts[0]] + [from_along(parts[k], -k) for k in range(1, ROW_BLOCKS)]
        for (dy, dx), summed in zip(homes, sum_parts(bias, parts)):
            received.append(from_side(summed, -dy, -dx) if dy or dx else summed)
    return received, exchange(main)


def on_device(
    main_inputs, cont_inputs, prefix_cache, prefix_len, boundary, rms_gain, qkv_bias, w_qkv, w_out, value_head
):
    main = main_inputs.reshape(STEPS, D)
    cont = cont_inputs.reshape(CONTS, STEPS, D)
    bias = qkv_bias[None, :]
    cache = prefix_cache[0]
    head = value_head[None, :]
    step = jnp.arange(CTOK, dtype=jnp.int32) % STEPS
    main_tables = rope_tables(prefix_len + step[:8])
    cont_tables = rope_tables(prefix_len + boundary + step)
    read = readout(value_head.reshape(COL_BLOCKS, D // COL_BLOCKS), w_out)
    parts, main_parts = project(norm_rows(main, cont, rms_gain[None, :]), w_qkv, bias)
    mixed, main_kv = attend_main(prefix_len, bias, *main_tables, cache, main_parts)
    mixed = exchange(mixed)
    cont_mixed = attend_cont(prefix_len, boundary, bias, *cont_tables, cache, main_kv, *parts)
    parts = exchange(out_product(mixed, read, w_out))
    main_out, score = finish(parts, main, cont, head, cont_mixed)
    return main_out[None], score[0, :1]


def solution(mesh):
    return jax.shard_map(
        on_device,
        mesh=mesh,
        in_specs=(
            P(("grp", "tp"), None, None),
            P(("grp", "tp"), None, None, None),
            P(("grp", "tp"), None, None),
            P(("grp", "tp")),
            P(("grp", "tp")),
            P(),
            P(),
            P("tp", None, None),
            P("tp", None, None),
            P(),
        ),
        out_specs=(P(("grp", "tp"), None, None), P(("grp", "tp"))),
        check_vma=False,
    )
```

```python
import functools
import math

import jax
import jax.numpy as jnp
from jax import lax
from jax.experimental import pallas as pl
from jax.experimental.pallas import tpu as pltpu
from jax.sharding import PartitionSpec as P

KVH = 8
HD = 128
D = 8192
QKV = 10240
ROW_BLOCKS = 4
COL_BLOCKS = 8
MEMBERS = ROW_BLOCKS * COL_BLOCKS
FEATURES = D // ROW_BLOCKS
CONTS = 8
STEPS = 2
CTOK = CONTS * STEPS
TILE = 256

THETA = 1000000.0
EPS = 1e-06
MASKED_SCORE = -1e30

VMEM_LIMIT = 32 * 1024 * 1024
VMEM = pl.BlockSpec(memory_space=pltpu.VMEM)
SMEM = pl.BlockSpec(memory_space=pltpu.SMEM)
HBM = pl.BlockSpec(memory_space=pltpu.HBM)


def whole(shape):
    return pl.BlockSpec(shape, lambda *_: (0,) * len(shape))


def cost(flops, moved):
    return pl.CostEstimate(flops=flops, bytes_accessed=moved, transcendentals=0)


def in_hbm(array):
    return pltpu.with_memory_space_constraint(array, pltpu.HBM)


def kernel_params():
    return pltpu.CompilerParams(vmem_limit_bytes=VMEM_LIMIT)


def norm_kernel(main_hbm, cont_hbm, gain_hbm, z0_ref, z1_ref, z2_ref, z3_ref, out_ref, main_ref, cont_ref, gain_ref, rows_ref, piece_ref, sems):
    pairs = ((main_hbm, main_ref), (cont_hbm, cont_ref), (gain_hbm, gain_ref))
    copies = [pltpu.make_async_copy(src, dst, sems.at[i]) for i, (src, dst) in enumerate(pairs)]
    for copy in copies:
        copy.start()
    for copy in copies:
        copy.wait()

    def normed(wide):
        inv = lax.rsqrt(jnp.mean(wide * wide, axis=-1, keepdims=True) + EPS)
        return wide * inv * gain_ref[...]

    for c in range(CONTS):
        rows_ref[c * STEPS : (c + 1) * STEPS, :] = cont_ref[c].astype(jnp.float32)
    cont = normed(rows_ref[...]).astype(jnp.bfloat16)
    main = normed(main_ref[...].astype(jnp.float32))
    for r in range(ROW_BLOCKS):
        for j in range(FEATURES // TILE):
            lanes = slice(r * FEATURES + j * TILE, r * FEATURES + (j + 1) * TILE)
            for s in range(STEPS):
                piece_ref[r, s * 8 + j : s * 8 + j + 1, :] = main[s : s + 1, lanes]
    for r in range(ROW_BLOCKS):
        piece = piece_ref[r].astype(jnp.bfloat16)
        for c in range(COL_BLOCKS):
            out_ref[r * COL_BLOCKS + c] = piece
        ahead = lax.rem(r + ROW_BLOCKS - lax.axis_index("tp") // COL_BLOCKS, ROW_BLOCKS)
        for k, z_ref in enumerate((z0_ref, z1_ref, z2_ref, z3_ref)):

            @pl.when(ahead == k)
            def _():
                z_ref[...] = cont[:, r * FEATURES : (r + 1) * FEATURES]


def norm_rows(main, cont, gain):
    return pl.pallas_call(
        norm_kernel,
        out_shape=[jax.ShapeDtypeStruct((CTOK, FEATURES), jnp.bfloat16)] * ROW_BLOCKS
        + [jax.ShapeDtypeStruct((MEMBERS, CTOK, TILE), jnp.bfloat16)],
        in_specs=[HBM] * 3,
        out_specs=[VMEM] * (1 + ROW_BLOCKS),
        scratch_shapes=[
            pltpu.VMEM((STEPS, D), jnp.bfloat16),
            pltpu.VMEM((CONTS, STEPS, D), jnp.bfloat16),
            pltpu.VMEM((1, D), jnp.float32),
            pltpu.VMEM((CTOK, D), jnp.float32),
            pltpu.VMEM((ROW_BLOCKS, 16, TILE), jnp.float32),
            pltpu.SemaphoreType.DMA((3,)),
        ],
        compiler_params=kernel_params(),
        cost_estimate=cost(10**6, 4 * 10**6),
        name="norm_rows",
    )(in_hbm(main), in_hbm(cont), in_hbm(gain))


def weight_tile(n, tiles, w_hbm, w_ref, sems):
    def copy(i):
        lanes = pl.ds(pl.multiple_of(i * TILE, TILE), TILE)
        return pltpu.make_async_copy(w_hbm.at[0, :, lanes], w_ref.at[i], sems.at[i])

    @pl.when(n == 0)
    def _():
        for i in range(tiles):
            copy(i).start()

    return copy(n)


REST = 768


def rest_tile(block):
    return jnp.where(block == 6, 2, 0)


def plane_place():
    column = lax.rem(lax.axis_index("tp"), COL_BLOCKS)
    return column // 4, lax.rem(column, 4)


def product_kernel(tiles, counts, places, *refs):
    x_refs, refs = refs[: len(counts)], refs[len(counts) :]
    if places:
        earlier_ref, w_hbm, out_ref, rows_ref, w_ref, sems, part_ref = refs
    else:
        w_hbm, part_ref, rows_ref, w_ref, sems = refs
    n = pl.program_id(0)
    members = sum(counts)
    tile = weight_tile(n, tiles, w_hbm, w_ref, sems)

    @pl.when(n == 0)
    def _():
        at = 0
        for x_ref, size in zip(x_refs, counts):
            rows_ref[at * CTOK : (at + size) * CTOK, :] = x_ref[...].reshape(size * CTOK, FEATURES)
            at += size

    tile.wait()
    prod = jnp.dot(rows_ref[...], w_ref[n], preferred_element_type=jnp.float32)
    high = prod.astype(jnp.bfloat16)
    part_ref[:, :, pl.ds(pl.multiple_of(n * TILE, TILE), TILE)] = high.reshape(members, CTOK, TILE)
    start = rest_tile(lax.rem(lax.axis_index("tp"), COL_BLOCKS))

    @pl.when((n >= start) & (n < start + REST // TILE))
    def _():
        low = (prod - high.astype(jnp.float32)).astype(jnp.bfloat16)
        lane = pl.multiple_of((tiles + n - start) * TILE, TILE)
        part_ref[:, :, pl.ds(lane, TILE)] = low.reshape(members, CTOK, TILE)

    if places:

        @pl.when(n == tiles - 1)
        def _():
            column = lax.rem(lax.axis_index("tp"), COL_BLOCKS)
            y, x = column // 4, lax.rem(column, 4)
            done = earlier_ref.shape[0] // ROW_BLOCKS
            for i, (dy, dx) in enumerate(places):
                home = lax.rem(y + dy, 2) * 4 + lax.rem(x + dx, 4)
                for r in range(ROW_BLOCKS):
                    if i < done:
                        message = earlier_ref[i * ROW_BLOCKS + r]
                    else:
                        message = part_ref[(i - done) * ROW_BLOCKS + r]
                    out_ref[r * COL_BLOCKS + home] = message


def block_product(messages, blocks, earlier=(), places=()):
    tiles = blocks.shape[2] // TILE
    counts = tuple(rows.shape[0] for rows in messages)
    members = sum(counts)
    part = (members, CTOK, tiles * TILE + REST)
    out = (MEMBERS,) + part[1:] if places else part
    return pl.pallas_call(
        functools.partial(product_kernel, tiles, counts, places),
        out_shape=jax.ShapeDtypeStruct(out, jnp.bfloat16),
        grid=(tiles,),
        in_specs=[VMEM] * (len(counts) + len(earlier)) + [HBM],
        out_specs=VMEM,
        scratch_shapes=[
            pltpu.VMEM((members * CTOK, FEATURES), jnp.bfloat16),
            pltpu.VMEM((tiles, FEATURES, TILE), jnp.bfloat16),
            pltpu.SemaphoreType.DMA((tiles,)),
        ]
        + ([pltpu.VMEM(part, jnp.bfloat16)] if places else []),
        compiler_params=kernel_params(),
        cost_estimate=cost(2 * members * CTOK * FEATURES * tiles * TILE, 12 * 10**6),
        name="block_product",
    )(*messages, *earlier, in_hbm(blocks))


def main_kernel(tiles, x_ref, w_hbm, out_ref, rows_ref, wide_ref, w_ref, sems):
    n = pl.program_id(0)
    members = x_ref.shape[0]
    lines = members * STEPS
    halves = TILE // 128
    tile = weight_tile(n, tiles, w_hbm, w_ref, sems)

    @pl.when(n == 0)
    def _():
        packed = x_ref[...].reshape(members * CTOK, TILE).astype(jnp.float32)
        for k in range(halves):
            wide_ref[k] = packed[:, k * 128 : (k + 1) * 128]
            for j in range(FEATURES // TILE):
                lane = j * TILE + k * 128
                rows_ref[:, lane : lane + 128] = wide_ref[k, pl.ds(j, lines, stride=8), :].astype(jnp.bfloat16)

    tile.wait()
    prod = jnp.dot(rows_ref[...], w_ref[n], preferred_element_type=jnp.float32)
    for k in range(halves):
        wide_ref[k, pl.ds(n, lines, stride=8), :] = prod[:, k * 128 : (k + 1) * 128]
    start = rest_tile(lax.rem(lax.axis_index("tp"), COL_BLOCKS))

    @pl.when((n >= start) & (n < start + REST // TILE))
    def _():
        low = prod - prod.astype(jnp.bfloat16).astype(jnp.float32)
        for k in range(halves):
            wide_ref[k, pl.ds(tiles + n - start, lines, stride=8), :] = low[:, k * 128 : (k + 1) * 128]

    @pl.when(n == tiles - 1)
    def _():
        for k in range(halves):
            packed = wide_ref[k].astype(jnp.bfloat16).reshape(members, CTOK, 128)
            out_ref[:, :, k * 128 : (k + 1) * 128] = packed


def main_product(rows, blocks):
    tiles = blocks.shape[2] // TILE
    return pl.pallas_call(
        functools.partial(main_kernel, tiles),
        out_shape=jax.ShapeDtypeStruct(rows.shape, jnp.bfloat16),
        grid=(tiles,),
        in_specs=[VMEM, HBM],
        out_specs=VMEM,
        scratch_shapes=[
            pltpu.VMEM((MEMBERS * STEPS, FEATURES), jnp.bfloat16),
            pltpu.VMEM((TILE // 128, MEMBERS * CTOK, 128), jnp.float32),
            pltpu.VMEM((tiles, FEATURES, TILE), jnp.bfloat16),
            pltpu.SemaphoreType.DMA((tiles,)),
        ],
        compiler_params=kernel_params(),
        cost_estimate=cost(3 * 10**8, 6 * 10**6),
        name="main_product",
    )(rows, in_hbm(blocks))


def gather_kernel(own_ref, ahead1_ref, ahead2_ref, ahead3_ref, out_ref):
    z = lax.axis_index("tp") // COL_BLOCKS
    for k, ref in enumerate((own_ref, ahead1_ref, ahead2_ref, ahead3_ref)):
        out_ref[lax.rem(z + k, ROW_BLOCKS)] = ref[...]


def gather_along(parts):
    return pl.pallas_call(
        gather_kernel,
        out_shape=jax.ShapeDtypeStruct((ROW_BLOCKS,) + parts[0].shape, jnp.bfloat16),
        in_specs=[VMEM] * ROW_BLOCKS,
        out_specs=VMEM,
        compiler_params=kernel_params(),
        cost_estimate=cost(10**5, 10**6),
        name="gather_along",
    )(*parts)


def summed_block(parts_ref, c, lanes):
    total = parts_ref[c, :, lanes].astype(jnp.float32)
    for r in range(1, ROW_BLOCKS):
        total = total + parts_ref[r * COL_BLOCKS + c, :, lanes].astype(jnp.float32)
    return total


def head_attention(query, key, value, fresh_key, fresh_value, seen, fresh_seen):
    inv_root = 1.0 / math.sqrt(HD)
    contract = (((1,), (1,)), ((), ()))
    old = lax.dot_general(query, key, contract, preferred_element_type=jnp.float32) * inv_root
    new = lax.dot_general(query, fresh_key, contract, preferred_element_type=jnp.float32) * inv_root
    old = jnp.where(seen, old, MASKED_SCORE)
    new = jnp.where(fresh_seen, new, MASKED_SCORE)
    highest = jnp.maximum(jnp.max(old, axis=-1, keepdims=True), jnp.max(new, axis=-1, keepdims=True))
    old = jnp.exp(old - highest)
    new = jnp.exp(new - highest)
    mass = jnp.sum(old, axis=-1, keepdims=True) + jnp.sum(new, axis=-1, keepdims=True)
    inv_mass = 1.0 / mass
    mixed = jnp.dot((old * inv_mass).astype(jnp.bfloat16), value, preferred_element_type=jnp.float32)
    return mixed + jnp.dot((new * inv_mass).astype(jnp.bfloat16), fresh_value, preferred_element_type=jnp.float32)


def load_qkv(main, parts_ref, qkv_ref):
    cols = QKV // COL_BLOCKS
    for c in range(COL_BLOCKS):
        first = 2 if c == 6 else 0
        total = summed_block(parts_ref, c, slice(0, TILE if main else cols + REST))
        for j in range(cols // TILE):
            lanes = slice(c * cols + j * TILE, c * cols + (j + 1) * TILE)
            rest = j - first
            has_rest = 0 <= rest < REST // TILE
            if main:
                for s in range(STEPS):
                    line = total[s * 8 + j : s * 8 + j + 1]
                    if has_rest:
                        at = s * 8 + cols // TILE + rest
                        line = line + total[at : at + 1]
                    qkv_ref[s : s + 1, lanes] = line
            else:
                value = total[:, j * TILE : (j + 1) * TILE]
                if has_rest:
                    value = value + total[:, cols + rest * TILE : cols + (rest + 1) * TILE]
                qkv_ref[:, lanes] = value


def head_readers(qkv_ref, bias_ref, cos_ref, sin_ref):
    cosine = cos_ref[...]
    sine = sin_ref[...]

    def plain(start):
        return qkv_ref[:, start : start + HD] + bias_ref[:, start : start + HD]

    def rotated(start):
        head = plain(start)
        return head * cosine + pltpu.roll(head, HD // 2, 1) * sine

    return plain, rotated


def fresh_block(pieces):
    rows = sum(piece.shape[0] for piece in pieces)
    pad = jnp.zeros((128 - rows, HD), jnp.float32)
    return jnp.concatenate(list(pieces) + [pad], axis=0).astype(jnp.bfloat16)


GROUP = D // HD // KVH
KV_WIDTH = KVH * HD


def attend_main_kernel(
    len_ref, bias_ref, cos_ref, sin_ref, cache_ref, parts_ref, out_ref, kv_ref, qkv_ref, piece_ref
):
    rows = qkv_ref.shape[0]
    qkv_ref[...] = jnp.zeros(qkv_ref.shape, jnp.float32)
    load_qkv(True, parts_ref, qkv_ref)
    plain, rotated = head_readers(qkv_ref, bias_ref, cos_ref, sin_ref)
    seen = lax.broadcasted_iota(jnp.int32, (1, cache_ref.shape[0]), 1) < len_ref[0]
    row = lax.broadcasted_iota(jnp.int32, (rows, 128), 0)
    col = lax.broadcasted_iota(jnp.int32, (rows, 128), 1)
    own = ((col <= row) & (col < STEPS)).astype(jnp.int32)
    fresh_seen = jnp.concatenate([own] * GROUP, axis=0) > 0
    for g in range(KVH):
        query = jnp.concatenate([rotated((g * GROUP + h) * HD) for h in range(GROUP)], axis=0).astype(jnp.bfloat16)
        fresh_key = rotated(D + g * HD)
        fresh_value = plain(D + KV_WIDTH + g * HD)
        kv_ref[:, g * HD : (g + 1) * HD] = fresh_key
        kv_ref[:, KV_WIDTH + g * HD : KV_WIDTH + (g + 1) * HD] = fresh_value
        key = cache_ref[:, g * HD : (g + 1) * HD]
        value = cache_ref[:, KV_WIDTH + g * HD : KV_WIDTH + (g + 1) * HD]
        mixed = head_attention(
            query, key, value, fresh_block([fresh_key]), fresh_block([fresh_value]), seen, fresh_seen
        )
        for h in range(GROUP):
            r, place = divmod(g * GROUP + h, FEATURES // HD)
            j, lane = place // 2, (place % 2) * HD
            for s in range(STEPS):
                at = s * 8 + j
                piece_ref[r, at : at + 1, lane : lane + HD] = mixed[h * rows + s : h * rows + s + 1]
    for r in range(ROW_BLOCKS):
        piece = piece_ref[r].astype(jnp.bfloat16)
        for c in range(COL_BLOCKS):
            out_ref[r * COL_BLOCKS + c] = piece


def attend_main(prefix_len, bias, cosine, sine, cache, parts):
    return pl.pallas_call(
        attend_main_kernel,
        out_shape=(
            jax.ShapeDtypeStruct((32, 16, TILE), jnp.bfloat16),
            jax.ShapeDtypeStruct((8, 2 * KV_WIDTH), jnp.float32),
        ),
        in_specs=[SMEM] + [VMEM] * 5,
        out_specs=(whole((32, 16, TILE)), whole((8, 2 * KV_WIDTH))),
        scratch_shapes=[
            pltpu.VMEM((8, QKV), jnp.float32),
            pltpu.VMEM((ROW_BLOCKS, 16, TILE), jnp.float32),
        ],
        compiler_params=kernel_params(),
        cost_estimate=cost(2 * 10**8, 6 * 10**6),
        name="attend_main",
    )(prefix_len, bias, cosine, sine, cache, parts)


def attend_cont_kernel(
    len_ref, bound_ref, bias_ref, cos_ref, sin_ref, cache_ref, kv_ref, parts_ref, out_ref, qkv_ref
):
    rows = qkv_ref.shape[0]
    load_qkv(False, parts_ref, qkv_ref)
    plain, rotated = head_readers(qkv_ref, bias_ref, cos_ref, sin_ref)
    seen = lax.broadcasted_iota(jnp.int32, (1, cache_ref.shape[0]), 1) < len_ref[0]
    row = lax.broadcasted_iota(jnp.int32, (rows, 128), 0)
    col = lax.broadcasted_iota(jnp.int32, (rows, 128), 1)
    own = (row // STEPS == col // STEPS) & (col <= row)
    main = (col >= rows) & (col < rows + bound_ref[0])
    fresh_seen = jnp.concatenate([(own | main).astype(jnp.int32)] * GROUP, axis=0) > 0
    for g in range(KVH):
        query = jnp.concatenate([rotated((g * GROUP + h) * HD) for h in range(GROUP)], axis=0).astype(jnp.bfloat16)
        at_key = slice(g * HD, (g + 1) * HD)
        at_value = slice(KV_WIDTH + g * HD, KV_WIDTH + (g + 1) * HD)
        fresh_key = fresh_block([rotated(D + g * HD), kv_ref[:, at_key]])
        fresh_value = fresh_block([plain(D + KV_WIDTH + g * HD), kv_ref[:, at_value]])
        mixed = head_attention(
            query, cache_ref[:, at_key], cache_ref[:, at_value], fresh_key, fresh_value, seen, fresh_seen
        )
        mixed = mixed.astype(jnp.bfloat16)
        for h in range(GROUP):
            out_ref[:, (g * GROUP + h) * HD : (g * GROUP + h + 1) * HD] = mixed[h * rows : (h + 1) * rows]


def attend_cont(*args):
    return pl.pallas_call(
        attend_cont_kernel,
        out_shape=jax.ShapeDtypeStruct((CTOK, D), jnp.bfloat16),
        in_specs=[SMEM, SMEM] + [VMEM] * 6,
        out_specs=whole((CTOK, D)),
        scratch_shapes=[pltpu.VMEM((CTOK, QKV), jnp.float32)],
        compiler_params=kernel_params(),
        cost_estimate=cost(4 * 10**8, 8 * 10**6),
        name="attend_cont",
    )(*args)


def readout_kernel(head_ref, w_hbm, out_ref, w_ref, sem):
    copy = pltpu.make_async_copy(w_hbm.at[0], w_ref, sem)
    copy.start()
    row = head_ref[pl.ds(lax.rem(lax.axis_index("tp"), COL_BLOCKS), 1), :]
    high = row.astype(jnp.bfloat16).astype(jnp.float32)
    middle = (row - high).astype(jnp.bfloat16).astype(jnp.float32)
    low = row - high - middle
    pieces = jnp.concatenate([high, middle, low, jnp.zeros((13, row.shape[1]), jnp.float32)], axis=0)
    copy.wait()
    prod = lax.dot_general(
        pieces.astype(jnp.bfloat16), w_ref[...], (((1,), (1,)), ((), ())), preferred_element_type=jnp.float32
    )
    out_ref[...] = prod[0:1] + prod[1:2] + prod[2:3]


def readout(value_head, blocks):
    return pl.pallas_call(
        readout_kernel,
        out_shape=jax.ShapeDtypeStruct((1, FEATURES), jnp.float32),
        in_specs=[whole(value_head.shape), HBM],
        out_specs=whole((1, FEATURES)),
        scratch_shapes=[pltpu.VMEM((FEATURES, D // COL_BLOCKS), jnp.bfloat16), pltpu.SemaphoreType.DMA],
        compiler_params=kernel_params(),
        cost_estimate=cost(2 * 10**8, 5 * 10**6),
        name="readout",
    )(value_head, in_hbm(blocks))


def out_kernel(tiles, x_ref, read_ref, w_hbm, out_ref, rows_ref, wide_ref, read8_ref, w_ref, sems):
    n = pl.program_id(0)
    members = x_ref.shape[0]
    lines = members * STEPS
    halves = TILE // 128
    tile = weight_tile(n, tiles, w_hbm, w_ref, sems)

    @pl.when(n == 0)
    def _():
        for j in range(FEATURES // TILE):
            read8_ref[j : j + 1, :] = read_ref[:, j * TILE : (j + 1) * TILE]
        out_ref[:, 8:, :] = jnp.broadcast_to(read8_ref[...][None], (members, 8, TILE))
        packed = x_ref[...].reshape(members * 16, TILE).astype(jnp.float32)
        for k in range(halves):
            wide_ref[k] = packed[:, k * 128 : (k + 1) * 128]
            for j in range(FEATURES // TILE):
                lane = j * TILE + k * 128
                rows_ref[:, lane : lane + 128] = wide_ref[k, pl.ds(j, lines, stride=8), :].astype(jnp.bfloat16)

    tile.wait()
    prod = jnp.dot(rows_ref[...], w_ref[n], preferred_element_type=jnp.float32)
    for k in range(halves):
        wide_ref[k, pl.ds(n, lines, stride=4), :] = prod[:, k * 128 : (k + 1) * 128]

    @pl.when(n == tiles - 1)
    def _():
        for k in range(halves):
            packed = wide_ref[k, : members * 8, :].reshape(members, 8, 128)
            out_ref[:, :8, k * 128 : (k + 1) * 128] = packed


def out_product(rows, read, blocks):
    members = rows.shape[0]
    tiles = blocks.shape[2] // TILE
    return pl.pallas_call(
        functools.partial(out_kernel, tiles),
        out_shape=jax.ShapeDtypeStruct((members, 16, TILE), jnp.float32),
        grid=(tiles,),
        in_specs=[whole(rows.shape), whole(read.shape), HBM],
        out_specs=whole((members, 16, TILE)),
        scratch_shapes=[
            pltpu.VMEM((members * STEPS, FEATURES), jnp.bfloat16),
            pltpu.VMEM((TILE // 128, members * 16, 128), jnp.float32),
            pltpu.VMEM((8, TILE), jnp.float32),
            pltpu.VMEM((tiles, FEATURES, TILE), jnp.bfloat16),
            pltpu.SemaphoreType.DMA((tiles,)),
        ],
        compiler_params=kernel_params(),
        cost_estimate=cost(3 * 10**8, 5 * 10**6),
        name="out_product",
    )(rows, read, in_hbm(blocks))


def finish_kernel(parts_ref, main_ref, cont_ref, head_ref, mixed_ref, out_ref, score_ref, wide_ref):
    cols = D // COL_BLOCKS
    for c in range(COL_BLOCKS):
        total = summed_block(parts_ref, c, slice(0, TILE))
        for j in range(cols // TILE):
            at = slice(c * cols + j * TILE, c * cols + (j + 1) * TILE)
            for s in range(STEPS):
                wide_ref[s : s + 1, at] = total[s * 4 + j : s * 4 + j + 1]
    out_ref[...] = (main_ref[...].astype(jnp.float32) + wide_ref[:STEPS, :]).astype(jnp.bfloat16)
    score = jnp.zeros((CTOK, TILE), jnp.float32)
    direct = jnp.zeros((STEPS, TILE), jnp.float32)
    for r in range(ROW_BLOCKS):
        read = parts_ref[r * COL_BLOCKS, 8:, :]
        for c in range(1, COL_BLOCKS):
            read = read + parts_ref[r * COL_BLOCKS + c, 8:, :]
        for j in range(FEATURES // TILE):
            lanes = slice(r * FEATURES + j * TILE, r * FEATURES + (j + 1) * TILE)
            score = score + mixed_ref[:, lanes].astype(jnp.float32) * read[j : j + 1, :]
            for c in range(CONTS):
                direct = direct + cont_ref[c, :, lanes].astype(jnp.float32) * head_ref[:, lanes]
    total = jnp.sum(score, axis=0, keepdims=True) + jnp.sum(direct, axis=0, keepdims=True)
    score_ref[...] = jnp.broadcast_to(jnp.sum(total, axis=1, keepdims=True) / CONTS, (8, 128))


def finish(parts, main, cont, head, mixed):
    return pl.pallas_call(
        finish_kernel,
        out_shape=(
            jax.ShapeDtypeStruct((STEPS, D), jnp.bfloat16),
            jax.ShapeDtypeStruct((8, 128), jnp.float32),
        ),
        in_specs=[whole(parts.shape), whole(main.shape), whole(cont.shape), whole(head.shape), whole(mixed.shape)],
        out_specs=(whole((STEPS, D)), whole((8, 128))),
        scratch_shapes=[pltpu.VMEM((8, D), jnp.float32)],
        compiler_params=kernel_params(),
        cost_estimate=cost(10**6, 2 * 10**6),
        name="finish",
    )(parts, main, cont, head, mixed)


def rope_tables(positions):
    half = HD // 2
    frequency = THETA ** (-(jnp.arange(half, dtype=jnp.float32) * 2.0) / HD)
    angles = positions.astype(jnp.float32)[:, None] * frequency[None, :]
    cosine = jnp.cos(angles)
    sine = jnp.sin(angles)
    return jnp.concatenate([cosine, cosine], axis=1), jnp.concatenate([-sine, sine], axis=1)


def exchange(rows):
    return lax.all_to_all(rows, "tp", split_axis=0, concat_axis=0, tiled=True)


def from_side(rows, dy, dx):
    route = []
    for to in range(MEMBERS):
        z, y, x = to // 8, to // 4 % 2, to % 4
        route.append((z * 8 + (y + dy) % 2 * 4 + (x + dx) % 4, to))
    return lax.ppermute(rows, "tp", route)


def from_along(rows, dz):
    route = [((to + dz * COL_BLOCKS) % MEMBERS, to) for to in range(MEMBERS)]
    return lax.ppermute(rows, "tp", route)


def project(rows, blocks):
    near = gather_along([rows[0]] + [from_along(rows[ROW_BLOCKS - k], k) for k in range(1, ROW_BLOCKS)])
    half = ROW_BLOCKS // 2
    over = from_side(near, 1, 0)
    here, far, places = [], [], []
    for dy, mine in ((0, near), (1, over)):
        after = from_side(mine, 0, 1)
        before = from_side(mine, 0, 3)
        far += [from_side(before[:half], 0, 3), from_side(after[half:], 0, 1)]
        here += [mine, after, before]
        places += [(dy, 0), (dy, 1), (dy, 3)]
    earlier = block_product(here, blocks)
    return exchange(block_product(far, blocks, (earlier,), tuple(places) + ((0, 2), (1, 2))))


def on_device(
    main_inputs, cont_inputs, prefix_cache, prefix_len, boundary, rms_gain, qkv_bias, w_qkv, w_out, value_head
):
    main = main_inputs.reshape(STEPS, D)
    cont = cont_inputs.reshape(CONTS, STEPS, D)
    bias = qkv_bias[None, :]
    cache = prefix_cache[0]
    head = value_head[None, :]
    step = jnp.arange(CTOK, dtype=jnp.int32) % STEPS
    main_tables = rope_tables(prefix_len + step[:8])
    cont_tables = rope_tables(prefix_len + boundary + step)
    read = readout(value_head.reshape(COL_BLOCKS, D // COL_BLOCKS), w_out)
    *rows, main_rows = norm_rows(main, cont, rms_gain[None, :])
    main_parts = exchange(main_product(exchange(main_rows), w_qkv))
    parts = project(rows, w_qkv)
    mixed, main_kv = attend_main(prefix_len, bias, *main_tables, cache, main_parts)
    mixed = exchange(mixed)
    cont_mixed = attend_cont(prefix_len, boundary, bias, *cont_tables, cache, main_kv, parts)
    parts = exchange(out_product(mixed, read, w_out))
    main_out, score = finish(parts, main, cont, head, cont_mixed)
    return main_out[None], score[0, :1]


def solution(mesh):
    return jax.shard_map(
        on_device,
        mesh=mesh,
        in_specs=(
            P(("grp", "tp"), None, None),
            P(("grp", "tp"), None, None, None),
            P(("grp", "tp"), None, None),
            P(("grp", "tp")),
            P(("grp", "tp")),
            P(),
            P(),
            P("tp", None, None),
            P("tp", None, None),
            P(),
        ),
        out_specs=(P(("grp", "tp"), None, None), P(("grp", "tp"))),
        check_vma=False,
    )
```

```python
import functools
import math

import jax
import jax.numpy as jnp
from jax import lax
from jax.experimental import pallas as pl
from jax.experimental.pallas import tpu as pltpu
from jax.sharding import PartitionSpec as P

KVH = 8
HD = 128
D = 8192
QKV = 10240
ROW_BLOCKS = 4
COL_BLOCKS = 8
MEMBERS = ROW_BLOCKS * COL_BLOCKS
FEATURES = D // ROW_BLOCKS
CONTS = 8
STEPS = 2
CTOK = CONTS * STEPS
TILE = 256

THETA = 1000000.0
EPS = 1e-06
MASKED_SCORE = -1e30

VMEM_LIMIT = 32 * 1024 * 1024
VMEM = pl.BlockSpec(memory_space=pltpu.VMEM)
SMEM = pl.BlockSpec(memory_space=pltpu.SMEM)
HBM = pl.BlockSpec(memory_space=pltpu.HBM)
UNREAD = pl.BlockSpec(memory_space=pl.ANY)


def whole(shape):
    return pl.BlockSpec(shape, lambda *_: (0,) * len(shape))


def cost(flops, moved):
    return pl.CostEstimate(flops=flops, bytes_accessed=moved, transcendentals=0)


def in_hbm(array):
    return pltpu.with_memory_space_constraint(array, pltpu.HBM)


def kernel_params():
    return pltpu.CompilerParams(vmem_limit_bytes=VMEM_LIMIT)


def fetch(pairs, sems):
    copies = [pltpu.make_async_copy(src, dst, sems.at[i]) for i, (src, dst) in enumerate(pairs)]
    for copy in copies:
        copy.start()
    for copy in copies:
        copy.wait()


def normed(wide, gain):
    inv = lax.rsqrt(jnp.mean(wide * wide, axis=-1, keepdims=True) + EPS)
    return wide * inv * gain


def norm_main_kernel(main_hbm, gain_hbm, out_ref, main_ref, gain_ref, piece_ref, sems):
    fetch(((main_hbm, main_ref), (gain_hbm, gain_ref)), sems)
    main = normed(main_ref[...].astype(jnp.float32), gain_ref[...])
    for r in range(ROW_BLOCKS):
        for j in range(FEATURES // TILE):
            lanes = slice(r * FEATURES + j * TILE, r * FEATURES + (j + 1) * TILE)
            for s in range(STEPS):
                piece_ref[r, s * 8 + j : s * 8 + j + 1, :] = main[s : s + 1, lanes]
    for r in range(ROW_BLOCKS):
        piece = piece_ref[r].astype(jnp.bfloat16)
        for c in range(COL_BLOCKS):
            out_ref[r * COL_BLOCKS + c] = piece


def norm_main(main, gain):
    return pl.pallas_call(
        norm_main_kernel,
        out_shape=jax.ShapeDtypeStruct((MEMBERS, CTOK, TILE), jnp.bfloat16),
        in_specs=[HBM] * 2,
        out_specs=VMEM,
        scratch_shapes=[
            pltpu.VMEM((STEPS, D), jnp.bfloat16),
            pltpu.VMEM((1, D), jnp.float32),
            pltpu.VMEM((ROW_BLOCKS, 16, TILE), jnp.float32),
            pltpu.SemaphoreType.DMA((2,)),
        ],
        compiler_params=kernel_params(),
        cost_estimate=cost(10**6, 4 * 10**6),
        name="norm_main",
    )(in_hbm(main), in_hbm(gain))


def norm_cont_kernel(cont_hbm, gain_hbm, after_ref, z0_ref, z1_ref, z2_ref, z3_ref, cont_ref, gain_ref, rows_ref, sems):
    fetch(((cont_hbm, cont_ref), (gain_hbm, gain_ref)), sems)
    for c in range(CONTS):
        rows_ref[c * STEPS : (c + 1) * STEPS, :] = cont_ref[c].astype(jnp.float32)
    cont = normed(rows_ref[...], gain_ref[...]).astype(jnp.bfloat16)
    for r in range(ROW_BLOCKS):
        ahead = lax.rem(r + ROW_BLOCKS - lax.axis_index("tp") // COL_BLOCKS, ROW_BLOCKS)
        for k, z_ref in enumerate((z0_ref, z1_ref, z2_ref, z3_ref)):

            @pl.when(ahead == k)
            def _():
                z_ref[...] = cont[:, r * FEATURES : (r + 1) * FEATURES]


def norm_cont(cont, gain, after):
    return pl.pallas_call(
        norm_cont_kernel,
        out_shape=[jax.ShapeDtypeStruct((CTOK, FEATURES), jnp.bfloat16)] * ROW_BLOCKS,
        in_specs=[HBM] * 2 + [UNREAD],
        out_specs=[VMEM] * ROW_BLOCKS,
        scratch_shapes=[
            pltpu.VMEM((CONTS, STEPS, D), jnp.bfloat16),
            pltpu.VMEM((1, D), jnp.float32),
            pltpu.VMEM((CTOK, D), jnp.float32),
            pltpu.SemaphoreType.DMA((2,)),
        ],
        compiler_params=kernel_params(),
        cost_estimate=cost(10**6, 5 * 10**6),
        name="norm_cont",
    )(in_hbm(cont), in_hbm(gain), after)


def weight_tile(n, tiles, w_hbm, w_ref, sems):
    def copy(i):
        lanes = pl.ds(pl.multiple_of(i * TILE, TILE), TILE)
        return pltpu.make_async_copy(w_hbm.at[0, :, lanes], w_ref.at[i], sems.at[i])

    @pl.when(n == 0)
    def _():
        for i in range(tiles):
            copy(i).start()

    return copy(n)


REST = 768
CONT_LANES = QKV // COL_BLOCKS + REST


def rest_tile(block):
    return jnp.where(block == 6, 2, 0)


def product_kernel(tiles, counts, places, *refs):
    x_refs, refs = refs[: len(counts)], refs[len(counts) :]
    if places:
        earlier_ref, w_hbm, out_ref, rows_ref, w_ref, sems, part_ref = refs
    else:
        w_hbm, part_ref, rows_ref, w_ref, sems = refs
    n = pl.program_id(0)
    members = sum(counts)
    tile = weight_tile(n, tiles, w_hbm, w_ref, sems)

    @pl.when(n == 0)
    def _():
        at = 0
        for x_ref, size in zip(x_refs, counts):
            rows_ref[at * CTOK : (at + size) * CTOK, :] = x_ref[...].reshape(size * CTOK, FEATURES)
            at += size

    tile.wait()
    prod = jnp.dot(rows_ref[...], w_ref[n], preferred_element_type=jnp.float32)
    high = prod.astype(jnp.bfloat16)
    part_ref[:, :, pl.ds(pl.multiple_of(n * TILE, TILE), TILE)] = high.reshape(members, CTOK, TILE)
    start = rest_tile(lax.rem(lax.axis_index("tp"), COL_BLOCKS))

    @pl.when((n >= start) & (n < start + REST // TILE))
    def _():
        low = (prod - high.astype(jnp.float32)).astype(jnp.bfloat16)
        lane = pl.multiple_of((tiles + n - start) * TILE, TILE)
        part_ref[:, :, pl.ds(lane, TILE)] = low.reshape(members, CTOK, TILE)

    if places:

        @pl.when(n == tiles - 1)
        def _():
            column = lax.rem(lax.axis_index("tp"), COL_BLOCKS)
            y, x = column // 4, lax.rem(column, 4)
            done = earlier_ref.shape[0] // ROW_BLOCKS
            for i, (dy, dx) in enumerate(places):
                home = lax.rem(y + dy, 2) * 4 + lax.rem(x + dx, 4)
                for r in range(ROW_BLOCKS):
                    if i < done:
                        message = earlier_ref[i * ROW_BLOCKS + r]
                    else:
                        message = part_ref[(i - done) * ROW_BLOCKS + r]
                    out_ref[r * COL_BLOCKS + home] = message


def block_product(messages, blocks, earlier=(), places=()):
    tiles = blocks.shape[2] // TILE
    counts = tuple(rows.shape[0] for rows in messages)
    members = sum(counts)
    part = (members, CTOK, tiles * TILE + REST)
    out = (MEMBERS,) + part[1:] if places else part
    return pl.pallas_call(
        functools.partial(product_kernel, tiles, counts, places),
        out_shape=jax.ShapeDtypeStruct(out, jnp.bfloat16),
        grid=(tiles,),
        in_specs=[VMEM] * (len(counts) + len(earlier)) + [HBM],
        out_specs=VMEM,
        scratch_shapes=[
            pltpu.VMEM((members * CTOK, FEATURES), jnp.bfloat16),
            pltpu.VMEM((tiles, FEATURES, TILE), jnp.bfloat16),
            pltpu.SemaphoreType.DMA((tiles,)),
        ]
        + ([pltpu.VMEM(part, jnp.bfloat16)] if places else []),
        compiler_params=kernel_params(),
        cost_estimate=cost(2 * members * CTOK * FEATURES * tiles * TILE, 14 * 10**6),
        name="block_product",
    )(*messages, *earlier, in_hbm(blocks))


def main_kernel(tiles, x_ref, w_hbm, after_ref, out_ref, rows_ref, wide_ref, w_ref, sems):
    n = pl.program_id(0)
    members = x_ref.shape[0]
    lines = members * STEPS
    halves = TILE // 128
    tile = weight_tile(n, tiles, w_hbm, w_ref, sems)

    @pl.when(n == 0)
    def _():
        packed = x_ref[...].reshape(members * CTOK, TILE).astype(jnp.float32)
        for k in range(halves):
            wide_ref[k] = packed[:, k * 128 : (k + 1) * 128]
            for j in range(FEATURES // TILE):
                lane = j * TILE + k * 128
                rows_ref[:, lane : lane + 128] = wide_ref[k, pl.ds(j, lines, stride=8), :].astype(jnp.bfloat16)

    tile.wait()
    prod = jnp.dot(rows_ref[...], w_ref[n], preferred_element_type=jnp.float32)
    for k in range(halves):
        wide_ref[k, pl.ds(n, lines, stride=8), :] = prod[:, k * 128 : (k + 1) * 128]
    start = rest_tile(lax.rem(lax.axis_index("tp"), COL_BLOCKS))

    @pl.when((n >= start) & (n < start + REST // TILE))
    def _():
        low = prod - prod.astype(jnp.bfloat16).astype(jnp.float32)
        for k in range(halves):
            wide_ref[k, pl.ds(tiles + n - start, lines, stride=8), :] = low[:, k * 128 : (k + 1) * 128]

    @pl.when(n == tiles - 1)
    def _():
        for k in range(halves):
            packed = wide_ref[k].astype(jnp.bfloat16).reshape(members, CTOK, 128)
            out_ref[:, :, k * 128 : (k + 1) * 128] = packed


def main_product(rows, blocks, after):
    tiles = blocks.shape[2] // TILE
    return pl.pallas_call(
        functools.partial(main_kernel, tiles),
        out_shape=jax.ShapeDtypeStruct(rows.shape, jnp.bfloat16),
        grid=(tiles,),
        in_specs=[VMEM, HBM, UNREAD],
        out_specs=VMEM,
        scratch_shapes=[
            pltpu.VMEM((MEMBERS * STEPS, FEATURES), jnp.bfloat16),
            pltpu.VMEM((TILE // 128, MEMBERS * CTOK, 128), jnp.float32),
            pltpu.VMEM((tiles, FEATURES, TILE), jnp.bfloat16),
            pltpu.SemaphoreType.DMA((tiles,)),
        ],
        compiler_params=kernel_params(),
        cost_estimate=cost(3 * 10**8, 13 * 10**6),
        name="main_product",
    )(rows, in_hbm(blocks), after)


def gather_kernel(own_ref, ahead1_ref, ahead2_ref, ahead3_ref, out_ref):
    z = lax.axis_index("tp") // COL_BLOCKS
    for k, ref in enumerate((own_ref, ahead1_ref, ahead2_ref, ahead3_ref)):
        out_ref[lax.rem(z + k, ROW_BLOCKS)] = ref[...]


def gather_along(parts):
    return pl.pallas_call(
        gather_kernel,
        out_shape=jax.ShapeDtypeStruct((ROW_BLOCKS,) + parts[0].shape, jnp.bfloat16),
        in_specs=[VMEM] * ROW_BLOCKS,
        out_specs=VMEM,
        compiler_params=kernel_params(),
        cost_estimate=cost(10**5, 10**6),
        name="gather_along",
    )(*parts)


def summed_block(parts_ref, c, lanes):
    total = parts_ref[c, :, lanes].astype(jnp.float32)
    for r in range(1, ROW_BLOCKS):
        total = total + parts_ref[r * COL_BLOCKS + c, :, lanes].astype(jnp.float32)
    return total


def head_attention(query, key, value, fresh_key, fresh_value, seen, fresh_seen):
    inv_root = 1.0 / math.sqrt(HD)
    contract = (((1,), (1,)), ((), ()))
    old = lax.dot_general(query, key, contract, preferred_element_type=jnp.float32) * inv_root
    new = lax.dot_general(query, fresh_key, contract, preferred_element_type=jnp.float32) * inv_root
    old = jnp.where(seen, old, MASKED_SCORE)
    new = jnp.where(fresh_seen, new, MASKED_SCORE)
    highest = jnp.maximum(jnp.max(old, axis=-1, keepdims=True), jnp.max(new, axis=-1, keepdims=True))
    old = jnp.exp(old - highest)
    new = jnp.exp(new - highest)
    mass = jnp.sum(old, axis=-1, keepdims=True) + jnp.sum(new, axis=-1, keepdims=True)
    inv_mass = 1.0 / mass
    mixed = jnp.dot((old * inv_mass).astype(jnp.bfloat16), value, preferred_element_type=jnp.float32)
    return mixed + jnp.dot((new * inv_mass).astype(jnp.bfloat16), fresh_value, preferred_element_type=jnp.float32)


def load_qkv(main, parts_ref, qkv_ref):
    cols = QKV // COL_BLOCKS
    for c in range(COL_BLOCKS):
        first = 2 if c == 6 else 0
        total = summed_block(parts_ref, c, slice(0, TILE if main else cols + REST))
        for j in range(cols // TILE):
            lanes = slice(c * cols + j * TILE, c * cols + (j + 1) * TILE)
            rest = j - first
            has_rest = 0 <= rest < REST // TILE
            if main:
                for s in range(STEPS):
                    line = total[s * 8 + j : s * 8 + j + 1]
                    if has_rest:
                        at = s * 8 + cols // TILE + rest
                        line = line + total[at : at + 1]
                    qkv_ref[s : s + 1, lanes] = line
            else:
                value = total[:, j * TILE : (j + 1) * TILE]
                if has_rest:
                    value = value + total[:, cols + rest * TILE : cols + (rest + 1) * TILE]
                qkv_ref[:, lanes] = value


def head_readers(qkv_ref, bias_ref, cos_ref, sin_ref):
    cosine = cos_ref[...]
    sine = sin_ref[...]

    def plain(start):
        return qkv_ref[:, start : start + HD] + bias_ref[:, start : start + HD]

    def rotated(start):
        head = plain(start)
        return head * cosine + pltpu.roll(head, HD // 2, 1) * sine

    return plain, rotated


def fresh_block(pieces):
    rows = sum(piece.shape[0] for piece in pieces)
    pad = jnp.zeros((128 - rows, HD), jnp.float32)
    return jnp.concatenate(list(pieces) + [pad], axis=0).astype(jnp.bfloat16)


GROUP = D // HD // KVH
KV_WIDTH = KVH * HD


def attend_main_kernel(
    len_ref, bias_ref, cos_ref, sin_ref, cache_ref, parts_ref, *refs
):
    out_ref, kv_ref, qkv_ref, piece_ref = refs[-4:]
    rows = qkv_ref.shape[0]
    qkv_ref[...] = jnp.zeros(qkv_ref.shape, jnp.float32)
    load_qkv(True, parts_ref, qkv_ref)
    plain, rotated = head_readers(qkv_ref, bias_ref, cos_ref, sin_ref)
    seen = lax.broadcasted_iota(jnp.int32, (1, cache_ref.shape[0]), 1) < len_ref[0]
    row = lax.broadcasted_iota(jnp.int32, (rows, 128), 0)
    col = lax.broadcasted_iota(jnp.int32, (rows, 128), 1)
    own = ((col <= row) & (col < STEPS)).astype(jnp.int32)
    fresh_seen = jnp.concatenate([own] * GROUP, axis=0) > 0
    for g in range(KVH):
        query = jnp.concatenate([rotated((g * GROUP + h) * HD) for h in range(GROUP)], axis=0).astype(jnp.bfloat16)
        fresh_key = rotated(D + g * HD)
        fresh_value = plain(D + KV_WIDTH + g * HD)
        kv_ref[:, g * HD : (g + 1) * HD] = fresh_key
        kv_ref[:, KV_WIDTH + g * HD : KV_WIDTH + (g + 1) * HD] = fresh_value
        key = cache_ref[:, g * HD : (g + 1) * HD]
        value = cache_ref[:, KV_WIDTH + g * HD : KV_WIDTH + (g + 1) * HD]
        mixed = head_attention(
            query, key, value, fresh_block([fresh_key]), fresh_block([fresh_value]), seen, fresh_seen
        )
        for h in range(GROUP):
            r, place = divmod(g * GROUP + h, FEATURES // HD)
            j, lane = place // 2, (place % 2) * HD
            for s in range(STEPS):
                at = s * 8 + j
                piece_ref[r, at : at + 1, lane : lane + HD] = mixed[h * rows + s : h * rows + s + 1]
    for r in range(ROW_BLOCKS):
        piece = piece_ref[r].astype(jnp.bfloat16)
        for c in range(COL_BLOCKS):
            out_ref[r * COL_BLOCKS + c] = piece


def attend_main(prefix_len, bias, cosine, sine, cache, parts, after):
    return pl.pallas_call(
        attend_main_kernel,
        out_shape=(
            jax.ShapeDtypeStruct((32, 16, TILE), jnp.bfloat16),
            jax.ShapeDtypeStruct((8, 2 * KV_WIDTH), jnp.float32),
        ),
        in_specs=[SMEM] + [VMEM] * 5 + [UNREAD] * len(after),
        out_specs=(whole((32, 16, TILE)), whole((8, 2 * KV_WIDTH))),
        scratch_shapes=[
            pltpu.VMEM((8, QKV), jnp.float32),
            pltpu.VMEM((ROW_BLOCKS, 16, TILE), jnp.float32),
        ],
        compiler_params=kernel_params(),
        cost_estimate=cost(2 * 10**8, 13 * 10**6),
        name="attend_main",
    )(prefix_len, bias, cosine, sine, cache, parts, *after)


def last_kernel(
    len_ref, bound_ref, bias_ref, cos_ref, sin_ref, cache_ref, kv_ref, parts_ref, main_ref, cont_ref, head_ref,
    out_ref, score_ref, qkv_ref, wide_ref, read_ref,
):
    out_cols = D // COL_BLOCKS
    for c in range(COL_BLOCKS):
        total = summed_block(parts_ref, c, slice(CONT_LANES, CONT_LANES + TILE))
        total = total[:8] + total[8:]
        for j in range(out_cols // TILE):
            at = slice(c * out_cols + j * TILE, c * out_cols + (j + 1) * TILE)
            for s in range(STEPS):
                wide_ref[s : s + 1, at] = total[s * 4 + j : s * 4 + j + 1]
    out_ref[...] = (main_ref[...].astype(jnp.float32) + wide_ref[:STEPS, :]).astype(jnp.bfloat16)
    for r in range(ROW_BLOCKS):
        read = parts_ref[r * COL_BLOCKS, :, CONT_LANES + TILE :].astype(jnp.float32)
        for c in range(1, COL_BLOCKS):
            read = read + parts_ref[r * COL_BLOCKS + c, :, CONT_LANES + TILE :].astype(jnp.float32)
        read_ref[r] = read[:8] + read[8:]
    rows = qkv_ref.shape[0]
    load_qkv(False, parts_ref, qkv_ref)
    plain, rotated = head_readers(qkv_ref, bias_ref, cos_ref, sin_ref)
    seen = lax.broadcasted_iota(jnp.int32, (1, cache_ref.shape[0]), 1) < len_ref[0]
    row = lax.broadcasted_iota(jnp.int32, (rows, 128), 0)
    col = lax.broadcasted_iota(jnp.int32, (rows, 128), 1)
    own = (row // STEPS == col // STEPS) & (col <= row)
    main = (col >= rows) & (col < rows + bound_ref[0])
    fresh_seen = jnp.concatenate([(own | main).astype(jnp.int32)] * GROUP, axis=0) > 0
    score = jnp.zeros((rows, HD), jnp.float32)
    direct = jnp.zeros((STEPS, HD), jnp.float32)
    for g in range(KVH):
        query = jnp.concatenate([rotated((g * GROUP + h) * HD) for h in range(GROUP)], axis=0).astype(jnp.bfloat16)
        at_key = slice(g * HD, (g + 1) * HD)
        at_value = slice(KV_WIDTH + g * HD, KV_WIDTH + (g + 1) * HD)
        fresh_key = fresh_block([rotated(D + g * HD), kv_ref[:, at_key]])
        fresh_value = fresh_block([plain(D + KV_WIDTH + g * HD), kv_ref[:, at_value]])
        mixed = head_attention(
            query, cache_ref[:, at_key], cache_ref[:, at_value], fresh_key, fresh_value, seen, fresh_seen
        )
        mixed = mixed.astype(jnp.bfloat16).astype(jnp.float32)
        for h in range(GROUP):
            head = g * GROUP + h
            r, place = divmod(head, FEATURES // HD)
            j, lane = place // 2, (place % 2) * HD
            score = score + mixed[h * rows : (h + 1) * rows] * read_ref[r, j : j + 1, lane : lane + HD]
            lanes = slice(head * HD, (head + 1) * HD)
            for c in range(CONTS):
                direct = direct + cont_ref[c, :, lanes].astype(jnp.float32) * head_ref[:, lanes]
    total = jnp.sum(score, axis=0, keepdims=True) + jnp.sum(direct, axis=0, keepdims=True)
    score_ref[...] = jnp.broadcast_to(jnp.sum(total, axis=1, keepdims=True) / CONTS, (8, 128))


def last(*args):
    return pl.pallas_call(
        last_kernel,
        out_shape=(
            jax.ShapeDtypeStruct((STEPS, D), jnp.bfloat16),
            jax.ShapeDtypeStruct((8, 128), jnp.float32),
        ),
        in_specs=[SMEM, SMEM] + [VMEM] * 9,
        out_specs=(VMEM, VMEM),
        scratch_shapes=[
            pltpu.VMEM((CTOK, QKV), jnp.float32),
            pltpu.VMEM((8, D), jnp.float32),
            pltpu.VMEM((ROW_BLOCKS, 8, TILE), jnp.float32),
        ],
        compiler_params=kernel_params(),
        cost_estimate=cost(4 * 10**8, 18 * 10**6),
        name="attend_cont",
    )(*args)


def readout_kernel(head_ref, w_hbm, out_ref, w_ref, sem):
    copy = pltpu.make_async_copy(w_hbm.at[0], w_ref, sem)
    copy.start()
    row = head_ref[pl.ds(lax.rem(lax.axis_index("tp"), COL_BLOCKS), 1), :]
    high = row.astype(jnp.bfloat16).astype(jnp.float32)
    middle = (row - high).astype(jnp.bfloat16).astype(jnp.float32)
    low = row - high - middle
    pieces = jnp.concatenate([high, middle, low, jnp.zeros((13, row.shape[1]), jnp.float32)], axis=0)
    copy.wait()
    prod = lax.dot_general(
        pieces.astype(jnp.bfloat16), w_ref[...], (((1,), (1,)), ((), ())), preferred_element_type=jnp.float32
    )
    out_ref[...] = prod[0:1] + prod[1:2] + prod[2:3]


def readout(value_head, blocks):
    return pl.pallas_call(
        readout_kernel,
        out_shape=jax.ShapeDtypeStruct((1, FEATURES), jnp.float32),
        in_specs=[whole(value_head.shape), HBM],
        out_specs=whole((1, FEATURES)),
        scratch_shapes=[pltpu.VMEM((FEATURES, D // COL_BLOCKS), jnp.bfloat16), pltpu.SemaphoreType.DMA],
        compiler_params=kernel_params(),
        cost_estimate=cost(2 * 10**8, 12 * 10**6),
        name="readout",
    )(value_head, in_hbm(blocks))


def split(wide):
    high = wide.astype(jnp.bfloat16).astype(jnp.float32)
    return jnp.concatenate([high, wide - high], axis=-2).astype(jnp.bfloat16)


def out_kernel(tiles, x_ref, read_ref, cont_ref, w_hbm, out_ref, rows_ref, wide_ref, read8_ref, w_ref, sems):
    n = pl.program_id(0)
    members = x_ref.shape[0]
    lines = members * STEPS
    halves = TILE // 128
    tile = weight_tile(n, tiles, w_hbm, w_ref, sems)

    @pl.when(n == 0)
    def _():
        out_ref[:, :, :CONT_LANES] = cont_ref[...]
        for j in range(FEATURES // TILE):
            read8_ref[j : j + 1, :] = read_ref[:, j * TILE : (j + 1) * TILE]
        out_ref[:, :, CONT_LANES + TILE :] = jnp.broadcast_to(split(read8_ref[...])[None], (members, 16, TILE))
        packed = x_ref[...].reshape(members * 16, TILE).astype(jnp.float32)
        for k in range(halves):
            wide_ref[k] = packed[:, k * 128 : (k + 1) * 128]
            for j in range(FEATURES // TILE):
                lane = j * TILE + k * 128
                rows_ref[:, lane : lane + 128] = wide_ref[k, pl.ds(j, lines, stride=8), :].astype(jnp.bfloat16)

    tile.wait()
    prod = jnp.dot(rows_ref[...], w_ref[n], preferred_element_type=jnp.float32)
    for k in range(halves):
        wide_ref[k, pl.ds(n, lines, stride=4), :] = prod[:, k * 128 : (k + 1) * 128]

    @pl.when(n == tiles - 1)
    def _():
        for k in range(halves):
            lane = CONT_LANES + k * 128
            out_ref[:, :, lane : lane + 128] = split(wide_ref[k, : members * 8, :].reshape(members, 8, 128))


def out_product(rows, read, cont_parts, blocks):
    members = rows.shape[0]
    tiles = blocks.shape[2] // TILE
    return pl.pallas_call(
        functools.partial(out_kernel, tiles),
        out_shape=jax.ShapeDtypeStruct((members, CTOK, CONT_LANES + 2 * TILE), jnp.bfloat16),
        grid=(tiles,),
        in_specs=[VMEM, VMEM, VMEM, HBM],
        out_specs=VMEM,
        scratch_shapes=[
            pltpu.VMEM((members * STEPS, FEATURES), jnp.bfloat16),
            pltpu.VMEM((TILE // 128, members * 16, 128), jnp.float32),
            pltpu.VMEM((8, TILE), jnp.float32),
            pltpu.VMEM((tiles, FEATURES, TILE), jnp.bfloat16),
            pltpu.SemaphoreType.DMA((tiles,)),
        ],
        compiler_params=kernel_params(),
        cost_estimate=cost(3 * 10**8, 8 * 10**6),
        name="out_product",
    )(rows, read, cont_parts, in_hbm(blocks))


def rope_tables(positions):
    half = HD // 2
    frequency = THETA ** (-(jnp.arange(half, dtype=jnp.float32) * 2.0) / HD)
    angles = positions.astype(jnp.float32)[:, None] * frequency[None, :]
    cosine = jnp.cos(angles)
    sine = jnp.sin(angles)
    return jnp.concatenate([cosine, cosine], axis=1), jnp.concatenate([-sine, sine], axis=1)


def exchange(rows):
    return lax.all_to_all(rows, "tp", split_axis=0, concat_axis=0, tiled=True)


def from_side(rows, dy, dx):
    route = []
    for to in range(MEMBERS):
        z, y, x = to // 8, to // 4 % 2, to % 4
        route.append((z * 8 + (y + dy) % 2 * 4 + (x + dx) % 4, to))
    return lax.ppermute(rows, "tp", route)


def from_along(rows, dz):
    route = [((to + dz * COL_BLOCKS) % MEMBERS, to) for to in range(MEMBERS)]
    return lax.ppermute(rows, "tp", route)


def ring(rows):
    near = gather_along([rows[0]] + [from_along(rows[ROW_BLOCKS - k], k) for k in range(1, ROW_BLOCKS)])
    half = ROW_BLOCKS // 2
    over = from_side(near, 1, 0)
    here, far = [], []
    for mine in (near, over):
        after = from_side(mine, 0, 1)
        before = from_side(mine, 0, 3)
        far += [from_side(before[:half], 0, 3), from_side(after[half:], 0, 1)]
        here += [mine, after, before]
    return here, far


HERE = ((0, 0), (0, 1), (0, 3), (1, 0), (1, 1), (1, 3))
FAR = ((0, 2), (1, 2))


def on_device(
    main_inputs, cont_inputs, prefix_cache, prefix_len, boundary, rms_gain, qkv_bias, w_qkv, w_out, value_head
):
    main = main_inputs.reshape(STEPS, D)
    cont = cont_inputs.reshape(CONTS, STEPS, D)
    bias = qkv_bias[None, :]
    cache = prefix_cache[0]
    head = value_head[None, :]
    step = jnp.arange(CTOK, dtype=jnp.int32) % STEPS
    main_tables = rope_tables(prefix_len + step[:8])
    cont_tables = rope_tables(prefix_len + boundary + step)
    read = readout(value_head.reshape(COL_BLOCKS, D // COL_BLOCKS), w_out)
    gain = rms_gain[None, :]
    main_rows = norm_main(main, gain)
    here, far = ring(norm_cont(cont, gain, main_rows))
    main_parts = exchange(main_product(exchange(main_rows), w_qkv, here[0]))
    mixed, main_kv = attend_main(prefix_len, bias, *main_tables, cache, main_parts, here)
    mixed, far = lax.optimization_barrier((mixed, far))
    mixed = exchange(mixed)
    cont_parts = block_product(far, w_qkv, (block_product(here, w_qkv),), HERE + FAR)
    parts = exchange(out_product(mixed, read, cont_parts, w_out))
    main_out, score = last(
        prefix_len, boundary, bias, *cont_tables, cache, main_kv, parts, main, cont, head
    )
    return main_out[None], score[0, :1]


def solution(mesh):
    return jax.shard_map(
        on_device,
        mesh=mesh,
        in_specs=(
            P(("grp", "tp"), None, None),
            P(("grp", "tp"), None, None, None),
            P(("grp", "tp"), None, None),
            P(("grp", "tp")),
            P(("grp", "tp")),
            P(),
            P(),
            P("tp", None, None),
            P("tp", None, None),
            P(),
        ),
        out_specs=(P(("grp", "tp"), None, None), P(("grp", "tp"))),
        check_vma=False,
    )
```

```python
import functools
import math

import jax
import jax.numpy as jnp
from jax import lax
from jax.experimental import pallas as pl
from jax.experimental.pallas import tpu as pltpu
from jax.sharding import PartitionSpec as P

KVH = 8
HD = 128
D = 8192
QKV = 10240
ROW_BLOCKS = 4
COL_BLOCKS = 8
MEMBERS = ROW_BLOCKS * COL_BLOCKS
FEATURES = D // ROW_BLOCKS
CONTS = 8
STEPS = 2
CTOK = CONTS * STEPS
TILE = 256

THETA = 1000000.0
EPS = 1e-06
MASKED_SCORE = -1e30

VMEM_LIMIT = 32 * 1024 * 1024
VMEM = pl.BlockSpec(memory_space=pltpu.VMEM)
SMEM = pl.BlockSpec(memory_space=pltpu.SMEM)
HBM = pl.BlockSpec(memory_space=pltpu.HBM)
UNREAD = pl.BlockSpec(memory_space=pl.ANY)


def whole(shape):
    return pl.BlockSpec(shape, lambda *_: (0,) * len(shape))


def cost(flops, moved):
    return pl.CostEstimate(flops=flops, bytes_accessed=moved, transcendentals=0)


def in_hbm(array):
    return pltpu.with_memory_space_constraint(array, pltpu.HBM)


def kernel_params():
    return pltpu.CompilerParams(vmem_limit_bytes=VMEM_LIMIT)


def fetch(pairs, sems):
    copies = [pltpu.make_async_copy(src, dst, sems.at[i]) for i, (src, dst) in enumerate(pairs)]
    for copy in copies:
        copy.start()
    for copy in copies:
        copy.wait()


def normed(wide, gain):
    inv = lax.rsqrt(jnp.mean(wide * wide, axis=-1, keepdims=True) + EPS)
    return wide * inv * gain


def norm_main_kernel(main_hbm, gain_hbm, out_ref, main_ref, gain_ref, piece_ref, sems):
    fetch(((main_hbm, main_ref), (gain_hbm, gain_ref)), sems)
    main = normed(main_ref[...].astype(jnp.float32), gain_ref[...])
    for r in range(ROW_BLOCKS):
        for j in range(FEATURES // TILE):
            lanes = slice(r * FEATURES + j * TILE, r * FEATURES + (j + 1) * TILE)
            for s in range(STEPS):
                piece_ref[r, s * 8 + j : s * 8 + j + 1, :] = main[s : s + 1, lanes]
    for r in range(ROW_BLOCKS):
        piece = piece_ref[r].astype(jnp.bfloat16)
        for c in range(COL_BLOCKS):
            out_ref[r * COL_BLOCKS + c] = piece


def norm_main(main, gain):
    return pl.pallas_call(
        norm_main_kernel,
        out_shape=jax.ShapeDtypeStruct((MEMBERS, CTOK, TILE), jnp.bfloat16),
        in_specs=[HBM] * 2,
        out_specs=VMEM,
        scratch_shapes=[
            pltpu.VMEM((STEPS, D), jnp.bfloat16),
            pltpu.VMEM((1, D), jnp.float32),
            pltpu.VMEM((ROW_BLOCKS, 16, TILE), jnp.float32),
            pltpu.SemaphoreType.DMA((2,)),
        ],
        compiler_params=kernel_params(),
        cost_estimate=cost(10**6, 4 * 10**6),
        name="norm_main",
    )(in_hbm(main), in_hbm(gain))


def norm_cont_kernel(cont_hbm, gain_hbm, after_ref, z0_ref, z1_ref, z2_ref, z3_ref, cont_ref, gain_ref, rows_ref, sems):
    fetch(((cont_hbm, cont_ref), (gain_hbm, gain_ref)), sems)
    for c in range(CONTS):
        rows_ref[c * STEPS : (c + 1) * STEPS, :] = cont_ref[c].astype(jnp.float32)
    cont = normed(rows_ref[...], gain_ref[...]).astype(jnp.bfloat16)
    for r in range(ROW_BLOCKS):
        ahead = lax.rem(r + ROW_BLOCKS - lax.axis_index("tp") // COL_BLOCKS, ROW_BLOCKS)
        for k, z_ref in enumerate((z0_ref, z1_ref, z2_ref, z3_ref)):

            @pl.when(ahead == k)
            def _():
                z_ref[...] = cont[:, r * FEATURES : (r + 1) * FEATURES]


def norm_cont(cont, gain, after):
    return pl.pallas_call(
        norm_cont_kernel,
        out_shape=[jax.ShapeDtypeStruct((CTOK, FEATURES), jnp.bfloat16)] * ROW_BLOCKS,
        in_specs=[HBM] * 2 + [UNREAD],
        out_specs=[VMEM] * ROW_BLOCKS,
        scratch_shapes=[
            pltpu.VMEM((CONTS, STEPS, D), jnp.bfloat16),
            pltpu.VMEM((1, D), jnp.float32),
            pltpu.VMEM((CTOK, D), jnp.float32),
            pltpu.SemaphoreType.DMA((2,)),
        ],
        compiler_params=kernel_params(),
        cost_estimate=cost(10**6, 5 * 10**6),
        name="norm_cont",
    )(in_hbm(cont), in_hbm(gain), after)


def weight_tile(n, tiles, w_hbm, w_ref, sems):
    def copy(i):
        lanes = pl.ds(pl.multiple_of(i * TILE, TILE), TILE)
        return pltpu.make_async_copy(w_hbm.at[0, :, lanes], w_ref.at[i], sems.at[i])

    @pl.when(n == 0)
    def _():
        for i in range(tiles):
            copy(i).start()

    return copy(n)


REST = 768
CONT_LANES = QKV // COL_BLOCKS + REST


def rest_tile(block):
    return jnp.where(block == 6, 2, 0)


def split(wide):
    high = wide.astype(jnp.bfloat16).astype(jnp.float32)
    return jnp.concatenate([high, wide - high], axis=-2).astype(jnp.bfloat16)


def product_kernel(tiles, counts, places, *refs):
    x_refs, refs = refs[: len(counts)], refs[len(counts) :]
    if places:
        earlier_ref, read_ref, w_hbm, out_ref, rows_ref, w_ref, sems, part_ref = refs
    else:
        w_hbm, part_ref, rows_ref, w_ref, sems = refs
    n = pl.program_id(0)
    members = sum(counts)
    tile = weight_tile(n, tiles, w_hbm, w_ref, sems)

    @pl.when(n == 0)
    def _():
        at = 0
        for x_ref, size in zip(x_refs, counts):
            rows_ref[at * CTOK : (at + size) * CTOK, :] = x_ref[...].reshape(size * CTOK, FEATURES)
            at += size

    tile.wait()
    prod = jnp.dot(rows_ref[...], w_ref[n], preferred_element_type=jnp.float32)
    high = prod.astype(jnp.bfloat16)
    part_ref[:, :, pl.ds(pl.multiple_of(n * TILE, TILE), TILE)] = high.reshape(members, CTOK, TILE)
    start = rest_tile(lax.rem(lax.axis_index("tp"), COL_BLOCKS))

    @pl.when((n >= start) & (n < start + REST // TILE))
    def _():
        low = (prod - high.astype(jnp.float32)).astype(jnp.bfloat16)
        lane = pl.multiple_of((tiles + n - start) * TILE, TILE)
        part_ref[:, :, pl.ds(lane, TILE)] = low.reshape(members, CTOK, TILE)

    if places:

        @pl.when(n == tiles - 1)
        def _():
            column = lax.rem(lax.axis_index("tp"), COL_BLOCKS)
            y, x = column // 4, lax.rem(column, 4)
            done = earlier_ref.shape[0] // ROW_BLOCKS
            out_ref[:, :, CONT_LANES:] = jnp.broadcast_to(split(read_ref[...])[None], (MEMBERS, CTOK, TILE))
            for i, (dy, dx) in enumerate(places):
                home = lax.rem(y + dy, 2) * 4 + lax.rem(x + dx, 4)
                for r in range(ROW_BLOCKS):
                    if i < done:
                        message = earlier_ref[i * ROW_BLOCKS + r]
                    else:
                        message = part_ref[(i - done) * ROW_BLOCKS + r]
                    out_ref[r * COL_BLOCKS + home, :, :CONT_LANES] = message


def block_product(messages, blocks, earlier=(), places=()):
    tiles = blocks.shape[2] // TILE
    counts = tuple(rows.shape[0] for rows in messages)
    members = sum(counts)
    part = (members, CTOK, tiles * TILE + REST)
    out = (MEMBERS, CTOK, CONT_LANES + TILE) if places else part
    return pl.pallas_call(
        functools.partial(product_kernel, tiles, counts, places),
        out_shape=jax.ShapeDtypeStruct(out, jnp.bfloat16),
        grid=(tiles,),
        in_specs=[VMEM] * (len(counts) + len(earlier)) + [HBM],
        out_specs=VMEM,
        scratch_shapes=[
            pltpu.VMEM((members * CTOK, FEATURES), jnp.bfloat16),
            pltpu.VMEM((tiles, FEATURES, TILE), jnp.bfloat16),
            pltpu.SemaphoreType.DMA((tiles,)),
        ]
        + ([pltpu.VMEM(part, jnp.bfloat16)] if places else []),
        compiler_params=kernel_params(),
        cost_estimate=cost(2 * members * CTOK * FEATURES * tiles * TILE, 14 * 10**6),
        name="block_product",
    )(*messages, *earlier, in_hbm(blocks))


def main_kernel(tiles, x_ref, w_hbm, after_ref, out_ref, rows_ref, wide_ref, w_ref, sems):
    n = pl.program_id(0)
    members = x_ref.shape[0]
    lines = members * STEPS
    halves = TILE // 128
    tile = weight_tile(n, tiles, w_hbm, w_ref, sems)

    @pl.when(n == 0)
    def _():
        packed = x_ref[...].reshape(members * CTOK, TILE).astype(jnp.float32)
        for k in range(halves):
            wide_ref[k] = packed[:, k * 128 : (k + 1) * 128]
            for j in range(FEATURES // TILE):
                lane = j * TILE + k * 128
                rows_ref[:, lane : lane + 128] = wide_ref[k, pl.ds(j, lines, stride=8), :].astype(jnp.bfloat16)

    tile.wait()
    prod = jnp.dot(rows_ref[...], w_ref[n], preferred_element_type=jnp.float32)
    for k in range(halves):
        wide_ref[k, pl.ds(n, lines, stride=8), :] = prod[:, k * 128 : (k + 1) * 128]
    start = rest_tile(lax.rem(lax.axis_index("tp"), COL_BLOCKS))

    @pl.when((n >= start) & (n < start + REST // TILE))
    def _():
        low = prod - prod.astype(jnp.bfloat16).astype(jnp.float32)
        for k in range(halves):
            wide_ref[k, pl.ds(tiles + n - start, lines, stride=8), :] = low[:, k * 128 : (k + 1) * 128]

    @pl.when(n == tiles - 1)
    def _():
        for k in range(halves):
            packed = wide_ref[k].astype(jnp.bfloat16).reshape(members, CTOK, 128)
            out_ref[:, :, k * 128 : (k + 1) * 128] = packed


def main_product(rows, blocks, after):
    tiles = blocks.shape[2] // TILE
    return pl.pallas_call(
        functools.partial(main_kernel, tiles),
        out_shape=jax.ShapeDtypeStruct(rows.shape, jnp.bfloat16),
        grid=(tiles,),
        in_specs=[VMEM, HBM, UNREAD],
        out_specs=VMEM,
        scratch_shapes=[
            pltpu.VMEM((MEMBERS * STEPS, FEATURES), jnp.bfloat16),
            pltpu.VMEM((TILE // 128, MEMBERS * CTOK, 128), jnp.float32),
            pltpu.VMEM((tiles, FEATURES, TILE), jnp.bfloat16),
            pltpu.SemaphoreType.DMA((tiles,)),
        ],
        compiler_params=kernel_params(),
        cost_estimate=cost(3 * 10**8, 13 * 10**6),
        name="main_product",
    )(rows, in_hbm(blocks), after)


def gather_kernel(own_ref, ahead1_ref, ahead2_ref, ahead3_ref, out_ref):
    z = lax.axis_index("tp") // COL_BLOCKS
    for k, ref in enumerate((own_ref, ahead1_ref, ahead2_ref, ahead3_ref)):
        out_ref[lax.rem(z + k, ROW_BLOCKS)] = ref[...]


def gather_along(parts):
    return pl.pallas_call(
        gather_kernel,
        out_shape=jax.ShapeDtypeStruct((ROW_BLOCKS,) + parts[0].shape, jnp.bfloat16),
        in_specs=[VMEM] * ROW_BLOCKS,
        out_specs=VMEM,
        compiler_params=kernel_params(),
        cost_estimate=cost(10**5, 10**6),
        name="gather_along",
    )(*parts)


def summed_block(parts_ref, c, lanes):
    total = parts_ref[c, :, lanes].astype(jnp.float32)
    for r in range(1, ROW_BLOCKS):
        total = total + parts_ref[r * COL_BLOCKS + c, :, lanes].astype(jnp.float32)
    return total


def head_attention(query, key, value, fresh_key, fresh_value, seen, fresh_seen):
    inv_root = 1.0 / math.sqrt(HD)
    contract = (((1,), (1,)), ((), ()))
    old = lax.dot_general(query, key, contract, preferred_element_type=jnp.float32) * inv_root
    new = lax.dot_general(query, fresh_key, contract, preferred_element_type=jnp.float32) * inv_root
    old = jnp.where(seen, old, MASKED_SCORE)
    new = jnp.where(fresh_seen, new, MASKED_SCORE)
    highest = jnp.maximum(jnp.max(old, axis=-1, keepdims=True), jnp.max(new, axis=-1, keepdims=True))
    old = jnp.exp(old - highest)
    new = jnp.exp(new - highest)
    mass = jnp.sum(old, axis=-1, keepdims=True) + jnp.sum(new, axis=-1, keepdims=True)
    inv_mass = 1.0 / mass
    mixed = jnp.dot((old * inv_mass).astype(jnp.bfloat16), value, preferred_element_type=jnp.float32)
    return mixed + jnp.dot((new * inv_mass).astype(jnp.bfloat16), fresh_value, preferred_element_type=jnp.float32)


def load_qkv(main, parts_ref, qkv_ref):
    cols = QKV // COL_BLOCKS
    for c in range(COL_BLOCKS):
        first = 2 if c == 6 else 0
        total = summed_block(parts_ref, c, slice(0, TILE if main else cols + REST))
        for j in range(cols // TILE):
            lanes = slice(c * cols + j * TILE, c * cols + (j + 1) * TILE)
            rest = j - first
            has_rest = 0 <= rest < REST // TILE
            if main:
                for s in range(STEPS):
                    line = total[s * 8 + j : s * 8 + j + 1]
                    if has_rest:
                        at = s * 8 + cols // TILE + rest
                        line = line + total[at : at + 1]
                    qkv_ref[s : s + 1, lanes] = line
            else:
                value = total[:, j * TILE : (j + 1) * TILE]
                if has_rest:
                    value = value + total[:, cols + rest * TILE : cols + (rest + 1) * TILE]
                qkv_ref[:, lanes] = value


def head_readers(qkv_ref, bias_ref, cos_ref, sin_ref):
    cosine = cos_ref[...]
    sine = sin_ref[...]

    def plain(start):
        return qkv_ref[:, start : start + HD] + bias_ref[:, start : start + HD]

    def rotated(start):
        head = plain(start)
        return head * cosine + pltpu.roll(head, HD // 2, 1) * sine

    return plain, rotated


def fresh_block(pieces):
    rows = sum(piece.shape[0] for piece in pieces)
    pad = jnp.zeros((128 - rows, HD), jnp.float32)
    return jnp.concatenate(list(pieces) + [pad], axis=0).astype(jnp.bfloat16)


GROUP = D // HD // KVH
KV_WIDTH = KVH * HD


def attend_main_kernel(
    len_ref, bias_ref, cos_ref, sin_ref, cache_ref, parts_ref, *refs
):
    out_ref, kv_ref, qkv_ref, piece_ref = refs[-4:]
    rows = qkv_ref.shape[0]
    qkv_ref[...] = jnp.zeros(qkv_ref.shape, jnp.float32)
    load_qkv(True, parts_ref, qkv_ref)
    plain, rotated = head_readers(qkv_ref, bias_ref, cos_ref, sin_ref)
    seen = lax.broadcasted_iota(jnp.int32, (1, cache_ref.shape[0]), 1) < len_ref[0]
    row = lax.broadcasted_iota(jnp.int32, (rows, 128), 0)
    col = lax.broadcasted_iota(jnp.int32, (rows, 128), 1)
    own = ((col <= row) & (col < STEPS)).astype(jnp.int32)
    fresh_seen = jnp.concatenate([own] * GROUP, axis=0) > 0
    for g in range(KVH):
        query = jnp.concatenate([rotated((g * GROUP + h) * HD) for h in range(GROUP)], axis=0).astype(jnp.bfloat16)
        fresh_key = rotated(D + g * HD)
        fresh_value = plain(D + KV_WIDTH + g * HD)
        kv_ref[:, g * HD : (g + 1) * HD] = fresh_key
        kv_ref[:, KV_WIDTH + g * HD : KV_WIDTH + (g + 1) * HD] = fresh_value
        key = cache_ref[:, g * HD : (g + 1) * HD]
        value = cache_ref[:, KV_WIDTH + g * HD : KV_WIDTH + (g + 1) * HD]
        mixed = head_attention(
            query, key, value, fresh_block([fresh_key]), fresh_block([fresh_value]), seen, fresh_seen
        )
        for h in range(GROUP):
            r, place = divmod(g * GROUP + h, FEATURES // HD)
            j, lane = place // 2, (place % 2) * HD
            for s in range(STEPS):
                at = s * 8 + j
                piece_ref[r, at : at + 1, lane : lane + HD] = mixed[h * rows + s : h * rows + s + 1]
    for r in range(ROW_BLOCKS):
        piece = piece_ref[r].astype(jnp.bfloat16)
        for c in range(COL_BLOCKS):
            out_ref[r * COL_BLOCKS + c] = piece


def attend_main(prefix_len, bias, cosine, sine, cache, parts, after):
    return pl.pallas_call(
        attend_main_kernel,
        out_shape=(
            jax.ShapeDtypeStruct((32, 16, TILE), jnp.bfloat16),
            jax.ShapeDtypeStruct((8, 2 * KV_WIDTH), jnp.float32),
        ),
        in_specs=[SMEM] + [VMEM] * 5 + [UNREAD] * len(after),
        out_specs=(whole((32, 16, TILE)), whole((8, 2 * KV_WIDTH))),
        scratch_shapes=[
            pltpu.VMEM((8, QKV), jnp.float32),
            pltpu.VMEM((ROW_BLOCKS, 16, TILE), jnp.float32),
        ],
        compiler_params=kernel_params(),
        cost_estimate=cost(2 * 10**8, 13 * 10**6),
        name="attend_main",
    )(prefix_len, bias, cosine, sine, cache, parts, *after)


def last_kernel(
    len_ref, bound_ref, bias_ref, cos_ref, sin_ref, cache_ref, kv_ref, parts_ref, main_ref, cont_ref, head_ref, *refs
):
    sum_refs = refs[:COL_BLOCKS]
    out_ref, score_ref, qkv_ref, wide_ref, read_ref, sums_ref = refs[COL_BLOCKS:]
    out_cols = D // COL_BLOCKS
    for (dy, dx), ref in zip(HERE + FAR, sum_refs):
        sums_ref[column_at(-dy, -dx)] = ref[...]
    for c in range(COL_BLOCKS):
        total = sums_ref[c]
        for j in range(out_cols // TILE):
            at = slice(c * out_cols + j * TILE, c * out_cols + (j + 1) * TILE)
            for s in range(STEPS):
                wide_ref[s : s + 1, at] = total[s * 4 + j : s * 4 + j + 1]
    out_ref[...] = (main_ref[...].astype(jnp.float32) + wide_ref[:STEPS, :]).astype(jnp.bfloat16)
    for r in range(ROW_BLOCKS):
        read = parts_ref[r * COL_BLOCKS, :, CONT_LANES:].astype(jnp.float32)
        for c in range(1, COL_BLOCKS):
            read = read + parts_ref[r * COL_BLOCKS + c, :, CONT_LANES:].astype(jnp.float32)
        read_ref[r] = read[:8] + read[8:]
    rows = qkv_ref.shape[0]
    load_qkv(False, parts_ref, qkv_ref)
    plain, rotated = head_readers(qkv_ref, bias_ref, cos_ref, sin_ref)
    seen = lax.broadcasted_iota(jnp.int32, (1, cache_ref.shape[0]), 1) < len_ref[0]
    row = lax.broadcasted_iota(jnp.int32, (rows, 128), 0)
    col = lax.broadcasted_iota(jnp.int32, (rows, 128), 1)
    own = (row // STEPS == col // STEPS) & (col <= row)
    main = (col >= rows) & (col < rows + bound_ref[0])
    fresh_seen = jnp.concatenate([(own | main).astype(jnp.int32)] * GROUP, axis=0) > 0
    score = jnp.zeros((rows, HD), jnp.float32)
    direct = jnp.zeros((STEPS, HD), jnp.float32)
    for g in range(KVH):
        query = jnp.concatenate([rotated((g * GROUP + h) * HD) for h in range(GROUP)], axis=0).astype(jnp.bfloat16)
        at_key = slice(g * HD, (g + 1) * HD)
        at_value = slice(KV_WIDTH + g * HD, KV_WIDTH + (g + 1) * HD)
        fresh_key = fresh_block([rotated(D + g * HD), kv_ref[:, at_key]])
        fresh_value = fresh_block([plain(D + KV_WIDTH + g * HD), kv_ref[:, at_value]])
        mixed = head_attention(
            query, cache_ref[:, at_key], cache_ref[:, at_value], fresh_key, fresh_value, seen, fresh_seen
        )
        mixed = mixed.astype(jnp.bfloat16).astype(jnp.float32)
        for h in range(GROUP):
            head = g * GROUP + h
            r, place = divmod(head, FEATURES // HD)
            j, lane = place // 2, (place % 2) * HD
            score = score + mixed[h * rows : (h + 1) * rows] * read_ref[r, j : j + 1, lane : lane + HD]
            lanes = slice(head * HD, (head + 1) * HD)
            for c in range(CONTS):
                direct = direct + cont_ref[c, :, lanes].astype(jnp.float32) * head_ref[:, lanes]
    total = jnp.sum(score, axis=0, keepdims=True) + jnp.sum(direct, axis=0, keepdims=True)
    score_ref[...] = jnp.broadcast_to(jnp.sum(total, axis=1, keepdims=True) / CONTS, (8, 128))


def last(*args):
    return pl.pallas_call(
        last_kernel,
        out_shape=(
            jax.ShapeDtypeStruct((STEPS, D), jnp.bfloat16),
            jax.ShapeDtypeStruct((8, 128), jnp.float32),
        ),
        in_specs=[SMEM, SMEM] + [VMEM] * (9 + COL_BLOCKS),
        out_specs=(VMEM, VMEM),
        scratch_shapes=[
            pltpu.VMEM((CTOK, QKV), jnp.float32),
            pltpu.VMEM((8, D), jnp.float32),
            pltpu.VMEM((ROW_BLOCKS, 8, TILE), jnp.float32),
            pltpu.VMEM((COL_BLOCKS, 8, TILE), jnp.float32),
        ],
        compiler_params=kernel_params(),
        cost_estimate=cost(4 * 10**8, 18 * 10**6),
        name="attend_cont",
    )(*args)


def readout_kernel(head_ref, w_hbm, after_ref, out_ref, w_ref, sem):
    copy = pltpu.make_async_copy(w_hbm.at[0], w_ref, sem)
    copy.start()
    row = head_ref[pl.ds(lax.rem(lax.axis_index("tp"), COL_BLOCKS), 1), :]
    high = row.astype(jnp.bfloat16).astype(jnp.float32)
    middle = (row - high).astype(jnp.bfloat16).astype(jnp.float32)
    low = row - high - middle
    pieces = jnp.concatenate([high, middle, low, jnp.zeros((13, row.shape[1]), jnp.float32)], axis=0)
    copy.wait()
    prod = lax.dot_general(
        pieces.astype(jnp.bfloat16), w_ref[...], (((1,), (1,)), ((), ())), preferred_element_type=jnp.float32
    )
    total = prod[0:1] + prod[1:2] + prod[2:3]
    for j in range(FEATURES // TILE):
        out_ref[j : j + 1, :] = total[:, j * TILE : (j + 1) * TILE]


def readout(value_head, blocks, after):
    return pl.pallas_call(
        readout_kernel,
        out_shape=jax.ShapeDtypeStruct((8, TILE), jnp.float32),
        in_specs=[VMEM, HBM, UNREAD],
        out_specs=VMEM,
        scratch_shapes=[pltpu.VMEM((FEATURES, D // COL_BLOCKS), jnp.bfloat16), pltpu.SemaphoreType.DMA],
        compiler_params=kernel_params(),
        cost_estimate=cost(2 * 10**8, 12 * 10**6),
        name="readout",
    )(value_head, in_hbm(blocks), after)


def split(wide):
    high = wide.astype(jnp.bfloat16).astype(jnp.float32)
    return jnp.concatenate([high, wide - high], axis=-2).astype(jnp.bfloat16)


def out_kernel(tiles, x_ref, w_hbm, after_ref, z0_ref, z1_ref, z2_ref, z3_ref, rows_ref, wide_ref, w_ref, sems):
    n = pl.program_id(0)
    members = x_ref.shape[0]
    lines = members * STEPS
    halves = TILE // 128
    tile = weight_tile(n, tiles, w_hbm, w_ref, sems)

    @pl.when(n == 0)
    def _():
        packed = x_ref[...].reshape(members * 16, TILE).astype(jnp.float32)
        for k in range(halves):
            wide_ref[k] = packed[:, k * 128 : (k + 1) * 128]
            for j in range(FEATURES // TILE):
                lane = j * TILE + k * 128
                rows_ref[:, lane : lane + 128] = wide_ref[k, pl.ds(j, lines, stride=8), :].astype(jnp.bfloat16)

    tile.wait()
    prod = jnp.dot(rows_ref[...], w_ref[n], preferred_element_type=jnp.float32)
    for k in range(halves):
        wide_ref[k, pl.ds(n, lines, stride=4), :] = prod[:, k * 128 : (k + 1) * 128]

    @pl.when(n == tiles - 1)
    def _():
        z = lax.axis_index("tp") // COL_BLOCKS
        size = COL_BLOCKS * 8
        for ahead, z_ref in enumerate((z0_ref, z1_ref, z2_ref, z3_ref)):
            start = pl.multiple_of(lax.rem(z + ahead, ROW_BLOCKS) * size, size)
            for k in range(halves):
                packed = wide_ref[k, pl.ds(start, size), :].reshape(COL_BLOCKS, 8, 128)
                z_ref[:, :, k * 128 : (k + 1) * 128] = packed


def out_product(rows, blocks, after):
    members = rows.shape[0]
    tiles = blocks.shape[2] // TILE
    return pl.pallas_call(
        functools.partial(out_kernel, tiles),
        out_shape=[jax.ShapeDtypeStruct((COL_BLOCKS, 8, TILE), jnp.float32)] * ROW_BLOCKS,
        grid=(tiles,),
        in_specs=[VMEM, HBM, UNREAD],
        out_specs=[VMEM] * ROW_BLOCKS,
        scratch_shapes=[
            pltpu.VMEM((members * STEPS, FEATURES), jnp.bfloat16),
            pltpu.VMEM((TILE // 128, members * 16, 128), jnp.float32),
            pltpu.VMEM((tiles, FEATURES, TILE), jnp.bfloat16),
            pltpu.SemaphoreType.DMA((tiles,)),
        ],
        compiler_params=kernel_params(),
        cost_estimate=cost(3 * 10**8, 9 * 10**6),
        name="out_product",
    )(rows, in_hbm(blocks), after)


def column_at(dy, dx):
    column = lax.rem(lax.axis_index("tp"), COL_BLOCKS)
    return lax.rem(column // 4 + dy + 2, 2) * 4 + lax.rem(column + dx + 4, 4)


def sum_kernel(*refs):
    for (dy, dx), out_ref in zip(HERE + FAR, refs[ROW_BLOCKS:]):
        home = column_at(dy, dx)
        total = refs[0][home]
        for ref in refs[1:ROW_BLOCKS]:
            total = total + ref[home]
        out_ref[...] = total


def sum_along(parts):
    return pl.pallas_call(
        sum_kernel,
        out_shape=[jax.ShapeDtypeStruct(parts[0].shape[1:], jnp.float32)] * COL_BLOCKS,
        in_specs=[VMEM] * ROW_BLOCKS,
        out_specs=[VMEM] * COL_BLOCKS,
        compiler_params=kernel_params(),
        cost_estimate=cost(10**5, 10**6),
        name="sum_along",
    )(*parts)


def rope_tables(positions):
    half = HD // 2
    frequency = THETA ** (-(jnp.arange(half, dtype=jnp.float32) * 2.0) / HD)
    angles = positions.astype(jnp.float32)[:, None] * frequency[None, :]
    cosine = jnp.cos(angles)
    sine = jnp.sin(angles)
    return jnp.concatenate([cosine, cosine], axis=1), jnp.concatenate([-sine, sine], axis=1)


def exchange(rows):
    return lax.all_to_all(rows, "tp", split_axis=0, concat_axis=0, tiled=True)


def from_side(rows, dy, dx):
    route = []
    for to in range(MEMBERS):
        z, y, x = to // 8, to // 4 % 2, to % 4
        route.append((z * 8 + (y + dy) % 2 * 4 + (x + dx) % 4, to))
    return lax.ppermute(rows, "tp", route)


def from_along(rows, dz):
    route = [((to + dz * COL_BLOCKS) % MEMBERS, to) for to in range(MEMBERS)]
    return lax.ppermute(rows, "tp", route)


def ring(rows):
    near = gather_along([rows[0]] + [from_along(rows[ROW_BLOCKS - k], k) for k in range(1, ROW_BLOCKS)])
    over = from_side(near, 1, 0)
    here = []
    for mine in (near, over):
        here += [mine, from_side(mine, 0, 1), from_side(mine, 0, 3)]
    return here, [from_side(here[2], 0, 3), from_side(here[4], 0, 1)]


HERE = ((0, 0), (0, 1), (0, 3), (1, 0), (1, 1), (1, 3))
FAR = ((0, 2), (1, 2))


def on_device(
    main_inputs, cont_inputs, prefix_cache, prefix_len, boundary, rms_gain, qkv_bias, w_qkv, w_out, value_head
):
    main = main_inputs.reshape(STEPS, D)
    cont = cont_inputs.reshape(CONTS, STEPS, D)
    bias = qkv_bias[None, :]
    cache = prefix_cache[0]
    head = value_head[None, :]
    step = jnp.arange(CTOK, dtype=jnp.int32) % STEPS
    main_tables = rope_tables(prefix_len + step[:8])
    cont_tables = rope_tables(prefix_len + boundary + step)
    gain = rms_gain[None, :]
    main_rows = norm_main(main, gain)
    here, far = ring(norm_cont(cont, gain, main_rows))
    read = readout(value_head.reshape(COL_BLOCKS, D // COL_BLOCKS), w_out, here[0])
    main_parts = exchange(main_product(exchange(main_rows), w_qkv, read))
    mixed, main_kv = attend_main(prefix_len, bias, *main_tables, cache, main_parts, here)
    mixed, far = lax.optimization_barrier((mixed, far))
    mixed = exchange(mixed)
    cont_parts = block_product(far, w_qkv, (block_product(here, w_qkv), read), HERE + FAR)
    sums = out_product(mixed, w_out, cont_parts)
    cont_parts = exchange(cont_parts)
    sums = sum_along([sums[0]] + [from_along(sums[k], -k) for k in range(1, ROW_BLOCKS)])
    sums = [from_side(rows, -dy, -dx) if dy or dx else rows for rows, (dy, dx) in zip(sums, HERE + FAR)]
    main_out, score = last(
        prefix_len, boundary, bias, *cont_tables, cache, main_kv, cont_parts, main, cont, head, *sums
    )
    return main_out[None], score[0, :1]


def solution(mesh):
    return jax.shard_map(
        on_device,
        mesh=mesh,
        in_specs=(
            P(("grp", "tp"), None, None),
            P(("grp", "tp"), None, None, None),
            P(("grp", "tp"), None, None),
            P(("grp", "tp")),
            P(("grp", "tp")),
            P(),
            P(),
            P("tp", None, None),
            P("tp", None, None),
            P(),
        ),
        out_specs=(P(("grp", "tp"), None, None), P(("grp", "tp"))),
        check_vma=False,
    )
```

```python
import functools
import math

import jax
import jax.numpy as jnp
from jax import lax
from jax.experimental import pallas as pl
from jax.experimental.pallas import tpu as pltpu
from jax.sharding import PartitionSpec as P

KVH = 8
HD = 128
D = 8192
QKV = 10240
ROW_BLOCKS = 4
COL_BLOCKS = 8
MEMBERS = ROW_BLOCKS * COL_BLOCKS
FEATURES = D // ROW_BLOCKS
CONTS = 8
STEPS = 2
CTOK = CONTS * STEPS
TILE = 256

THETA = 1000000.0
EPS = 1e-06
MASKED_SCORE = -1e30

VMEM_LIMIT = 32 * 1024 * 1024
VMEM = pl.BlockSpec(memory_space=pltpu.VMEM)
SMEM = pl.BlockSpec(memory_space=pltpu.SMEM)
HBM = pl.BlockSpec(memory_space=pltpu.HBM)
UNREAD = pl.BlockSpec(memory_space=pl.ANY)


def whole(shape):
    return pl.BlockSpec(shape, lambda *_: (0,) * len(shape))


def cost(flops, moved):
    return pl.CostEstimate(flops=flops, bytes_accessed=moved, transcendentals=0)


def in_hbm(array):
    return pltpu.with_memory_space_constraint(array, pltpu.HBM)


def kernel_params():
    return pltpu.CompilerParams(vmem_limit_bytes=VMEM_LIMIT)


def norm_kernel(main_hbm, cont_hbm, gain_hbm, out_ref, main_ref, cont_ref, gain_ref, rows_ref, piece_ref, sems):
    pairs = ((main_hbm, main_ref), (cont_hbm, cont_ref), (gain_hbm, gain_ref))
    copies = [pltpu.make_async_copy(src, dst, sems.at[i]) for i, (src, dst) in enumerate(pairs)]
    for copy in copies:
        copy.start()
    for copy in copies:
        copy.wait()

    def normed(wide):
        inv = lax.rsqrt(jnp.mean(wide * wide, axis=-1, keepdims=True) + EPS)
        return wide * inv * gain_ref[...]

    for c in range(CONTS):
        rows_ref[c * STEPS : (c + 1) * STEPS, :] = cont_ref[c].astype(jnp.float32)
    cont = normed(rows_ref[...]).astype(jnp.bfloat16)
    main = normed(main_ref[...].astype(jnp.float32))
    for r in range(ROW_BLOCKS):
        for j in range(FEATURES // TILE):
            lanes = slice(r * FEATURES + j * TILE, r * FEATURES + (j + 1) * TILE)
            for s in range(STEPS):
                piece_ref[r, s * 8 + j : s * 8 + j + 1, :] = main[s : s + 1, lanes]
    for r in range(ROW_BLOCKS):
        piece = piece_ref[r].astype(jnp.bfloat16)
        out_ref[r, :, :FEATURES] = cont[:, r * FEATURES : (r + 1) * FEATURES]
        out_ref[r, :, FEATURES:] = piece


def norm_rows(main, cont, gain):
    return pl.pallas_call(
        norm_kernel,
        out_shape=jax.ShapeDtypeStruct((ROW_BLOCKS, CTOK, FEATURES + TILE), jnp.bfloat16),
        in_specs=[HBM] * 3,
        out_specs=VMEM,
        scratch_shapes=[
            pltpu.VMEM((STEPS, D), jnp.bfloat16),
            pltpu.VMEM((CONTS, STEPS, D), jnp.bfloat16),
            pltpu.VMEM((1, D), jnp.float32),
            pltpu.VMEM((CTOK, D), jnp.float32),
            pltpu.VMEM((ROW_BLOCKS, 16, TILE), jnp.float32),
            pltpu.SemaphoreType.DMA((3,)),
        ],
        compiler_params=kernel_params(),
        cost_estimate=cost(10**6, 4 * 10**6),
        name="norm_rows",
    )(in_hbm(main), in_hbm(cont), in_hbm(gain))


def weight_tile(n, tiles, w_hbm, w_ref, sems):
    def copy(i):
        lanes = pl.ds(pl.multiple_of(i * TILE, TILE), TILE)
        return pltpu.make_async_copy(w_hbm.at[0, :, lanes], w_ref.at[i], sems.at[i])

    @pl.when(n == 0)
    def _():
        for i in range(tiles):
            copy(i).start()

    return copy(n)


REST = 768


def rest_tile(block):
    return jnp.where(block == 6, 2, 0)


def product_kernel(tiles, counts, places, *refs):
    x_refs = refs[: len(counts)]
    refs = refs[len(counts) :]
    if places:
        earlier_ref, w_hbm, out_ref, rows_ref, wide_ref, w_ref, sems, part_ref = refs
    else:
        w_hbm, part_ref, rows_ref, wide_ref, w_ref, sems = refs
    n = pl.program_id(0)
    members = sum(counts)
    count = members * CTOK
    lines = members * STEPS
    halves = TILE // 128
    width = tiles * TILE
    tile = weight_tile(n, tiles, w_hbm, w_ref, sems)

    @pl.when(n == 0)
    def _():
        at = 0
        for x_ref, size in zip(x_refs, counts):
            rows = slice(at * CTOK, (at + size) * CTOK)
            rows_ref[rows, :] = x_ref[:, :, :FEATURES].reshape(size * CTOK, FEATURES)
            packed = x_ref[:, :, FEATURES:].reshape(size * CTOK, TILE).astype(jnp.float32)
            for k in range(halves):
                wide_ref[k, rows, :] = packed[:, k * 128 : (k + 1) * 128]
            at += size
        for k in range(halves):
            for j in range(FEATURES // TILE):
                lane = j * TILE + k * 128
                rows_ref[count:, lane : lane + 128] = wide_ref[k, pl.ds(j, lines, stride=8), :].astype(jnp.bfloat16)

    tile.wait()
    prod = jnp.dot(rows_ref[...], w_ref[n], preferred_element_type=jnp.float32)
    high = prod.astype(jnp.bfloat16)
    part_ref[:, :, pl.ds(pl.multiple_of(n * TILE, TILE), TILE)] = high[:count].reshape(members, CTOK, TILE)
    for k in range(halves):
        wide_ref[k, pl.ds(n, lines, stride=8), :] = prod[count:, k * 128 : (k + 1) * 128]
    start = rest_tile(lax.rem(lax.axis_index("tp"), COL_BLOCKS))

    @pl.when((n >= start) & (n < start + REST // TILE))
    def _():
        low = prod - high.astype(jnp.float32)
        place = n - start
        lane = pl.multiple_of(width + place * TILE, TILE)
        part_ref[:, :, pl.ds(lane, TILE)] = low[:count].astype(jnp.bfloat16).reshape(members, CTOK, TILE)
        for k in range(halves):
            wide_ref[k, pl.ds(tiles + place, lines, stride=8), :] = low[count:, k * 128 : (k + 1) * 128]

    @pl.when(n == tiles - 1)
    def _():
        for k in range(halves):
            lane = width + REST + k * 128
            part_ref[:, :, lane : lane + 128] = wide_ref[k].astype(jnp.bfloat16).reshape(members, CTOK, 128)
        if places:
            me = lax.rem(lax.axis_index("tp"), COL_BLOCKS)
            y, x = me // 4, lax.rem(me, 4)
            done = earlier_ref.shape[0] // ROW_BLOCKS
            for i, (dy, dx) in enumerate(places):
                column = lax.rem(y + dy, 2) * 4 + lax.rem(x + dx, 4)
                for z in range(ROW_BLOCKS):
                    if i < done:
                        message = earlier_ref[i * ROW_BLOCKS + z]
                    else:
                        message = part_ref[(i - done) * ROW_BLOCKS + z]
                    out_ref[z * COL_BLOCKS + column] = message


def block_product(messages, blocks, earlier=None, places=()):
    tiles = blocks.shape[2] // TILE
    lanes = (tiles + 1) * TILE + REST
    counts = tuple(rows.shape[0] for rows in messages)
    members = sum(counts)
    part = (members, CTOK, lanes)
    scratch = [
        pltpu.VMEM((members * (CTOK + STEPS), FEATURES), jnp.bfloat16),
        pltpu.VMEM((TILE // 128, members * CTOK, 128), jnp.float32),
        pltpu.VMEM((tiles, FEATURES, TILE), jnp.bfloat16),
        pltpu.SemaphoreType.DMA((tiles,)),
    ]
    operands = list(messages)
    out = part
    if places:
        operands.append(earlier)
        out = (MEMBERS, CTOK, lanes)
        scratch.append(pltpu.VMEM(part, jnp.bfloat16))
    return pl.pallas_call(
        functools.partial(product_kernel, tiles, counts, places),
        out_shape=jax.ShapeDtypeStruct(out, jnp.bfloat16),
        grid=(tiles,),
        in_specs=[VMEM] * len(operands) + [HBM],
        out_specs=VMEM,
        scratch_shapes=scratch,
        compiler_params=kernel_params(),
        cost_estimate=cost(2 * members * (CTOK + STEPS) * FEATURES * tiles * TILE, 12 * 10**6),
        name="block_product",
    )(*operands, in_hbm(blocks))


def summed_block(parts_ref, c, lanes):
    total = parts_ref[c, :, lanes].astype(jnp.float32)
    for r in range(1, ROW_BLOCKS):
        total = total + parts_ref[r * COL_BLOCKS + c, :, lanes].astype(jnp.float32)
    return total


def head_attention(query, key, value, fresh_key, fresh_value, seen, fresh_seen):
    inv_root = 1.0 / math.sqrt(HD)
    contract = (((1,), (1,)), ((), ()))
    old = lax.dot_general(query, key, contract, preferred_element_type=jnp.float32) * inv_root
    new = lax.dot_general(query, fresh_key, contract, preferred_element_type=jnp.float32) * inv_root
    old = jnp.where(seen, old, MASKED_SCORE)
    new = jnp.where(fresh_seen, new, MASKED_SCORE)
    highest = jnp.maximum(jnp.max(old, axis=-1, keepdims=True), jnp.max(new, axis=-1, keepdims=True))
    old = jnp.exp(old - highest)
    new = jnp.exp(new - highest)
    mass = jnp.sum(old, axis=-1, keepdims=True) + jnp.sum(new, axis=-1, keepdims=True)
    inv_mass = 1.0 / mass
    mixed = jnp.dot((old * inv_mass).astype(jnp.bfloat16), value, preferred_element_type=jnp.float32)
    return mixed + jnp.dot((new * inv_mass).astype(jnp.bfloat16), fresh_value, preferred_element_type=jnp.float32)


def load_qkv(main, parts_ref, qkv_ref):
    cols = QKV // COL_BLOCKS
    for c in range(COL_BLOCKS):
        first = 2 if c == 6 else 0
        if main:
            total = summed_block(parts_ref, c, slice(cols + REST, cols + REST + TILE))
        else:
            total = summed_block(parts_ref, c, slice(0, cols + REST))
        for j in range(cols // TILE):
            lanes = slice(c * cols + j * TILE, c * cols + (j + 1) * TILE)
            rest = j - first
            has_rest = 0 <= rest < REST // TILE
            if main:
                for s in range(STEPS):
                    line = total[s * 8 + j : s * 8 + j + 1]
                    if has_rest:
                        at = s * 8 + cols // TILE + rest
                        line = line + total[at : at + 1]
                    qkv_ref[s : s + 1, lanes] = line
            else:
                value = total[:, j * TILE : (j + 1) * TILE]
                if has_rest:
                    value = value + total[:, cols + rest * TILE : cols + (rest + 1) * TILE]
                qkv_ref[:, lanes] = value


def head_readers(qkv_ref, bias_ref, cos_ref, sin_ref):
    cosine = cos_ref[...]
    sine = sin_ref[...]

    def plain(start):
        return qkv_ref[:, start : start + HD] + bias_ref[:, start : start + HD]

    def rotated(start):
        head = plain(start)
        return head * cosine + pltpu.roll(head, HD // 2, 1) * sine

    return plain, rotated


def fresh_block(pieces):
    rows = sum(piece.shape[0] for piece in pieces)
    pad = jnp.zeros((128 - rows, HD), jnp.float32)
    return jnp.concatenate(list(pieces) + [pad], axis=0).astype(jnp.bfloat16)


GROUP = D // HD // KVH
KV_WIDTH = KVH * HD


def attend_main_kernel(len_ref, parts_ref, bias_ref, cos_ref, sin_ref, cache_ref, out_ref, kv_ref, qkv_ref, piece_ref):
    rows = qkv_ref.shape[0]
    qkv_ref[...] = jnp.zeros(qkv_ref.shape, jnp.float32)
    load_qkv(True, parts_ref, qkv_ref)
    plain, rotated = head_readers(qkv_ref, bias_ref, cos_ref, sin_ref)
    seen = lax.broadcasted_iota(jnp.int32, (1, cache_ref.shape[0]), 1) < len_ref[0]
    row = lax.broadcasted_iota(jnp.int32, (rows, 128), 0)
    col = lax.broadcasted_iota(jnp.int32, (rows, 128), 1)
    own = ((col <= row) & (col < STEPS)).astype(jnp.int32)
    fresh_seen = jnp.concatenate([own] * GROUP, axis=0) > 0
    for g in range(KVH):
        query = jnp.concatenate([rotated((g * GROUP + h) * HD) for h in range(GROUP)], axis=0).astype(jnp.bfloat16)
        fresh_key = rotated(D + g * HD)
        fresh_value = plain(D + KV_WIDTH + g * HD)
        kv_ref[:, g * HD : (g + 1) * HD] = fresh_key
        kv_ref[:, KV_WIDTH + g * HD : KV_WIDTH + (g + 1) * HD] = fresh_value
        key = cache_ref[:, g * HD : (g + 1) * HD]
        value = cache_ref[:, KV_WIDTH + g * HD : KV_WIDTH + (g + 1) * HD]
        mixed = head_attention(
            query, key, value, fresh_block([fresh_key]), fresh_block([fresh_value]), seen, fresh_seen
        )
        for h in range(GROUP):
            r, place = divmod(g * GROUP + h, FEATURES // HD)
            j, lane = place // 2, (place % 2) * HD
            for s in range(STEPS):
                at = s * 8 + j
                piece_ref[r, at : at + 1, lane : lane + HD] = mixed[h * rows + s : h * rows + s + 1]
    for r in range(ROW_BLOCKS):
        piece = piece_ref[r].astype(jnp.bfloat16)
        for c in range(COL_BLOCKS):
            out_ref[r * COL_BLOCKS + c] = piece


def attend_main(prefix_len, parts, bias, cosine, sine, cache):
    return pl.pallas_call(
        attend_main_kernel,
        out_shape=(
            jax.ShapeDtypeStruct((32, 16, TILE), jnp.bfloat16),
            jax.ShapeDtypeStruct((8, 2 * KV_WIDTH), jnp.float32),
        ),
        in_specs=[SMEM] + [VMEM] * 5,
        out_specs=(VMEM, VMEM),
        scratch_shapes=[
            pltpu.VMEM((8, QKV), jnp.float32),
            pltpu.VMEM((ROW_BLOCKS, 16, TILE), jnp.float32),
        ],
        compiler_params=kernel_params(),
        cost_estimate=cost(2 * 10**8, 6 * 10**6),
        name="attend_main",
    )(prefix_len, parts, bias, cosine, sine, cache)


def attend_cont_kernel(
    len_ref, bound_ref, parts_ref, bias_ref, cos_ref, sin_ref, cache_ref, kv_ref, out_ref, qkv_ref
):
    rows = qkv_ref.shape[0]
    load_qkv(False, parts_ref, qkv_ref)
    plain, rotated = head_readers(qkv_ref, bias_ref, cos_ref, sin_ref)
    seen = lax.broadcasted_iota(jnp.int32, (1, cache_ref.shape[0]), 1) < len_ref[0]
    row = lax.broadcasted_iota(jnp.int32, (rows, 128), 0)
    col = lax.broadcasted_iota(jnp.int32, (rows, 128), 1)
    own = (row // STEPS == col // STEPS) & (col <= row)
    main = (col >= rows) & (col < rows + bound_ref[0])
    fresh_seen = jnp.concatenate([(own | main).astype(jnp.int32)] * GROUP, axis=0) > 0
    for g in range(KVH):
        query = jnp.concatenate([rotated((g * GROUP + h) * HD) for h in range(GROUP)], axis=0).astype(jnp.bfloat16)
        at_key = slice(g * HD, (g + 1) * HD)
        at_value = slice(KV_WIDTH + g * HD, KV_WIDTH + (g + 1) * HD)
        fresh_key = fresh_block([rotated(D + g * HD), kv_ref[:, at_key]])
        fresh_value = fresh_block([plain(D + KV_WIDTH + g * HD), kv_ref[:, at_value]])
        mixed = head_attention(
            query, cache_ref[:, at_key], cache_ref[:, at_value], fresh_key, fresh_value, seen, fresh_seen
        )
        mixed = mixed.astype(jnp.bfloat16)
        for h in range(GROUP):
            out_ref[:, (g * GROUP + h) * HD : (g * GROUP + h + 1) * HD] = mixed[h * rows : (h + 1) * rows]


def attend_cont(*args):
    return pl.pallas_call(
        attend_cont_kernel,
        out_shape=jax.ShapeDtypeStruct((CTOK, D), jnp.bfloat16),
        in_specs=[SMEM, SMEM] + [VMEM] * 6,
        out_specs=VMEM,
        scratch_shapes=[pltpu.VMEM((CTOK, QKV), jnp.float32)],
        compiler_params=kernel_params(),
        cost_estimate=cost(4 * 10**8, 8 * 10**6),
        name="attend_cont",
    )(*args)


def readout_kernel(head_ref, w_hbm, after_ref, out_ref, w_ref, sem):
    copy = pltpu.make_async_copy(w_hbm.at[0], w_ref, sem)
    copy.start()
    row = head_ref[pl.ds(lax.rem(lax.axis_index("tp"), COL_BLOCKS), 1), :]
    high = row.astype(jnp.bfloat16).astype(jnp.float32)
    middle = (row - high).astype(jnp.bfloat16).astype(jnp.float32)
    low = row - high - middle
    pieces = jnp.concatenate([high, middle, low, jnp.zeros((13, row.shape[1]), jnp.float32)], axis=0)
    copy.wait()
    prod = lax.dot_general(
        pieces.astype(jnp.bfloat16), w_ref[...], (((1,), (1,)), ((), ())), preferred_element_type=jnp.float32
    )
    out_ref[...] = prod[0:1] + prod[1:2] + prod[2:3]


def readout(value_head, blocks, after):
    return pl.pallas_call(
        readout_kernel,
        out_shape=jax.ShapeDtypeStruct((1, FEATURES), jnp.float32),
        in_specs=[VMEM, HBM, UNREAD],
        out_specs=VMEM,
        scratch_shapes=[pltpu.VMEM((FEATURES, D // COL_BLOCKS), jnp.bfloat16), pltpu.SemaphoreType.DMA],
        compiler_params=kernel_params(),
        cost_estimate=cost(2 * 10**8, 5 * 10**6),
        name="readout",
    )(value_head, in_hbm(blocks), after)


def out_kernel(tiles, x_ref, read_ref, w_hbm, out_ref, rows_ref, wide_ref, read8_ref, w_ref, sems):
    n = pl.program_id(0)
    members = x_ref.shape[0]
    lines = members * STEPS
    halves = TILE // 128
    tile = weight_tile(n, tiles, w_hbm, w_ref, sems)

    @pl.when(n == 0)
    def _():
        for j in range(FEATURES // TILE):
            read8_ref[j : j + 1, :] = read_ref[:, j * TILE : (j + 1) * TILE]
        out_ref[:, 8:, :] = jnp.broadcast_to(read8_ref[...][None], (members, 8, TILE))
        packed = x_ref[...].reshape(members * 16, TILE).astype(jnp.float32)
        for k in range(halves):
            wide_ref[k] = packed[:, k * 128 : (k + 1) * 128]
            for j in range(FEATURES // TILE):
                lane = j * TILE + k * 128
                rows_ref[:, lane : lane + 128] = wide_ref[k, pl.ds(j, lines, stride=8), :].astype(jnp.bfloat16)

    tile.wait()
    prod = jnp.dot(rows_ref[...], w_ref[n], preferred_element_type=jnp.float32)
    for k in range(halves):
        wide_ref[k, pl.ds(n, lines, stride=4), :] = prod[:, k * 128 : (k + 1) * 128]

    @pl.when(n == tiles - 1)
    def _():
        for k in range(halves):
            packed = wide_ref[k, : members * 8, :].reshape(members, 8, 128)
            out_ref[:, :8, k * 128 : (k + 1) * 128] = packed


def out_product(rows, read, blocks):
    members = rows.shape[0]
    tiles = blocks.shape[2] // TILE
    return pl.pallas_call(
        functools.partial(out_kernel, tiles),
        out_shape=jax.ShapeDtypeStruct((members, 16, TILE), jnp.float32),
        grid=(tiles,),
        in_specs=[VMEM, VMEM, HBM],
        out_specs=VMEM,
        scratch_shapes=[
            pltpu.VMEM((members * STEPS, FEATURES), jnp.bfloat16),
            pltpu.VMEM((TILE // 128, members * 16, 128), jnp.float32),
            pltpu.VMEM((8, TILE), jnp.float32),
            pltpu.VMEM((tiles, FEATURES, TILE), jnp.bfloat16),
            pltpu.SemaphoreType.DMA((tiles,)),
        ],
        compiler_params=kernel_params(),
        cost_estimate=cost(3 * 10**8, 5 * 10**6),
        name="out_product",
    )(rows, read, in_hbm(blocks))


def finish_kernel(parts_ref, main_ref, cont_ref, head_ref, mixed_ref, out_ref, score_ref, wide_ref):
    cols = D // COL_BLOCKS
    for c in range(COL_BLOCKS):
        total = summed_block(parts_ref, c, slice(0, TILE))
        for j in range(cols // TILE):
            at = slice(c * cols + j * TILE, c * cols + (j + 1) * TILE)
            for s in range(STEPS):
                wide_ref[s : s + 1, at] = total[s * 4 + j : s * 4 + j + 1]
    out_ref[...] = (main_ref[...].astype(jnp.float32) + wide_ref[:STEPS, :]).astype(jnp.bfloat16)
    score = jnp.zeros((CTOK, TILE), jnp.float32)
    direct = jnp.zeros((STEPS, TILE), jnp.float32)
    for r in range(ROW_BLOCKS):
        read = parts_ref[r * COL_BLOCKS, 8:, :]
        for c in range(1, COL_BLOCKS):
            read = read + parts_ref[r * COL_BLOCKS + c, 8:, :]
        for j in range(FEATURES // TILE):
            lanes = slice(r * FEATURES + j * TILE, r * FEATURES + (j + 1) * TILE)
            score = score + mixed_ref[:, lanes].astype(jnp.float32) * read[j : j + 1, :]
            for c in range(CONTS):
                direct = direct + cont_ref[c, :, lanes].astype(jnp.float32) * head_ref[:, lanes]
    total = jnp.sum(score, axis=0, keepdims=True) + jnp.sum(direct, axis=0, keepdims=True)
    score_ref[...] = jnp.broadcast_to(jnp.sum(total, axis=1, keepdims=True) / CONTS, (8, 128))


def finish(parts, main, cont, head, mixed):
    return pl.pallas_call(
        finish_kernel,
        out_shape=(
            jax.ShapeDtypeStruct((STEPS, D), jnp.bfloat16),
            jax.ShapeDtypeStruct((8, 128), jnp.float32),
        ),
        in_specs=[VMEM] * 5,
        out_specs=(whole((STEPS, D)), whole((8, 128))),
        scratch_shapes=[pltpu.VMEM((8, D), jnp.float32)],
        compiler_params=kernel_params(),
        cost_estimate=cost(10**6, 2 * 10**6),
        name="finish",
    )(parts, main, cont, head, mixed)


def rope_tables(positions):
    half = HD // 2
    frequency = THETA ** (-(jnp.arange(half, dtype=jnp.float32) * 2.0) / HD)
    angles = positions.astype(jnp.float32)[:, None] * frequency[None, :]
    cosine = jnp.cos(angles)
    sine = jnp.sin(angles)
    return jnp.concatenate([cosine, cosine], axis=1), jnp.concatenate([-sine, sine], axis=1)


def exchange(rows):
    return lax.all_to_all(rows, "tp", split_axis=0, concat_axis=0, tiled=True)


ALONG = [[z * COL_BLOCKS + c for z in range(ROW_BLOCKS)] for c in range(COL_BLOCKS)]


def from_side(rows, dy, dx):
    route = []
    for to in range(MEMBERS):
        z, y, x = to // 8, to // 4 % 2, to % 4
        route.append((z * 8 + (y + dy) % 2 * 4 + (x + dx) % 4, to))
    return lax.ppermute(rows, "tp", route)


def forward_product(rows, blocks):
    near = lax.all_to_all(rows, "tp", split_axis=0, concat_axis=0, tiled=True, axis_index_groups=ALONG)
    over = from_side(near, 1, 0)
    here, places = [], []
    for dy, mine in ((0, near), (1, over)):
        here += [mine, from_side(mine, 0, 1), from_side(mine, 0, 3)]
        places += [(dy, 0), (dy, 1), (dy, 3)]
    far = [from_side(here[2], 0, 3), from_side(here[4], 0, 1)]
    earlier = block_product(here, blocks)
    return block_product(far, blocks, earlier, tuple(places) + ((0, 2), (1, 2))), near


def on_device(
    main_inputs, cont_inputs, prefix_cache, prefix_len, boundary, rms_gain, qkv_bias, w_qkv, w_out, value_head
):
    main = main_inputs.reshape(STEPS, D)
    cont = cont_inputs.reshape(CONTS, STEPS, D)
    bias = qkv_bias[None, :]
    cache = prefix_cache[0]
    head = value_head[None, :]
    step = jnp.arange(CTOK, dtype=jnp.int32) % STEPS
    main_tables = rope_tables(prefix_len + step[:8])
    cont_tables = rope_tables(prefix_len + boundary + step)
    parts, near = forward_product(norm_rows(main, cont, rms_gain[None, :]), w_qkv)
    parts = exchange(parts)
    read = readout(value_head.reshape(COL_BLOCKS, D // COL_BLOCKS), w_out, near)
    mixed, main_kv = attend_main(prefix_len, parts, bias, *main_tables, cache)
    mixed = exchange(mixed)
    cont_mixed = attend_cont(prefix_len, boundary, parts, bias, *cont_tables, cache, main_kv)
    parts = exchange(out_product(mixed, read, w_out))
    main_out, score = finish(parts, main, cont, head, cont_mixed)
    return main_out[None], score[0, :1]


def solution(mesh):
    return jax.shard_map(
        on_device,
        mesh=mesh,
        in_specs=(
            P(("grp", "tp"), None, None),
            P(("grp", "tp"), None, None, None),
            P(("grp", "tp"), None, None),
            P(("grp", "tp")),
            P(("grp", "tp")),
            P(),
            P(),
            P("tp", None, None),
            P("tp", None, None),
            P(),
        ),
        out_specs=(P(("grp", "tp"), None, None), P(("grp", "tp"))),
        check_vma=False,
    )
```

```python
import functools
import math

import jax
import jax.numpy as jnp
from jax import lax
from jax.experimental import pallas as pl
from jax.experimental.pallas import tpu as pltpu
from jax.sharding import PartitionSpec as P

KVH = 8
HD = 128
D = 8192
QKV = 10240
ROW_BLOCKS = 4
COL_BLOCKS = 8
MEMBERS = ROW_BLOCKS * COL_BLOCKS
FEATURES = D // ROW_BLOCKS
CONTS = 8
STEPS = 2
CTOK = CONTS * STEPS
TILE = 256

THETA = 1000000.0
EPS = 1e-06
MASKED_SCORE = -1e30

VMEM_LIMIT = 32 * 1024 * 1024
VMEM = pl.BlockSpec(memory_space=pltpu.VMEM)
SMEM = pl.BlockSpec(memory_space=pltpu.SMEM)
HBM = pl.BlockSpec(memory_space=pltpu.HBM)


def whole(shape):
    return pl.BlockSpec(shape, lambda *_: (0,) * len(shape))


def cost(flops, moved):
    return pl.CostEstimate(flops=flops, bytes_accessed=moved, transcendentals=0)


def in_hbm(array):
    return pltpu.with_memory_space_constraint(array, pltpu.HBM)


def kernel_params():
    return pltpu.CompilerParams(vmem_limit_bytes=VMEM_LIMIT)


def norm_kernel(main_hbm, cont_hbm, gain_hbm, out_ref, main_ref, cont_ref, gain_ref, rows_ref, piece_ref, sems):
    pairs = ((main_hbm, main_ref), (cont_hbm, cont_ref), (gain_hbm, gain_ref))
    copies = [pltpu.make_async_copy(src, dst, sems.at[i]) for i, (src, dst) in enumerate(pairs)]
    for copy in copies:
        copy.start()
    for copy in copies:
        copy.wait()

    def normed(wide):
        inv = lax.rsqrt(jnp.mean(wide * wide, axis=-1, keepdims=True) + EPS)
        return wide * inv * gain_ref[...]

    for c in range(CONTS):
        rows_ref[c * STEPS : (c + 1) * STEPS, :] = cont_ref[c].astype(jnp.float32)
    cont = normed(rows_ref[...]).astype(jnp.bfloat16)
    main = normed(main_ref[...].astype(jnp.float32))
    for r in range(ROW_BLOCKS):
        for j in range(FEATURES // TILE):
            lanes = slice(r * FEATURES + j * TILE, r * FEATURES + (j + 1) * TILE)
            for s in range(STEPS):
                piece_ref[r, s * 8 + j : s * 8 + j + 1, :] = main[s : s + 1, lanes]
    for r in range(ROW_BLOCKS):
        piece = piece_ref[r].astype(jnp.bfloat16)
        out_ref[r, :, :FEATURES] = cont[:, r * FEATURES : (r + 1) * FEATURES]
        out_ref[r, :, FEATURES:] = piece


def norm_rows(main, cont, gain):
    return pl.pallas_call(
        norm_kernel,
        out_shape=jax.ShapeDtypeStruct((ROW_BLOCKS, CTOK, FEATURES + TILE), jnp.bfloat16),
        in_specs=[HBM] * 3,
        out_specs=VMEM,
        scratch_shapes=[
            pltpu.VMEM((STEPS, D), jnp.bfloat16),
            pltpu.VMEM((CONTS, STEPS, D), jnp.bfloat16),
            pltpu.VMEM((1, D), jnp.float32),
            pltpu.VMEM((CTOK, D), jnp.float32),
            pltpu.VMEM((ROW_BLOCKS, 16, TILE), jnp.float32),
            pltpu.SemaphoreType.DMA((3,)),
        ],
        compiler_params=kernel_params(),
        cost_estimate=cost(10**6, 4 * 10**6),
        name="norm_rows",
    )(in_hbm(main), in_hbm(cont), in_hbm(gain))


def weight_tile(n, tiles, w_hbm, w_ref, sems):
    def copy(i):
        lanes = pl.ds(pl.multiple_of(i * TILE, TILE), TILE)
        return pltpu.make_async_copy(w_hbm.at[0, :, lanes], w_ref.at[i], sems.at[i])

    @pl.when(n == 0)
    def _():
        for i in range(tiles):
            copy(i).start()

    return copy(n)


REST = 768


def rest_tile(block):
    return jnp.where(block == 6, 2, 0)


def plane_place():
    column = lax.rem(lax.axis_index("tp"), COL_BLOCKS)
    return column // 4, lax.rem(column, 4)


def product_kernel(tiles, counts, places, *refs):
    x_refs, refs = refs[: len(counts)], refs[len(counts) :]
    if places:
        earlier_ref, refs = refs[0], refs[1:]
    w_hbm, *out_refs = refs[: 1 + ROW_BLOCKS]
    main_ref, rows_ref, wide_ref, w_ref, sems, part_ref = refs[1 + ROW_BLOCKS :]
    n = pl.program_id(0)
    members = sum(counts)
    count = members * CTOK
    lines = members * STEPS
    halves = TILE // 128
    width = tiles * TILE
    tile = weight_tile(n, tiles, w_hbm, w_ref, sems)

    @pl.when(n == 0)
    def _():
        at = 0
        for x_ref, size in zip(x_refs, counts):
            rows = slice(at * CTOK, (at + size) * CTOK)
            rows_ref[rows, :] = x_ref[:, :, :FEATURES].reshape(size * CTOK, FEATURES)
            packed = x_ref[:, :, FEATURES:].reshape(size * CTOK, TILE).astype(jnp.float32)
            for k in range(halves):
                wide_ref[k, rows, :] = packed[:, k * 128 : (k + 1) * 128]
            at += size
        for k in range(halves):
            for j in range(FEATURES // TILE):
                lane = j * TILE + k * 128
                rows_ref[count:, lane : lane + 128] = wide_ref[k, pl.ds(j, lines, stride=8), :].astype(jnp.bfloat16)

    tile.wait()
    prod = jnp.dot(rows_ref[...], w_ref[n], preferred_element_type=jnp.float32)
    high = prod.astype(jnp.bfloat16)
    part_ref[:, :, pl.ds(pl.multiple_of(n * TILE, TILE), TILE)] = high[:count].reshape(members, CTOK, TILE)
    for k in range(halves):
        wide_ref[k, pl.ds(n, lines, stride=8), :] = prod[count:, k * 128 : (k + 1) * 128]
    start = rest_tile(lax.rem(lax.axis_index("tp"), COL_BLOCKS))

    @pl.when((n >= start) & (n < start + REST // TILE))
    def _():
        low = prod - high.astype(jnp.float32)
        place = n - start
        lane = pl.multiple_of(width + place * TILE, TILE)
        part_ref[:, :, pl.ds(lane, TILE)] = low[:count].astype(jnp.bfloat16).reshape(members, CTOK, TILE)
        for k in range(halves):
            wide_ref[k, pl.ds(tiles + place, lines, stride=8), :] = low[count:, k * 128 : (k + 1) * 128]

    @pl.when(n == tiles - 1)
    def _():
        z = lax.axis_index("tp") // COL_BLOCKS
        done = earlier_ref.shape[0] // ROW_BLOCKS if places else 0
        for k in range(halves):
            lanes = slice(k * 128, (k + 1) * 128)
            packed = wide_ref[k].astype(jnp.bfloat16).reshape(members, CTOK, 128)
            if not places:
                main_ref[:, :, lanes] = packed
            for i, (dy, dx) in enumerate(places):
                y, x = plane_place()
                column = lax.rem(y + dy, 2) * 4 + lax.rem(x + dx, 4)
                for r in range(ROW_BLOCKS):
                    if i < done:
                        message = earlier_ref[i * ROW_BLOCKS + r, :, lanes]
                    else:
                        message = packed[(i - done) * ROW_BLOCKS + r]
                    main_ref[r * COL_BLOCKS + column, :, lanes] = message
        for k, out_ref in enumerate(out_refs):
            to = lax.rem(z + k, ROW_BLOCKS)
            for g in range(members // ROW_BLOCKS):
                out_ref[g] = part_ref[g * ROW_BLOCKS + to]


def block_product(messages, blocks, earlier=(), places=()):
    tiles = blocks.shape[2] // TILE
    lanes = tiles * TILE + REST
    counts = tuple(rows.shape[0] for rows in messages)
    members = sum(counts)
    return pl.pallas_call(
        functools.partial(product_kernel, tiles, counts, places),
        out_shape=[jax.ShapeDtypeStruct((members // ROW_BLOCKS, CTOK, lanes), jnp.bfloat16)] * ROW_BLOCKS
        + [jax.ShapeDtypeStruct((MEMBERS if places else members, CTOK, TILE), jnp.bfloat16)],
        grid=(tiles,),
        in_specs=[VMEM] * (len(counts) + len(earlier)) + [HBM],
        out_specs=[VMEM] * (1 + ROW_BLOCKS),
        scratch_shapes=[
            pltpu.VMEM((members * (CTOK + STEPS), FEATURES), jnp.bfloat16),
            pltpu.VMEM((TILE // 128, members * CTOK, 128), jnp.float32),
            pltpu.VMEM((tiles, FEATURES, TILE), jnp.bfloat16),
            pltpu.SemaphoreType.DMA((tiles,)),
            pltpu.VMEM((members, CTOK, lanes), jnp.bfloat16),
        ],
        compiler_params=kernel_params(),
        cost_estimate=cost(2 * members * (CTOK + STEPS) * FEATURES * tiles * TILE, 12 * 10**6),
        name="block_product",
    )(*messages, *earlier, in_hbm(blocks))


def sum_kernel(bias_ref, *refs):
    part_refs, out_refs = refs[:ROW_BLOCKS], refs[ROW_BLOCKS:]
    column = lax.rem(lax.axis_index("tp"), COL_BLOCKS)
    late = column == 6
    last = (column == COL_BLOCKS - 1).astype(jnp.float32)
    cols = QKV // COL_BLOCKS
    tiles = cols // TILE
    kept = REST // TILE
    zero = jnp.zeros((CTOK, TILE), jnp.float32)

    def value_bias(j):
        if j == 0:
            return jnp.zeros((1, TILE), jnp.float32)
        at = QKV - cols + j * TILE
        return bias_ref[:, at : at + TILE] * last

    for g, out_ref in enumerate(out_refs):

        def total(lane):
            value = part_refs[0][g, :, lane : lane + TILE].astype(jnp.float32)
            for ref in part_refs[1:]:
                value = value + ref[g, :, lane : lane + TILE].astype(jnp.float32)
            return value

        rest = [total(cols + i * TILE) for i in range(kept)] + [zero] * (tiles - kept)
        lows = []
        for j in range(tiles):
            shifted = rest[j - tiles + kept] if j >= tiles - kept else zero
            value = total(j * TILE) + jnp.where(late, shifted, rest[j]) + value_bias(j)
            high = value.astype(jnp.bfloat16)
            out_ref[:, j * TILE : (j + 1) * TILE] = high
            lows.append(value - high.astype(jnp.float32))
        for i in range(kept):
            low = jnp.where(late, lows[i + tiles - kept], lows[i])
            out_ref[:, cols + i * TILE : cols + (i + 1) * TILE] = low.astype(jnp.bfloat16)


def sum_parts(bias, parts):
    groups, rows, lanes = parts[0].shape
    return pl.pallas_call(
        sum_kernel,
        out_shape=[jax.ShapeDtypeStruct((rows, lanes), jnp.bfloat16)] * groups,
        in_specs=[VMEM] * (1 + len(parts)),
        out_specs=[VMEM] * groups,
        compiler_params=kernel_params(),
        cost_estimate=cost(10**6, 3 * 10**6),
        name="sum_parts",
    )(bias, *parts)


def load_parts(part_refs, parts_ref):
    y, x = plane_place()
    for ref, (dy, dx) in zip(part_refs, HOMES):
        column = lax.rem(y + dy, 2) * 4 + lax.rem(x + 4 - dx, 4)
        parts_ref[column] = ref[...]


def summed_block(parts_ref, c, lanes):
    total = parts_ref[c, :, lanes].astype(jnp.float32)
    for r in range(1, ROW_BLOCKS):
        total = total + parts_ref[r * COL_BLOCKS + c, :, lanes].astype(jnp.float32)
    return total


def head_attention(query, key, value, fresh_key, fresh_value, seen, fresh_seen):
    inv_root = 1.0 / math.sqrt(HD)
    contract = (((1,), (1,)), ((), ()))
    old = lax.dot_general(query, key, contract, preferred_element_type=jnp.float32) * inv_root
    new = lax.dot_general(query, fresh_key, contract, preferred_element_type=jnp.float32) * inv_root
    old = jnp.where(seen, old, MASKED_SCORE)
    new = jnp.where(fresh_seen, new, MASKED_SCORE)
    highest = jnp.maximum(jnp.max(old, axis=-1, keepdims=True), jnp.max(new, axis=-1, keepdims=True))
    old = jnp.exp(old - highest)
    new = jnp.exp(new - highest)
    mass = jnp.sum(old, axis=-1, keepdims=True) + jnp.sum(new, axis=-1, keepdims=True)
    inv_mass = 1.0 / mass
    mixed = jnp.dot((old * inv_mass).astype(jnp.bfloat16), value, preferred_element_type=jnp.float32)
    return mixed + jnp.dot((new * inv_mass).astype(jnp.bfloat16), fresh_value, preferred_element_type=jnp.float32)


def load_qkv(main, parts_ref, qkv_ref):
    cols = QKV // COL_BLOCKS
    for c in range(COL_BLOCKS):
        first = 2 if c == 6 else 0
        total = summed_block(parts_ref, c, slice(0, TILE)) if main else parts_ref[c].astype(jnp.float32)
        for j in range(cols // TILE):
            lanes = slice(c * cols + j * TILE, c * cols + (j + 1) * TILE)
            rest = j - first
            has_rest = 0 <= rest < REST // TILE
            if main:
                for s in range(STEPS):
                    line = total[s * 8 + j : s * 8 + j + 1]
                    if has_rest:
                        at = s * 8 + cols // TILE + rest
                        line = line + total[at : at + 1]
                    qkv_ref[s : s + 1, lanes] = line
            else:
                value = total[:, j * TILE : (j + 1) * TILE]
                if has_rest:
                    value = value + total[:, cols + rest * TILE : cols + (rest + 1) * TILE]
                qkv_ref[:, lanes] = value


def head_readers(qkv_ref, bias_ref, cos_ref, sin_ref):
    cosine = cos_ref[...]
    sine = sin_ref[...]

    def plain(start):
        return qkv_ref[:, start : start + HD]

    def rotated(start):
        head = plain(start) + bias_ref[:, start : start + HD]
        return head * cosine + pltpu.roll(head, HD // 2, 1) * sine

    return plain, rotated


def fresh_block(pieces):
    rows = sum(piece.shape[0] for piece in pieces)
    pad = jnp.zeros((128 - rows, HD), jnp.float32)
    return jnp.concatenate(list(pieces) + [pad], axis=0).astype(jnp.bfloat16)


GROUP = D // HD // KVH
KV_WIDTH = KVH * HD


def attend_main_kernel(
    len_ref, bias_ref, cos_ref, sin_ref, cache_ref, parts_ref, out_ref, kv_ref, qkv_ref, piece_ref
):
    rows = qkv_ref.shape[0]
    qkv_ref[...] = jnp.zeros(qkv_ref.shape, jnp.float32)
    load_qkv(True, parts_ref, qkv_ref)
    qkv_ref[:, D + KV_WIDTH :] = qkv_ref[:, D + KV_WIDTH :] + bias_ref[:, D + KV_WIDTH :]
    plain, rotated = head_readers(qkv_ref, bias_ref, cos_ref, sin_ref)
    seen = lax.broadcasted_iota(jnp.int32, (1, cache_ref.shape[0]), 1) < len_ref[0]
    row = lax.broadcasted_iota(jnp.int32, (rows, 128), 0)
    col = lax.broadcasted_iota(jnp.int32, (rows, 128), 1)
    own = ((col <= row) & (col < STEPS)).astype(jnp.int32)
    fresh_seen = jnp.concatenate([own] * GROUP, axis=0) > 0
    for g in range(KVH):
        query = jnp.concatenate([rotated((g * GROUP + h) * HD) for h in range(GROUP)], axis=0).astype(jnp.bfloat16)
        fresh_key = rotated(D + g * HD)
        fresh_value = plain(D + KV_WIDTH + g * HD)
        kv_ref[:, g * HD : (g + 1) * HD] = fresh_key
        kv_ref[:, KV_WIDTH + g * HD : KV_WIDTH + (g + 1) * HD] = fresh_value
        key = cache_ref[:, g * HD : (g + 1) * HD]
        value = cache_ref[:, KV_WIDTH + g * HD : KV_WIDTH + (g + 1) * HD]
        mixed = head_attention(
            query, key, value, fresh_block([fresh_key]), fresh_block([fresh_value]), seen, fresh_seen
        )
        for h in range(GROUP):
            r, place = divmod(g * GROUP + h, FEATURES // HD)
            j, lane = place // 2, (place % 2) * HD
            for s in range(STEPS):
                at = s * 8 + j
                piece_ref[r, at : at + 1, lane : lane + HD] = mixed[h * rows + s : h * rows + s + 1]
    for r in range(ROW_BLOCKS):
        piece = piece_ref[r].astype(jnp.bfloat16)
        for c in range(COL_BLOCKS):
            out_ref[r * COL_BLOCKS + c] = piece


def attend_main(prefix_len, bias, cosine, sine, cache, parts):
    return pl.pallas_call(
        attend_main_kernel,
        out_shape=(
            jax.ShapeDtypeStruct((32, 16, TILE), jnp.bfloat16),
            jax.ShapeDtypeStruct((8, 2 * KV_WIDTH), jnp.float32),
        ),
        in_specs=[SMEM] + [VMEM] * 5,
        out_specs=(whole((32, 16, TILE)), whole((8, 2 * KV_WIDTH))),
        scratch_shapes=[
            pltpu.VMEM((8, QKV), jnp.float32),
            pltpu.VMEM((ROW_BLOCKS, 16, TILE), jnp.float32),
        ],
        compiler_params=kernel_params(),
        cost_estimate=cost(2 * 10**8, 6 * 10**6),
        name="attend_main",
    )(prefix_len, bias, cosine, sine, cache, parts)


def attend_cont_kernel(len_ref, bound_ref, bias_ref, cos_ref, sin_ref, cache_ref, kv_ref, *refs):
    part_refs = refs[:COL_BLOCKS]
    out_ref, qkv_ref, parts_ref = refs[COL_BLOCKS:]
    load_parts(part_refs, parts_ref)
    rows = qkv_ref.shape[0]
    load_qkv(False, parts_ref, qkv_ref)
    plain, rotated = head_readers(qkv_ref, bias_ref, cos_ref, sin_ref)
    seen = lax.broadcasted_iota(jnp.int32, (1, cache_ref.shape[0]), 1) < len_ref[0]
    row = lax.broadcasted_iota(jnp.int32, (rows, 128), 0)
    col = lax.broadcasted_iota(jnp.int32, (rows, 128), 1)
    own = (row // STEPS == col // STEPS) & (col <= row)
    main = (col >= rows) & (col < rows + bound_ref[0])
    fresh_seen = jnp.concatenate([(own | main).astype(jnp.int32)] * GROUP, axis=0) > 0
    for g in range(KVH):
        query = jnp.concatenate([rotated((g * GROUP + h) * HD) for h in range(GROUP)], axis=0).astype(jnp.bfloat16)
        at_key = slice(g * HD, (g + 1) * HD)
        at_value = slice(KV_WIDTH + g * HD, KV_WIDTH + (g + 1) * HD)
        fresh_key = fresh_block([rotated(D + g * HD), kv_ref[:, at_key]])
        fresh_value = fresh_block([plain(D + KV_WIDTH + g * HD), kv_ref[:, at_value]])
        mixed = head_attention(
            query, cache_ref[:, at_key], cache_ref[:, at_value], fresh_key, fresh_value, seen, fresh_seen
        )
        mixed = mixed.astype(jnp.bfloat16)
        for h in range(GROUP):
            out_ref[:, (g * GROUP + h) * HD : (g * GROUP + h + 1) * HD] = mixed[h * rows : (h + 1) * rows]


def attend_cont(*args):
    return pl.pallas_call(
        attend_cont_kernel,
        out_shape=jax.ShapeDtypeStruct((CTOK, D), jnp.bfloat16),
        in_specs=[SMEM, SMEM] + [VMEM] * 4 + [whole((8, 2 * KV_WIDTH))] + [VMEM] * COL_BLOCKS,
        out_specs=whole((CTOK, D)),
        scratch_shapes=[
            pltpu.VMEM((CTOK, QKV), jnp.float32),
            pltpu.VMEM((COL_BLOCKS,) + args[-1].shape, jnp.bfloat16),
        ],
        compiler_params=kernel_params(),
        cost_estimate=cost(4 * 10**8, 8 * 10**6),
        name="attend_cont",
    )(*args)


def readout_kernel(head_ref, w_hbm, out_ref, w_ref, sem):
    copy = pltpu.make_async_copy(w_hbm.at[0], w_ref, sem)
    copy.start()
    row = head_ref[pl.ds(lax.rem(lax.axis_index("tp"), COL_BLOCKS), 1), :]
    high = row.astype(jnp.bfloat16).astype(jnp.float32)
    middle = (row - high).astype(jnp.bfloat16).astype(jnp.float32)
    low = row - high - middle
    pieces = jnp.concatenate([high, middle, low, jnp.zeros((13, row.shape[1]), jnp.float32)], axis=0)
    copy.wait()
    prod = lax.dot_general(
        pieces.astype(jnp.bfloat16), w_ref[...], (((1,), (1,)), ((), ())), preferred_element_type=jnp.float32
    )
    out_ref[...] = prod[0:1] + prod[1:2] + prod[2:3]


def readout(value_head, blocks):
    return pl.pallas_call(
        readout_kernel,
        out_shape=jax.ShapeDtypeStruct((1, FEATURES), jnp.float32),
        in_specs=[whole(value_head.shape), HBM],
        out_specs=whole((1, FEATURES)),
        scratch_shapes=[pltpu.VMEM((FEATURES, D // COL_BLOCKS), jnp.bfloat16), pltpu.SemaphoreType.DMA],
        compiler_params=kernel_params(),
        cost_estimate=cost(2 * 10**8, 5 * 10**6),
        name="readout",
    )(value_head, in_hbm(blocks))


def out_kernel(tiles, x_ref, read_ref, w_hbm, out_ref, rows_ref, wide_ref, read8_ref, w_ref, sems):
    n = pl.program_id(0)
    members = x_ref.shape[0]
    lines = members * STEPS
    halves = TILE // 128
    tile = weight_tile(n, tiles, w_hbm, w_ref, sems)

    @pl.when(n == 0)
    def _():
        for j in range(FEATURES // TILE):
            read8_ref[j : j + 1, :] = read_ref[:, j * TILE : (j + 1) * TILE]
        out_ref[:, 8:, :] = jnp.broadcast_to(read8_ref[...][None], (members, 8, TILE))
        packed = x_ref[...].reshape(members * 16, TILE).astype(jnp.float32)
        for k in range(halves):
            wide_ref[k] = packed[:, k * 128 : (k + 1) * 128]
            for j in range(FEATURES // TILE):
                lane = j * TILE + k * 128
                rows_ref[:, lane : lane + 128] = wide_ref[k, pl.ds(j, lines, stride=8), :].astype(jnp.bfloat16)

    tile.wait()
    prod = jnp.dot(rows_ref[...], w_ref[n], preferred_element_type=jnp.float32)
    for k in range(halves):
        wide_ref[k, pl.ds(n, lines, stride=4), :] = prod[:, k * 128 : (k + 1) * 128]

    @pl.when(n == tiles - 1)
    def _():
        for k in range(halves):
            packed = wide_ref[k, : members * 8, :].reshape(members, 8, 128)
            out_ref[:, :8, k * 128 : (k + 1) * 128] = packed


def out_product(rows, read, blocks):
    members = rows.shape[0]
    tiles = blocks.shape[2] // TILE
    return pl.pallas_call(
        functools.partial(out_kernel, tiles),
        out_shape=jax.ShapeDtypeStruct((members, 16, TILE), jnp.float32),
        grid=(tiles,),
        in_specs=[whole(rows.shape), whole(read.shape), HBM],
        out_specs=whole((members, 16, TILE)),
        scratch_shapes=[
            pltpu.VMEM((members * STEPS, FEATURES), jnp.bfloat16),
            pltpu.VMEM((TILE // 128, members * 16, 128), jnp.float32),
            pltpu.VMEM((8, TILE), jnp.float32),
            pltpu.VMEM((tiles, FEATURES, TILE), jnp.bfloat16),
            pltpu.SemaphoreType.DMA((tiles,)),
        ],
        compiler_params=kernel_params(),
        cost_estimate=cost(3 * 10**8, 5 * 10**6),
        name="out_product",
    )(rows, read, in_hbm(blocks))


def finish_kernel(parts_ref, main_ref, cont_ref, head_ref, mixed_ref, out_ref, score_ref, wide_ref):
    cols = D // COL_BLOCKS
    for c in range(COL_BLOCKS):
        total = summed_block(parts_ref, c, slice(0, TILE))
        for j in range(cols // TILE):
            at = slice(c * cols + j * TILE, c * cols + (j + 1) * TILE)
            for s in range(STEPS):
                wide_ref[s : s + 1, at] = total[s * 4 + j : s * 4 + j + 1]
    out_ref[...] = (main_ref[...].astype(jnp.float32) + wide_ref[:STEPS, :]).astype(jnp.bfloat16)
    score = jnp.zeros((CTOK, TILE), jnp.float32)
    direct = jnp.zeros((STEPS, TILE), jnp.float32)
    for r in range(ROW_BLOCKS):
        read = parts_ref[r * COL_BLOCKS, 8:, :]
        for c in range(1, COL_BLOCKS):
            read = read + parts_ref[r * COL_BLOCKS + c, 8:, :]
        for j in range(FEATURES // TILE):
            lanes = slice(r * FEATURES + j * TILE, r * FEATURES + (j + 1) * TILE)
            score = score + mixed_ref[:, lanes].astype(jnp.float32) * read[j : j + 1, :]
            for c in range(CONTS):
                direct = direct + cont_ref[c, :, lanes].astype(jnp.float32) * head_ref[:, lanes]
    total = jnp.sum(score, axis=0, keepdims=True) + jnp.sum(direct, axis=0, keepdims=True)
    score_ref[...] = jnp.broadcast_to(jnp.sum(total, axis=1, keepdims=True) / CONTS, (8, 128))


def finish(parts, main, cont, head, mixed):
    return pl.pallas_call(
        finish_kernel,
        out_shape=(
            jax.ShapeDtypeStruct((STEPS, D), jnp.bfloat16),
            jax.ShapeDtypeStruct((8, 128), jnp.float32),
        ),
        in_specs=[whole(parts.shape), whole(main.shape), whole(cont.shape), whole(head.shape), whole(mixed.shape)],
        out_specs=(whole((STEPS, D)), whole((8, 128))),
        scratch_shapes=[pltpu.VMEM((8, D), jnp.float32)],
        compiler_params=kernel_params(),
        cost_estimate=cost(10**6, 2 * 10**6),
        name="finish",
    )(parts, main, cont, head, mixed)


def rope_tables(positions):
    half = HD // 2
    frequency = THETA ** (-(jnp.arange(half, dtype=jnp.float32) * 2.0) / HD)
    angles = positions.astype(jnp.float32)[:, None] * frequency[None, :]
    cosine = jnp.cos(angles)
    sine = jnp.sin(angles)
    return jnp.concatenate([cosine, cosine], axis=1), jnp.concatenate([-sine, sine], axis=1)


def exchange(rows):
    return lax.all_to_all(rows, "tp", split_axis=0, concat_axis=0, tiled=True)


ALONG = [[z * COL_BLOCKS + c for z in range(ROW_BLOCKS)] for c in range(COL_BLOCKS)]


def from_side(rows, dy, dx):
    route = []
    for to in range(MEMBERS):
        z, y, x = to // 8, to // 4 % 2, to % 4
        route.append((z * 8 + (y + dy) % 2 * 4 + (x + dx) % 4, to))
    return lax.ppermute(rows, "tp", route)


def from_along(rows, dz):
    route = [((to + dz * COL_BLOCKS) % MEMBERS, to) for to in range(MEMBERS)]
    return lax.ppermute(rows, "tp", route)


FIRST_HOMES = ((0, 0), (1, 0), (0, 1), (0, 3))
SECOND_HOMES = ((1, 1), (1, 3), (0, 2), (1, 2))
HOMES = FIRST_HOMES + SECOND_HOMES


def project(rows, blocks, bias):
    near = lax.all_to_all(rows, "tp", split_axis=0, concat_axis=0, tiled=True, axis_index_groups=ALONG)
    over = from_side(near, 1, 0)
    after, before = from_side(near, 0, 1), from_side(near, 0, 3)
    over_after, over_before = from_side(over, 0, 1), from_side(over, 0, 3)
    far = [from_side(before, 0, 3), from_side(over_after, 0, 1)]
    *first, main = block_product([near, over, after, before], blocks)
    first = [first[0]] + [from_along(first[k], -k) for k in range(1, ROW_BLOCKS)]
    *second, main = block_product([over_after, over_before] + far, blocks, (main,), HOMES)
    main, first = lax.optimization_barrier((main, first))
    second = [second[0]] + [from_along(second[k], -k) for k in range(1, ROW_BLOCKS)]
    received = []
    for homes, parts in ((FIRST_HOMES, first), (SECOND_HOMES, second)):
        for (dy, dx), summed in zip(homes, sum_parts(bias, parts)):
            received.append(from_side(summed, -dy, -dx) if dy or dx else summed)
    return received, exchange(main)


def on_device(
    main_inputs, cont_inputs, prefix_cache, prefix_len, boundary, rms_gain, qkv_bias, w_qkv, w_out, value_head
):
    main = main_inputs.reshape(STEPS, D)
    cont = cont_inputs.reshape(CONTS, STEPS, D)
    bias = qkv_bias[None, :]
    cache = prefix_cache[0]
    head = value_head[None, :]
    step = jnp.arange(CTOK, dtype=jnp.int32) % STEPS
    main_tables = rope_tables(prefix_len + step[:8])
    cont_tables = rope_tables(prefix_len + boundary + step)
    read = readout(value_head.reshape(COL_BLOCKS, D // COL_BLOCKS), w_out)
    parts, main_parts = project(norm_rows(main, cont, rms_gain[None, :]), w_qkv, bias)
    mixed, main_kv = attend_main(prefix_len, bias, *main_tables, cache, main_parts)
    mixed = exchange(mixed)
    cont_mixed = attend_cont(prefix_len, boundary, bias, *cont_tables, cache, main_kv, *parts)
    parts = exchange(out_product(mixed, read, w_out))
    main_out, score = finish(parts, main, cont, head, cont_mixed)
    return main_out[None], score[0, :1]


def solution(mesh):
    return jax.shard_map(
        on_device,
        mesh=mesh,
        in_specs=(
            P(("grp", "tp"), None, None),
            P(("grp", "tp"), None, None, None),
            P(("grp", "tp"), None, None),
            P(("grp", "tp")),
            P(("grp", "tp")),
            P(),
            P(),
            P("tp", None, None),
            P("tp", None, None),
            P(),
        ),
        out_specs=(P(("grp", "tp"), None, None), P(("grp", "tp"))),
        check_vma=False,
    )
```

```python
import functools
import math

import jax
import jax.numpy as jnp
from jax import lax
from jax.experimental import pallas as pl
from jax.experimental.pallas import tpu as pltpu
from jax.sharding import PartitionSpec as P

KVH = 8
HD = 128
D = 8192
QKV = 10240
ROW_BLOCKS = 4
COL_BLOCKS = 8
MEMBERS = ROW_BLOCKS * COL_BLOCKS
FEATURES = D // ROW_BLOCKS
CONTS = 8
STEPS = 2
CTOK = CONTS * STEPS
TILE = 256

THETA = 1000000.0
EPS = 1e-06
MASKED_SCORE = -1e30

VMEM_LIMIT = 32 * 1024 * 1024
VMEM = pl.BlockSpec(memory_space=pltpu.VMEM)
SMEM = pl.BlockSpec(memory_space=pltpu.SMEM)
HBM = pl.BlockSpec(memory_space=pltpu.HBM)
UNREAD = pl.BlockSpec(memory_space=pl.ANY)


def whole(shape):
    return pl.BlockSpec(shape, lambda *_: (0,) * len(shape))


def cost(flops, moved):
    return pl.CostEstimate(flops=flops, bytes_accessed=moved, transcendentals=0)


def in_hbm(array):
    return pltpu.with_memory_space_constraint(array, pltpu.HBM)


def kernel_params():
    return pltpu.CompilerParams(vmem_limit_bytes=VMEM_LIMIT)


def norm_kernel(main_hbm, cont_hbm, gain_hbm, out_ref, main_ref, cont_ref, gain_ref, rows_ref, piece_ref, sems):
    pairs = ((main_hbm, main_ref), (cont_hbm, cont_ref), (gain_hbm, gain_ref))
    copies = [pltpu.make_async_copy(src, dst, sems.at[i]) for i, (src, dst) in enumerate(pairs)]
    for copy in copies:
        copy.start()
    for copy in copies:
        copy.wait()

    def normed(wide):
        inv = lax.rsqrt(jnp.mean(wide * wide, axis=-1, keepdims=True) + EPS)
        return wide * inv * gain_ref[...]

    for c in range(CONTS):
        rows_ref[c * STEPS : (c + 1) * STEPS, :] = cont_ref[c].astype(jnp.float32)
    cont = normed(rows_ref[...]).astype(jnp.bfloat16)
    main = normed(main_ref[...].astype(jnp.float32))
    for r in range(ROW_BLOCKS):
        for j in range(FEATURES // TILE):
            lanes = slice(r * FEATURES + j * TILE, r * FEATURES + (j + 1) * TILE)
            for s in range(STEPS):
                piece_ref[r, s * 8 + j : s * 8 + j + 1, :] = main[s : s + 1, lanes]
    for r in range(ROW_BLOCKS):
        piece = piece_ref[r].astype(jnp.bfloat16)
        out_ref[r, :, :FEATURES] = cont[:, r * FEATURES : (r + 1) * FEATURES]
        out_ref[r, :, FEATURES:] = piece


def norm_rows(main, cont, gain):
    return pl.pallas_call(
        norm_kernel,
        out_shape=jax.ShapeDtypeStruct((ROW_BLOCKS, CTOK, FEATURES + TILE), jnp.bfloat16),
        in_specs=[HBM] * 3,
        out_specs=VMEM,
        scratch_shapes=[
            pltpu.VMEM((STEPS, D), jnp.bfloat16),
            pltpu.VMEM((CONTS, STEPS, D), jnp.bfloat16),
            pltpu.VMEM((1, D), jnp.float32),
            pltpu.VMEM((CTOK, D), jnp.float32),
            pltpu.VMEM((ROW_BLOCKS, 16, TILE), jnp.float32),
            pltpu.SemaphoreType.DMA((3,)),
        ],
        compiler_params=kernel_params(),
        cost_estimate=cost(10**6, 4 * 10**6),
        name="norm_rows",
    )(in_hbm(main), in_hbm(cont), in_hbm(gain))


def weight_tile(n, tiles, w_hbm, w_ref, sems):
    def copy(i):
        lanes = pl.ds(pl.multiple_of(i * TILE, TILE), TILE)
        return pltpu.make_async_copy(w_hbm.at[0, :, lanes], w_ref.at[i], sems.at[i])

    @pl.when(n == 0)
    def _():
        for i in range(tiles):
            copy(i).start()

    return copy(n)


REST = 768


def rest_tile(block):
    return jnp.where(block == 6, 2, 0)


def plane_place():
    column = lax.rem(lax.axis_index("tp"), COL_BLOCKS)
    return column // 4, lax.rem(column, 4)


def product_kernel(tiles, counts, places, *refs):
    x_refs, refs = refs[: len(counts)], refs[len(counts) :]
    if places:
        earlier_ref, refs = refs[0], refs[1:]
    w_hbm, *out_refs = refs[: 1 + ROW_BLOCKS]
    main_ref, rows_ref, wide_ref, w_ref, sems, part_ref = refs[1 + ROW_BLOCKS :]
    n = pl.program_id(0)
    members = sum(counts)
    count = members * CTOK
    lines = members * STEPS
    halves = TILE // 128
    width = tiles * TILE
    tile = weight_tile(n, tiles, w_hbm, w_ref, sems)

    @pl.when(n == 0)
    def _():
        at = 0
        for x_ref, size in zip(x_refs, counts):
            rows = slice(at * CTOK, (at + size) * CTOK)
            rows_ref[rows, :] = x_ref[:, :, :FEATURES].reshape(size * CTOK, FEATURES)
            packed = x_ref[:, :, FEATURES:].reshape(size * CTOK, TILE).astype(jnp.float32)
            for k in range(halves):
                wide_ref[k, rows, :] = packed[:, k * 128 : (k + 1) * 128]
            at += size
        for k in range(halves):
            for j in range(FEATURES // TILE):
                lane = j * TILE + k * 128
                rows_ref[count:, lane : lane + 128] = wide_ref[k, pl.ds(j, lines, stride=8), :].astype(jnp.bfloat16)

    tile.wait()
    prod = jnp.dot(rows_ref[...], w_ref[n], preferred_element_type=jnp.float32)
    high = prod.astype(jnp.bfloat16)
    part_ref[:, :, pl.ds(pl.multiple_of(n * TILE, TILE), TILE)] = high[:count].reshape(members, CTOK, TILE)
    for k in range(halves):
        wide_ref[k, pl.ds(n, lines, stride=8), :] = prod[count:, k * 128 : (k + 1) * 128]
    start = rest_tile(lax.rem(lax.axis_index("tp"), COL_BLOCKS))

    @pl.when((n >= start) & (n < start + REST // TILE))
    def _():
        low = prod - high.astype(jnp.float32)
        place = n - start
        lane = pl.multiple_of(width + place * TILE, TILE)
        part_ref[:, :, pl.ds(lane, TILE)] = low[:count].astype(jnp.bfloat16).reshape(members, CTOK, TILE)
        for k in range(halves):
            wide_ref[k, pl.ds(tiles + place, lines, stride=8), :] = low[count:, k * 128 : (k + 1) * 128]

    @pl.when(n == tiles - 1)
    def _():
        z = lax.axis_index("tp") // COL_BLOCKS
        done = earlier_ref.shape[0] // ROW_BLOCKS if places else 0
        for k in range(halves):
            lanes = slice(k * 128, (k + 1) * 128)
            packed = wide_ref[k].astype(jnp.bfloat16).reshape(members, CTOK, 128)
            if not places:
                main_ref[:, :, lanes] = packed
            for i, (dy, dx) in enumerate(places):
                y, x = plane_place()
                column = lax.rem(y + dy, 2) * 4 + lax.rem(x + dx, 4)
                for r in range(ROW_BLOCKS):
                    if i < done:
                        message = earlier_ref[i * ROW_BLOCKS + r, :, lanes]
                    else:
                        message = packed[(i - done) * ROW_BLOCKS + r]
                    main_ref[r * COL_BLOCKS + column, :, lanes] = message
        for k, out_ref in enumerate(out_refs):
            to = lax.rem(z + k, ROW_BLOCKS)
            for g in range(members // ROW_BLOCKS):
                out_ref[g] = part_ref[g * ROW_BLOCKS + to]


def block_product(messages, blocks, earlier=(), places=()):
    tiles = blocks.shape[2] // TILE
    lanes = tiles * TILE + REST
    counts = tuple(rows.shape[0] for rows in messages)
    members = sum(counts)
    return pl.pallas_call(
        functools.partial(product_kernel, tiles, counts, places),
        out_shape=[jax.ShapeDtypeStruct((members // ROW_BLOCKS, CTOK, lanes), jnp.bfloat16)] * ROW_BLOCKS
        + [jax.ShapeDtypeStruct((MEMBERS if places else members, CTOK, TILE), jnp.bfloat16)],
        grid=(tiles,),
        in_specs=[VMEM] * (len(counts) + len(earlier)) + [HBM],
        out_specs=[VMEM] * (1 + ROW_BLOCKS),
        scratch_shapes=[
            pltpu.VMEM((members * (CTOK + STEPS), FEATURES), jnp.bfloat16),
            pltpu.VMEM((TILE // 128, members * CTOK, 128), jnp.float32),
            pltpu.VMEM((tiles, FEATURES, TILE), jnp.bfloat16),
            pltpu.SemaphoreType.DMA((tiles,)),
            pltpu.VMEM((members, CTOK, lanes), jnp.bfloat16),
        ],
        compiler_params=kernel_params(),
        cost_estimate=cost(2 * members * (CTOK + STEPS) * FEATURES * tiles * TILE, 12 * 10**6),
        name="block_product",
    )(*messages, *earlier, in_hbm(blocks))


def sum_kernel(bias_ref, *refs):
    part_refs, out_refs = refs[:ROW_BLOCKS], refs[ROW_BLOCKS:]
    column = lax.rem(lax.axis_index("tp"), COL_BLOCKS)
    late = column == 6
    last = (column == COL_BLOCKS - 1).astype(jnp.float32)
    cols = QKV // COL_BLOCKS
    tiles = cols // TILE
    kept = REST // TILE
    zero = jnp.zeros((CTOK, TILE), jnp.float32)

    def value_bias(j):
        if j == 0:
            return jnp.zeros((1, TILE), jnp.float32)
        at = QKV - cols + j * TILE
        return bias_ref[:, at : at + TILE] * last

    for g, out_ref in enumerate(out_refs):

        def total(lane):
            value = part_refs[0][g, :, lane : lane + TILE].astype(jnp.float32)
            for ref in part_refs[1:]:
                value = value + ref[g, :, lane : lane + TILE].astype(jnp.float32)
            return value

        rest = [total(cols + i * TILE) for i in range(kept)] + [zero] * (tiles - kept)
        lows = []
        for j in range(tiles):
            shifted = rest[j - tiles + kept] if j >= tiles - kept else zero
            value = total(j * TILE) + jnp.where(late, shifted, rest[j]) + value_bias(j)
            high = value.astype(jnp.bfloat16)
            out_ref[:, j * TILE : (j + 1) * TILE] = high
            lows.append(value - high.astype(jnp.float32))
        for i in range(kept):
            low = jnp.where(late, lows[i + tiles - kept], lows[i])
            out_ref[:, cols + i * TILE : cols + (i + 1) * TILE] = low.astype(jnp.bfloat16)


def sum_parts(bias, parts):
    groups, rows, lanes = parts[0].shape
    return pl.pallas_call(
        sum_kernel,
        out_shape=[jax.ShapeDtypeStruct((rows, lanes), jnp.bfloat16)] * groups,
        in_specs=[VMEM] * (1 + len(parts)),
        out_specs=[VMEM] * groups,
        compiler_params=kernel_params(),
        cost_estimate=cost(10**6, 3 * 10**6),
        name="sum_parts",
    )(bias, *parts)


def load_parts(part_refs, parts_ref):
    y, x = plane_place()
    for ref, (dy, dx) in zip(part_refs, HOMES):
        column = lax.rem(y + dy, 2) * 4 + lax.rem(x + 4 - dx, 4)
        parts_ref[column] = ref[...]


def summed_block(parts_ref, c, lanes):
    total = parts_ref[c, :, lanes].astype(jnp.float32)
    for r in range(1, ROW_BLOCKS):
        total = total + parts_ref[r * COL_BLOCKS + c, :, lanes].astype(jnp.float32)
    return total


def head_attention(query, key, value, fresh_key, fresh_value, seen, fresh_seen):
    inv_root = 1.0 / math.sqrt(HD)
    contract = (((1,), (1,)), ((), ()))
    old = lax.dot_general(query, key, contract, preferred_element_type=jnp.float32) * inv_root
    new = lax.dot_general(query, fresh_key, contract, preferred_element_type=jnp.float32) * inv_root
    old = jnp.where(seen, old, MASKED_SCORE)
    new = jnp.where(fresh_seen, new, MASKED_SCORE)
    highest = jnp.maximum(jnp.max(old, axis=-1, keepdims=True), jnp.max(new, axis=-1, keepdims=True))
    old = jnp.exp(old - highest)
    new = jnp.exp(new - highest)
    mass = jnp.sum(old, axis=-1, keepdims=True) + jnp.sum(new, axis=-1, keepdims=True)
    inv_mass = 1.0 / mass
    mixed = jnp.dot((old * inv_mass).astype(jnp.bfloat16), value, preferred_element_type=jnp.float32)
    return mixed + jnp.dot((new * inv_mass).astype(jnp.bfloat16), fresh_value, preferred_element_type=jnp.float32)


def load_qkv(main, parts_ref, qkv_ref):
    cols = QKV // COL_BLOCKS
    for c in range(COL_BLOCKS):
        first = 2 if c == 6 else 0
        total = summed_block(parts_ref, c, slice(0, TILE)) if main else parts_ref[c].astype(jnp.float32)
        for j in range(cols // TILE):
            lanes = slice(c * cols + j * TILE, c * cols + (j + 1) * TILE)
            rest = j - first
            has_rest = 0 <= rest < REST // TILE
            if main:
                for s in range(STEPS):
                    line = total[s * 8 + j : s * 8 + j + 1]
                    if has_rest:
                        at = s * 8 + cols // TILE + rest
                        line = line + total[at : at + 1]
                    qkv_ref[s : s + 1, lanes] = line
            else:
                value = total[:, j * TILE : (j + 1) * TILE]
                if has_rest:
                    value = value + total[:, cols + rest * TILE : cols + (rest + 1) * TILE]
                qkv_ref[:, lanes] = value


def head_readers(qkv_ref, bias_ref, cos_ref, sin_ref):
    cosine = cos_ref[...]
    sine = sin_ref[...]

    def plain(start):
        return qkv_ref[:, start : start + HD]

    def rotated(start):
        head = plain(start) + bias_ref[:, start : start + HD]
        return head * cosine + pltpu.roll(head, HD // 2, 1) * sine

    return plain, rotated


def fresh_block(pieces):
    rows = sum(piece.shape[0] for piece in pieces)
    pad = jnp.zeros((128 - rows, HD), jnp.float32)
    return jnp.concatenate(list(pieces) + [pad], axis=0).astype(jnp.bfloat16)


GROUP = D // HD // KVH
KV_WIDTH = KVH * HD


def attend_main_kernel(
    len_ref, bias_ref, cos_ref, sin_ref, cache_ref, parts_ref, *refs
):
    out_ref, kv_ref, qkv_ref, piece_ref = refs[-4:]
    rows = qkv_ref.shape[0]
    qkv_ref[...] = jnp.zeros(qkv_ref.shape, jnp.float32)
    load_qkv(True, parts_ref, qkv_ref)
    qkv_ref[:, D + KV_WIDTH :] = qkv_ref[:, D + KV_WIDTH :] + bias_ref[:, D + KV_WIDTH :]
    plain, rotated = head_readers(qkv_ref, bias_ref, cos_ref, sin_ref)
    seen = lax.broadcasted_iota(jnp.int32, (1, cache_ref.shape[0]), 1) < len_ref[0]
    row = lax.broadcasted_iota(jnp.int32, (rows, 128), 0)
    col = lax.broadcasted_iota(jnp.int32, (rows, 128), 1)
    own = ((col <= row) & (col < STEPS)).astype(jnp.int32)
    fresh_seen = jnp.concatenate([own] * GROUP, axis=0) > 0
    for g in range(KVH):
        query = jnp.concatenate([rotated((g * GROUP + h) * HD) for h in range(GROUP)], axis=0).astype(jnp.bfloat16)
        fresh_key = rotated(D + g * HD)
        fresh_value = plain(D + KV_WIDTH + g * HD)
        kv_ref[:, g * HD : (g + 1) * HD] = fresh_key
        kv_ref[:, KV_WIDTH + g * HD : KV_WIDTH + (g + 1) * HD] = fresh_value
        key = cache_ref[:, g * HD : (g + 1) * HD]
        value = cache_ref[:, KV_WIDTH + g * HD : KV_WIDTH + (g + 1) * HD]
        mixed = head_attention(
            query, key, value, fresh_block([fresh_key]), fresh_block([fresh_value]), seen, fresh_seen
        )
        for h in range(GROUP):
            r, place = divmod(g * GROUP + h, FEATURES // HD)
            j, lane = place // 2, (place % 2) * HD
            for s in range(STEPS):
                at = s * 8 + j
                piece_ref[r, at : at + 1, lane : lane + HD] = mixed[h * rows + s : h * rows + s + 1]
    for r in range(ROW_BLOCKS):
        piece = piece_ref[r].astype(jnp.bfloat16)
        for c in range(COL_BLOCKS):
            out_ref[r * COL_BLOCKS + c] = piece


def attend_main(prefix_len, bias, cosine, sine, cache, parts, after):
    return pl.pallas_call(
        attend_main_kernel,
        out_shape=(
            jax.ShapeDtypeStruct((32, 16, TILE), jnp.bfloat16),
            jax.ShapeDtypeStruct((8, 2 * KV_WIDTH), jnp.float32),
        ),
        in_specs=[SMEM] + [VMEM] * 5 + [UNREAD] * len(after),
        out_specs=(whole((32, 16, TILE)), whole((8, 2 * KV_WIDTH))),
        scratch_shapes=[
            pltpu.VMEM((8, QKV), jnp.float32),
            pltpu.VMEM((ROW_BLOCKS, 16, TILE), jnp.float32),
        ],
        compiler_params=kernel_params(),
        cost_estimate=cost(2 * 10**8, 6 * 10**6),
        name="attend_main",
    )(prefix_len, bias, cosine, sine, cache, parts, *after)


def attend_cont_kernel(len_ref, bound_ref, bias_ref, cos_ref, sin_ref, cache_ref, kv_ref, *refs):
    part_refs = refs[:COL_BLOCKS]
    out_ref, qkv_ref, parts_ref = refs[COL_BLOCKS:]
    load_parts(part_refs, parts_ref)
    rows = qkv_ref.shape[0]
    load_qkv(False, parts_ref, qkv_ref)
    plain, rotated = head_readers(qkv_ref, bias_ref, cos_ref, sin_ref)
    seen = lax.broadcasted_iota(jnp.int32, (1, cache_ref.shape[0]), 1) < len_ref[0]
    row = lax.broadcasted_iota(jnp.int32, (rows, 128), 0)
    col = lax.broadcasted_iota(jnp.int32, (rows, 128), 1)
    own = (row // STEPS == col // STEPS) & (col <= row)
    main = (col >= rows) & (col < rows + bound_ref[0])
    fresh_seen = jnp.concatenate([(own | main).astype(jnp.int32)] * GROUP, axis=0) > 0
    for g in range(KVH):
        query = jnp.concatenate([rotated((g * GROUP + h) * HD) for h in range(GROUP)], axis=0).astype(jnp.bfloat16)
        at_key = slice(g * HD, (g + 1) * HD)
        at_value = slice(KV_WIDTH + g * HD, KV_WIDTH + (g + 1) * HD)
        fresh_key = fresh_block([rotated(D + g * HD), kv_ref[:, at_key]])
        fresh_value = fresh_block([plain(D + KV_WIDTH + g * HD), kv_ref[:, at_value]])
        mixed = head_attention(
            query, cache_ref[:, at_key], cache_ref[:, at_value], fresh_key, fresh_value, seen, fresh_seen
        )
        mixed = mixed.astype(jnp.bfloat16)
        for h in range(GROUP):
            out_ref[:, (g * GROUP + h) * HD : (g * GROUP + h + 1) * HD] = mixed[h * rows : (h + 1) * rows]


def attend_cont(*args):
    return pl.pallas_call(
        attend_cont_kernel,
        out_shape=jax.ShapeDtypeStruct((CTOK, D), jnp.bfloat16),
        in_specs=[SMEM, SMEM] + [VMEM] * 4 + [whole((8, 2 * KV_WIDTH))] + [VMEM] * COL_BLOCKS,
        out_specs=whole((CTOK, D)),
        scratch_shapes=[
            pltpu.VMEM((CTOK, QKV), jnp.float32),
            pltpu.VMEM((COL_BLOCKS,) + args[-1].shape, jnp.bfloat16),
        ],
        compiler_params=kernel_params(),
        cost_estimate=cost(4 * 10**8, 8 * 10**6),
        name="attend_cont",
    )(*args)


def readout_kernel(head_ref, w_hbm, out_ref, w_ref, sem):
    copy = pltpu.make_async_copy(w_hbm.at[0], w_ref, sem)
    copy.start()
    row = head_ref[pl.ds(lax.rem(lax.axis_index("tp"), COL_BLOCKS), 1), :]
    high = row.astype(jnp.bfloat16).astype(jnp.float32)
    middle = (row - high).astype(jnp.bfloat16).astype(jnp.float32)
    low = row - high - middle
    pieces = jnp.concatenate([high, middle, low, jnp.zeros((13, row.shape[1]), jnp.float32)], axis=0)
    copy.wait()
    prod = lax.dot_general(
        pieces.astype(jnp.bfloat16), w_ref[...], (((1,), (1,)), ((), ())), preferred_element_type=jnp.float32
    )
    out_ref[...] = prod[0:1] + prod[1:2] + prod[2:3]


def readout(value_head, blocks):
    return pl.pallas_call(
        readout_kernel,
        out_shape=jax.ShapeDtypeStruct((1, FEATURES), jnp.float32),
        in_specs=[whole(value_head.shape), HBM],
        out_specs=whole((1, FEATURES)),
        scratch_shapes=[pltpu.VMEM((FEATURES, D // COL_BLOCKS), jnp.bfloat16), pltpu.SemaphoreType.DMA],
        compiler_params=kernel_params(),
        cost_estimate=cost(2 * 10**8, 5 * 10**6),
        name="readout",
    )(value_head, in_hbm(blocks))


def out_kernel(tiles, x_ref, read_ref, w_hbm, *refs):
    out_ref, rows_ref, wide_ref, read8_ref, w_ref, sems = refs[-6:]
    n = pl.program_id(0)
    members = x_ref.shape[0]
    lines = members * STEPS
    halves = TILE // 128
    tile = weight_tile(n, tiles, w_hbm, w_ref, sems)

    @pl.when(n == 0)
    def _():
        for j in range(FEATURES // TILE):
            read8_ref[j : j + 1, :] = read_ref[:, j * TILE : (j + 1) * TILE]
        out_ref[:, 8:, :] = jnp.broadcast_to(read8_ref[...][None], (members, 8, TILE))
        packed = x_ref[...].reshape(members * 16, TILE).astype(jnp.float32)
        for k in range(halves):
            wide_ref[k] = packed[:, k * 128 : (k + 1) * 128]
            for j in range(FEATURES // TILE):
                lane = j * TILE + k * 128
                rows_ref[:, lane : lane + 128] = wide_ref[k, pl.ds(j, lines, stride=8), :].astype(jnp.bfloat16)

    tile.wait()
    prod = jnp.dot(rows_ref[...], w_ref[n], preferred_element_type=jnp.float32)
    for k in range(halves):
        wide_ref[k, pl.ds(n, lines, stride=4), :] = prod[:, k * 128 : (k + 1) * 128]

    @pl.when(n == tiles - 1)
    def _():
        for k in range(halves):
            packed = wide_ref[k, : members * 8, :].reshape(members, 8, 128)
            out_ref[:, :8, k * 128 : (k + 1) * 128] = packed


def out_product(rows, read, blocks, after):
    members = rows.shape[0]
    tiles = blocks.shape[2] // TILE
    return pl.pallas_call(
        functools.partial(out_kernel, tiles),
        out_shape=jax.ShapeDtypeStruct((members, 16, TILE), jnp.float32),
        grid=(tiles,),
        in_specs=[whole(rows.shape), whole(read.shape), HBM] + [UNREAD] * len(after),
        out_specs=whole((members, 16, TILE)),
        scratch_shapes=[
            pltpu.VMEM((members * STEPS, FEATURES), jnp.bfloat16),
            pltpu.VMEM((TILE // 128, members * 16, 128), jnp.float32),
            pltpu.VMEM((8, TILE), jnp.float32),
            pltpu.VMEM((tiles, FEATURES, TILE), jnp.bfloat16),
            pltpu.SemaphoreType.DMA((tiles,)),
        ],
        compiler_params=kernel_params(),
        cost_estimate=cost(3 * 10**8, 5 * 10**6),
        name="out_product",
    )(rows, read, in_hbm(blocks), *after)


def finish_kernel(parts_ref, main_ref, cont_ref, head_ref, mixed_ref, out_ref, score_ref, wide_ref):
    cols = D // COL_BLOCKS
    for c in range(COL_BLOCKS):
        total = summed_block(parts_ref, c, slice(0, TILE))
        for j in range(cols // TILE):
            at = slice(c * cols + j * TILE, c * cols + (j + 1) * TILE)
            for s in range(STEPS):
                wide_ref[s : s + 1, at] = total[s * 4 + j : s * 4 + j + 1]
    out_ref[...] = (main_ref[...].astype(jnp.float32) + wide_ref[:STEPS, :]).astype(jnp.bfloat16)
    score = jnp.zeros((CTOK, TILE), jnp.float32)
    direct = jnp.zeros((STEPS, TILE), jnp.float32)
    for r in range(ROW_BLOCKS):
        read = parts_ref[r * COL_BLOCKS, 8:, :]
        for c in range(1, COL_BLOCKS):
            read = read + parts_ref[r * COL_BLOCKS + c, 8:, :]
        for j in range(FEATURES // TILE):
            lanes = slice(r * FEATURES + j * TILE, r * FEATURES + (j + 1) * TILE)
            score = score + mixed_ref[:, lanes].astype(jnp.float32) * read[j : j + 1, :]
            for c in range(CONTS):
                direct = direct + cont_ref[c, :, lanes].astype(jnp.float32) * head_ref[:, lanes]
    total = jnp.sum(score, axis=0, keepdims=True) + jnp.sum(direct, axis=0, keepdims=True)
    score_ref[...] = jnp.broadcast_to(jnp.sum(total, axis=1, keepdims=True) / CONTS, (8, 128))


def finish(parts, main, cont, head, mixed):
    return pl.pallas_call(
        finish_kernel,
        out_shape=(
            jax.ShapeDtypeStruct((STEPS, D), jnp.bfloat16),
            jax.ShapeDtypeStruct((8, 128), jnp.float32),
        ),
        in_specs=[whole(parts.shape), whole(main.shape), whole(cont.shape), whole(head.shape), whole(mixed.shape)],
        out_specs=(whole((STEPS, D)), whole((8, 128))),
        scratch_shapes=[pltpu.VMEM((8, D), jnp.float32)],
        compiler_params=kernel_params(),
        cost_estimate=cost(10**6, 2 * 10**6),
        name="finish",
    )(parts, main, cont, head, mixed)


def rope_tables(positions):
    half = HD // 2
    frequency = THETA ** (-(jnp.arange(half, dtype=jnp.float32) * 2.0) / HD)
    angles = positions.astype(jnp.float32)[:, None] * frequency[None, :]
    cosine = jnp.cos(angles)
    sine = jnp.sin(angles)
    return jnp.concatenate([cosine, cosine], axis=1), jnp.concatenate([-sine, sine], axis=1)


def exchange(rows):
    return lax.all_to_all(rows, "tp", split_axis=0, concat_axis=0, tiled=True)


ALONG = [[z * COL_BLOCKS + c for z in range(ROW_BLOCKS)] for c in range(COL_BLOCKS)]


def from_side(rows, dy, dx):
    route = []
    for to in range(MEMBERS):
        z, y, x = to // 8, to // 4 % 2, to % 4
        route.append((z * 8 + (y + dy) % 2 * 4 + (x + dx) % 4, to))
    return lax.ppermute(rows, "tp", route)


def from_along(rows, dz):
    route = [((to + dz * COL_BLOCKS) % MEMBERS, to) for to in range(MEMBERS)]
    return lax.ppermute(rows, "tp", route)


FIRST_HOMES = ((0, 0), (1, 0), (0, 1), (0, 3))
SECOND_HOMES = ((1, 1), (1, 3), (0, 2), (1, 2))
HOMES = FIRST_HOMES + SECOND_HOMES


def project(rows, blocks, bias):
    near = lax.all_to_all(rows, "tp", split_axis=0, concat_axis=0, tiled=True, axis_index_groups=ALONG)
    over = from_side(near, 1, 0)
    after, before = from_side(near, 0, 1), from_side(near, 0, 3)
    over_after, over_before = from_side(over, 0, 1), from_side(over, 0, 3)
    far = [from_side(before, 0, 3), from_side(over_after, 0, 1)]
    *first, main = block_product([near, over, after, before], blocks)
    first = [first[0]] + [from_along(first[k], -k) for k in range(1, ROW_BLOCKS)]
    *second, main = block_product([over_after, over_before] + far, blocks, (main,), HOMES)
    main, first = lax.optimization_barrier((main, first))
    second = [second[0]] + [from_along(second[k], -k) for k in range(1, ROW_BLOCKS)]
    received = []
    for homes, parts in ((FIRST_HOMES, first), (SECOND_HOMES, second)):
        for (dy, dx), summed in zip(homes, sum_parts(bias, parts)):
            received.append(from_side(summed, -dy, -dx) if dy or dx else summed)
    return received, exchange(main), second[1:] + received[1:4]


def on_device(
    main_inputs, cont_inputs, prefix_cache, prefix_len, boundary, rms_gain, qkv_bias, w_qkv, w_out, value_head
):
    main = main_inputs.reshape(STEPS, D)
    cont = cont_inputs.reshape(CONTS, STEPS, D)
    bias = qkv_bias[None, :]
    cache = prefix_cache[0]
    head = value_head[None, :]
    step = jnp.arange(CTOK, dtype=jnp.int32) % STEPS
    main_tables = rope_tables(prefix_len + step[:8])
    cont_tables = rope_tables(prefix_len + boundary + step)
    read = readout(value_head.reshape(COL_BLOCKS, D // COL_BLOCKS), w_out)
    parts, main_parts, before = project(norm_rows(main, cont, rms_gain[None, :]), w_qkv, bias)
    mixed, main_kv = attend_main(prefix_len, bias, *main_tables, cache, main_parts, before)
    mixed = exchange(mixed)
    cont_mixed = attend_cont(prefix_len, boundary, bias, *cont_tables, cache, main_kv, *parts)
    parts = exchange(out_product(mixed, read, w_out, parts[4:]))
    main_out, score = finish(parts, main, cont, head, cont_mixed)
    return main_out[None], score[0, :1]


def solution(mesh):
    return jax.shard_map(
        on_device,
        mesh=mesh,
        in_specs=(
            P(("grp", "tp"), None, None),
            P(("grp", "tp"), None, None, None),
            P(("grp", "tp"), None, None),
            P(("grp", "tp")),
            P(("grp", "tp")),
            P(),
            P(),
            P("tp", None, None),
            P("tp", None, None),
            P(),
        ),
        out_specs=(P(("grp", "tp"), None, None), P(("grp", "tp"))),
        check_vma=False,
    )
```

```python
import functools
import math

import jax
import jax.numpy as jnp
from jax import lax
from jax.experimental import pallas as pl
from jax.experimental.pallas import tpu as pltpu
from jax.sharding import PartitionSpec as P

KVH = 8
HD = 128
D = 8192
QKV = 10240
ROW_BLOCKS = 4
COL_BLOCKS = 8
MEMBERS = ROW_BLOCKS * COL_BLOCKS
FEATURES = D // ROW_BLOCKS
CONTS = 8
STEPS = 2
CTOK = CONTS * STEPS
TILE = 256

THETA = 1000000.0
EPS = 1e-06
MASKED_SCORE = -1e30

VMEM_LIMIT = 32 * 1024 * 1024
VMEM = pl.BlockSpec(memory_space=pltpu.VMEM)
SMEM = pl.BlockSpec(memory_space=pltpu.SMEM)
HBM = pl.BlockSpec(memory_space=pltpu.HBM)
UNREAD = pl.BlockSpec(memory_space=pl.ANY)


def whole(shape):
    return pl.BlockSpec(shape, lambda *_: (0,) * len(shape))


def cost(flops, moved):
    return pl.CostEstimate(flops=flops, bytes_accessed=moved, transcendentals=0)


def in_hbm(array):
    return pltpu.with_memory_space_constraint(array, pltpu.HBM)


def kernel_params():
    return pltpu.CompilerParams(vmem_limit_bytes=VMEM_LIMIT)


def norm_kernel(main_hbm, cont_hbm, gain_hbm, out_ref, main_ref, cont_ref, gain_ref, rows_ref, piece_ref, sems):
    pairs = ((main_hbm, main_ref), (cont_hbm, cont_ref), (gain_hbm, gain_ref))
    copies = [pltpu.make_async_copy(src, dst, sems.at[i]) for i, (src, dst) in enumerate(pairs)]
    for copy in copies:
        copy.start()
    for copy in copies:
        copy.wait()

    def normed(wide):
        inv = lax.rsqrt(jnp.mean(wide * wide, axis=-1, keepdims=True) + EPS)
        return wide * inv * gain_ref[...]

    for c in range(CONTS):
        rows_ref[c * STEPS : (c + 1) * STEPS, :] = cont_ref[c].astype(jnp.float32)
    cont = normed(rows_ref[...]).astype(jnp.bfloat16)
    main = normed(main_ref[...].astype(jnp.float32))
    for r in range(ROW_BLOCKS):
        for j in range(FEATURES // TILE):
            lanes = slice(r * FEATURES + j * TILE, r * FEATURES + (j + 1) * TILE)
            for s in range(STEPS):
                piece_ref[r, s * 8 + j : s * 8 + j + 1, :] = main[s : s + 1, lanes]
    for r in range(ROW_BLOCKS):
        piece = piece_ref[r].astype(jnp.bfloat16)
        out_ref[r, :, :FEATURES] = cont[:, r * FEATURES : (r + 1) * FEATURES]
        out_ref[r, :, FEATURES:] = piece


def norm_rows(main, cont, gain):
    return pl.pallas_call(
        norm_kernel,
        out_shape=jax.ShapeDtypeStruct((ROW_BLOCKS, CTOK, FEATURES + TILE), jnp.bfloat16),
        in_specs=[HBM] * 3,
        out_specs=VMEM,
        scratch_shapes=[
            pltpu.VMEM((STEPS, D), jnp.bfloat16),
            pltpu.VMEM((CONTS, STEPS, D), jnp.bfloat16),
            pltpu.VMEM((1, D), jnp.float32),
            pltpu.VMEM((CTOK, D), jnp.float32),
            pltpu.VMEM((ROW_BLOCKS, 16, TILE), jnp.float32),
            pltpu.SemaphoreType.DMA((3,)),
        ],
        compiler_params=kernel_params(),
        cost_estimate=cost(10**6, 4 * 10**6),
        name="norm_rows",
    )(in_hbm(main), in_hbm(cont), in_hbm(gain))


def weight_tile(n, tiles, w_hbm, w_ref, sems):
    def copy(i):
        lanes = pl.ds(pl.multiple_of(i * TILE, TILE), TILE)
        return pltpu.make_async_copy(w_hbm.at[0, :, lanes], w_ref.at[i], sems.at[i])

    @pl.when(n == 0)
    def _():
        for i in range(tiles):
            copy(i).start()

    return copy(n)


REST = 768


def rest_tile(block):
    return jnp.where(block == 6, 2, 0)


def plane_place():
    column = lax.rem(lax.axis_index("tp"), COL_BLOCKS)
    return column // 4, lax.rem(column, 4)


def product_kernel(tiles, counts, places, unread, *refs):
    x_refs, refs = refs[: len(counts)], refs[len(counts) :]
    if places:
        earlier_ref, refs = refs[0], refs[1:]
    w_hbm, refs = refs[0], refs[1 + unread :]
    out_refs = refs[:ROW_BLOCKS]
    main_ref, rows_ref, wide_ref, w_ref, sems, part_ref = refs[ROW_BLOCKS:]
    n = pl.program_id(0)
    members = sum(counts)
    count = members * CTOK
    lines = members * STEPS
    halves = TILE // 128
    width = tiles * TILE
    tile = weight_tile(n, tiles, w_hbm, w_ref, sems)

    @pl.when(n == 0)
    def _():
        at = 0
        for x_ref, size in zip(x_refs, counts):
            rows = slice(at * CTOK, (at + size) * CTOK)
            rows_ref[rows, :] = x_ref[:, :, :FEATURES].reshape(size * CTOK, FEATURES)
            packed = x_ref[:, :, FEATURES:].reshape(size * CTOK, TILE).astype(jnp.float32)
            for k in range(halves):
                wide_ref[k, rows, :] = packed[:, k * 128 : (k + 1) * 128]
            at += size
        for k in range(halves):
            for j in range(FEATURES // TILE):
                lane = j * TILE + k * 128
                rows_ref[count:, lane : lane + 128] = wide_ref[k, pl.ds(j, lines, stride=8), :].astype(jnp.bfloat16)

    tile.wait()
    prod = jnp.dot(rows_ref[...], w_ref[n], preferred_element_type=jnp.float32)
    high = prod.astype(jnp.bfloat16)
    part_ref[:, :, pl.ds(pl.multiple_of(n * TILE, TILE), TILE)] = high[:count].reshape(members, CTOK, TILE)
    for k in range(halves):
        wide_ref[k, pl.ds(n, lines, stride=8), :] = prod[count:, k * 128 : (k + 1) * 128]
    start = rest_tile(lax.rem(lax.axis_index("tp"), COL_BLOCKS))

    @pl.when((n >= start) & (n < start + REST // TILE))
    def _():
        low = prod - high.astype(jnp.float32)
        place = n - start
        lane = pl.multiple_of(width + place * TILE, TILE)
        part_ref[:, :, pl.ds(lane, TILE)] = low[:count].astype(jnp.bfloat16).reshape(members, CTOK, TILE)
        for k in range(halves):
            wide_ref[k, pl.ds(tiles + place, lines, stride=8), :] = low[count:, k * 128 : (k + 1) * 128]

    @pl.when(n == tiles - 1)
    def _():
        z = lax.axis_index("tp") // COL_BLOCKS
        done = earlier_ref.shape[0] // ROW_BLOCKS if places else 0
        for k in range(halves):
            lanes = slice(k * 128, (k + 1) * 128)
            packed = wide_ref[k].astype(jnp.bfloat16).reshape(members, CTOK, 128)
            if not places:
                main_ref[:, :, lanes] = packed
            for i, (dy, dx) in enumerate(places):
                y, x = plane_place()
                column = lax.rem(y + dy, 2) * 4 + lax.rem(x + dx, 4)
                for r in range(ROW_BLOCKS):
                    if i < done:
                        message = earlier_ref[i * ROW_BLOCKS + r, :, lanes]
                    else:
                        message = packed[(i - done) * ROW_BLOCKS + r]
                    main_ref[r * COL_BLOCKS + column, :, lanes] = message
        for k, out_ref in enumerate(out_refs):
            to = lax.rem(z + k, ROW_BLOCKS)
            for g in range(members // ROW_BLOCKS):
                out_ref[g] = part_ref[g * ROW_BLOCKS + to]


def block_product(messages, blocks, earlier=(), places=(), after=()):
    tiles = blocks.shape[2] // TILE
    lanes = tiles * TILE + REST
    counts = tuple(rows.shape[0] for rows in messages)
    members = sum(counts)
    return pl.pallas_call(
        functools.partial(product_kernel, tiles, counts, places, len(after)),
        out_shape=[jax.ShapeDtypeStruct((members // ROW_BLOCKS, CTOK, lanes), jnp.bfloat16)] * ROW_BLOCKS
        + [jax.ShapeDtypeStruct((MEMBERS if places else members, CTOK, TILE), jnp.bfloat16)],
        grid=(tiles,),
        in_specs=[VMEM] * (len(counts) + len(earlier)) + [HBM] + [UNREAD] * len(after),
        out_specs=[VMEM] * (1 + ROW_BLOCKS),
        scratch_shapes=[
            pltpu.VMEM((members * (CTOK + STEPS), FEATURES), jnp.bfloat16),
            pltpu.VMEM((TILE // 128, members * CTOK, 128), jnp.float32),
            pltpu.VMEM((tiles, FEATURES, TILE), jnp.bfloat16),
            pltpu.SemaphoreType.DMA((tiles,)),
            pltpu.VMEM((members, CTOK, lanes), jnp.bfloat16),
        ],
        compiler_params=kernel_params(),
        cost_estimate=cost(2 * members * (CTOK + STEPS) * FEATURES * tiles * TILE, 12 * 10**6),
        name="block_product",
    )(*messages, *earlier, in_hbm(blocks), *after)


def sum_kernel(bias_ref, *refs):
    part_refs, out_refs = refs[:ROW_BLOCKS], refs[ROW_BLOCKS:]
    column = lax.rem(lax.axis_index("tp"), COL_BLOCKS)
    late = column == 6
    last = (column == COL_BLOCKS - 1).astype(jnp.float32)
    cols = QKV // COL_BLOCKS
    tiles = cols // TILE
    kept = REST // TILE
    zero = jnp.zeros((CTOK, TILE), jnp.float32)

    def value_bias(j):
        if j == 0:
            return jnp.zeros((1, TILE), jnp.float32)
        at = QKV - cols + j * TILE
        return bias_ref[:, at : at + TILE] * last

    for g, out_ref in enumerate(out_refs):

        def total(lane):
            value = part_refs[0][g, :, lane : lane + TILE].astype(jnp.float32)
            for ref in part_refs[1:]:
                value = value + ref[g, :, lane : lane + TILE].astype(jnp.float32)
            return value

        rest = [total(cols + i * TILE) for i in range(kept)] + [zero] * (tiles - kept)
        lows = []
        for j in range(tiles):
            shifted = rest[j - tiles + kept] if j >= tiles - kept else zero
            value = total(j * TILE) + jnp.where(late, shifted, rest[j]) + value_bias(j)
            high = value.astype(jnp.bfloat16)
            out_ref[:, j * TILE : (j + 1) * TILE] = high
            lows.append(value - high.astype(jnp.float32))
        for i in range(kept):
            low = jnp.where(late, lows[i + tiles - kept], lows[i])
            out_ref[:, cols + i * TILE : cols + (i + 1) * TILE] = low.astype(jnp.bfloat16)


def sum_parts(bias, parts):
    groups, rows, lanes = parts[0].shape
    return pl.pallas_call(
        sum_kernel,
        out_shape=[jax.ShapeDtypeStruct((rows, lanes), jnp.bfloat16)] * groups,
        in_specs=[VMEM] * (1 + len(parts)),
        out_specs=[VMEM] * groups,
        compiler_params=kernel_params(),
        cost_estimate=cost(10**6, 3 * 10**6),
        name="sum_parts",
    )(bias, *parts)


def load_parts(part_refs, parts_ref):
    y, x = plane_place()
    for ref, (dy, dx) in zip(part_refs, HOMES):
        column = lax.rem(y + dy, 2) * 4 + lax.rem(x + 4 - dx, 4)
        parts_ref[column] = ref[...]


def summed_block(parts_ref, c, lanes):
    total = parts_ref[c, :, lanes].astype(jnp.float32)
    for r in range(1, ROW_BLOCKS):
        total = total + parts_ref[r * COL_BLOCKS + c, :, lanes].astype(jnp.float32)
    return total


def head_attention(query, key, value, fresh_key, fresh_value, seen, fresh_seen):
    inv_root = 1.0 / math.sqrt(HD)
    contract = (((1,), (1,)), ((), ()))
    old = lax.dot_general(query, key, contract, preferred_element_type=jnp.float32) * inv_root
    new = lax.dot_general(query, fresh_key, contract, preferred_element_type=jnp.float32) * inv_root
    old = jnp.where(seen, old, MASKED_SCORE)
    new = jnp.where(fresh_seen, new, MASKED_SCORE)
    highest = jnp.maximum(jnp.max(old, axis=-1, keepdims=True), jnp.max(new, axis=-1, keepdims=True))
    old = jnp.exp(old - highest)
    new = jnp.exp(new - highest)
    mass = jnp.sum(old, axis=-1, keepdims=True) + jnp.sum(new, axis=-1, keepdims=True)
    inv_mass = 1.0 / mass
    mixed = jnp.dot((old * inv_mass).astype(jnp.bfloat16), value, preferred_element_type=jnp.float32)
    return mixed + jnp.dot((new * inv_mass).astype(jnp.bfloat16), fresh_value, preferred_element_type=jnp.float32)


def load_qkv(main, parts_ref, qkv_ref):
    cols = QKV // COL_BLOCKS
    for c in range(COL_BLOCKS):
        first = 2 if c == 6 else 0
        total = summed_block(parts_ref, c, slice(0, TILE)) if main else parts_ref[c].astype(jnp.float32)
        for j in range(cols // TILE):
            lanes = slice(c * cols + j * TILE, c * cols + (j + 1) * TILE)
            rest = j - first
            has_rest = 0 <= rest < REST // TILE
            if main:
                for s in range(STEPS):
                    line = total[s * 8 + j : s * 8 + j + 1]
                    if has_rest:
                        at = s * 8 + cols // TILE + rest
                        line = line + total[at : at + 1]
                    qkv_ref[s : s + 1, lanes] = line
            else:
                value = total[:, j * TILE : (j + 1) * TILE]
                if has_rest:
                    value = value + total[:, cols + rest * TILE : cols + (rest + 1) * TILE]
                qkv_ref[:, lanes] = value


def head_readers(qkv_ref, bias_ref, cos_ref, sin_ref):
    cosine = cos_ref[...]
    sine = sin_ref[...]

    def plain(start):
        return qkv_ref[:, start : start + HD]

    def rotated(start):
        head = plain(start) + bias_ref[:, start : start + HD]
        return head * cosine + pltpu.roll(head, HD // 2, 1) * sine

    return plain, rotated


def fresh_block(pieces):
    rows = sum(piece.shape[0] for piece in pieces)
    pad = jnp.zeros((128 - rows, HD), jnp.float32)
    return jnp.concatenate(list(pieces) + [pad], axis=0).astype(jnp.bfloat16)


GROUP = D // HD // KVH
KV_WIDTH = KVH * HD


def attend_main_kernel(
    len_ref, bias_ref, cos_ref, sin_ref, cache_ref, parts_ref, *refs
):
    out_ref, kv_ref, qkv_ref, piece_ref = refs[-4:]
    rows = qkv_ref.shape[0]
    qkv_ref[...] = jnp.zeros(qkv_ref.shape, jnp.float32)
    load_qkv(True, parts_ref, qkv_ref)
    qkv_ref[:, D + KV_WIDTH :] = qkv_ref[:, D + KV_WIDTH :] + bias_ref[:, D + KV_WIDTH :]
    plain, rotated = head_readers(qkv_ref, bias_ref, cos_ref, sin_ref)
    seen = lax.broadcasted_iota(jnp.int32, (1, cache_ref.shape[0]), 1) < len_ref[0]
    row = lax.broadcasted_iota(jnp.int32, (rows, 128), 0)
    col = lax.broadcasted_iota(jnp.int32, (rows, 128), 1)
    own = ((col <= row) & (col < STEPS)).astype(jnp.int32)
    fresh_seen = jnp.concatenate([own] * GROUP, axis=0) > 0
    for g in range(KVH):
        query = jnp.concatenate([rotated((g * GROUP + h) * HD) for h in range(GROUP)], axis=0).astype(jnp.bfloat16)
        fresh_key = rotated(D + g * HD)
        fresh_value = plain(D + KV_WIDTH + g * HD)
        kv_ref[:, g * HD : (g + 1) * HD] = fresh_key
        kv_ref[:, KV_WIDTH + g * HD : KV_WIDTH + (g + 1) * HD] = fresh_value
        key = cache_ref[:, g * HD : (g + 1) * HD]
        value = cache_ref[:, KV_WIDTH + g * HD : KV_WIDTH + (g + 1) * HD]
        mixed = head_attention(
            query, key, value, fresh_block([fresh_key]), fresh_block([fresh_value]), seen, fresh_seen
        )
        for h in range(GROUP):
            r, place = divmod(g * GROUP + h, FEATURES // HD)
            j, lane = place // 2, (place % 2) * HD
            for s in range(STEPS):
                at = s * 8 + j
                piece_ref[r, at : at + 1, lane : lane + HD] = mixed[h * rows + s : h * rows + s + 1]
    for r in range(ROW_BLOCKS):
        piece = piece_ref[r].astype(jnp.bfloat16)
        for c in range(COL_BLOCKS):
            out_ref[r * COL_BLOCKS + c] = piece


def attend_main(prefix_len, bias, cosine, sine, cache, parts, after):
    return pl.pallas_call(
        attend_main_kernel,
        out_shape=(
            jax.ShapeDtypeStruct((32, 16, TILE), jnp.bfloat16),
            jax.ShapeDtypeStruct((8, 2 * KV_WIDTH), jnp.float32),
        ),
        in_specs=[SMEM] + [VMEM] * 5 + [UNREAD] * len(after),
        out_specs=(whole((32, 16, TILE)), whole((8, 2 * KV_WIDTH))),
        scratch_shapes=[
            pltpu.VMEM((8, QKV), jnp.float32),
            pltpu.VMEM((ROW_BLOCKS, 16, TILE), jnp.float32),
        ],
        compiler_params=kernel_params(),
        cost_estimate=cost(2 * 10**8, 6 * 10**6),
        name="attend_main",
    )(prefix_len, bias, cosine, sine, cache, parts, *after)


def attend_cont_kernel(len_ref, bound_ref, bias_ref, cos_ref, sin_ref, cache_ref, kv_ref, *refs):
    part_refs = refs[:COL_BLOCKS]
    out_ref, qkv_ref, parts_ref = refs[COL_BLOCKS:]
    load_parts(part_refs, parts_ref)
    rows = qkv_ref.shape[0]
    load_qkv(False, parts_ref, qkv_ref)
    plain, rotated = head_readers(qkv_ref, bias_ref, cos_ref, sin_ref)
    seen = lax.broadcasted_iota(jnp.int32, (1, cache_ref.shape[0]), 1) < len_ref[0]
    row = lax.broadcasted_iota(jnp.int32, (rows, 128), 0)
    col = lax.broadcasted_iota(jnp.int32, (rows, 128), 1)
    own = (row // STEPS == col // STEPS) & (col <= row)
    main = (col >= rows) & (col < rows + bound_ref[0])
    fresh_seen = jnp.concatenate([(own | main).astype(jnp.int32)] * GROUP, axis=0) > 0
    for g in range(KVH):
        query = jnp.concatenate([rotated((g * GROUP + h) * HD) for h in range(GROUP)], axis=0).astype(jnp.bfloat16)
        at_key = slice(g * HD, (g + 1) * HD)
        at_value = slice(KV_WIDTH + g * HD, KV_WIDTH + (g + 1) * HD)
        fresh_key = fresh_block([rotated(D + g * HD), kv_ref[:, at_key]])
        fresh_value = fresh_block([plain(D + KV_WIDTH + g * HD), kv_ref[:, at_value]])
        mixed = head_attention(
            query, cache_ref[:, at_key], cache_ref[:, at_value], fresh_key, fresh_value, seen, fresh_seen
        )
        mixed = mixed.astype(jnp.bfloat16)
        for h in range(GROUP):
            out_ref[:, (g * GROUP + h) * HD : (g * GROUP + h + 1) * HD] = mixed[h * rows : (h + 1) * rows]


def attend_cont(*args):
    return pl.pallas_call(
        attend_cont_kernel,
        out_shape=jax.ShapeDtypeStruct((CTOK, D), jnp.bfloat16),
        in_specs=[SMEM, SMEM] + [VMEM] * 4 + [whole((8, 2 * KV_WIDTH))] + [VMEM] * COL_BLOCKS,
        out_specs=whole((CTOK, D)),
        scratch_shapes=[
            pltpu.VMEM((CTOK, QKV), jnp.float32),
            pltpu.VMEM((COL_BLOCKS,) + args[-1].shape, jnp.bfloat16),
        ],
        compiler_params=kernel_params(),
        cost_estimate=cost(4 * 10**8, 8 * 10**6),
        name="attend_cont",
    )(*args)


def readout_kernel(head_ref, w_hbm, out_ref, w_ref, sem):
    copy = pltpu.make_async_copy(w_hbm.at[0], w_ref, sem)
    copy.start()
    row = head_ref[pl.ds(lax.rem(lax.axis_index("tp"), COL_BLOCKS), 1), :]
    high = row.astype(jnp.bfloat16).astype(jnp.float32)
    middle = (row - high).astype(jnp.bfloat16).astype(jnp.float32)
    low = row - high - middle
    pieces = jnp.concatenate([high, middle, low, jnp.zeros((13, row.shape[1]), jnp.float32)], axis=0)
    copy.wait()
    prod = lax.dot_general(
        pieces.astype(jnp.bfloat16), w_ref[...], (((1,), (1,)), ((), ())), preferred_element_type=jnp.float32
    )
    out_ref[...] = prod[0:1] + prod[1:2] + prod[2:3]


def readout(value_head, blocks):
    return pl.pallas_call(
        readout_kernel,
        out_shape=jax.ShapeDtypeStruct((1, FEATURES), jnp.float32),
        in_specs=[whole(value_head.shape), HBM],
        out_specs=whole((1, FEATURES)),
        scratch_shapes=[pltpu.VMEM((FEATURES, D // COL_BLOCKS), jnp.bfloat16), pltpu.SemaphoreType.DMA],
        compiler_params=kernel_params(),
        cost_estimate=cost(2 * 10**8, 5 * 10**6),
        name="readout",
    )(value_head, in_hbm(blocks))


def out_kernel(tiles, x_ref, read_ref, w_hbm, *refs):
    out_ref, rows_ref, wide_ref, read8_ref, w_ref, sems = refs[-6:]
    n = pl.program_id(0)
    members = x_ref.shape[0]
    lines = members * STEPS
    halves = TILE // 128
    tile = weight_tile(n, tiles, w_hbm, w_ref, sems)

    @pl.when(n == 0)
    def _():
        for j in range(FEATURES // TILE):
            read8_ref[j : j + 1, :] = read_ref[:, j * TILE : (j + 1) * TILE]
        out_ref[:, 8:, :] = jnp.broadcast_to(read8_ref[...][None], (members, 8, TILE))
        packed = x_ref[...].reshape(members * 16, TILE).astype(jnp.float32)
        for k in range(halves):
            wide_ref[k] = packed[:, k * 128 : (k + 1) * 128]
            for j in range(FEATURES // TILE):
                lane = j * TILE + k * 128
                rows_ref[:, lane : lane + 128] = wide_ref[k, pl.ds(j, lines, stride=8), :].astype(jnp.bfloat16)

    tile.wait()
    prod = jnp.dot(rows_ref[...], w_ref[n], preferred_element_type=jnp.float32)
    for k in range(halves):
        wide_ref[k, pl.ds(n, lines, stride=4), :] = prod[:, k * 128 : (k + 1) * 128]

    @pl.when(n == tiles - 1)
    def _():
        for k in range(halves):
            packed = wide_ref[k, : members * 8, :].reshape(members, 8, 128)
            out_ref[:, :8, k * 128 : (k + 1) * 128] = packed


def out_product(rows, read, blocks, after):
    members = rows.shape[0]
    tiles = blocks.shape[2] // TILE
    return pl.pallas_call(
        functools.partial(out_kernel, tiles),
        out_shape=jax.ShapeDtypeStruct((members, 16, TILE), jnp.float32),
        grid=(tiles,),
        in_specs=[whole(rows.shape), whole(read.shape), HBM] + [UNREAD] * len(after),
        out_specs=whole((members, 16, TILE)),
        scratch_shapes=[
            pltpu.VMEM((members * STEPS, FEATURES), jnp.bfloat16),
            pltpu.VMEM((TILE // 128, members * 16, 128), jnp.float32),
            pltpu.VMEM((8, TILE), jnp.float32),
            pltpu.VMEM((tiles, FEATURES, TILE), jnp.bfloat16),
            pltpu.SemaphoreType.DMA((tiles,)),
        ],
        compiler_params=kernel_params(),
        cost_estimate=cost(3 * 10**8, 5 * 10**6),
        name="out_product",
    )(rows, read, in_hbm(blocks), *after)


def finish_kernel(parts_ref, main_ref, cont_ref, head_ref, mixed_ref, out_ref, score_ref, wide_ref):
    cols = D // COL_BLOCKS
    for c in range(COL_BLOCKS):
        total = summed_block(parts_ref, c, slice(0, TILE))
        for j in range(cols // TILE):
            at = slice(c * cols + j * TILE, c * cols + (j + 1) * TILE)
            for s in range(STEPS):
                wide_ref[s : s + 1, at] = total[s * 4 + j : s * 4 + j + 1]
    out_ref[...] = (main_ref[...].astype(jnp.float32) + wide_ref[:STEPS, :]).astype(jnp.bfloat16)
    score = jnp.zeros((CTOK, TILE), jnp.float32)
    direct = jnp.zeros((STEPS, TILE), jnp.float32)
    for r in range(ROW_BLOCKS):
        read = parts_ref[r * COL_BLOCKS, 8:, :]
        for c in range(1, COL_BLOCKS):
            read = read + parts_ref[r * COL_BLOCKS + c, 8:, :]
        for j in range(FEATURES // TILE):
            lanes = slice(r * FEATURES + j * TILE, r * FEATURES + (j + 1) * TILE)
            score = score + mixed_ref[:, lanes].astype(jnp.float32) * read[j : j + 1, :]
            for c in range(CONTS):
                direct = direct + cont_ref[c, :, lanes].astype(jnp.float32) * head_ref[:, lanes]
    total = jnp.sum(score, axis=0, keepdims=True) + jnp.sum(direct, axis=0, keepdims=True)
    score_ref[...] = jnp.broadcast_to(jnp.sum(total, axis=1, keepdims=True) / CONTS, (8, 128))


def finish(parts, main, cont, head, mixed):
    return pl.pallas_call(
        finish_kernel,
        out_shape=(
            jax.ShapeDtypeStruct((STEPS, D), jnp.bfloat16),
            jax.ShapeDtypeStruct((8, 128), jnp.float32),
        ),
        in_specs=[whole(parts.shape), whole(main.shape), whole(cont.shape), whole(head.shape), whole(mixed.shape)],
        out_specs=(whole((STEPS, D)), whole((8, 128))),
        scratch_shapes=[pltpu.VMEM((8, D), jnp.float32)],
        compiler_params=kernel_params(),
        cost_estimate=cost(10**6, 2 * 10**6),
        name="finish",
    )(parts, main, cont, head, mixed)


def rope_tables(positions):
    half = HD // 2
    frequency = THETA ** (-(jnp.arange(half, dtype=jnp.float32) * 2.0) / HD)
    angles = positions.astype(jnp.float32)[:, None] * frequency[None, :]
    cosine = jnp.cos(angles)
    sine = jnp.sin(angles)
    return jnp.concatenate([cosine, cosine], axis=1), jnp.concatenate([-sine, sine], axis=1)


def exchange(rows):
    return lax.all_to_all(rows, "tp", split_axis=0, concat_axis=0, tiled=True)


ALONG = [[z * COL_BLOCKS + c for z in range(ROW_BLOCKS)] for c in range(COL_BLOCKS)]


def from_side(rows, dy, dx):
    route = []
    for to in range(MEMBERS):
        z, y, x = to // 8, to // 4 % 2, to % 4
        route.append((z * 8 + (y + dy) % 2 * 4 + (x + dx) % 4, to))
    return lax.ppermute(rows, "tp", route)


def from_along(rows, dz):
    route = [((to + dz * COL_BLOCKS) % MEMBERS, to) for to in range(MEMBERS)]
    return lax.ppermute(rows, "tp", route)


FIRST_HOMES = ((0, 0), (1, 0), (0, 1), (0, 3))
SECOND_HOMES = ((1, 1), (1, 3), (0, 2), (1, 2))
HOMES = FIRST_HOMES + SECOND_HOMES


def project(rows, blocks, bias, read):
    near = lax.all_to_all(rows, "tp", split_axis=0, concat_axis=0, tiled=True, axis_index_groups=ALONG)
    over = from_side(near, 1, 0)
    after, before = from_side(near, 0, 1), from_side(near, 0, 3)
    over_after, over_before = from_side(over, 0, 1), from_side(over, 0, 3)
    far = [from_side(before, 0, 3), from_side(over_after, 0, 1)]
    *first, main = block_product([near, over, after, before], blocks)
    first = [first[0]] + [from_along(first[k], -k) for k in range(1, ROW_BLOCKS)]
    *second, main = block_product([over_after, over_before] + far, blocks, (main,), HOMES, (read,))
    main, first = lax.optimization_barrier((main, first))
    second = [second[0]] + [from_along(second[k], -k) for k in range(1, ROW_BLOCKS)]
    received = []
    for homes, parts in ((FIRST_HOMES, first), (SECOND_HOMES, second)):
        for (dy, dx), summed in zip(homes, sum_parts(bias, parts)):
            received.append(from_side(summed, -dy, -dx) if dy or dx else summed)
    return received, exchange(main), second[1:] + received[1:4]


def on_device(
    main_inputs, cont_inputs, prefix_cache, prefix_len, boundary, rms_gain, qkv_bias, w_qkv, w_out, value_head
):
    main = main_inputs.reshape(STEPS, D)
    cont = cont_inputs.reshape(CONTS, STEPS, D)
    bias = qkv_bias[None, :]
    cache = prefix_cache[0]
    head = value_head[None, :]
    step = jnp.arange(CTOK, dtype=jnp.int32) % STEPS
    main_tables = rope_tables(prefix_len + step[:8])
    cont_tables = rope_tables(prefix_len + boundary + step)
    read = readout(value_head.reshape(COL_BLOCKS, D // COL_BLOCKS), w_out)
    parts, main_parts, before = project(norm_rows(main, cont, rms_gain[None, :]), w_qkv, bias, read)
    mixed, main_kv = attend_main(prefix_len, bias, *main_tables, cache, main_parts, before)
    mixed = exchange(mixed)
    cont_mixed = attend_cont(prefix_len, boundary, bias, *cont_tables, cache, main_kv, *parts)
    parts = exchange(out_product(mixed, read, w_out, parts[4:]))
    main_out, score = finish(parts, main, cont, head, cont_mixed)
    return main_out[None], score[0, :1]


def solution(mesh):
    return jax.shard_map(
        on_device,
        mesh=mesh,
        in_specs=(
            P(("grp", "tp"), None, None),
            P(("grp", "tp"), None, None, None),
            P(("grp", "tp"), None, None),
            P(("grp", "tp")),
            P(("grp", "tp")),
            P(),
            P(),
            P("tp", None, None),
            P("tp", None, None),
            P(),
        ),
        out_specs=(P(("grp", "tp"), None, None), P(("grp", "tp"))),
        check_vma=False,
    )
```

```python
import functools
import math

import jax
import jax.numpy as jnp
from jax import lax
from jax.experimental import pallas as pl
from jax.experimental.pallas import tpu as pltpu
from jax.sharding import PartitionSpec as P

KVH = 8
HD = 128
D = 8192
QKV = 10240
ROW_BLOCKS = 4
COL_BLOCKS = 8
MEMBERS = ROW_BLOCKS * COL_BLOCKS
FEATURES = D // ROW_BLOCKS
CONTS = 8
STEPS = 2
CTOK = CONTS * STEPS
TILE = 256

THETA = 1000000.0
EPS = 1e-06
MASKED_SCORE = -1e30

VMEM_LIMIT = 32 * 1024 * 1024
VMEM = pl.BlockSpec(memory_space=pltpu.VMEM)
SMEM = pl.BlockSpec(memory_space=pltpu.SMEM)
HBM = pl.BlockSpec(memory_space=pltpu.HBM)
UNREAD = pl.BlockSpec(memory_space=pl.ANY)


def whole(shape):
    return pl.BlockSpec(shape, lambda *_: (0,) * len(shape))


def cost(flops, moved):
    return pl.CostEstimate(flops=flops, bytes_accessed=moved, transcendentals=0)


def in_hbm(array):
    return pltpu.with_memory_space_constraint(array, pltpu.HBM)


def kernel_params():
    return pltpu.CompilerParams(vmem_limit_bytes=VMEM_LIMIT)


def norm_kernel(main_hbm, cont_hbm, gain_hbm, out_ref, main_ref, cont_ref, gain_ref, rows_ref, piece_ref, sems):
    pairs = ((main_hbm, main_ref), (cont_hbm, cont_ref), (gain_hbm, gain_ref))
    copies = [pltpu.make_async_copy(src, dst, sems.at[i]) for i, (src, dst) in enumerate(pairs)]
    for copy in copies:
        copy.start()
    for copy in copies:
        copy.wait()

    def normed(wide):
        inv = lax.rsqrt(jnp.mean(wide * wide, axis=-1, keepdims=True) + EPS)
        return wide * inv * gain_ref[...]

    for c in range(CONTS):
        rows_ref[c * STEPS : (c + 1) * STEPS, :] = cont_ref[c].astype(jnp.float32)
    cont = normed(rows_ref[...]).astype(jnp.bfloat16)
    main = normed(main_ref[...].astype(jnp.float32))
    for r in range(ROW_BLOCKS):
        for j in range(FEATURES // TILE):
            lanes = slice(r * FEATURES + j * TILE, r * FEATURES + (j + 1) * TILE)
            for s in range(STEPS):
                piece_ref[r, s * 8 + j : s * 8 + j + 1, :] = main[s : s + 1, lanes]
    for r in range(ROW_BLOCKS):
        piece = piece_ref[r].astype(jnp.bfloat16)
        out_ref[r, :, :FEATURES] = cont[:, r * FEATURES : (r + 1) * FEATURES]
        out_ref[r, :, FEATURES:] = piece


def norm_rows(main, cont, gain):
    return pl.pallas_call(
        norm_kernel,
        out_shape=jax.ShapeDtypeStruct((ROW_BLOCKS, CTOK, FEATURES + TILE), jnp.bfloat16),
        in_specs=[HBM] * 3,
        out_specs=VMEM,
        scratch_shapes=[
            pltpu.VMEM((STEPS, D), jnp.bfloat16),
            pltpu.VMEM((CONTS, STEPS, D), jnp.bfloat16),
            pltpu.VMEM((1, D), jnp.float32),
            pltpu.VMEM((CTOK, D), jnp.float32),
            pltpu.VMEM((ROW_BLOCKS, 16, TILE), jnp.float32),
            pltpu.SemaphoreType.DMA((3,)),
        ],
        compiler_params=kernel_params(),
        cost_estimate=cost(10**6, 4 * 10**6),
        name="norm_rows",
    )(in_hbm(main), in_hbm(cont), in_hbm(gain))


def weight_tile(n, tiles, w_hbm, w_ref, sems):
    def copy(i):
        lanes = pl.ds(pl.multiple_of(i * TILE, TILE), TILE)
        return pltpu.make_async_copy(w_hbm.at[0, :, lanes], w_ref.at[i], sems.at[i])

    @pl.when(n == 0)
    def _():
        for i in range(tiles):
            copy(i).start()

    return copy(n)


REST = 768


def rest_tile(block):
    return jnp.where(block == 6, 2, 0)


def plane_place():
    column = lax.rem(lax.axis_index("tp"), COL_BLOCKS)
    return column // 4, lax.rem(column, 4)


def product_kernel(tiles, counts, places, *refs):
    x_refs, refs = refs[: len(counts)], refs[len(counts) :]
    if places:
        earlier_ref, refs = refs[0], refs[1:]
    w_hbm, *out_refs = refs[: 1 + ROW_BLOCKS]
    main_ref, rows_ref, wide_ref, w_ref, sems, part_ref = refs[1 + ROW_BLOCKS :]
    n = pl.program_id(0)
    members = sum(counts)
    count = members * CTOK
    lines = members * STEPS
    halves = TILE // 128
    width = tiles * TILE
    tile = weight_tile(n, tiles, w_hbm, w_ref, sems)

    @pl.when(n == 0)
    def _():
        at = 0
        for x_ref, size in zip(x_refs, counts):
            rows = slice(at * CTOK, (at + size) * CTOK)
            rows_ref[rows, :] = x_ref[:, :, :FEATURES].reshape(size * CTOK, FEATURES)
            packed = x_ref[:, :, FEATURES:].reshape(size * CTOK, TILE).astype(jnp.float32)
            for k in range(halves):
                wide_ref[k, rows, :] = packed[:, k * 128 : (k + 1) * 128]
            at += size
        for k in range(halves):
            for j in range(FEATURES // TILE):
                lane = j * TILE + k * 128
                rows_ref[count:, lane : lane + 128] = wide_ref[k, pl.ds(j, lines, stride=8), :].astype(jnp.bfloat16)

    tile.wait()
    prod = jnp.dot(rows_ref[...], w_ref[n], preferred_element_type=jnp.float32)
    high = prod.astype(jnp.bfloat16)
    part_ref[:, :, pl.ds(pl.multiple_of(n * TILE, TILE), TILE)] = high[:count].reshape(members, CTOK, TILE)
    for k in range(halves):
        wide_ref[k, pl.ds(n, lines, stride=8), :] = prod[count:, k * 128 : (k + 1) * 128]
    start = rest_tile(lax.rem(lax.axis_index("tp"), COL_BLOCKS))

    @pl.when((n >= start) & (n < start + REST // TILE))
    def _():
        low = prod - high.astype(jnp.float32)
        place = n - start
        lane = pl.multiple_of(width + place * TILE, TILE)
        part_ref[:, :, pl.ds(lane, TILE)] = low[:count].astype(jnp.bfloat16).reshape(members, CTOK, TILE)
        for k in range(halves):
            wide_ref[k, pl.ds(tiles + place, lines, stride=8), :] = low[count:, k * 128 : (k + 1) * 128]

    @pl.when(n == tiles - 1)
    def _():
        z = lax.axis_index("tp") // COL_BLOCKS
        done = earlier_ref.shape[0] // ROW_BLOCKS if places else 0
        for k in range(halves):
            lanes = slice(k * 128, (k + 1) * 128)
            packed = wide_ref[k].astype(jnp.bfloat16).reshape(members, CTOK, 128)
            if not places:
                main_ref[:, :, lanes] = packed
            for i, (dy, dx) in enumerate(places):
                y, x = plane_place()
                column = lax.rem(y + dy, 2) * 4 + lax.rem(x + dx, 4)
                for r in range(ROW_BLOCKS):
                    if i < done:
                        message = earlier_ref[i * ROW_BLOCKS + r, :, lanes]
                    else:
                        message = packed[(i - done) * ROW_BLOCKS + r]
                    main_ref[r * COL_BLOCKS + column, :, lanes] = message
        for k, out_ref in enumerate(out_refs):
            to = lax.rem(z + k, ROW_BLOCKS)
            for g in range(members // ROW_BLOCKS):
                out_ref[g] = part_ref[g * ROW_BLOCKS + to]


def block_product(messages, blocks, earlier=(), places=()):
    tiles = blocks.shape[2] // TILE
    lanes = tiles * TILE + REST
    counts = tuple(rows.shape[0] for rows in messages)
    members = sum(counts)
    return pl.pallas_call(
        functools.partial(product_kernel, tiles, counts, places),
        out_shape=[jax.ShapeDtypeStruct((members // ROW_BLOCKS, CTOK, lanes), jnp.bfloat16)] * ROW_BLOCKS
        + [jax.ShapeDtypeStruct((MEMBERS if places else members, CTOK, TILE), jnp.bfloat16)],
        grid=(tiles,),
        in_specs=[VMEM] * (len(counts) + len(earlier)) + [HBM],
        out_specs=[VMEM] * (1 + ROW_BLOCKS),
        scratch_shapes=[
            pltpu.VMEM((members * (CTOK + STEPS), FEATURES), jnp.bfloat16),
            pltpu.VMEM((TILE // 128, members * CTOK, 128), jnp.float32),
            pltpu.VMEM((tiles, FEATURES, TILE), jnp.bfloat16),
            pltpu.SemaphoreType.DMA((tiles,)),
            pltpu.VMEM((members, CTOK, lanes), jnp.bfloat16),
        ],
        compiler_params=kernel_params(),
        cost_estimate=cost(2 * members * (CTOK + STEPS) * FEATURES * tiles * TILE, 12 * 10**6),
        name="block_product",
    )(*messages, *earlier, in_hbm(blocks))


def sum_kernel(bias_ref, *refs):
    part_refs, out_refs = refs[:ROW_BLOCKS], refs[ROW_BLOCKS:]
    column = lax.rem(lax.axis_index("tp"), COL_BLOCKS)
    late = column == 6
    last = (column == COL_BLOCKS - 1).astype(jnp.float32)
    cols = QKV // COL_BLOCKS
    tiles = cols // TILE
    kept = REST // TILE
    zero = jnp.zeros((CTOK, TILE), jnp.float32)

    def value_bias(j):
        if j == 0:
            return jnp.zeros((1, TILE), jnp.float32)
        at = QKV - cols + j * TILE
        return bias_ref[:, at : at + TILE] * last

    for g, out_ref in enumerate(out_refs):

        def total(lane):
            value = part_refs[0][g, :, lane : lane + TILE].astype(jnp.float32)
            for ref in part_refs[1:]:
                value = value + ref[g, :, lane : lane + TILE].astype(jnp.float32)
            return value

        rest = [total(cols + i * TILE) for i in range(kept)] + [zero] * (tiles - kept)
        lows = []
        for j in range(tiles):
            shifted = rest[j - tiles + kept] if j >= tiles - kept else zero
            value = total(j * TILE) + jnp.where(late, shifted, rest[j]) + value_bias(j)
            high = value.astype(jnp.bfloat16)
            out_ref[:, j * TILE : (j + 1) * TILE] = high
            lows.append(value - high.astype(jnp.float32))
        for i in range(kept):
            low = jnp.where(late, lows[i + tiles - kept], lows[i])
            out_ref[:, cols + i * TILE : cols + (i + 1) * TILE] = low.astype(jnp.bfloat16)


def sum_parts(bias, parts):
    groups, rows, lanes = parts[0].shape
    return pl.pallas_call(
        sum_kernel,
        out_shape=[jax.ShapeDtypeStruct((rows, lanes), jnp.bfloat16)] * groups,
        in_specs=[VMEM] * (1 + len(parts)),
        out_specs=[VMEM] * groups,
        compiler_params=kernel_params(),
        cost_estimate=cost(10**6, 3 * 10**6),
        name="sum_parts",
    )(bias, *parts)


def load_parts(part_refs, parts_ref):
    y, x = plane_place()
    for ref, (dy, dx) in zip(part_refs, HOMES):
        column = lax.rem(y + dy, 2) * 4 + lax.rem(x + 4 - dx, 4)
        parts_ref[column] = ref[...]


def summed_block(parts_ref, c, lanes):
    total = parts_ref[c, :, lanes].astype(jnp.float32)
    for r in range(1, ROW_BLOCKS):
        total = total + parts_ref[r * COL_BLOCKS + c, :, lanes].astype(jnp.float32)
    return total


def head_attention(query, key, value, fresh_key, fresh_value, seen, fresh_seen):
    inv_root = 1.0 / math.sqrt(HD)
    contract = (((1,), (1,)), ((), ()))
    old = lax.dot_general(query, key, contract, preferred_element_type=jnp.float32) * inv_root
    new = lax.dot_general(query, fresh_key, contract, preferred_element_type=jnp.float32) * inv_root
    old = jnp.where(seen, old, MASKED_SCORE)
    new = jnp.where(fresh_seen, new, MASKED_SCORE)
    highest = jnp.maximum(jnp.max(old, axis=-1, keepdims=True), jnp.max(new, axis=-1, keepdims=True))
    old = jnp.exp(old - highest)
    new = jnp.exp(new - highest)
    mass = jnp.sum(old, axis=-1, keepdims=True) + jnp.sum(new, axis=-1, keepdims=True)
    inv_mass = 1.0 / mass
    mixed = jnp.dot((old * inv_mass).astype(jnp.bfloat16), value, preferred_element_type=jnp.float32)
    return mixed + jnp.dot((new * inv_mass).astype(jnp.bfloat16), fresh_value, preferred_element_type=jnp.float32)


def load_qkv(main, parts_ref, qkv_ref):
    cols = QKV // COL_BLOCKS
    for c in range(COL_BLOCKS):
        first = 2 if c == 6 else 0
        total = summed_block(parts_ref, c, slice(0, TILE)) if main else parts_ref[c].astype(jnp.float32)
        for j in range(cols // TILE):
            lanes = slice(c * cols + j * TILE, c * cols + (j + 1) * TILE)
            rest = j - first
            has_rest = 0 <= rest < REST // TILE
            if main:
                for s in range(STEPS):
                    line = total[s * 8 + j : s * 8 + j + 1]
                    if has_rest:
                        at = s * 8 + cols // TILE + rest
                        line = line + total[at : at + 1]
                    qkv_ref[s : s + 1, lanes] = line
            else:
                value = total[:, j * TILE : (j + 1) * TILE]
                if has_rest:
                    value = value + total[:, cols + rest * TILE : cols + (rest + 1) * TILE]
                qkv_ref[:, lanes] = value


def head_readers(qkv_ref, bias_ref, cos_ref, sin_ref):
    cosine = cos_ref[...]
    sine = sin_ref[...]

    def plain(start):
        return qkv_ref[:, start : start + HD]

    def rotated(start):
        head = plain(start) + bias_ref[:, start : start + HD]
        return head * cosine + pltpu.roll(head, HD // 2, 1) * sine

    return plain, rotated


def fresh_block(pieces):
    rows = sum(piece.shape[0] for piece in pieces)
    pad = jnp.zeros((128 - rows, HD), jnp.float32)
    return jnp.concatenate(list(pieces) + [pad], axis=0).astype(jnp.bfloat16)


GROUP = D // HD // KVH
KV_WIDTH = KVH * HD


def attend_main_kernel(
    len_ref, bias_ref, cos_ref, sin_ref, cache_ref, parts_ref, *refs
):
    out_ref, kv_ref, qkv_ref, piece_ref = refs[-4:]
    rows = qkv_ref.shape[0]
    qkv_ref[...] = jnp.zeros(qkv_ref.shape, jnp.float32)
    load_qkv(True, parts_ref, qkv_ref)
    qkv_ref[:, D + KV_WIDTH :] = qkv_ref[:, D + KV_WIDTH :] + bias_ref[:, D + KV_WIDTH :]
    plain, rotated = head_readers(qkv_ref, bias_ref, cos_ref, sin_ref)
    seen = lax.broadcasted_iota(jnp.int32, (1, cache_ref.shape[0]), 1) < len_ref[0]
    row = lax.broadcasted_iota(jnp.int32, (rows, 128), 0)
    col = lax.broadcasted_iota(jnp.int32, (rows, 128), 1)
    own = ((col <= row) & (col < STEPS)).astype(jnp.int32)
    fresh_seen = jnp.concatenate([own] * GROUP, axis=0) > 0
    for g in range(KVH):
        query = jnp.concatenate([rotated((g * GROUP + h) * HD) for h in range(GROUP)], axis=0).astype(jnp.bfloat16)
        fresh_key = rotated(D + g * HD)
        fresh_value = plain(D + KV_WIDTH + g * HD)
        kv_ref[:, g * HD : (g + 1) * HD] = fresh_key
        kv_ref[:, KV_WIDTH + g * HD : KV_WIDTH + (g + 1) * HD] = fresh_value
        key = cache_ref[:, g * HD : (g + 1) * HD]
        value = cache_ref[:, KV_WIDTH + g * HD : KV_WIDTH + (g + 1) * HD]
        mixed = head_attention(
            query, key, value, fresh_block([fresh_key]), fresh_block([fresh_value]), seen, fresh_seen
        )
        for h in range(GROUP):
            r, place = divmod(g * GROUP + h, FEATURES // HD)
            j, lane = place // 2, (place % 2) * HD
            for s in range(STEPS):
                at = s * 8 + j
                piece_ref[r, at : at + 1, lane : lane + HD] = mixed[h * rows + s : h * rows + s + 1]
    for r in range(ROW_BLOCKS):
        piece = piece_ref[r].astype(jnp.bfloat16)
        for c in range(COL_BLOCKS):
            out_ref[r * COL_BLOCKS + c] = piece


def attend_main(prefix_len, bias, cosine, sine, cache, parts, after):
    return pl.pallas_call(
        attend_main_kernel,
        out_shape=(
            jax.ShapeDtypeStruct((32, 16, TILE), jnp.bfloat16),
            jax.ShapeDtypeStruct((8, 2 * KV_WIDTH), jnp.float32),
        ),
        in_specs=[SMEM] + [VMEM] * 5 + [UNREAD] * len(after),
        out_specs=(whole((32, 16, TILE)), whole((8, 2 * KV_WIDTH))),
        scratch_shapes=[
            pltpu.VMEM((8, QKV), jnp.float32),
            pltpu.VMEM((ROW_BLOCKS, 16, TILE), jnp.float32),
        ],
        compiler_params=kernel_params(),
        cost_estimate=cost(2 * 10**8, 6 * 10**6),
        name="attend_main",
    )(prefix_len, bias, cosine, sine, cache, parts, *after)


def attend_cont_kernel(len_ref, bound_ref, bias_ref, cos_ref, sin_ref, cache_ref, kv_ref, *refs):
    part_refs = refs[:COL_BLOCKS]
    out_ref, qkv_ref, parts_ref = refs[COL_BLOCKS:]
    load_parts(part_refs, parts_ref)
    rows = qkv_ref.shape[0]
    load_qkv(False, parts_ref, qkv_ref)
    plain, rotated = head_readers(qkv_ref, bias_ref, cos_ref, sin_ref)
    seen = lax.broadcasted_iota(jnp.int32, (1, cache_ref.shape[0]), 1) < len_ref[0]
    row = lax.broadcasted_iota(jnp.int32, (rows, 128), 0)
    col = lax.broadcasted_iota(jnp.int32, (rows, 128), 1)
    own = (row // STEPS == col // STEPS) & (col <= row)
    main = (col >= rows) & (col < rows + bound_ref[0])
    fresh_seen = jnp.concatenate([(own | main).astype(jnp.int32)] * GROUP, axis=0) > 0
    for g in range(KVH):
        query = jnp.concatenate([rotated((g * GROUP + h) * HD) for h in range(GROUP)], axis=0).astype(jnp.bfloat16)
        at_key = slice(g * HD, (g + 1) * HD)
        at_value = slice(KV_WIDTH + g * HD, KV_WIDTH + (g + 1) * HD)
        fresh_key = fresh_block([rotated(D + g * HD), kv_ref[:, at_key]])
        fresh_value = fresh_block([plain(D + KV_WIDTH + g * HD), kv_ref[:, at_value]])
        mixed = head_attention(
            query, cache_ref[:, at_key], cache_ref[:, at_value], fresh_key, fresh_value, seen, fresh_seen
        )
        mixed = mixed.astype(jnp.bfloat16)
        for h in range(GROUP):
            out_ref[:, (g * GROUP + h) * HD : (g * GROUP + h + 1) * HD] = mixed[h * rows : (h + 1) * rows]


def attend_cont(*args):
    return pl.pallas_call(
        attend_cont_kernel,
        out_shape=jax.ShapeDtypeStruct((CTOK, D), jnp.bfloat16),
        in_specs=[SMEM, SMEM] + [VMEM] * 4 + [whole((8, 2 * KV_WIDTH))] + [VMEM] * COL_BLOCKS,
        out_specs=whole((CTOK, D)),
        scratch_shapes=[
            pltpu.VMEM((CTOK, QKV), jnp.float32),
            pltpu.VMEM((COL_BLOCKS,) + args[-1].shape, jnp.bfloat16),
        ],
        compiler_params=kernel_params(),
        cost_estimate=cost(4 * 10**8, 8 * 10**6),
        name="attend_cont",
    )(*args)


def readout_kernel(head_ref, w_hbm, out_ref, w_ref, sem):
    copy = pltpu.make_async_copy(w_hbm.at[0], w_ref, sem)
    copy.start()
    row = head_ref[pl.ds(lax.rem(lax.axis_index("tp"), COL_BLOCKS), 1), :]
    high = row.astype(jnp.bfloat16).astype(jnp.float32)
    middle = (row - high).astype(jnp.bfloat16).astype(jnp.float32)
    low = row - high - middle
    pieces = jnp.concatenate([high, middle, low, jnp.zeros((13, row.shape[1]), jnp.float32)], axis=0)
    copy.wait()
    prod = lax.dot_general(
        pieces.astype(jnp.bfloat16), w_ref[...], (((1,), (1,)), ((), ())), preferred_element_type=jnp.float32
    )
    out_ref[...] = prod[0:1] + prod[1:2] + prod[2:3]


def readout(value_head, blocks):
    return pl.pallas_call(
        readout_kernel,
        out_shape=jax.ShapeDtypeStruct((1, FEATURES), jnp.float32),
        in_specs=[whole(value_head.shape), HBM],
        out_specs=whole((1, FEATURES)),
        scratch_shapes=[pltpu.VMEM((FEATURES, D // COL_BLOCKS), jnp.bfloat16), pltpu.SemaphoreType.DMA],
        compiler_params=kernel_params(),
        cost_estimate=cost(2 * 10**8, 5 * 10**6),
        name="readout",
    )(value_head, in_hbm(blocks))


def out_kernel(tiles, x_ref, read_ref, w_hbm, *refs):
    out_ref, rows_ref, wide_ref, read8_ref, w_ref, sems = refs[-6:]
    n = pl.program_id(0)
    members = x_ref.shape[0]
    lines = members * STEPS
    halves = TILE // 128
    tile = weight_tile(n, tiles, w_hbm, w_ref, sems)

    @pl.when(n == 0)
    def _():
        for j in range(FEATURES // TILE):
            read8_ref[j : j + 1, :] = read_ref[:, j * TILE : (j + 1) * TILE]
        out_ref[:, 8:, :] = jnp.broadcast_to(read8_ref[...][None], (members, 8, TILE))
        packed = x_ref[...].reshape(members * 16, TILE).astype(jnp.float32)
        for k in range(halves):
            wide_ref[k] = packed[:, k * 128 : (k + 1) * 128]
            for j in range(FEATURES // TILE):
                lane = j * TILE + k * 128
                rows_ref[:, lane : lane + 128] = wide_ref[k, pl.ds(j, lines, stride=8), :].astype(jnp.bfloat16)

    tile.wait()
    prod = jnp.dot(rows_ref[...], w_ref[n], preferred_element_type=jnp.float32)
    for k in range(halves):
        wide_ref[k, pl.ds(n, lines, stride=4), :] = prod[:, k * 128 : (k + 1) * 128]

    @pl.when(n == tiles - 1)
    def _():
        for k in range(halves):
            packed = wide_ref[k, : members * 8, :].reshape(members, 8, 128)
            out_ref[:, :8, k * 128 : (k + 1) * 128] = packed


def out_product(rows, read, blocks, after):
    members = rows.shape[0]
    tiles = blocks.shape[2] // TILE
    return pl.pallas_call(
        functools.partial(out_kernel, tiles),
        out_shape=jax.ShapeDtypeStruct((members, 16, TILE), jnp.float32),
        grid=(tiles,),
        in_specs=[whole(rows.shape), whole(read.shape), HBM] + [UNREAD] * len(after),
        out_specs=whole((members, 16, TILE)),
        scratch_shapes=[
            pltpu.VMEM((members * STEPS, FEATURES), jnp.bfloat16),
            pltpu.VMEM((TILE // 128, members * 16, 128), jnp.float32),
            pltpu.VMEM((8, TILE), jnp.float32),
            pltpu.VMEM((tiles, FEATURES, TILE), jnp.bfloat16),
            pltpu.SemaphoreType.DMA((tiles,)),
        ],
        compiler_params=kernel_params(),
        cost_estimate=cost(3 * 10**8, 5 * 10**6),
        name="out_product",
    )(rows, read, in_hbm(blocks), *after)


def finish_kernel(parts_ref, main_ref, cont_ref, head_ref, mixed_ref, out_ref, score_ref, wide_ref):
    cols = D // COL_BLOCKS
    for c in range(COL_BLOCKS):
        total = summed_block(parts_ref, c, slice(0, TILE))
        for j in range(cols // TILE):
            at = slice(c * cols + j * TILE, c * cols + (j + 1) * TILE)
            for s in range(STEPS):
                wide_ref[s : s + 1, at] = total[s * 4 + j : s * 4 + j + 1]
    out_ref[...] = (main_ref[...].astype(jnp.float32) + wide_ref[:STEPS, :]).astype(jnp.bfloat16)
    score = jnp.zeros((CTOK, TILE), jnp.float32)
    direct = jnp.zeros((STEPS, TILE), jnp.float32)
    for r in range(ROW_BLOCKS):
        read = parts_ref[r * COL_BLOCKS, 8:, :]
        for c in range(1, COL_BLOCKS):
            read = read + parts_ref[r * COL_BLOCKS + c, 8:, :]
        for j in range(FEATURES // TILE):
            lanes = slice(r * FEATURES + j * TILE, r * FEATURES + (j + 1) * TILE)
            score = score + mixed_ref[:, lanes].astype(jnp.float32) * read[j : j + 1, :]
            for c in range(CONTS):
                direct = direct + cont_ref[c, :, lanes].astype(jnp.float32) * head_ref[:, lanes]
    total = jnp.sum(score, axis=0, keepdims=True) + jnp.sum(direct, axis=0, keepdims=True)
    score_ref[...] = jnp.broadcast_to(jnp.sum(total, axis=1, keepdims=True) / CONTS, (8, 128))


def finish(parts, main, cont, head, mixed):
    return pl.pallas_call(
        finish_kernel,
        out_shape=(
            jax.ShapeDtypeStruct((STEPS, D), jnp.bfloat16),
            jax.ShapeDtypeStruct((8, 128), jnp.float32),
        ),
        in_specs=[whole(parts.shape), whole(main.shape), whole(cont.shape), whole(head.shape), whole(mixed.shape)],
        out_specs=(whole((STEPS, D)), whole((8, 128))),
        scratch_shapes=[pltpu.VMEM((8, D), jnp.float32)],
        compiler_params=kernel_params(),
        cost_estimate=cost(10**6, 2 * 10**6),
        name="finish",
    )(parts, main, cont, head, mixed)


def rope_tables(positions):
    half = HD // 2
    frequency = THETA ** (-(jnp.arange(half, dtype=jnp.float32) * 2.0) / HD)
    angles = positions.astype(jnp.float32)[:, None] * frequency[None, :]
    cosine = jnp.cos(angles)
    sine = jnp.sin(angles)
    return jnp.concatenate([cosine, cosine], axis=1), jnp.concatenate([-sine, sine], axis=1)


def exchange(rows):
    return lax.all_to_all(rows, "tp", split_axis=0, concat_axis=0, tiled=True)


ALONG = [[z * COL_BLOCKS + c for z in range(ROW_BLOCKS)] for c in range(COL_BLOCKS)]


def from_side(rows, dy, dx):
    route = []
    for to in range(MEMBERS):
        z, y, x = to // 8, to // 4 % 2, to % 4
        route.append((z * 8 + (y + dy) % 2 * 4 + (x + dx) % 4, to))
    return lax.ppermute(rows, "tp", route)


def from_along(rows, dz):
    route = [((to + dz * COL_BLOCKS) % MEMBERS, to) for to in range(MEMBERS)]
    return lax.ppermute(rows, "tp", route)


FIRST_HOMES = ((0, 0), (1, 0), (0, 1), (0, 3))
SECOND_HOMES = ((1, 1), (1, 3), (0, 2), (1, 2))
HOMES = FIRST_HOMES + SECOND_HOMES


def project(rows, blocks, bias):
    near = lax.all_to_all(rows, "tp", split_axis=0, concat_axis=0, tiled=True, axis_index_groups=ALONG)
    over = from_side(near, 1, 0)
    after, before = from_side(near, 0, 1), from_side(near, 0, 3)
    over_after, over_before = from_side(over, 0, 1), from_side(over, 0, 3)
    far = [from_side(before, 0, 3), from_side(over_after, 0, 1)]
    *first, main = block_product([near, over, after, before], blocks)
    first = [first[0]] + [from_along(first[k], -k) for k in range(1, ROW_BLOCKS)]
    *second, main = block_product([over_after, over_before] + far, blocks, (main,), HOMES)
    main, first = lax.optimization_barrier((main, first))
    second = [second[0]] + [from_along(second[k], -k) for k in range(1, ROW_BLOCKS)]
    received = []
    for homes, parts in ((FIRST_HOMES, first), (SECOND_HOMES, second)):
        for (dy, dx), summed in zip(homes, sum_parts(bias, parts)):
            received.append(from_side(summed, -dy, -dx) if dy or dx else summed)
    return received, exchange(main), second[1:] + received[1:4]


def on_device(
    main_inputs, cont_inputs, prefix_cache, prefix_len, boundary, rms_gain, qkv_bias, w_qkv, w_out, value_head
):
    main = main_inputs.reshape(STEPS, D)
    cont = cont_inputs.reshape(CONTS, STEPS, D)
    bias = qkv_bias[None, :]
    cache = prefix_cache[0]
    head = value_head[None, :]
    step = jnp.arange(CTOK, dtype=jnp.int32) % STEPS
    main_tables = rope_tables(prefix_len + step[:8])
    cont_tables = rope_tables(prefix_len + boundary + step)
    read = readout(value_head.reshape(COL_BLOCKS, D // COL_BLOCKS), w_out)
    parts, main_parts, before = project(norm_rows(main, cont, rms_gain[None, :]), w_qkv, bias)
    mixed, main_kv = attend_main(prefix_len, bias, *main_tables, cache, main_parts, before + [read])
    mixed = exchange(mixed)
    cont_mixed = attend_cont(prefix_len, boundary, bias, *cont_tables, cache, main_kv, *parts)
    parts = exchange(out_product(mixed, read, w_out, parts[4:]))
    main_out, score = finish(parts, main, cont, head, cont_mixed)
    return main_out[None], score[0, :1]


def solution(mesh):
    return jax.shard_map(
        on_device,
        mesh=mesh,
        in_specs=(
            P(("grp", "tp"), None, None),
            P(("grp", "tp"), None, None, None),
            P(("grp", "tp"), None, None),
            P(("grp", "tp")),
            P(("grp", "tp")),
            P(),
            P(),
            P("tp", None, None),
            P("tp", None, None),
            P(),
        ),
        out_specs=(P(("grp", "tp"), None, None), P(("grp", "tp"))),
        check_vma=False,
    )
```

```python
import functools
import math

import jax
import jax.numpy as jnp
from jax import lax
from jax.experimental import pallas as pl
from jax.experimental.pallas import tpu as pltpu
from jax.sharding import PartitionSpec as P

KVH = 8
HD = 128
D = 8192
QKV = 10240
ROW_BLOCKS = 4
COL_BLOCKS = 8
MEMBERS = ROW_BLOCKS * COL_BLOCKS
FEATURES = D // ROW_BLOCKS
CONTS = 8
STEPS = 2
CTOK = CONTS * STEPS
TILE = 256

THETA = 1000000.0
EPS = 1e-06
MASKED_SCORE = -1e30

VMEM_LIMIT = 32 * 1024 * 1024
VMEM = pl.BlockSpec(memory_space=pltpu.VMEM)
SMEM = pl.BlockSpec(memory_space=pltpu.SMEM)
HBM = pl.BlockSpec(memory_space=pltpu.HBM)
UNREAD = pl.BlockSpec(memory_space=pl.ANY)


def whole(shape):
    return pl.BlockSpec(shape, lambda *_: (0,) * len(shape))


def cost(flops, moved):
    return pl.CostEstimate(flops=flops, bytes_accessed=moved, transcendentals=0)


def in_hbm(array):
    return pltpu.with_memory_space_constraint(array, pltpu.HBM)


def kernel_params():
    return pltpu.CompilerParams(vmem_limit_bytes=VMEM_LIMIT)


def norm_kernel(main_hbm, cont_hbm, gain_hbm, out_ref, main_ref, cont_ref, gain_ref, rows_ref, piece_ref, sems):
    pairs = ((main_hbm, main_ref), (cont_hbm, cont_ref), (gain_hbm, gain_ref))
    copies = [pltpu.make_async_copy(src, dst, sems.at[i]) for i, (src, dst) in enumerate(pairs)]
    for copy in copies:
        copy.start()
    for copy in copies:
        copy.wait()

    def normed(wide):
        inv = lax.rsqrt(jnp.mean(wide * wide, axis=-1, keepdims=True) + EPS)
        return wide * inv * gain_ref[...]

    for c in range(CONTS):
        rows_ref[c * STEPS : (c + 1) * STEPS, :] = cont_ref[c].astype(jnp.float32)
    cont = normed(rows_ref[...]).astype(jnp.bfloat16)
    main = normed(main_ref[...].astype(jnp.float32))
    for r in range(ROW_BLOCKS):
        for j in range(FEATURES // TILE):
            lanes = slice(r * FEATURES + j * TILE, r * FEATURES + (j + 1) * TILE)
            for s in range(STEPS):
                piece_ref[r, s * 8 + j : s * 8 + j + 1, :] = main[s : s + 1, lanes]
    for r in range(ROW_BLOCKS):
        piece = piece_ref[r].astype(jnp.bfloat16)
        out_ref[r, :, :FEATURES] = cont[:, r * FEATURES : (r + 1) * FEATURES]
        out_ref[r, :, FEATURES:] = piece


def norm_rows(main, cont, gain):
    return pl.pallas_call(
        norm_kernel,
        out_shape=jax.ShapeDtypeStruct((ROW_BLOCKS, CTOK, FEATURES + TILE), jnp.bfloat16),
        in_specs=[HBM] * 3,
        out_specs=VMEM,
        scratch_shapes=[
            pltpu.VMEM((STEPS, D), jnp.bfloat16),
            pltpu.VMEM((CONTS, STEPS, D), jnp.bfloat16),
            pltpu.VMEM((1, D), jnp.float32),
            pltpu.VMEM((CTOK, D), jnp.float32),
            pltpu.VMEM((ROW_BLOCKS, 16, TILE), jnp.float32),
            pltpu.SemaphoreType.DMA((3,)),
        ],
        compiler_params=kernel_params(),
        cost_estimate=cost(10**6, 4 * 10**6),
        name="norm_rows",
    )(in_hbm(main), in_hbm(cont), in_hbm(gain))


def weight_tile(n, tiles, w_hbm, w_ref, sems):
    def copy(i):
        lanes = pl.ds(pl.multiple_of(i * TILE, TILE), TILE)
        return pltpu.make_async_copy(w_hbm.at[0, :, lanes], w_ref.at[i], sems.at[i])

    @pl.when(n == 0)
    def _():
        for i in range(tiles):
            copy(i).start()

    return copy(n)


REST = 768


def rest_tile(block):
    return jnp.where(block == 6, 2, 0)


def plane_place():
    column = lax.rem(lax.axis_index("tp"), COL_BLOCKS)
    return column // 4, lax.rem(column, 4)


def product_kernel(tiles, counts, places, *refs):
    x_refs, refs = refs[: len(counts)], refs[len(counts) :]
    if places:
        earlier_ref, refs = refs[0], refs[1:]
    w_hbm, *out_refs = refs[: 1 + ROW_BLOCKS]
    main_ref, rows_ref, wide_ref, w_ref, sems, part_ref = refs[1 + ROW_BLOCKS :]
    n = pl.program_id(0)
    members = sum(counts)
    count = members * CTOK
    lines = members * STEPS
    halves = TILE // 128
    width = tiles * TILE
    tile = weight_tile(n, tiles, w_hbm, w_ref, sems)

    @pl.when(n == 0)
    def _():
        at = 0
        for x_ref, size in zip(x_refs, counts):
            rows = slice(at * CTOK, (at + size) * CTOK)
            rows_ref[rows, :] = x_ref[:, :, :FEATURES].reshape(size * CTOK, FEATURES)
            packed = x_ref[:, :, FEATURES:].reshape(size * CTOK, TILE).astype(jnp.float32)
            for k in range(halves):
                wide_ref[k, rows, :] = packed[:, k * 128 : (k + 1) * 128]
            at += size
        for k in range(halves):
            for j in range(FEATURES // TILE):
                lane = j * TILE + k * 128
                rows_ref[count:, lane : lane + 128] = wide_ref[k, pl.ds(j, lines, stride=8), :].astype(jnp.bfloat16)

    tile.wait()
    prod = jnp.dot(rows_ref[...], w_ref[n], preferred_element_type=jnp.float32)
    high = prod.astype(jnp.bfloat16)
    part_ref[:, :, pl.ds(pl.multiple_of(n * TILE, TILE), TILE)] = high[:count].reshape(members, CTOK, TILE)
    for k in range(halves):
        wide_ref[k, pl.ds(n, lines, stride=8), :] = prod[count:, k * 128 : (k + 1) * 128]
    start = rest_tile(lax.rem(lax.axis_index("tp"), COL_BLOCKS))

    @pl.when((n >= start) & (n < start + REST // TILE))
    def _():
        low = prod - high.astype(jnp.float32)
        place = n - start
        lane = pl.multiple_of(width + place * TILE, TILE)
        part_ref[:, :, pl.ds(lane, TILE)] = low[:count].astype(jnp.bfloat16).reshape(members, CTOK, TILE)
        for k in range(halves):
            wide_ref[k, pl.ds(tiles + place, lines, stride=8), :] = low[count:, k * 128 : (k + 1) * 128]

    @pl.when(n == tiles - 1)
    def _():
        z = lax.axis_index("tp") // COL_BLOCKS
        done = earlier_ref.shape[0] // ROW_BLOCKS if places else 0
        for k in range(halves):
            lanes = slice(k * 128, (k + 1) * 128)
            packed = wide_ref[k].astype(jnp.bfloat16).reshape(members, CTOK, 128)
            if not places:
                main_ref[:, :, lanes] = packed
            for i, (dy, dx) in enumerate(places):
                y, x = plane_place()
                column = lax.rem(y + dy, 2) * 4 + lax.rem(x + dx, 4)
                for r in range(ROW_BLOCKS):
                    if i < done:
                        message = earlier_ref[i * ROW_BLOCKS + r, :, lanes]
                    else:
                        message = packed[(i - done) * ROW_BLOCKS + r]
                    main_ref[r * COL_BLOCKS + column, :, lanes] = message
        for k, out_ref in enumerate(out_refs):
            to = lax.rem(z + k, ROW_BLOCKS)
            for g in range(members // ROW_BLOCKS):
                out_ref[g] = part_ref[g * ROW_BLOCKS + to]


def block_product(messages, blocks, earlier=(), places=()):
    tiles = blocks.shape[2] // TILE
    lanes = tiles * TILE + REST
    counts = tuple(rows.shape[0] for rows in messages)
    members = sum(counts)
    return pl.pallas_call(
        functools.partial(product_kernel, tiles, counts, places),
        out_shape=[jax.ShapeDtypeStruct((members // ROW_BLOCKS, CTOK, lanes), jnp.bfloat16)] * ROW_BLOCKS
        + [jax.ShapeDtypeStruct((MEMBERS if places else members, CTOK, TILE), jnp.bfloat16)],
        grid=(tiles,),
        in_specs=[VMEM] * (len(counts) + len(earlier)) + [HBM],
        out_specs=[VMEM] * (1 + ROW_BLOCKS),
        scratch_shapes=[
            pltpu.VMEM((members * (CTOK + STEPS), FEATURES), jnp.bfloat16),
            pltpu.VMEM((TILE // 128, members * CTOK, 128), jnp.float32),
            pltpu.VMEM((tiles, FEATURES, TILE), jnp.bfloat16),
            pltpu.SemaphoreType.DMA((tiles,)),
            pltpu.VMEM((members, CTOK, lanes), jnp.bfloat16),
        ],
        compiler_params=kernel_params(),
        cost_estimate=cost(2 * members * (CTOK + STEPS) * FEATURES * tiles * TILE, 12 * 10**6),
        name="block_product",
    )(*messages, *earlier, in_hbm(blocks))


def sum_kernel(bias_ref, *refs):
    part_refs, out_refs = refs[:ROW_BLOCKS], refs[ROW_BLOCKS:]
    column = lax.rem(lax.axis_index("tp"), COL_BLOCKS)
    late = column == 6
    last = (column == COL_BLOCKS - 1).astype(jnp.float32)
    cols = QKV // COL_BLOCKS
    tiles = cols // TILE
    kept = REST // TILE
    zero = jnp.zeros((CTOK, TILE), jnp.float32)

    def value_bias(j):
        if j == 0:
            return jnp.zeros((1, TILE), jnp.float32)
        at = QKV - cols + j * TILE
        return bias_ref[:, at : at + TILE] * last

    for g, out_ref in enumerate(out_refs):

        def total(lane):
            value = part_refs[0][g, :, lane : lane + TILE].astype(jnp.float32)
            for ref in part_refs[1:]:
                value = value + ref[g, :, lane : lane + TILE].astype(jnp.float32)
            return value

        rest = [total(cols + i * TILE) for i in range(kept)] + [zero] * (tiles - kept)
        lows = []
        for j in range(tiles):
            shifted = rest[j - tiles + kept] if j >= tiles - kept else zero
            value = total(j * TILE) + jnp.where(late, shifted, rest[j]) + value_bias(j)
            high = value.astype(jnp.bfloat16)
            out_ref[:, j * TILE : (j + 1) * TILE] = high
            lows.append(value - high.astype(jnp.float32))
        for i in range(kept):
            low = jnp.where(late, lows[i + tiles - kept], lows[i])
            out_ref[:, cols + i * TILE : cols + (i + 1) * TILE] = low.astype(jnp.bfloat16)


def sum_parts(bias, parts):
    groups, rows, lanes = parts[0].shape
    return pl.pallas_call(
        sum_kernel,
        out_shape=[jax.ShapeDtypeStruct((rows, lanes), jnp.bfloat16)] * groups,
        in_specs=[VMEM] * (1 + len(parts)),
        out_specs=[VMEM] * groups,
        compiler_params=kernel_params(),
        cost_estimate=cost(10**6, 3 * 10**6),
        name="sum_parts",
    )(bias, *parts)


def load_parts(part_refs, parts_ref):
    y, x = plane_place()
    for ref, (dy, dx) in zip(part_refs, HOMES):
        column = lax.rem(y + dy, 2) * 4 + lax.rem(x + 4 - dx, 4)
        parts_ref[column] = ref[...]


def summed_block(parts_ref, c, lanes):
    total = parts_ref[c, :, lanes].astype(jnp.float32)
    for r in range(1, ROW_BLOCKS):
        total = total + parts_ref[r * COL_BLOCKS + c, :, lanes].astype(jnp.float32)
    return total


def head_attention(query, key, value, fresh_key, fresh_value, seen, fresh_seen):
    inv_root = 1.0 / math.sqrt(HD)
    contract = (((1,), (1,)), ((), ()))
    old = lax.dot_general(query, key, contract, preferred_element_type=jnp.float32) * inv_root
    new = lax.dot_general(query, fresh_key, contract, preferred_element_type=jnp.float32) * inv_root
    old = jnp.where(seen, old, MASKED_SCORE)
    new = jnp.where(fresh_seen, new, MASKED_SCORE)
    highest = jnp.maximum(jnp.max(old, axis=-1, keepdims=True), jnp.max(new, axis=-1, keepdims=True))
    old = jnp.exp(old - highest)
    new = jnp.exp(new - highest)
    mass = jnp.sum(old, axis=-1, keepdims=True) + jnp.sum(new, axis=-1, keepdims=True)
    inv_mass = 1.0 / mass
    mixed = jnp.dot((old * inv_mass).astype(jnp.bfloat16), value, preferred_element_type=jnp.float32)
    return mixed + jnp.dot((new * inv_mass).astype(jnp.bfloat16), fresh_value, preferred_element_type=jnp.float32)


def load_qkv(main, parts_ref, qkv_ref):
    cols = QKV // COL_BLOCKS
    for c in range(COL_BLOCKS):
        first = 2 if c == 6 else 0
        total = summed_block(parts_ref, c, slice(0, TILE)) if main else parts_ref[c].astype(jnp.float32)
        for j in range(cols // TILE):
            lanes = slice(c * cols + j * TILE, c * cols + (j + 1) * TILE)
            rest = j - first
            has_rest = 0 <= rest < REST // TILE
            if main:
                for s in range(STEPS):
                    line = total[s * 8 + j : s * 8 + j + 1]
                    if has_rest:
                        at = s * 8 + cols // TILE + rest
                        line = line + total[at : at + 1]
                    qkv_ref[s : s + 1, lanes] = line
            else:
                value = total[:, j * TILE : (j + 1) * TILE]
                if has_rest:
                    value = value + total[:, cols + rest * TILE : cols + (rest + 1) * TILE]
                qkv_ref[:, lanes] = value


def head_readers(qkv_ref, bias_ref, cos_ref, sin_ref):
    cosine = cos_ref[...]
    sine = sin_ref[...]

    def plain(start):
        return qkv_ref[:, start : start + HD]

    def rotated(start):
        head = plain(start) + bias_ref[:, start : start + HD]
        return head * cosine + pltpu.roll(head, HD // 2, 1) * sine

    return plain, rotated


def fresh_block(pieces):
    rows = sum(piece.shape[0] for piece in pieces)
    pad = jnp.zeros((128 - rows, HD), jnp.float32)
    return jnp.concatenate(list(pieces) + [pad], axis=0).astype(jnp.bfloat16)


GROUP = D // HD // KVH
KV_WIDTH = KVH * HD


def attend_main_kernel(
    len_ref, bias_ref, cos_ref, sin_ref, cache_ref, parts_ref, *refs
):
    out_ref, kv_ref, qkv_ref, piece_ref = refs[-4:]
    rows = qkv_ref.shape[0]
    qkv_ref[...] = jnp.zeros(qkv_ref.shape, jnp.float32)
    load_qkv(True, parts_ref, qkv_ref)
    qkv_ref[:, D + KV_WIDTH :] = qkv_ref[:, D + KV_WIDTH :] + bias_ref[:, D + KV_WIDTH :]
    plain, rotated = head_readers(qkv_ref, bias_ref, cos_ref, sin_ref)
    seen = lax.broadcasted_iota(jnp.int32, (1, cache_ref.shape[0]), 1) < len_ref[0]
    row = lax.broadcasted_iota(jnp.int32, (rows, 128), 0)
    col = lax.broadcasted_iota(jnp.int32, (rows, 128), 1)
    own = ((col <= row) & (col < STEPS)).astype(jnp.int32)
    fresh_seen = jnp.concatenate([own] * GROUP, axis=0) > 0
    for g in range(KVH):
        query = jnp.concatenate([rotated((g * GROUP + h) * HD) for h in range(GROUP)], axis=0).astype(jnp.bfloat16)
        fresh_key = rotated(D + g * HD)
        fresh_value = plain(D + KV_WIDTH + g * HD)
        kv_ref[:, g * HD : (g + 1) * HD] = fresh_key
        kv_ref[:, KV_WIDTH + g * HD : KV_WIDTH + (g + 1) * HD] = fresh_value
        key = cache_ref[:, g * HD : (g + 1) * HD]
        value = cache_ref[:, KV_WIDTH + g * HD : KV_WIDTH + (g + 1) * HD]
        mixed = head_attention(
            query, key, value, fresh_block([fresh_key]), fresh_block([fresh_value]), seen, fresh_seen
        )
        for h in range(GROUP):
            r, place = divmod(g * GROUP + h, FEATURES // HD)
            j, lane = place // 2, (place % 2) * HD
            for s in range(STEPS):
                at = s * 8 + j
                piece_ref[r, at : at + 1, lane : lane + HD] = mixed[h * rows + s : h * rows + s + 1]
    for r in range(ROW_BLOCKS):
        piece = piece_ref[r].astype(jnp.bfloat16)
        for c in range(COL_BLOCKS):
            out_ref[r * COL_BLOCKS + c] = piece


def attend_main(prefix_len, bias, cosine, sine, cache, parts, after):
    return pl.pallas_call(
        attend_main_kernel,
        out_shape=(
            jax.ShapeDtypeStruct((32, 16, TILE), jnp.bfloat16),
            jax.ShapeDtypeStruct((8, 2 * KV_WIDTH), jnp.float32),
        ),
        in_specs=[SMEM] + [VMEM] * 5 + [UNREAD] * len(after),
        out_specs=(whole((32, 16, TILE)), whole((8, 2 * KV_WIDTH))),
        scratch_shapes=[
            pltpu.VMEM((8, QKV), jnp.float32),
            pltpu.VMEM((ROW_BLOCKS, 16, TILE), jnp.float32),
        ],
        compiler_params=kernel_params(),
        cost_estimate=cost(2 * 10**8, 6 * 10**6),
        name="attend_main",
    )(prefix_len, bias, cosine, sine, cache, parts, *after)


def attend_cont_kernel(len_ref, bound_ref, bias_ref, cos_ref, sin_ref, cache_ref, kv_ref, *refs):
    part_refs = refs[:COL_BLOCKS]
    out_ref, qkv_ref, parts_ref = refs[COL_BLOCKS:]
    load_parts(part_refs, parts_ref)
    rows = qkv_ref.shape[0]
    load_qkv(False, parts_ref, qkv_ref)
    plain, rotated = head_readers(qkv_ref, bias_ref, cos_ref, sin_ref)
    seen = lax.broadcasted_iota(jnp.int32, (1, cache_ref.shape[0]), 1) < len_ref[0]
    row = lax.broadcasted_iota(jnp.int32, (rows, 128), 0)
    col = lax.broadcasted_iota(jnp.int32, (rows, 128), 1)
    own = (row // STEPS == col // STEPS) & (col <= row)
    main = (col >= rows) & (col < rows + bound_ref[0])
    fresh_seen = jnp.concatenate([(own | main).astype(jnp.int32)] * GROUP, axis=0) > 0
    for g in range(KVH):
        query = jnp.concatenate([rotated((g * GROUP + h) * HD) for h in range(GROUP)], axis=0).astype(jnp.bfloat16)
        at_key = slice(g * HD, (g + 1) * HD)
        at_value = slice(KV_WIDTH + g * HD, KV_WIDTH + (g + 1) * HD)
        fresh_key = fresh_block([rotated(D + g * HD), kv_ref[:, at_key]])
        fresh_value = fresh_block([plain(D + KV_WIDTH + g * HD), kv_ref[:, at_value]])
        mixed = head_attention(
            query, cache_ref[:, at_key], cache_ref[:, at_value], fresh_key, fresh_value, seen, fresh_seen
        )
        mixed = mixed.astype(jnp.bfloat16)
        for h in range(GROUP):
            out_ref[:, (g * GROUP + h) * HD : (g * GROUP + h + 1) * HD] = mixed[h * rows : (h + 1) * rows]


def attend_cont(*args):
    return pl.pallas_call(
        attend_cont_kernel,
        out_shape=jax.ShapeDtypeStruct((CTOK, D), jnp.bfloat16),
        in_specs=[SMEM, SMEM] + [VMEM] * 4 + [whole((8, 2 * KV_WIDTH))] + [VMEM] * COL_BLOCKS,
        out_specs=whole((CTOK, D)),
        scratch_shapes=[
            pltpu.VMEM((CTOK, QKV), jnp.float32),
            pltpu.VMEM((COL_BLOCKS,) + args[-1].shape, jnp.bfloat16),
        ],
        compiler_params=kernel_params(),
        cost_estimate=cost(4 * 10**8, 8 * 10**6),
        name="attend_cont",
    )(*args)


def readout_kernel(head_ref, w_hbm, out_ref, w_ref, sem):
    copy = pltpu.make_async_copy(w_hbm.at[0], w_ref, sem)
    copy.start()
    row = head_ref[pl.ds(lax.rem(lax.axis_index("tp"), COL_BLOCKS), 1), :]
    high = row.astype(jnp.bfloat16).astype(jnp.float32)
    middle = (row - high).astype(jnp.bfloat16).astype(jnp.float32)
    low = row - high - middle
    pieces = jnp.concatenate([high, middle, low, jnp.zeros((13, row.shape[1]), jnp.float32)], axis=0)
    copy.wait()
    prod = lax.dot_general(
        pieces.astype(jnp.bfloat16), w_ref[...], (((1,), (1,)), ((), ())), preferred_element_type=jnp.float32
    )
    out_ref[...] = prod[0:1] + prod[1:2] + prod[2:3]


def readout(value_head, blocks):
    return pl.pallas_call(
        readout_kernel,
        out_shape=jax.ShapeDtypeStruct((1, FEATURES), jnp.float32),
        in_specs=[whole(value_head.shape), HBM],
        out_specs=whole((1, FEATURES)),
        scratch_shapes=[pltpu.VMEM((FEATURES, D // COL_BLOCKS), jnp.bfloat16), pltpu.SemaphoreType.DMA],
        compiler_params=kernel_params(),
        cost_estimate=cost(2 * 10**8, 5 * 10**6),
        name="readout",
    )(value_head, in_hbm(blocks))


def out_kernel(tiles, x_ref, read_ref, w_hbm, *refs):
    out_ref, rows_ref, wide_ref, read8_ref, w_ref, sems = refs[-6:]
    n = pl.program_id(0)
    members = x_ref.shape[0]
    lines = members * STEPS
    halves = TILE // 128
    tile = weight_tile(n, tiles, w_hbm, w_ref, sems)

    @pl.when(n == 0)
    def _():
        for j in range(FEATURES // TILE):
            read8_ref[j : j + 1, :] = read_ref[:, j * TILE : (j + 1) * TILE]
        out_ref[:, 8:, :] = jnp.broadcast_to(read8_ref[...][None], (members, 8, TILE))
        packed = x_ref[...].reshape(members * 16, TILE).astype(jnp.float32)
        for k in range(halves):
            wide_ref[k] = packed[:, k * 128 : (k + 1) * 128]
            for j in range(FEATURES // TILE):
                lane = j * TILE + k * 128
                rows_ref[:, lane : lane + 128] = wide_ref[k, pl.ds(j, lines, stride=8), :].astype(jnp.bfloat16)

    tile.wait()
    prod = jnp.dot(rows_ref[...], w_ref[n], preferred_element_type=jnp.float32)
    for k in range(halves):
        wide_ref[k, pl.ds(n, lines, stride=4), :] = prod[:, k * 128 : (k + 1) * 128]

    @pl.when(n == tiles - 1)
    def _():
        for k in range(halves):
            packed = wide_ref[k, : members * 8, :].reshape(members, 8, 128)
            out_ref[:, :8, k * 128 : (k + 1) * 128] = packed


def out_product(rows, read, blocks, after):
    members = rows.shape[0]
    tiles = blocks.shape[2] // TILE
    return pl.pallas_call(
        functools.partial(out_kernel, tiles),
        out_shape=jax.ShapeDtypeStruct((members, 16, TILE), jnp.float32),
        grid=(tiles,),
        in_specs=[whole(rows.shape), whole(read.shape), HBM] + [UNREAD] * len(after),
        out_specs=whole((members, 16, TILE)),
        scratch_shapes=[
            pltpu.VMEM((members * STEPS, FEATURES), jnp.bfloat16),
            pltpu.VMEM((TILE // 128, members * 16, 128), jnp.float32),
            pltpu.VMEM((8, TILE), jnp.float32),
            pltpu.VMEM((tiles, FEATURES, TILE), jnp.bfloat16),
            pltpu.SemaphoreType.DMA((tiles,)),
        ],
        compiler_params=kernel_params(),
        cost_estimate=cost(3 * 10**8, 5 * 10**6),
        name="out_product",
    )(rows, read, in_hbm(blocks), *after)


def finish_kernel(parts_ref, main_ref, cont_ref, head_ref, mixed_ref, out_ref, score_ref, wide_ref):
    cols = D // COL_BLOCKS
    for c in range(COL_BLOCKS):
        total = summed_block(parts_ref, c, slice(0, TILE))
        for j in range(cols // TILE):
            at = slice(c * cols + j * TILE, c * cols + (j + 1) * TILE)
            for s in range(STEPS):
                wide_ref[s : s + 1, at] = total[s * 4 + j : s * 4 + j + 1]
    out_ref[...] = (main_ref[...].astype(jnp.float32) + wide_ref[:STEPS, :]).astype(jnp.bfloat16)
    score = jnp.zeros((CTOK, TILE), jnp.float32)
    direct = jnp.zeros((STEPS, TILE), jnp.float32)
    for r in range(ROW_BLOCKS):
        read = parts_ref[r * COL_BLOCKS, 8:, :]
        for c in range(1, COL_BLOCKS):
            read = read + parts_ref[r * COL_BLOCKS + c, 8:, :]
        for j in range(FEATURES // TILE):
            lanes = slice(r * FEATURES + j * TILE, r * FEATURES + (j + 1) * TILE)
            score = score + mixed_ref[:, lanes].astype(jnp.float32) * read[j : j + 1, :]
            for c in range(CONTS):
                direct = direct + cont_ref[c, :, lanes].astype(jnp.float32) * head_ref[:, lanes]
    total = jnp.sum(score, axis=0, keepdims=True) + jnp.sum(direct, axis=0, keepdims=True)
    score_ref[...] = jnp.broadcast_to(jnp.sum(total, axis=1, keepdims=True) / CONTS, (8, 128))


def finish(parts, main, cont, head, mixed):
    return pl.pallas_call(
        finish_kernel,
        out_shape=(
            jax.ShapeDtypeStruct((STEPS, D), jnp.bfloat16),
            jax.ShapeDtypeStruct((8, 128), jnp.float32),
        ),
        in_specs=[whole(parts.shape), whole(main.shape), whole(cont.shape), whole(head.shape), whole(mixed.shape)],
        out_specs=(whole((STEPS, D)), whole((8, 128))),
        scratch_shapes=[pltpu.VMEM((8, D), jnp.float32)],
        compiler_params=kernel_params(),
        cost_estimate=cost(10**6, 2 * 10**6),
        name="finish",
    )(parts, main, cont, head, mixed)


def rope_tables(positions):
    half = HD // 2
    frequency = THETA ** (-(jnp.arange(half, dtype=jnp.float32) * 2.0) / HD)
    angles = positions.astype(jnp.float32)[:, None] * frequency[None, :]
    cosine = jnp.cos(angles)
    sine = jnp.sin(angles)
    return jnp.concatenate([cosine, cosine], axis=1), jnp.concatenate([-sine, sine], axis=1)


def exchange(rows):
    return lax.all_to_all(rows, "tp", split_axis=0, concat_axis=0, tiled=True)


ALONG = [[z * COL_BLOCKS + c for z in range(ROW_BLOCKS)] for c in range(COL_BLOCKS)]


def from_side(rows, dy, dx):
    route = []
    for to in range(MEMBERS):
        z, y, x = to // 8, to // 4 % 2, to % 4
        route.append((z * 8 + (y + dy) % 2 * 4 + (x + dx) % 4, to))
    return lax.ppermute(rows, "tp", route)


def from_along(rows, dz):
    route = [((to + dz * COL_BLOCKS) % MEMBERS, to) for to in range(MEMBERS)]
    return lax.ppermute(rows, "tp", route)


FIRST_HOMES = ((0, 0), (1, 0), (0, 1), (0, 3))
SECOND_HOMES = ((1, 1), (1, 3), (0, 2), (1, 2))
HOMES = FIRST_HOMES + SECOND_HOMES


def project(rows, blocks, bias):
    near = lax.all_to_all(rows, "tp", split_axis=0, concat_axis=0, tiled=True, axis_index_groups=ALONG)
    over = from_side(near, 1, 0)
    after, before = from_side(near, 0, 1), from_side(near, 0, 3)
    over_after, over_before = from_side(over, 0, 1), from_side(over, 0, 3)
    far = [from_side(before, 0, 3), from_side(over_after, 0, 1)]
    *first, main = block_product([near, over, after, before], blocks)
    first = [first[0]] + [from_along(first[k], -k) for k in range(1, ROW_BLOCKS)]
    *second, main = block_product([over_after, over_before] + far, blocks, (main,), HOMES)
    main, first = lax.optimization_barrier((main, first))
    second = [second[0]] + [from_along(second[k], -k) for k in range(1, ROW_BLOCKS)]
    received = []
    for homes, parts in ((FIRST_HOMES, first), (SECOND_HOMES, second)):
        for (dy, dx), summed in zip(homes, sum_parts(bias, parts)):
            received.append(from_side(summed, -dy, -dx) if dy or dx else summed)
    return received, exchange(main), second[1:] + received[1:4]


def on_device(
    main_inputs, cont_inputs, prefix_cache, prefix_len, boundary, rms_gain, qkv_bias, w_qkv, w_out, value_head
):
    main = main_inputs.reshape(STEPS, D)
    cont = cont_inputs.reshape(CONTS, STEPS, D)
    bias = qkv_bias[None, :]
    cache = prefix_cache[0]
    head = value_head[None, :]
    step = jnp.arange(CTOK, dtype=jnp.int32) % STEPS
    main_tables = rope_tables(prefix_len + step[:8])
    cont_tables = rope_tables(prefix_len + boundary + step)
    read = readout(value_head.reshape(COL_BLOCKS, D // COL_BLOCKS), w_out)
    parts, main_parts, before = project(norm_rows(main, cont, rms_gain[None, :]), w_qkv, bias)
    mixed, main_kv = attend_main(prefix_len, bias, *main_tables, cache, main_parts, before + [read])
    mixed = exchange(mixed)
    cont_mixed = attend_cont(prefix_len, boundary, bias, *cont_tables, cache, main_kv, *parts)
    parts = exchange(out_product(mixed, read, w_out, parts[4:6]))
    main_out, score = finish(parts, main, cont, head, cont_mixed)
    return main_out[None], score[0, :1]


def solution(mesh):
    return jax.shard_map(
        on_device,
        mesh=mesh,
        in_specs=(
            P(("grp", "tp"), None, None),
            P(("grp", "tp"), None, None, None),
            P(("grp", "tp"), None, None),
            P(("grp", "tp")),
            P(("grp", "tp")),
            P(),
            P(),
            P("tp", None, None),
            P("tp", None, None),
            P(),
        ),
        out_specs=(P(("grp", "tp"), None, None), P(("grp", "tp"))),
        check_vma=False,
    )
```

```python
import functools
import math

import jax
import jax.numpy as jnp
from jax import lax
from jax.experimental import pallas as pl
from jax.experimental.pallas import tpu as pltpu
from jax.sharding import PartitionSpec as P

KVH = 8
HD = 128
D = 8192
QKV = 10240
ROW_BLOCKS = 4
COL_BLOCKS = 8
MEMBERS = ROW_BLOCKS * COL_BLOCKS
FEATURES = D // ROW_BLOCKS
CONTS = 8
STEPS = 2
CTOK = CONTS * STEPS
TILE = 256

THETA = 1000000.0
EPS = 1e-06
MASKED_SCORE = -1e30

VMEM_LIMIT = 32 * 1024 * 1024
VMEM = pl.BlockSpec(memory_space=pltpu.VMEM)
SMEM = pl.BlockSpec(memory_space=pltpu.SMEM)
HBM = pl.BlockSpec(memory_space=pltpu.HBM)
UNREAD = pl.BlockSpec(memory_space=pl.ANY)


def whole(shape):
    return pl.BlockSpec(shape, lambda *_: (0,) * len(shape))


def cost(flops, moved):
    return pl.CostEstimate(flops=flops, bytes_accessed=moved, transcendentals=0)


def in_hbm(array):
    return pltpu.with_memory_space_constraint(array, pltpu.HBM)


def kernel_params():
    return pltpu.CompilerParams(vmem_limit_bytes=VMEM_LIMIT)


def norm_kernel(main_hbm, cont_hbm, gain_hbm, out_ref, main_ref, cont_ref, gain_ref, rows_ref, piece_ref, sems):
    pairs = ((main_hbm, main_ref), (cont_hbm, cont_ref), (gain_hbm, gain_ref))
    copies = [pltpu.make_async_copy(src, dst, sems.at[i]) for i, (src, dst) in enumerate(pairs)]
    for copy in copies:
        copy.start()
    for copy in copies:
        copy.wait()

    def normed(wide):
        inv = lax.rsqrt(jnp.mean(wide * wide, axis=-1, keepdims=True) + EPS)
        return wide * inv * gain_ref[...]

    for c in range(CONTS):
        rows_ref[c * STEPS : (c + 1) * STEPS, :] = cont_ref[c].astype(jnp.float32)
    cont = normed(rows_ref[...]).astype(jnp.bfloat16)
    main = normed(main_ref[...].astype(jnp.float32))
    for r in range(ROW_BLOCKS):
        for j in range(FEATURES // TILE):
            lanes = slice(r * FEATURES + j * TILE, r * FEATURES + (j + 1) * TILE)
            for s in range(STEPS):
                piece_ref[r, s * 8 + j : s * 8 + j + 1, :] = main[s : s + 1, lanes]
    for r in range(ROW_BLOCKS):
        piece = piece_ref[r].astype(jnp.bfloat16)
        out_ref[r, :, :FEATURES] = cont[:, r * FEATURES : (r + 1) * FEATURES]
        out_ref[r, :, FEATURES:] = piece


def norm_rows(main, cont, gain):
    return pl.pallas_call(
        norm_kernel,
        out_shape=jax.ShapeDtypeStruct((ROW_BLOCKS, CTOK, FEATURES + TILE), jnp.bfloat16),
        in_specs=[HBM] * 3,
        out_specs=VMEM,
        scratch_shapes=[
            pltpu.VMEM((STEPS, D), jnp.bfloat16),
            pltpu.VMEM((CONTS, STEPS, D), jnp.bfloat16),
            pltpu.VMEM((1, D), jnp.float32),
            pltpu.VMEM((CTOK, D), jnp.float32),
            pltpu.VMEM((ROW_BLOCKS, 16, TILE), jnp.float32),
            pltpu.SemaphoreType.DMA((3,)),
        ],
        compiler_params=kernel_params(),
        cost_estimate=cost(10**6, 4 * 10**6),
        name="norm_rows",
    )(in_hbm(main), in_hbm(cont), in_hbm(gain))


def weight_copies(pieces, w_hbm, w_ref, sems):
    copies = []
    for i, (start, width) in enumerate(pieces):
        lanes = slice(start, start + width)
        copies.append(pltpu.make_async_copy(w_hbm.at[0, :, lanes], w_ref.at[:, lanes], sems.at[i]))
        copies[-1].start()
    return copies


QKV_PIECES = ((0, 512), (512, 768))
OUT_PIECES = ((0, 512), (512, 512))


REST = 768


def rest_tile(block):
    return jnp.where(block == 6, 2, 0)


def plane_place():
    column = lax.rem(lax.axis_index("tp"), COL_BLOCKS)
    return column // 4, lax.rem(column, 4)


def product_kernel(tiles, counts, places, *refs):
    x_refs, refs = refs[: len(counts)], refs[len(counts) :]
    if places:
        earlier_ref, refs = refs[0], refs[1:]
    w_hbm, *out_refs = refs[: 1 + ROW_BLOCKS]
    main_ref, rows_ref, wide_ref, w_ref, sems, part_ref = refs[1 + ROW_BLOCKS :]
    copies = weight_copies(QKV_PIECES, w_hbm, w_ref, sems)
    members = sum(counts)
    count = members * CTOK
    lines = members * STEPS
    halves = TILE // 128
    width = tiles * TILE
    at = 0
    for x_ref, size in zip(x_refs, counts):
        rows = slice(at * CTOK, (at + size) * CTOK)
        rows_ref[rows, :] = x_ref[:, :, :FEATURES].reshape(size * CTOK, FEATURES)
        packed = x_ref[:, :, FEATURES:].reshape(size * CTOK, TILE).astype(jnp.float32)
        for k in range(halves):
            wide_ref[k, rows, :] = packed[:, k * 128 : (k + 1) * 128]
        at += size
    for k in range(halves):
        for j in range(FEATURES // TILE):
            lane = j * TILE + k * 128
            rows_ref[count:, lane : lane + 128] = wide_ref[k, pl.ds(j, lines, stride=8), :].astype(jnp.bfloat16)

    late = lax.rem(lax.axis_index("tp"), COL_BLOCKS) == 6
    for (first, size), copy in zip(QKV_PIECES, copies):
        copy.wait()
        prod = jnp.dot(rows_ref[...], w_ref[:, first : first + size], preferred_element_type=jnp.float32)
        high = prod.astype(jnp.bfloat16)
        part_ref[:, :, first : first + size] = high[:count].reshape(members, CTOK, size)
        low = prod - high.astype(jnp.float32)
        for start in range(0, size, 128):
            n, k = divmod((first + start) // 128, halves)
            wide_ref[k, pl.ds(n, lines, stride=8), :] = prod[count:, start : start + 128]
        for begin, here in ((width - REST, late), (0, jnp.logical_not(late))):
            start, end = max(begin, first), min(begin + REST, first + size)
            if start >= end:
                continue

            @pl.when(here)
            def _():
                kept = low[:, start - first : end - first]
                lanes = slice(width + start - begin, width + end - begin)
                part_ref[:, :, lanes] = kept[:count].astype(jnp.bfloat16).reshape(members, CTOK, end - start)
                for lane in range(0, end - start, 128):
                    n, k = divmod((start - begin + lane) // 128, halves)
                    wide_ref[k, pl.ds(tiles + n, lines, stride=8), :] = kept[count:, lane : lane + 128]

    z = lax.axis_index("tp") // COL_BLOCKS
    done = earlier_ref.shape[0] // ROW_BLOCKS if places else 0
    for k in range(halves):
        lanes = slice(k * 128, (k + 1) * 128)
        packed = wide_ref[k].astype(jnp.bfloat16).reshape(members, CTOK, 128)
        if not places:
            main_ref[:, :, lanes] = packed
        for i, (dy, dx) in enumerate(places):
            y, x = plane_place()
            column = lax.rem(y + dy, 2) * 4 + lax.rem(x + dx, 4)
            for r in range(ROW_BLOCKS):
                if i < done:
                    message = earlier_ref[i * ROW_BLOCKS + r, :, lanes]
                else:
                    message = packed[(i - done) * ROW_BLOCKS + r]
                main_ref[r * COL_BLOCKS + column, :, lanes] = message
    for k, out_ref in enumerate(out_refs):
        to = lax.rem(z + k, ROW_BLOCKS)
        for g in range(members // ROW_BLOCKS):
            out_ref[g] = part_ref[g * ROW_BLOCKS + to]


def block_product(messages, blocks, earlier=(), places=()):
    tiles = blocks.shape[2] // TILE
    lanes = tiles * TILE + REST
    counts = tuple(rows.shape[0] for rows in messages)
    members = sum(counts)
    return pl.pallas_call(
        functools.partial(product_kernel, tiles, counts, places),
        out_shape=[jax.ShapeDtypeStruct((members // ROW_BLOCKS, CTOK, lanes), jnp.bfloat16)] * ROW_BLOCKS
        + [jax.ShapeDtypeStruct((MEMBERS if places else members, CTOK, TILE), jnp.bfloat16)],
        in_specs=[VMEM] * (len(counts) + len(earlier)) + [HBM],
        out_specs=[VMEM] * (1 + ROW_BLOCKS),
        scratch_shapes=[
            pltpu.VMEM((members * (CTOK + STEPS), FEATURES), jnp.bfloat16),
            pltpu.VMEM((TILE // 128, members * CTOK, 128), jnp.float32),
            pltpu.VMEM((FEATURES, tiles * TILE), jnp.bfloat16),
            pltpu.SemaphoreType.DMA((len(QKV_PIECES),)),
            pltpu.VMEM((members, CTOK, lanes), jnp.bfloat16),
        ],
        compiler_params=kernel_params(),
        cost_estimate=cost(2 * members * (CTOK + STEPS) * FEATURES * tiles * TILE, 12 * 10**6),
        name="block_product",
    )(*messages, *earlier, in_hbm(blocks))


def sum_kernel(bias_ref, *refs):
    part_refs, out_refs = refs[:ROW_BLOCKS], refs[ROW_BLOCKS:]
    column = lax.rem(lax.axis_index("tp"), COL_BLOCKS)
    late = column == 6
    last = (column == COL_BLOCKS - 1).astype(jnp.float32)
    cols = QKV // COL_BLOCKS
    tiles = cols // TILE
    kept = REST // TILE
    zero = jnp.zeros((CTOK, TILE), jnp.float32)

    def value_bias(j):
        if j == 0:
            return jnp.zeros((1, TILE), jnp.float32)
        at = QKV - cols + j * TILE
        return bias_ref[:, at : at + TILE] * last

    for g, out_ref in enumerate(out_refs):

        def total(lane):
            value = part_refs[0][g, :, lane : lane + TILE].astype(jnp.float32)
            for ref in part_refs[1:]:
                value = value + ref[g, :, lane : lane + TILE].astype(jnp.float32)
            return value

        rest = [total(cols + i * TILE) for i in range(kept)] + [zero] * (tiles - kept)
        lows = []
        for j in range(tiles):
            shifted = rest[j - tiles + kept] if j >= tiles - kept else zero
            value = total(j * TILE) + jnp.where(late, shifted, rest[j]) + value_bias(j)
            high = value.astype(jnp.bfloat16)
            out_ref[:, j * TILE : (j + 1) * TILE] = high
            lows.append(value - high.astype(jnp.float32))
        for i in range(kept):
            low = jnp.where(late, lows[i + tiles - kept], lows[i])
            out_ref[:, cols + i * TILE : cols + (i + 1) * TILE] = low.astype(jnp.bfloat16)


def sum_parts(bias, parts):
    groups, rows, lanes = parts[0].shape
    return pl.pallas_call(
        sum_kernel,
        out_shape=[jax.ShapeDtypeStruct((rows, lanes), jnp.bfloat16)] * groups,
        in_specs=[VMEM] * (1 + len(parts)),
        out_specs=[VMEM] * groups,
        compiler_params=kernel_params(),
        cost_estimate=cost(10**6, 3 * 10**6),
        name="sum_parts",
    )(bias, *parts)


def load_parts(part_refs, parts_ref):
    y, x = plane_place()
    for ref, (dy, dx) in zip(part_refs, HOMES):
        column = lax.rem(y + dy, 2) * 4 + lax.rem(x + 4 - dx, 4)
        parts_ref[column] = ref[...]


def summed_block(parts_ref, c, lanes):
    total = parts_ref[c, :, lanes].astype(jnp.float32)
    for r in range(1, ROW_BLOCKS):
        total = total + parts_ref[r * COL_BLOCKS + c, :, lanes].astype(jnp.float32)
    return total


def head_attention(query, key, value, fresh_key, fresh_value, seen, fresh_seen):
    inv_root = 1.0 / math.sqrt(HD)
    contract = (((1,), (1,)), ((), ()))
    old = lax.dot_general(query, key, contract, preferred_element_type=jnp.float32) * inv_root
    new = lax.dot_general(query, fresh_key, contract, preferred_element_type=jnp.float32) * inv_root
    old = jnp.where(seen, old, MASKED_SCORE)
    new = jnp.where(fresh_seen, new, MASKED_SCORE)
    highest = jnp.maximum(jnp.max(old, axis=-1, keepdims=True), jnp.max(new, axis=-1, keepdims=True))
    old = jnp.exp(old - highest)
    new = jnp.exp(new - highest)
    mass = jnp.sum(old, axis=-1, keepdims=True) + jnp.sum(new, axis=-1, keepdims=True)
    inv_mass = 1.0 / mass
    mixed = jnp.dot((old * inv_mass).astype(jnp.bfloat16), value, preferred_element_type=jnp.float32)
    return mixed + jnp.dot((new * inv_mass).astype(jnp.bfloat16), fresh_value, preferred_element_type=jnp.float32)


def load_qkv(main, parts_ref, qkv_ref):
    cols = QKV // COL_BLOCKS
    for c in range(COL_BLOCKS):
        first = 2 if c == 6 else 0
        total = summed_block(parts_ref, c, slice(0, TILE)) if main else parts_ref[c].astype(jnp.float32)
        for j in range(cols // TILE):
            lanes = slice(c * cols + j * TILE, c * cols + (j + 1) * TILE)
            rest = j - first
            has_rest = 0 <= rest < REST // TILE
            if main:
                for s in range(STEPS):
                    line = total[s * 8 + j : s * 8 + j + 1]
                    if has_rest:
                        at = s * 8 + cols // TILE + rest
                        line = line + total[at : at + 1]
                    qkv_ref[s : s + 1, lanes] = line
            else:
                value = total[:, j * TILE : (j + 1) * TILE]
                if has_rest:
                    value = value + total[:, cols + rest * TILE : cols + (rest + 1) * TILE]
                qkv_ref[:, lanes] = value


def head_readers(qkv_ref, bias_ref, cos_ref, sin_ref):
    cosine = cos_ref[...]
    sine = sin_ref[...]

    def plain(start):
        return qkv_ref[:, start : start + HD]

    def rotated(start):
        head = plain(start) + bias_ref[:, start : start + HD]
        return head * cosine + pltpu.roll(head, HD // 2, 1) * sine

    return plain, rotated


def fresh_block(pieces):
    rows = sum(piece.shape[0] for piece in pieces)
    pad = jnp.zeros((128 - rows, HD), jnp.float32)
    return jnp.concatenate(list(pieces) + [pad], axis=0).astype(jnp.bfloat16)


GROUP = D // HD // KVH
KV_WIDTH = KVH * HD


def attend_main_kernel(
    len_ref, bias_ref, cos_ref, sin_ref, cache_ref, parts_ref, *refs
):
    out_ref, kv_ref, qkv_ref, piece_ref = refs[-4:]
    rows = qkv_ref.shape[0]
    qkv_ref[...] = jnp.zeros(qkv_ref.shape, jnp.float32)
    load_qkv(True, parts_ref, qkv_ref)
    qkv_ref[:, D + KV_WIDTH :] = qkv_ref[:, D + KV_WIDTH :] + bias_ref[:, D + KV_WIDTH :]
    plain, rotated = head_readers(qkv_ref, bias_ref, cos_ref, sin_ref)
    seen = lax.broadcasted_iota(jnp.int32, (1, cache_ref.shape[0]), 1) < len_ref[0]
    row = lax.broadcasted_iota(jnp.int32, (rows, 128), 0)
    col = lax.broadcasted_iota(jnp.int32, (rows, 128), 1)
    own = ((col <= row) & (col < STEPS)).astype(jnp.int32)
    fresh_seen = jnp.concatenate([own] * GROUP, axis=0) > 0
    for g in range(KVH):
        query = jnp.concatenate([rotated((g * GROUP + h) * HD) for h in range(GROUP)], axis=0).astype(jnp.bfloat16)
        fresh_key = rotated(D + g * HD)
        fresh_value = plain(D + KV_WIDTH + g * HD)
        kv_ref[:, g * HD : (g + 1) * HD] = fresh_key
        kv_ref[:, KV_WIDTH + g * HD : KV_WIDTH + (g + 1) * HD] = fresh_value
        key = cache_ref[:, g * HD : (g + 1) * HD]
        value = cache_ref[:, KV_WIDTH + g * HD : KV_WIDTH + (g + 1) * HD]
        mixed = head_attention(
            query, key, value, fresh_block([fresh_key]), fresh_block([fresh_value]), seen, fresh_seen
        )
        for h in range(GROUP):
            r, place = divmod(g * GROUP + h, FEATURES // HD)
            j, lane = place // 2, (place % 2) * HD
            for s in range(STEPS):
                at = s * 8 + j
                piece_ref[r, at : at + 1, lane : lane + HD] = mixed[h * rows + s : h * rows + s + 1]
    for r in range(ROW_BLOCKS):
        piece = piece_ref[r].astype(jnp.bfloat16)
        for c in range(COL_BLOCKS):
            out_ref[r * COL_BLOCKS + c] = piece


def attend_main(prefix_len, bias, cosine, sine, cache, parts, after):
    return pl.pallas_call(
        attend_main_kernel,
        out_shape=(
            jax.ShapeDtypeStruct((32, 16, TILE), jnp.bfloat16),
            jax.ShapeDtypeStruct((8, 2 * KV_WIDTH), jnp.float32),
        ),
        in_specs=[SMEM] + [VMEM] * 5 + [UNREAD] * len(after),
        out_specs=(whole((32, 16, TILE)), whole((8, 2 * KV_WIDTH))),
        scratch_shapes=[
            pltpu.VMEM((8, QKV), jnp.float32),
            pltpu.VMEM((ROW_BLOCKS, 16, TILE), jnp.float32),
        ],
        compiler_params=kernel_params(),
        cost_estimate=cost(2 * 10**8, 6 * 10**6),
        name="attend_main",
    )(prefix_len, bias, cosine, sine, cache, parts, *after)


def attend_cont_kernel(len_ref, bound_ref, bias_ref, cos_ref, sin_ref, cache_ref, kv_ref, *refs):
    part_refs = refs[:COL_BLOCKS]
    out_ref, qkv_ref, parts_ref = refs[COL_BLOCKS:]
    load_parts(part_refs, parts_ref)
    rows = qkv_ref.shape[0]
    load_qkv(False, parts_ref, qkv_ref)
    plain, rotated = head_readers(qkv_ref, bias_ref, cos_ref, sin_ref)
    seen = lax.broadcasted_iota(jnp.int32, (1, cache_ref.shape[0]), 1) < len_ref[0]
    row = lax.broadcasted_iota(jnp.int32, (rows, 128), 0)
    col = lax.broadcasted_iota(jnp.int32, (rows, 128), 1)
    own = (row // STEPS == col // STEPS) & (col <= row)
    main = (col >= rows) & (col < rows + bound_ref[0])
    fresh_seen = jnp.concatenate([(own | main).astype(jnp.int32)] * GROUP, axis=0) > 0
    for g in range(KVH):
        query = jnp.concatenate([rotated((g * GROUP + h) * HD) for h in range(GROUP)], axis=0).astype(jnp.bfloat16)
        at_key = slice(g * HD, (g + 1) * HD)
        at_value = slice(KV_WIDTH + g * HD, KV_WIDTH + (g + 1) * HD)
        fresh_key = fresh_block([rotated(D + g * HD), kv_ref[:, at_key]])
        fresh_value = fresh_block([plain(D + KV_WIDTH + g * HD), kv_ref[:, at_value]])
        mixed = head_attention(
            query, cache_ref[:, at_key], cache_ref[:, at_value], fresh_key, fresh_value, seen, fresh_seen
        )
        mixed = mixed.astype(jnp.bfloat16)
        for h in range(GROUP):
            out_ref[:, (g * GROUP + h) * HD : (g * GROUP + h + 1) * HD] = mixed[h * rows : (h + 1) * rows]


def attend_cont(*args):
    return pl.pallas_call(
        attend_cont_kernel,
        out_shape=jax.ShapeDtypeStruct((CTOK, D), jnp.bfloat16),
        in_specs=[SMEM, SMEM] + [VMEM] * 4 + [whole((8, 2 * KV_WIDTH))] + [VMEM] * COL_BLOCKS,
        out_specs=whole((CTOK, D)),
        scratch_shapes=[
            pltpu.VMEM((CTOK, QKV), jnp.float32),
            pltpu.VMEM((COL_BLOCKS,) + args[-1].shape, jnp.bfloat16),
        ],
        compiler_params=kernel_params(),
        cost_estimate=cost(4 * 10**8, 8 * 10**6),
        name="attend_cont",
    )(*args)


def readout_kernel(head_ref, w_hbm, out_ref, w_ref, sem):
    copy = pltpu.make_async_copy(w_hbm.at[0], w_ref, sem)
    copy.start()
    row = head_ref[pl.ds(lax.rem(lax.axis_index("tp"), COL_BLOCKS), 1), :]
    high = row.astype(jnp.bfloat16).astype(jnp.float32)
    middle = (row - high).astype(jnp.bfloat16).astype(jnp.float32)
    low = row - high - middle
    pieces = jnp.concatenate([high, middle, low, jnp.zeros((13, row.shape[1]), jnp.float32)], axis=0)
    copy.wait()
    prod = lax.dot_general(
        pieces.astype(jnp.bfloat16), w_ref[...], (((1,), (1,)), ((), ())), preferred_element_type=jnp.float32
    )
    out_ref[...] = prod[0:1] + prod[1:2] + prod[2:3]


def readout(value_head, blocks):
    return pl.pallas_call(
        readout_kernel,
        out_shape=jax.ShapeDtypeStruct((1, FEATURES), jnp.float32),
        in_specs=[whole(value_head.shape), HBM],
        out_specs=whole((1, FEATURES)),
        scratch_shapes=[pltpu.VMEM((FEATURES, D // COL_BLOCKS), jnp.bfloat16), pltpu.SemaphoreType.DMA],
        compiler_params=kernel_params(),
        cost_estimate=cost(2 * 10**8, 5 * 10**6),
        name="readout",
    )(value_head, in_hbm(blocks))


def out_kernel(x_ref, read_ref, w_hbm, *refs):
    out_ref, rows_ref, wide_ref, read8_ref, w_ref, sems = refs[-6:]
    copies = weight_copies(OUT_PIECES, w_hbm, w_ref, sems)
    members = x_ref.shape[0]
    lines = members * STEPS
    halves = TILE // 128
    for j in range(FEATURES // TILE):
        read8_ref[j : j + 1, :] = read_ref[:, j * TILE : (j + 1) * TILE]
    out_ref[:, 8:, :] = jnp.broadcast_to(read8_ref[...][None], (members, 8, TILE))
    packed = x_ref[...].reshape(members * 16, TILE).astype(jnp.float32)
    for k in range(halves):
        wide_ref[k] = packed[:, k * 128 : (k + 1) * 128]
        for j in range(FEATURES // TILE):
            lane = j * TILE + k * 128
            rows_ref[:, lane : lane + 128] = wide_ref[k, pl.ds(j, lines, stride=8), :].astype(jnp.bfloat16)

    for (first, size), copy in zip(OUT_PIECES, copies):
        copy.wait()
        prod = jnp.dot(rows_ref[...], w_ref[:, first : first + size], preferred_element_type=jnp.float32)
        for start in range(0, size, 128):
            n, k = divmod((first + start) // 128, halves)
            wide_ref[k, pl.ds(n, lines, stride=4), :] = prod[:, start : start + 128]
    for k in range(halves):
        out_ref[:, :8, k * 128 : (k + 1) * 128] = wide_ref[k, : members * 8, :].reshape(members, 8, 128)


def out_product(rows, read, blocks, after):
    members = rows.shape[0]
    return pl.pallas_call(
        out_kernel,
        out_shape=jax.ShapeDtypeStruct((members, 16, TILE), jnp.float32),
        in_specs=[VMEM, VMEM, HBM] + [UNREAD] * len(after),
        out_specs=VMEM,
        scratch_shapes=[
            pltpu.VMEM((members * STEPS, FEATURES), jnp.bfloat16),
            pltpu.VMEM((TILE // 128, members * 16, 128), jnp.float32),
            pltpu.VMEM((8, TILE), jnp.float32),
            pltpu.VMEM(blocks.shape[1:], jnp.bfloat16),
            pltpu.SemaphoreType.DMA((len(OUT_PIECES),)),
        ],
        compiler_params=kernel_params(),
        cost_estimate=cost(3 * 10**8, 5 * 10**6),
        name="out_product",
    )(rows, read, in_hbm(blocks), *after)


def finish_kernel(parts_ref, main_ref, cont_ref, head_ref, mixed_ref, out_ref, score_ref, wide_ref):
    cols = D // COL_BLOCKS
    for c in range(COL_BLOCKS):
        total = summed_block(parts_ref, c, slice(0, TILE))
        for j in range(cols // TILE):
            at = slice(c * cols + j * TILE, c * cols + (j + 1) * TILE)
            for s in range(STEPS):
                wide_ref[s : s + 1, at] = total[s * 4 + j : s * 4 + j + 1]
    out_ref[...] = (main_ref[...].astype(jnp.float32) + wide_ref[:STEPS, :]).astype(jnp.bfloat16)
    score = jnp.zeros((CTOK, TILE), jnp.float32)
    direct = jnp.zeros((STEPS, TILE), jnp.float32)
    for r in range(ROW_BLOCKS):
        read = parts_ref[r * COL_BLOCKS, 8:, :]
        for c in range(1, COL_BLOCKS):
            read = read + parts_ref[r * COL_BLOCKS + c, 8:, :]
        for j in range(FEATURES // TILE):
            lanes = slice(r * FEATURES + j * TILE, r * FEATURES + (j + 1) * TILE)
            score = score + mixed_ref[:, lanes].astype(jnp.float32) * read[j : j + 1, :]
            for c in range(CONTS):
                direct = direct + cont_ref[c, :, lanes].astype(jnp.float32) * head_ref[:, lanes]
    total = jnp.sum(score, axis=0, keepdims=True) + jnp.sum(direct, axis=0, keepdims=True)
    score_ref[...] = jnp.broadcast_to(jnp.sum(total, axis=1, keepdims=True) / CONTS, (8, 128))


def finish(parts, main, cont, head, mixed):
    return pl.pallas_call(
        finish_kernel,
        out_shape=(
            jax.ShapeDtypeStruct((STEPS, D), jnp.bfloat16),
            jax.ShapeDtypeStruct((8, 128), jnp.float32),
        ),
        in_specs=[whole(parts.shape), whole(main.shape), whole(cont.shape), whole(head.shape), whole(mixed.shape)],
        out_specs=(whole((STEPS, D)), whole((8, 128))),
        scratch_shapes=[pltpu.VMEM((8, D), jnp.float32)],
        compiler_params=kernel_params(),
        cost_estimate=cost(10**6, 2 * 10**6),
        name="finish",
    )(parts, main, cont, head, mixed)


def rope_tables(positions):
    half = HD // 2
    frequency = THETA ** (-(jnp.arange(half, dtype=jnp.float32) * 2.0) / HD)
    angles = positions.astype(jnp.float32)[:, None] * frequency[None, :]
    cosine = jnp.cos(angles)
    sine = jnp.sin(angles)
    return jnp.concatenate([cosine, cosine], axis=1), jnp.concatenate([-sine, sine], axis=1)


def exchange(rows):
    return lax.all_to_all(rows, "tp", split_axis=0, concat_axis=0, tiled=True)


ALONG = [[z * COL_BLOCKS + c for z in range(ROW_BLOCKS)] for c in range(COL_BLOCKS)]


def from_side(rows, dy, dx):
    route = []
    for to in range(MEMBERS):
        z, y, x = to // 8, to // 4 % 2, to % 4
        route.append((z * 8 + (y + dy) % 2 * 4 + (x + dx) % 4, to))
    return lax.ppermute(rows, "tp", route)


def from_along(rows, dz):
    route = [((to + dz * COL_BLOCKS) % MEMBERS, to) for to in range(MEMBERS)]
    return lax.ppermute(rows, "tp", route)


FIRST_HOMES = ((0, 0), (1, 0), (0, 1), (0, 3))
SECOND_HOMES = ((1, 1), (1, 3), (0, 2), (1, 2))
HOMES = FIRST_HOMES + SECOND_HOMES


def project(rows, blocks, bias):
    near = lax.all_to_all(rows, "tp", split_axis=0, concat_axis=0, tiled=True, axis_index_groups=ALONG)
    over = from_side(near, 1, 0)
    after, before = from_side(near, 0, 1), from_side(near, 0, 3)
    over_after, over_before = from_side(over, 0, 1), from_side(over, 0, 3)
    far = [from_side(before, 0, 3), from_side(over_after, 0, 1)]
    *first, main = block_product([near, over, after, before], blocks)
    first = [first[0]] + [from_along(first[k], -k) for k in range(1, ROW_BLOCKS)]
    *second, main = block_product([over_after, over_before] + far, blocks, (main,), HOMES)
    main, first = lax.optimization_barrier((main, first))
    second = [second[0]] + [from_along(second[k], -k) for k in range(1, ROW_BLOCKS)]
    received = []
    for homes, parts in ((FIRST_HOMES, first), (SECOND_HOMES, second)):
        for (dy, dx), summed in zip(homes, sum_parts(bias, parts)):
            received.append(from_side(summed, -dy, -dx) if dy or dx else summed)
    return received, exchange(main), second[1:] + received[1:4]


def on_device(
    main_inputs, cont_inputs, prefix_cache, prefix_len, boundary, rms_gain, qkv_bias, w_qkv, w_out, value_head
):
    main = main_inputs.reshape(STEPS, D)
    cont = cont_inputs.reshape(CONTS, STEPS, D)
    bias = qkv_bias[None, :]
    cache = prefix_cache[0]
    head = value_head[None, :]
    step = jnp.arange(CTOK, dtype=jnp.int32) % STEPS
    main_tables = rope_tables(prefix_len + step[:8])
    cont_tables = rope_tables(prefix_len + boundary + step)
    read = readout(value_head.reshape(COL_BLOCKS, D // COL_BLOCKS), w_out)
    parts, main_parts, before = project(norm_rows(main, cont, rms_gain[None, :]), w_qkv, bias)
    mixed, main_kv = attend_main(prefix_len, bias, *main_tables, cache, main_parts, before + [read])
    mixed = exchange(mixed)
    cont_mixed = attend_cont(prefix_len, boundary, bias, *cont_tables, cache, main_kv, *parts)
    parts = exchange(out_product(mixed, read, w_out, parts[4:6]))
    main_out, score = finish(parts, main, cont, head, cont_mixed)
    return main_out[None], score[0, :1]


def solution(mesh):
    return jax.shard_map(
        on_device,
        mesh=mesh,
        in_specs=(
            P(("grp", "tp"), None, None),
            P(("grp", "tp"), None, None, None),
            P(("grp", "tp"), None, None),
            P(("grp", "tp")),
            P(("grp", "tp")),
            P(),
            P(),
            P("tp", None, None),
            P("tp", None, None),
            P(),
        ),
        out_specs=(P(("grp", "tp"), None, None), P(("grp", "tp"))),
        check_vma=False,
    )
```

```python
import functools
import math

import jax
import jax.numpy as jnp
from jax import lax
from jax.experimental import pallas as pl
from jax.experimental.pallas import tpu as pltpu
from jax.sharding import PartitionSpec as P

KVH = 8
HD = 128
D = 8192
QKV = 10240
ROW_BLOCKS = 4
COL_BLOCKS = 8
MEMBERS = ROW_BLOCKS * COL_BLOCKS
FEATURES = D // ROW_BLOCKS
CONTS = 8
STEPS = 2
CTOK = CONTS * STEPS
TILE = 256

THETA = 1000000.0
EPS = 1e-06
MASKED_SCORE = -1e30

VMEM_LIMIT = 28 * 1024 * 1024
VMEM = pl.BlockSpec(memory_space=pltpu.VMEM)
SMEM = pl.BlockSpec(memory_space=pltpu.SMEM)
HBM = pl.BlockSpec(memory_space=pltpu.HBM)
UNREAD = pl.BlockSpec(memory_space=pl.ANY)


def whole(shape):
    return pl.BlockSpec(shape, lambda *_: (0,) * len(shape))


def cost(flops, moved):
    return pl.CostEstimate(flops=flops, bytes_accessed=moved, transcendentals=0)


def in_hbm(array):
    return pltpu.with_memory_space_constraint(array, pltpu.HBM)


def kernel_params():
    return pltpu.CompilerParams(vmem_limit_bytes=VMEM_LIMIT)


def norm_kernel(main_hbm, cont_hbm, gain_hbm, out_ref, main_ref, cont_ref, gain_ref, rows_ref, piece_ref, sems):
    pairs = ((main_hbm, main_ref), (cont_hbm, cont_ref), (gain_hbm, gain_ref))
    copies = [pltpu.make_async_copy(src, dst, sems.at[i]) for i, (src, dst) in enumerate(pairs)]
    for copy in copies:
        copy.start()
    for copy in copies:
        copy.wait()

    def normed(wide):
        inv = lax.rsqrt(jnp.mean(wide * wide, axis=-1, keepdims=True) + EPS)
        return wide * inv * gain_ref[...]

    for c in range(CONTS):
        rows_ref[c * STEPS : (c + 1) * STEPS, :] = cont_ref[c].astype(jnp.float32)
    cont = normed(rows_ref[...]).astype(jnp.bfloat16)
    main = normed(main_ref[...].astype(jnp.float32))
    for r in range(ROW_BLOCKS):
        for j in range(FEATURES // TILE):
            lanes = slice(r * FEATURES + j * TILE, r * FEATURES + (j + 1) * TILE)
            for s in range(STEPS):
                piece_ref[r, s * 8 + j : s * 8 + j + 1, :] = main[s : s + 1, lanes]
    for r in range(ROW_BLOCKS):
        piece = piece_ref[r].astype(jnp.bfloat16)
        out_ref[r, :, :FEATURES] = cont[:, r * FEATURES : (r + 1) * FEATURES]
        out_ref[r, :, FEATURES:] = piece


def norm_rows(main, cont, gain):
    return pl.pallas_call(
        norm_kernel,
        out_shape=jax.ShapeDtypeStruct((ROW_BLOCKS, CTOK, FEATURES + TILE), jnp.bfloat16),
        in_specs=[HBM] * 3,
        out_specs=VMEM,
        scratch_shapes=[
            pltpu.VMEM((STEPS, D), jnp.bfloat16),
            pltpu.VMEM((CONTS, STEPS, D), jnp.bfloat16),
            pltpu.VMEM((1, D), jnp.float32),
            pltpu.VMEM((CTOK, D), jnp.float32),
            pltpu.VMEM((ROW_BLOCKS, 16, TILE), jnp.float32),
            pltpu.SemaphoreType.DMA((3,)),
        ],
        compiler_params=kernel_params(),
        cost_estimate=cost(10**6, 4 * 10**6),
        name="norm_rows",
    )(in_hbm(main), in_hbm(cont), in_hbm(gain))


def weight_tile(n, tiles, w_hbm, w_ref, sems):
    def copy(i):
        lanes = pl.ds(pl.multiple_of(i * TILE, TILE), TILE)
        return pltpu.make_async_copy(w_hbm.at[0, :, lanes], w_ref.at[i], sems.at[i])

    @pl.when(n == 0)
    def _():
        for i in range(tiles):
            copy(i).start()

    return copy(n)


REST = 768


def rest_tile(block):
    return jnp.where(block == 6, 2, 0)


def plane_place():
    column = lax.rem(lax.axis_index("tp"), COL_BLOCKS)
    return column // 4, lax.rem(column, 4)


def product_kernel(tiles, counts, places, *refs):
    x_refs, refs = refs[: len(counts)], refs[len(counts) :]
    if places:
        earlier_ref, w_ref, *out_refs = refs[: 2 + ROW_BLOCKS]
        main_ref, rows_ref, wide_ref, part_ref = refs[2 + ROW_BLOCKS :]
    else:
        w_hbm, *out_refs = refs[: 1 + ROW_BLOCKS]
        main_ref, w_ref, rows_ref, wide_ref, part_ref, sems = refs[1 + ROW_BLOCKS :]
    n = pl.program_id(0)
    members = sum(counts)
    count = members * CTOK
    lines = members * STEPS
    halves = TILE // 128
    width = tiles * TILE
    if not places:
        tile = weight_tile(n, tiles, w_hbm, w_ref, sems)

    @pl.when(n == 0)
    def _():
        at = 0
        for x_ref, size in zip(x_refs, counts):
            rows = slice(at * CTOK, (at + size) * CTOK)
            rows_ref[rows, :] = x_ref[:, :, :FEATURES].reshape(size * CTOK, FEATURES)
            packed = x_ref[:, :, FEATURES:].reshape(size * CTOK, TILE).astype(jnp.float32)
            for k in range(halves):
                wide_ref[k, rows, :] = packed[:, k * 128 : (k + 1) * 128]
            at += size
        for k in range(halves):
            for j in range(FEATURES // TILE):
                lane = j * TILE + k * 128
                rows_ref[count:, lane : lane + 128] = wide_ref[k, pl.ds(j, lines, stride=8), :].astype(jnp.bfloat16)

    if not places:
        tile.wait()
    prod = jnp.dot(rows_ref[...], w_ref[n], preferred_element_type=jnp.float32)
    high = prod.astype(jnp.bfloat16)
    part_ref[:, :, pl.ds(pl.multiple_of(n * TILE, TILE), TILE)] = high[:count].reshape(members, CTOK, TILE)
    for k in range(halves):
        wide_ref[k, pl.ds(n, lines, stride=8), :] = prod[count:, k * 128 : (k + 1) * 128]
    start = rest_tile(lax.rem(lax.axis_index("tp"), COL_BLOCKS))

    @pl.when((n >= start) & (n < start + REST // TILE))
    def _():
        low = prod - high.astype(jnp.float32)
        place = n - start
        lane = pl.multiple_of(width + place * TILE, TILE)
        part_ref[:, :, pl.ds(lane, TILE)] = low[:count].astype(jnp.bfloat16).reshape(members, CTOK, TILE)
        for k in range(halves):
            wide_ref[k, pl.ds(tiles + place, lines, stride=8), :] = low[count:, k * 128 : (k + 1) * 128]

    @pl.when(n == tiles - 1)
    def _():
        z = lax.axis_index("tp") // COL_BLOCKS
        done = earlier_ref.shape[0] // ROW_BLOCKS if places else 0
        for k in range(halves):
            lanes = slice(k * 128, (k + 1) * 128)
            packed = wide_ref[k].astype(jnp.bfloat16).reshape(members, CTOK, 128)
            if not places:
                main_ref[:, :, lanes] = packed
            for i, (dy, dx) in enumerate(places):
                y, x = plane_place()
                column = lax.rem(y + dy, 2) * 4 + lax.rem(x + dx, 4)
                for r in range(ROW_BLOCKS):
                    if i < done:
                        message = earlier_ref[i * ROW_BLOCKS + r, :, lanes]
                    else:
                        message = packed[(i - done) * ROW_BLOCKS + r]
                    main_ref[r * COL_BLOCKS + column, :, lanes] = message
        for k, out_ref in enumerate(out_refs):
            to = lax.rem(z + k, ROW_BLOCKS)
            for g in range(members // ROW_BLOCKS):
                out_ref[g] = part_ref[g * ROW_BLOCKS + to]


def block_product(messages, weight, earlier=None, places=()):
    tiles = QKV // COL_BLOCKS // TILE
    lanes = tiles * TILE + REST
    counts = tuple(rows.shape[0] for rows in messages)
    members = sum(counts)
    out = [jax.ShapeDtypeStruct((members // ROW_BLOCKS, CTOK, lanes), jnp.bfloat16)] * ROW_BLOCKS
    out.append(jax.ShapeDtypeStruct((MEMBERS if places else members, CTOK, TILE), jnp.bfloat16))
    scratch = [
        pltpu.VMEM((members * (CTOK + STEPS), FEATURES), jnp.bfloat16),
        pltpu.VMEM((TILE // 128, members * CTOK, 128), jnp.float32),
        pltpu.VMEM((members, CTOK, lanes), jnp.bfloat16),
    ]
    if places:
        operands = list(messages) + [earlier, weight]
        in_specs = [VMEM] * len(operands)
    else:
        operands = list(messages) + [in_hbm(weight)]
        in_specs = [VMEM] * len(messages) + [HBM]
        out.append(jax.ShapeDtypeStruct((tiles, FEATURES, TILE), jnp.bfloat16))
        scratch.append(pltpu.SemaphoreType.DMA((tiles,)))
    return pl.pallas_call(
        functools.partial(product_kernel, tiles, counts, places),
        out_shape=out,
        grid=(tiles,),
        in_specs=in_specs,
        out_specs=[VMEM] * len(out),
        scratch_shapes=scratch,
        compiler_params=kernel_params(),
        cost_estimate=cost(2 * members * (CTOK + STEPS) * FEATURES * tiles * TILE, 12 * 10**6),
        name="block_product",
    )(*operands)


def sum_kernel(bias_ref, *refs):
    part_refs, out_refs = refs[:ROW_BLOCKS], refs[ROW_BLOCKS:]
    column = lax.rem(lax.axis_index("tp"), COL_BLOCKS)
    late = column == 6
    last = (column == COL_BLOCKS - 1).astype(jnp.float32)
    cols = QKV // COL_BLOCKS
    tiles = cols // TILE
    kept = REST // TILE
    zero = jnp.zeros((CTOK, TILE), jnp.float32)

    def value_bias(j):
        if j == 0:
            return jnp.zeros((1, TILE), jnp.float32)
        at = QKV - cols + j * TILE
        return bias_ref[:, at : at + TILE] * last

    for g, out_ref in enumerate(out_refs):

        def total(lane):
            value = part_refs[0][g, :, lane : lane + TILE].astype(jnp.float32)
            for ref in part_refs[1:]:
                value = value + ref[g, :, lane : lane + TILE].astype(jnp.float32)
            return value

        rest = [total(cols + i * TILE) for i in range(kept)] + [zero] * (tiles - kept)
        lows = []
        for j in range(tiles):
            shifted = rest[j - tiles + kept] if j >= tiles - kept else zero
            value = total(j * TILE) + jnp.where(late, shifted, rest[j]) + value_bias(j)
            high = value.astype(jnp.bfloat16)
            out_ref[:, j * TILE : (j + 1) * TILE] = high
            lows.append(value - high.astype(jnp.float32))
        for i in range(kept):
            low = jnp.where(late, lows[i + tiles - kept], lows[i])
            out_ref[:, cols + i * TILE : cols + (i + 1) * TILE] = low.astype(jnp.bfloat16)


def sum_parts(bias, parts):
    groups, rows, lanes = parts[0].shape
    return pl.pallas_call(
        sum_kernel,
        out_shape=[jax.ShapeDtypeStruct((rows, lanes), jnp.bfloat16)] * groups,
        in_specs=[VMEM] * (1 + len(parts)),
        out_specs=[VMEM] * groups,
        compiler_params=kernel_params(),
        cost_estimate=cost(10**6, 3 * 10**6),
        name="sum_parts",
    )(bias, *parts)


def load_parts(part_refs, parts_ref):
    y, x = plane_place()
    for ref, (dy, dx) in zip(part_refs, HOMES):
        column = lax.rem(y + dy, 2) * 4 + lax.rem(x + 4 - dx, 4)
        parts_ref[column] = ref[...]


def summed_block(parts_ref, c, lanes):
    total = parts_ref[c, :, lanes].astype(jnp.float32)
    for r in range(1, ROW_BLOCKS):
        total = total + parts_ref[r * COL_BLOCKS + c, :, lanes].astype(jnp.float32)
    return total


def head_attention(query, key, value, fresh_key, fresh_value, seen, fresh_seen):
    inv_root = 1.0 / math.sqrt(HD)
    contract = (((1,), (1,)), ((), ()))
    old = lax.dot_general(query, key, contract, preferred_element_type=jnp.float32) * inv_root
    new = lax.dot_general(query, fresh_key, contract, preferred_element_type=jnp.float32) * inv_root
    old = jnp.where(seen, old, MASKED_SCORE)
    new = jnp.where(fresh_seen, new, MASKED_SCORE)
    highest = jnp.maximum(jnp.max(old, axis=-1, keepdims=True), jnp.max(new, axis=-1, keepdims=True))
    old = jnp.exp(old - highest)
    new = jnp.exp(new - highest)
    mass = jnp.sum(old, axis=-1, keepdims=True) + jnp.sum(new, axis=-1, keepdims=True)
    inv_mass = 1.0 / mass
    mixed = jnp.dot((old * inv_mass).astype(jnp.bfloat16), value, preferred_element_type=jnp.float32)
    return mixed + jnp.dot((new * inv_mass).astype(jnp.bfloat16), fresh_value, preferred_element_type=jnp.float32)


def load_qkv(main, parts_ref, qkv_ref):
    cols = QKV // COL_BLOCKS
    for c in range(COL_BLOCKS):
        first = 2 if c == 6 else 0
        total = summed_block(parts_ref, c, slice(0, TILE)) if main else parts_ref[c].astype(jnp.float32)
        for j in range(cols // TILE):
            lanes = slice(c * cols + j * TILE, c * cols + (j + 1) * TILE)
            rest = j - first
            has_rest = 0 <= rest < REST // TILE
            if main:
                for s in range(STEPS):
                    line = total[s * 8 + j : s * 8 + j + 1]
                    if has_rest:
                        at = s * 8 + cols // TILE + rest
                        line = line + total[at : at + 1]
                    qkv_ref[s : s + 1, lanes] = line
            else:
                value = total[:, j * TILE : (j + 1) * TILE]
                if has_rest:
                    value = value + total[:, cols + rest * TILE : cols + (rest + 1) * TILE]
                qkv_ref[:, lanes] = value


def head_readers(qkv_ref, bias_ref, cos_ref, sin_ref):
    cosine = cos_ref[...]
    sine = sin_ref[...]

    def plain(start):
        return qkv_ref[:, start : start + HD]

    def rotated(start):
        head = plain(start) + bias_ref[:, start : start + HD]
        return head * cosine + pltpu.roll(head, HD // 2, 1) * sine

    return plain, rotated


def fresh_block(pieces):
    rows = sum(piece.shape[0] for piece in pieces)
    pad = jnp.zeros((128 - rows, HD), jnp.float32)
    return jnp.concatenate(list(pieces) + [pad], axis=0).astype(jnp.bfloat16)


GROUP = D // HD // KVH
KV_WIDTH = KVH * HD


def attend_main_kernel(
    len_ref, bias_ref, cos_ref, sin_ref, cache_ref, parts_ref, *refs
):
    out_ref, kv_ref, qkv_ref, piece_ref = refs[-4:]
    rows = qkv_ref.shape[0]
    qkv_ref[...] = jnp.zeros(qkv_ref.shape, jnp.float32)
    load_qkv(True, parts_ref, qkv_ref)
    qkv_ref[:, D + KV_WIDTH :] = qkv_ref[:, D + KV_WIDTH :] + bias_ref[:, D + KV_WIDTH :]
    plain, rotated = head_readers(qkv_ref, bias_ref, cos_ref, sin_ref)
    seen = lax.broadcasted_iota(jnp.int32, (1, cache_ref.shape[0]), 1) < len_ref[0]
    row = lax.broadcasted_iota(jnp.int32, (rows, 128), 0)
    col = lax.broadcasted_iota(jnp.int32, (rows, 128), 1)
    own = ((col <= row) & (col < STEPS)).astype(jnp.int32)
    fresh_seen = jnp.concatenate([own] * GROUP, axis=0) > 0
    for g in range(KVH):
        query = jnp.concatenate([rotated((g * GROUP + h) * HD) for h in range(GROUP)], axis=0).astype(jnp.bfloat16)
        fresh_key = rotated(D + g * HD)
        fresh_value = plain(D + KV_WIDTH + g * HD)
        kv_ref[:, g * HD : (g + 1) * HD] = fresh_key
        kv_ref[:, KV_WIDTH + g * HD : KV_WIDTH + (g + 1) * HD] = fresh_value
        key = cache_ref[:, g * HD : (g + 1) * HD]
        value = cache_ref[:, KV_WIDTH + g * HD : KV_WIDTH + (g + 1) * HD]
        mixed = head_attention(
            query, key, value, fresh_block([fresh_key]), fresh_block([fresh_value]), seen, fresh_seen
        )
        for h in range(GROUP):
            r, place = divmod(g * GROUP + h, FEATURES // HD)
            j, lane = place // 2, (place % 2) * HD
            for s in range(STEPS):
                at = s * 8 + j
                piece_ref[r, at : at + 1, lane : lane + HD] = mixed[h * rows + s : h * rows + s + 1]
    for r in range(ROW_BLOCKS):
        piece = piece_ref[r].astype(jnp.bfloat16)
        for c in range(COL_BLOCKS):
            out_ref[r * COL_BLOCKS + c] = piece


def attend_main(prefix_len, bias, cosine, sine, cache, parts, after):
    return pl.pallas_call(
        attend_main_kernel,
        out_shape=(
            jax.ShapeDtypeStruct((32, 16, TILE), jnp.bfloat16),
            jax.ShapeDtypeStruct((8, 2 * KV_WIDTH), jnp.float32),
        ),
        in_specs=[SMEM] + [VMEM] * 5 + [UNREAD] * len(after),
        out_specs=(whole((32, 16, TILE)), whole((8, 2 * KV_WIDTH))),
        scratch_shapes=[
            pltpu.VMEM((8, QKV), jnp.float32),
            pltpu.VMEM((ROW_BLOCKS, 16, TILE), jnp.float32),
        ],
        compiler_params=kernel_params(),
        cost_estimate=cost(2 * 10**8, 6 * 10**6),
        name="attend_main",
    )(prefix_len, bias, cosine, sine, cache, parts, *after)


def attend_cont_kernel(len_ref, bound_ref, bias_ref, cos_ref, sin_ref, cache_ref, kv_ref, *refs):
    part_refs = refs[:COL_BLOCKS]
    out_ref, qkv_ref, parts_ref = refs[COL_BLOCKS:]
    load_parts(part_refs, parts_ref)
    rows = qkv_ref.shape[0]
    load_qkv(False, parts_ref, qkv_ref)
    plain, rotated = head_readers(qkv_ref, bias_ref, cos_ref, sin_ref)
    seen = lax.broadcasted_iota(jnp.int32, (1, cache_ref.shape[0]), 1) < len_ref[0]
    row = lax.broadcasted_iota(jnp.int32, (rows, 128), 0)
    col = lax.broadcasted_iota(jnp.int32, (rows, 128), 1)
    own = (row // STEPS == col // STEPS) & (col <= row)
    main = (col >= rows) & (col < rows + bound_ref[0])
    fresh_seen = jnp.concatenate([(own | main).astype(jnp.int32)] * GROUP, axis=0) > 0
    for g in range(KVH):
        query = jnp.concatenate([rotated((g * GROUP + h) * HD) for h in range(GROUP)], axis=0).astype(jnp.bfloat16)
        at_key = slice(g * HD, (g + 1) * HD)
        at_value = slice(KV_WIDTH + g * HD, KV_WIDTH + (g + 1) * HD)
        fresh_key = fresh_block([rotated(D + g * HD), kv_ref[:, at_key]])
        fresh_value = fresh_block([plain(D + KV_WIDTH + g * HD), kv_ref[:, at_value]])
        mixed = head_attention(
            query, cache_ref[:, at_key], cache_ref[:, at_value], fresh_key, fresh_value, seen, fresh_seen
        )
        mixed = mixed.astype(jnp.bfloat16)
        for h in range(GROUP):
            out_ref[:, (g * GROUP + h) * HD : (g * GROUP + h + 1) * HD] = mixed[h * rows : (h + 1) * rows]


def attend_cont(*args):
    return pl.pallas_call(
        attend_cont_kernel,
        out_shape=jax.ShapeDtypeStruct((CTOK, D), jnp.bfloat16),
        in_specs=[SMEM, SMEM] + [VMEM] * 4 + [whole((8, 2 * KV_WIDTH))] + [VMEM] * COL_BLOCKS,
        out_specs=whole((CTOK, D)),
        scratch_shapes=[
            pltpu.VMEM((CTOK, QKV), jnp.float32),
            pltpu.VMEM((COL_BLOCKS,) + args[-1].shape, jnp.bfloat16),
        ],
        compiler_params=kernel_params(),
        cost_estimate=cost(4 * 10**8, 8 * 10**6),
        name="attend_cont",
    )(*args)


def readout_kernel(head_ref, w_hbm, out_ref, w_ref, sems):
    tiles = w_ref.shape[0]
    copies = []
    for i in range(tiles):
        copies.append(
            pltpu.make_async_copy(w_hbm.at[0, :, i * TILE : (i + 1) * TILE], w_ref.at[i], sems.at[i])
        )
        copies[-1].start()
    row = head_ref[pl.ds(lax.rem(lax.axis_index("tp"), COL_BLOCKS), 1), :]
    high = row.astype(jnp.bfloat16).astype(jnp.float32)
    middle = (row - high).astype(jnp.bfloat16).astype(jnp.float32)
    low = row - high - middle
    pieces = jnp.concatenate([high, middle, low, jnp.zeros((13, row.shape[1]), jnp.float32)], axis=0)
    pieces = pieces.astype(jnp.bfloat16)
    total = jnp.zeros((1, FEATURES), jnp.float32)
    for i, copy in enumerate(copies):
        copy.wait()
        prod = lax.dot_general(
            pieces[:, i * TILE : (i + 1) * TILE],
            w_ref[i],
            (((1,), (1,)), ((), ())),
            preferred_element_type=jnp.float32,
        )
        total = total + (prod[0:1] + prod[1:2] + prod[2:3])
    out_ref[...] = total


def readout(value_head, blocks):
    tiles = blocks.shape[2] // TILE
    return pl.pallas_call(
        readout_kernel,
        out_shape=(
            jax.ShapeDtypeStruct((1, FEATURES), jnp.float32),
            jax.ShapeDtypeStruct((tiles, FEATURES, TILE), jnp.bfloat16),
        ),
        in_specs=[VMEM, HBM],
        out_specs=(VMEM, VMEM),
        scratch_shapes=[pltpu.SemaphoreType.DMA((tiles,))],
        compiler_params=kernel_params(),
        cost_estimate=cost(2 * 10**8, 5 * 10**6),
        name="readout",
    )(value_head, in_hbm(blocks))


def out_kernel(tiles, x_ref, read_ref, w_ref, *refs):
    out_ref, rows_ref, wide_ref, read8_ref = refs[-4:]
    n = pl.program_id(0)
    members = x_ref.shape[0]
    lines = members * STEPS
    halves = TILE // 128

    @pl.when(n == 0)
    def _():
        for j in range(FEATURES // TILE):
            read8_ref[j : j + 1, :] = read_ref[:, j * TILE : (j + 1) * TILE]
        out_ref[:, 8:, :] = jnp.broadcast_to(read8_ref[...][None], (members, 8, TILE))
        packed = x_ref[...].reshape(members * 16, TILE).astype(jnp.float32)
        for k in range(halves):
            wide_ref[k] = packed[:, k * 128 : (k + 1) * 128]
            for j in range(FEATURES // TILE):
                lane = j * TILE + k * 128
                rows_ref[:, lane : lane + 128] = wide_ref[k, pl.ds(j, lines, stride=8), :].astype(jnp.bfloat16)

    prod = jnp.dot(rows_ref[...], w_ref[n], preferred_element_type=jnp.float32)
    for k in range(halves):
        wide_ref[k, pl.ds(n, lines, stride=4), :] = prod[:, k * 128 : (k + 1) * 128]

    @pl.when(n == tiles - 1)
    def _():
        for k in range(halves):
            packed = wide_ref[k, : members * 8, :].reshape(members, 8, 128)
            out_ref[:, :8, k * 128 : (k + 1) * 128] = packed


def out_product(rows, read, weight, after):
    members = rows.shape[0]
    tiles = weight.shape[0]
    return pl.pallas_call(
        functools.partial(out_kernel, tiles),
        out_shape=jax.ShapeDtypeStruct((members, 16, TILE), jnp.float32),
        grid=(tiles,),
        in_specs=[VMEM] * 3 + [UNREAD] * len(after),
        out_specs=VMEM,
        scratch_shapes=[
            pltpu.VMEM((members * STEPS, FEATURES), jnp.bfloat16),
            pltpu.VMEM((TILE // 128, members * 16, 128), jnp.float32),
            pltpu.VMEM((8, TILE), jnp.float32),
        ],
        compiler_params=kernel_params(),
        cost_estimate=cost(3 * 10**8, 5 * 10**6),
        name="out_product",
    )(rows, read, weight, *after)


def finish_kernel(parts_ref, main_ref, cont_ref, head_ref, mixed_ref, out_ref, score_ref, wide_ref):
    cols = D // COL_BLOCKS
    for c in range(COL_BLOCKS):
        total = summed_block(parts_ref, c, slice(0, TILE))
        for j in range(cols // TILE):
            at = slice(c * cols + j * TILE, c * cols + (j + 1) * TILE)
            for s in range(STEPS):
                wide_ref[s : s + 1, at] = total[s * 4 + j : s * 4 + j + 1]
    out_ref[...] = (main_ref[...].astype(jnp.float32) + wide_ref[:STEPS, :]).astype(jnp.bfloat16)
    score = jnp.zeros((CTOK, TILE), jnp.float32)
    direct = jnp.zeros((STEPS, TILE), jnp.float32)
    for r in range(ROW_BLOCKS):
        read = parts_ref[r * COL_BLOCKS, 8:, :]
        for c in range(1, COL_BLOCKS):
            read = read + parts_ref[r * COL_BLOCKS + c, 8:, :]
        for j in range(FEATURES // TILE):
            lanes = slice(r * FEATURES + j * TILE, r * FEATURES + (j + 1) * TILE)
            score = score + mixed_ref[:, lanes].astype(jnp.float32) * read[j : j + 1, :]
            for c in range(CONTS):
                direct = direct + cont_ref[c, :, lanes].astype(jnp.float32) * head_ref[:, lanes]
    total = jnp.sum(score, axis=0, keepdims=True) + jnp.sum(direct, axis=0, keepdims=True)
    score_ref[...] = jnp.broadcast_to(jnp.sum(total, axis=1, keepdims=True) / CONTS, (8, 128))


def finish(parts, main, cont, head, mixed):
    return pl.pallas_call(
        finish_kernel,
        out_shape=(
            jax.ShapeDtypeStruct((STEPS, D), jnp.bfloat16),
            jax.ShapeDtypeStruct((8, 128), jnp.float32),
        ),
        in_specs=[whole(parts.shape), whole(main.shape), whole(cont.shape), whole(head.shape), whole(mixed.shape)],
        out_specs=(whole((STEPS, D)), whole((8, 128))),
        scratch_shapes=[pltpu.VMEM((8, D), jnp.float32)],
        compiler_params=kernel_params(),
        cost_estimate=cost(10**6, 2 * 10**6),
        name="finish",
    )(parts, main, cont, head, mixed)


def rope_tables(positions):
    half = HD // 2
    frequency = THETA ** (-(jnp.arange(half, dtype=jnp.float32) * 2.0) / HD)
    angles = positions.astype(jnp.float32)[:, None] * frequency[None, :]
    cosine = jnp.cos(angles)
    sine = jnp.sin(angles)
    return jnp.concatenate([cosine, cosine], axis=1), jnp.concatenate([-sine, sine], axis=1)


def exchange(rows):
    return lax.all_to_all(rows, "tp", split_axis=0, concat_axis=0, tiled=True)


ALONG = [[z * COL_BLOCKS + c for z in range(ROW_BLOCKS)] for c in range(COL_BLOCKS)]


def from_side(rows, dy, dx):
    route = []
    for to in range(MEMBERS):
        z, y, x = to // 8, to // 4 % 2, to % 4
        route.append((z * 8 + (y + dy) % 2 * 4 + (x + dx) % 4, to))
    return lax.ppermute(rows, "tp", route)


def from_along(rows, dz):
    route = [((to + dz * COL_BLOCKS) % MEMBERS, to) for to in range(MEMBERS)]
    return lax.ppermute(rows, "tp", route)


FIRST_HOMES = ((0, 0), (1, 0), (0, 1), (0, 3))
SECOND_HOMES = ((1, 1), (1, 3), (0, 2), (1, 2))
HOMES = FIRST_HOMES + SECOND_HOMES


def project(rows, blocks, bias):
    near = lax.all_to_all(rows, "tp", split_axis=0, concat_axis=0, tiled=True, axis_index_groups=ALONG)
    over = from_side(near, 1, 0)
    after, before = from_side(near, 0, 1), from_side(near, 0, 3)
    over_after, over_before = from_side(over, 0, 1), from_side(over, 0, 3)
    far = [from_side(before, 0, 3), from_side(over_after, 0, 1)]
    *first, main, weight = block_product([near, over, after, before], blocks)
    first = [first[0]] + [from_along(first[k], -k) for k in range(1, ROW_BLOCKS)]
    *second, main = block_product([over_after, over_before] + far, weight, main, HOMES)
    main, first = lax.optimization_barrier((main, first))
    second = [second[0]] + [from_along(second[k], -k) for k in range(1, ROW_BLOCKS)]
    received = []
    for homes, parts in ((FIRST_HOMES, first), (SECOND_HOMES, second)):
        for (dy, dx), summed in zip(homes, sum_parts(bias, parts)):
            received.append(from_side(summed, -dy, -dx) if dy or dx else summed)
    return received, exchange(main), second[1:] + received[1:4]


def on_device(
    main_inputs, cont_inputs, prefix_cache, prefix_len, boundary, rms_gain, qkv_bias, w_qkv, w_out, value_head
):
    main = main_inputs.reshape(STEPS, D)
    cont = cont_inputs.reshape(CONTS, STEPS, D)
    bias = qkv_bias[None, :]
    cache = prefix_cache[0]
    head = value_head[None, :]
    step = jnp.arange(CTOK, dtype=jnp.int32) % STEPS
    main_tables = rope_tables(prefix_len + step[:8])
    cont_tables = rope_tables(prefix_len + boundary + step)
    read, out_weight = readout(value_head.reshape(COL_BLOCKS, D // COL_BLOCKS), w_out)
    parts, main_parts, before = project(norm_rows(main, cont, rms_gain[None, :]), w_qkv, bias)
    mixed, main_kv = attend_main(prefix_len, bias, *main_tables, cache, main_parts, before + [read])
    mixed = exchange(mixed)
    cont_mixed = attend_cont(prefix_len, boundary, bias, *cont_tables, cache, main_kv, *parts)
    parts = exchange(out_product(mixed, read, out_weight, parts[4:6]))
    main_out, score = finish(parts, main, cont, head, cont_mixed)
    return main_out[None], score[0, :1]


def solution(mesh):
    return jax.shard_map(
        on_device,
        mesh=mesh,
        in_specs=(
            P(("grp", "tp"), None, None),
            P(("grp", "tp"), None, None, None),
            P(("grp", "tp"), None, None),
            P(("grp", "tp")),
            P(("grp", "tp")),
            P(),
            P(),
            P("tp", None, None),
            P("tp", None, None),
            P(),
        ),
        out_specs=(P(("grp", "tp"), None, None), P(("grp", "tp"))),
        check_vma=False,
    )
```

```python
import functools
import math

import jax
import jax.numpy as jnp
from jax import lax
from jax.experimental import pallas as pl
from jax.experimental.pallas import tpu as pltpu
from jax.sharding import PartitionSpec as P

KVH = 8
HD = 128
D = 8192
QKV = 10240
ROW_BLOCKS = 4
COL_BLOCKS = 8
MEMBERS = ROW_BLOCKS * COL_BLOCKS
FEATURES = D // ROW_BLOCKS
CONTS = 8
STEPS = 2
CTOK = CONTS * STEPS
TILE = 256

THETA = 1000000.0
EPS = 1e-06
MASKED_SCORE = -1e30

VMEM_LIMIT = 28 * 1024 * 1024
VMEM = pl.BlockSpec(memory_space=pltpu.VMEM)
SMEM = pl.BlockSpec(memory_space=pltpu.SMEM)
HBM = pl.BlockSpec(memory_space=pltpu.HBM)
UNREAD = pl.BlockSpec(memory_space=pl.ANY)


def whole(shape):
    return pl.BlockSpec(shape, lambda *_: (0,) * len(shape))


def cost(flops, moved):
    return pl.CostEstimate(flops=flops, bytes_accessed=moved, transcendentals=0)


def in_hbm(array):
    return pltpu.with_memory_space_constraint(array, pltpu.HBM)


def kernel_params():
    return pltpu.CompilerParams(vmem_limit_bytes=VMEM_LIMIT)


def norm_kernel(main_hbm, cont_hbm, gain_hbm, out_ref, main_ref, cont_ref, gain_ref, rows_ref, piece_ref, sems):
    pairs = ((main_hbm, main_ref), (cont_hbm, cont_ref), (gain_hbm, gain_ref))
    copies = [pltpu.make_async_copy(src, dst, sems.at[i]) for i, (src, dst) in enumerate(pairs)]
    for copy in copies:
        copy.start()
    for copy in copies:
        copy.wait()

    def normed(wide):
        inv = lax.rsqrt(jnp.mean(wide * wide, axis=-1, keepdims=True) + EPS)
        return wide * inv * gain_ref[...]

    for c in range(CONTS):
        rows_ref[c * STEPS : (c + 1) * STEPS, :] = cont_ref[c].astype(jnp.float32)
    cont = normed(rows_ref[...]).astype(jnp.bfloat16)
    main = normed(main_ref[...].astype(jnp.float32))
    for r in range(ROW_BLOCKS):
        for j in range(FEATURES // TILE):
            lanes = slice(r * FEATURES + j * TILE, r * FEATURES + (j + 1) * TILE)
            for s in range(STEPS):
                piece_ref[r, s * 8 + j : s * 8 + j + 1, :] = main[s : s + 1, lanes]
    for r in range(ROW_BLOCKS):
        piece = piece_ref[r].astype(jnp.bfloat16)
        out_ref[r, :, :FEATURES] = cont[:, r * FEATURES : (r + 1) * FEATURES]
        out_ref[r, :, FEATURES:] = piece


def norm_rows(main, cont, gain):
    return pl.pallas_call(
        norm_kernel,
        out_shape=jax.ShapeDtypeStruct((ROW_BLOCKS, CTOK, FEATURES + TILE), jnp.bfloat16),
        in_specs=[HBM] * 3,
        out_specs=VMEM,
        scratch_shapes=[
            pltpu.VMEM((STEPS, D), jnp.bfloat16),
            pltpu.VMEM((CONTS, STEPS, D), jnp.bfloat16),
            pltpu.VMEM((1, D), jnp.float32),
            pltpu.VMEM((CTOK, D), jnp.float32),
            pltpu.VMEM((ROW_BLOCKS, 16, TILE), jnp.float32),
            pltpu.SemaphoreType.DMA((3,)),
        ],
        compiler_params=kernel_params(),
        cost_estimate=cost(10**6, 4 * 10**6),
        name="norm_rows",
    )(in_hbm(main), in_hbm(cont), in_hbm(gain))


def weight_tile(n, tiles, w_hbm, w_ref, sems):
    def copy(i):
        lanes = pl.ds(pl.multiple_of(i * TILE, TILE), TILE)
        return pltpu.make_async_copy(w_hbm.at[0, :, lanes], w_ref.at[i], sems.at[i])

    @pl.when(n == 0)
    def _():
        for i in range(tiles):
            copy(i).start()

    return copy(n)


REST = 768


def rest_tile(block):
    return jnp.where(block == 6, 2, 0)


def plane_place():
    column = lax.rem(lax.axis_index("tp"), COL_BLOCKS)
    return column // 4, lax.rem(column, 4)


def product_kernel(tiles, counts, places, *refs):
    x_refs, refs = refs[: len(counts)], refs[len(counts) :]
    if places:
        earlier_ref, w_ref, *out_refs = refs[: 2 + ROW_BLOCKS]
        main_ref, rows_ref, wide_ref, part_ref = refs[2 + ROW_BLOCKS :]
    else:
        w_hbm, *out_refs = refs[: 1 + ROW_BLOCKS]
        main_ref, w_ref, rows_ref, wide_ref, part_ref, sems = refs[1 + ROW_BLOCKS :]
    n = pl.program_id(0)
    members = sum(counts)
    count = members * CTOK
    lines = members * STEPS
    halves = TILE // 128
    width = tiles * TILE
    if not places:
        tile = weight_tile(n, tiles, w_hbm, w_ref, sems)

    @pl.when(n == 0)
    def _():
        at = 0
        for x_ref, size in zip(x_refs, counts):
            rows = slice(at * CTOK, (at + size) * CTOK)
            rows_ref[rows, :] = x_ref[:, :, :FEATURES].reshape(size * CTOK, FEATURES)
            packed = x_ref[:, :, FEATURES:].reshape(size * CTOK, TILE).astype(jnp.float32)
            for k in range(halves):
                wide_ref[k, rows, :] = packed[:, k * 128 : (k + 1) * 128]
            at += size
        for k in range(halves):
            for j in range(FEATURES // TILE):
                lane = j * TILE + k * 128
                rows_ref[count:, lane : lane + 128] = wide_ref[k, pl.ds(j, lines, stride=8), :].astype(jnp.bfloat16)

    if not places:
        tile.wait()
    prod = jnp.dot(rows_ref[...], w_ref[n], preferred_element_type=jnp.float32)
    high = prod.astype(jnp.bfloat16)
    part_ref[:, :, pl.ds(pl.multiple_of(n * TILE, TILE), TILE)] = high[:count].reshape(members, CTOK, TILE)
    for k in range(halves):
        wide_ref[k, pl.ds(n, lines, stride=8), :] = prod[count:, k * 128 : (k + 1) * 128]
    start = rest_tile(lax.rem(lax.axis_index("tp"), COL_BLOCKS))

    @pl.when((n >= start) & (n < start + REST // TILE))
    def _():
        low = prod - high.astype(jnp.float32)
        place = n - start
        lane = pl.multiple_of(width + place * TILE, TILE)
        part_ref[:, :, pl.ds(lane, TILE)] = low[:count].astype(jnp.bfloat16).reshape(members, CTOK, TILE)
        for k in range(halves):
            wide_ref[k, pl.ds(tiles + place, lines, stride=8), :] = low[count:, k * 128 : (k + 1) * 128]

    @pl.when(n == tiles - 1)
    def _():
        z = lax.axis_index("tp") // COL_BLOCKS
        done = earlier_ref.shape[0] // ROW_BLOCKS if places else 0
        for k in range(halves):
            lanes = slice(k * 128, (k + 1) * 128)
            packed = wide_ref[k].astype(jnp.bfloat16).reshape(members, CTOK, 128)
            if not places:
                main_ref[:, :, lanes] = packed
            for i, (dy, dx) in enumerate(places):
                y, x = plane_place()
                column = lax.rem(y + dy, 2) * 4 + lax.rem(x + dx, 4)
                for r in range(ROW_BLOCKS):
                    if i < done:
                        message = earlier_ref[i * ROW_BLOCKS + r, :, lanes]
                    else:
                        message = packed[(i - done) * ROW_BLOCKS + r]
                    main_ref[r * COL_BLOCKS + column, :, lanes] = message
        for k, out_ref in enumerate(out_refs):
            to = lax.rem(z + k, ROW_BLOCKS)
            for g in range(members // ROW_BLOCKS):
                out_ref[g] = part_ref[g * ROW_BLOCKS + to]


def block_product(messages, weight, earlier=None, places=()):
    tiles = QKV // COL_BLOCKS // TILE
    lanes = tiles * TILE + REST
    counts = tuple(rows.shape[0] for rows in messages)
    members = sum(counts)
    out = [jax.ShapeDtypeStruct((members // ROW_BLOCKS, CTOK, lanes), jnp.bfloat16)] * ROW_BLOCKS
    out.append(jax.ShapeDtypeStruct((MEMBERS if places else members, CTOK, TILE), jnp.bfloat16))
    scratch = [
        pltpu.VMEM((members * (CTOK + STEPS), FEATURES), jnp.bfloat16),
        pltpu.VMEM((TILE // 128, members * CTOK, 128), jnp.float32),
        pltpu.VMEM((members, CTOK, lanes), jnp.bfloat16),
    ]
    if places:
        operands = list(messages) + [earlier, weight]
        in_specs = [VMEM] * len(operands)
    else:
        operands = list(messages) + [in_hbm(weight)]
        in_specs = [VMEM] * len(messages) + [HBM]
        out.append(jax.ShapeDtypeStruct((tiles, FEATURES, TILE), jnp.bfloat16))
        scratch.append(pltpu.SemaphoreType.DMA((tiles,)))
    return pl.pallas_call(
        functools.partial(product_kernel, tiles, counts, places),
        out_shape=out,
        grid=(tiles,),
        in_specs=in_specs,
        out_specs=[VMEM] * len(out),
        scratch_shapes=scratch,
        compiler_params=kernel_params(),
        cost_estimate=cost(2 * members * (CTOK + STEPS) * FEATURES * tiles * TILE, 12 * 10**6),
        name="block_product",
    )(*operands)


def sum_kernel(bias_ref, *refs):
    part_refs, out_refs = refs[:ROW_BLOCKS], refs[ROW_BLOCKS:]
    column = lax.rem(lax.axis_index("tp"), COL_BLOCKS)
    late = column == 6
    last = (column == COL_BLOCKS - 1).astype(jnp.float32)
    cols = QKV // COL_BLOCKS
    tiles = cols // TILE
    kept = REST // TILE
    zero = jnp.zeros((CTOK, TILE), jnp.float32)

    def value_bias(j):
        if j == 0:
            return jnp.zeros((1, TILE), jnp.float32)
        at = QKV - cols + j * TILE
        return bias_ref[:, at : at + TILE] * last

    for g, out_ref in enumerate(out_refs):

        def total(lane):
            value = part_refs[0][g, :, lane : lane + TILE].astype(jnp.float32)
            for ref in part_refs[1:]:
                value = value + ref[g, :, lane : lane + TILE].astype(jnp.float32)
            return value

        rest = [total(cols + i * TILE) for i in range(kept)] + [zero] * (tiles - kept)
        lows = []
        for j in range(tiles):
            shifted = rest[j - tiles + kept] if j >= tiles - kept else zero
            value = total(j * TILE) + jnp.where(late, shifted, rest[j]) + value_bias(j)
            high = value.astype(jnp.bfloat16)
            out_ref[:, j * TILE : (j + 1) * TILE] = high
            lows.append(value - high.astype(jnp.float32))
        for i in range(kept):
            low = jnp.where(late, lows[i + tiles - kept], lows[i])
            out_ref[:, cols + i * TILE : cols + (i + 1) * TILE] = low.astype(jnp.bfloat16)


def sum_parts(bias, parts):
    groups, rows, lanes = parts[0].shape
    return pl.pallas_call(
        sum_kernel,
        out_shape=[jax.ShapeDtypeStruct((rows, lanes), jnp.bfloat16)] * groups,
        in_specs=[VMEM] * (1 + len(parts)),
        out_specs=[VMEM] * groups,
        compiler_params=kernel_params(),
        cost_estimate=cost(10**6, 3 * 10**6),
        name="sum_parts",
    )(bias, *parts)


def load_parts(part_refs, parts_ref):
    y, x = plane_place()
    for ref, (dy, dx) in zip(part_refs, HOMES):
        column = lax.rem(y + dy, 2) * 4 + lax.rem(x + 4 - dx, 4)
        parts_ref[column] = ref[...]


def summed_block(parts_ref, c, lanes):
    total = parts_ref[c, :, lanes].astype(jnp.float32)
    for r in range(1, ROW_BLOCKS):
        total = total + parts_ref[r * COL_BLOCKS + c, :, lanes].astype(jnp.float32)
    return total


def head_attention(query, key, value, fresh_key, fresh_value, seen, fresh_seen):
    inv_root = 1.0 / math.sqrt(HD)
    contract = (((1,), (1,)), ((), ()))
    old = lax.dot_general(query, key, contract, preferred_element_type=jnp.float32) * inv_root
    new = lax.dot_general(query, fresh_key, contract, preferred_element_type=jnp.float32) * inv_root
    old = jnp.where(seen, old, MASKED_SCORE)
    new = jnp.where(fresh_seen, new, MASKED_SCORE)
    highest = jnp.maximum(jnp.max(old, axis=-1, keepdims=True), jnp.max(new, axis=-1, keepdims=True))
    old = jnp.exp(old - highest)
    new = jnp.exp(new - highest)
    mass = jnp.sum(old, axis=-1, keepdims=True) + jnp.sum(new, axis=-1, keepdims=True)
    inv_mass = 1.0 / mass
    mixed = jnp.dot((old * inv_mass).astype(jnp.bfloat16), value, preferred_element_type=jnp.float32)
    return mixed + jnp.dot((new * inv_mass).astype(jnp.bfloat16), fresh_value, preferred_element_type=jnp.float32)


def load_qkv(main, parts_ref, qkv_ref):
    cols = QKV // COL_BLOCKS
    for c in range(COL_BLOCKS):
        first = 2 if c == 6 else 0
        total = summed_block(parts_ref, c, slice(0, TILE)) if main else parts_ref[c].astype(jnp.float32)
        for j in range(cols // TILE):
            lanes = slice(c * cols + j * TILE, c * cols + (j + 1) * TILE)
            rest = j - first
            has_rest = 0 <= rest < REST // TILE
            if main:
                for s in range(STEPS):
                    line = total[s * 8 + j : s * 8 + j + 1]
                    if has_rest:
                        at = s * 8 + cols // TILE + rest
                        line = line + total[at : at + 1]
                    qkv_ref[s : s + 1, lanes] = line
            else:
                value = total[:, j * TILE : (j + 1) * TILE]
                if has_rest:
                    value = value + total[:, cols + rest * TILE : cols + (rest + 1) * TILE]
                qkv_ref[:, lanes] = value


def head_readers(qkv_ref, bias_ref, cos_ref, sin_ref):
    cosine = cos_ref[...]
    sine = sin_ref[...]

    def plain(start):
        return qkv_ref[:, start : start + HD]

    def rotated(start):
        head = plain(start) + bias_ref[:, start : start + HD]
        return head * cosine + pltpu.roll(head, HD // 2, 1) * sine

    return plain, rotated


def fresh_block(pieces):
    rows = sum(piece.shape[0] for piece in pieces)
    pad = jnp.zeros((128 - rows, HD), jnp.float32)
    return jnp.concatenate(list(pieces) + [pad], axis=0).astype(jnp.bfloat16)


GROUP = D // HD // KVH
KV_WIDTH = KVH * HD


def attend_main_kernel(
    len_ref, bias_ref, cos_ref, sin_ref, cache_ref, parts_ref, *refs
):
    out_ref, kv_ref, qkv_ref, piece_ref = refs[-4:]
    rows = qkv_ref.shape[0]
    qkv_ref[...] = jnp.zeros(qkv_ref.shape, jnp.float32)
    load_qkv(True, parts_ref, qkv_ref)
    qkv_ref[:, D + KV_WIDTH :] = qkv_ref[:, D + KV_WIDTH :] + bias_ref[:, D + KV_WIDTH :]
    plain, rotated = head_readers(qkv_ref, bias_ref, cos_ref, sin_ref)
    seen = lax.broadcasted_iota(jnp.int32, (1, cache_ref.shape[0]), 1) < len_ref[0]
    row = lax.broadcasted_iota(jnp.int32, (rows, 128), 0)
    col = lax.broadcasted_iota(jnp.int32, (rows, 128), 1)
    own = ((col <= row) & (col < STEPS)).astype(jnp.int32)
    fresh_seen = jnp.concatenate([own] * GROUP, axis=0) > 0
    for g in range(KVH):
        query = jnp.concatenate([rotated((g * GROUP + h) * HD) for h in range(GROUP)], axis=0).astype(jnp.bfloat16)
        fresh_key = rotated(D + g * HD)
        fresh_value = plain(D + KV_WIDTH + g * HD)
        kv_ref[:, g * HD : (g + 1) * HD] = fresh_key
        kv_ref[:, KV_WIDTH + g * HD : KV_WIDTH + (g + 1) * HD] = fresh_value
        key = cache_ref[:, g * HD : (g + 1) * HD]
        value = cache_ref[:, KV_WIDTH + g * HD : KV_WIDTH + (g + 1) * HD]
        mixed = head_attention(
            query, key, value, fresh_block([fresh_key]), fresh_block([fresh_value]), seen, fresh_seen
        )
        for h in range(GROUP):
            r, place = divmod(g * GROUP + h, FEATURES // HD)
            j, lane = place // 2, (place % 2) * HD
            for s in range(STEPS):
                at = s * 8 + j
                piece_ref[r, at : at + 1, lane : lane + HD] = mixed[h * rows + s : h * rows + s + 1]
    for r in range(ROW_BLOCKS):
        piece = piece_ref[r].astype(jnp.bfloat16)
        for c in range(COL_BLOCKS):
            out_ref[r * COL_BLOCKS + c] = piece


def attend_main(prefix_len, bias, cosine, sine, cache, parts, after):
    return pl.pallas_call(
        attend_main_kernel,
        out_shape=(
            jax.ShapeDtypeStruct((32, 16, TILE), jnp.bfloat16),
            jax.ShapeDtypeStruct((8, 2 * KV_WIDTH), jnp.float32),
        ),
        in_specs=[SMEM] + [VMEM] * 5 + [UNREAD] * len(after),
        out_specs=(whole((32, 16, TILE)), whole((8, 2 * KV_WIDTH))),
        scratch_shapes=[
            pltpu.VMEM((8, QKV), jnp.float32),
            pltpu.VMEM((ROW_BLOCKS, 16, TILE), jnp.float32),
        ],
        compiler_params=kernel_params(),
        cost_estimate=cost(2 * 10**8, 6 * 10**6),
        name="attend_main",
    )(prefix_len, bias, cosine, sine, cache, parts, *after)


def attend_cont_kernel(len_ref, bound_ref, bias_ref, cos_ref, sin_ref, cache_ref, kv_ref, *refs):
    part_refs = refs[:COL_BLOCKS]
    out_ref, qkv_ref, parts_ref = refs[COL_BLOCKS:]
    load_parts(part_refs, parts_ref)
    rows = qkv_ref.shape[0]
    load_qkv(False, parts_ref, qkv_ref)
    plain, rotated = head_readers(qkv_ref, bias_ref, cos_ref, sin_ref)
    seen = lax.broadcasted_iota(jnp.int32, (1, cache_ref.shape[0]), 1) < len_ref[0]
    row = lax.broadcasted_iota(jnp.int32, (rows, 128), 0)
    col = lax.broadcasted_iota(jnp.int32, (rows, 128), 1)
    own = (row // STEPS == col // STEPS) & (col <= row)
    main = (col >= rows) & (col < rows + bound_ref[0])
    fresh_seen = jnp.concatenate([(own | main).astype(jnp.int32)] * GROUP, axis=0) > 0
    for g in range(KVH):
        query = jnp.concatenate([rotated((g * GROUP + h) * HD) for h in range(GROUP)], axis=0).astype(jnp.bfloat16)
        at_key = slice(g * HD, (g + 1) * HD)
        at_value = slice(KV_WIDTH + g * HD, KV_WIDTH + (g + 1) * HD)
        fresh_key = fresh_block([rotated(D + g * HD), kv_ref[:, at_key]])
        fresh_value = fresh_block([plain(D + KV_WIDTH + g * HD), kv_ref[:, at_value]])
        mixed = head_attention(
            query, cache_ref[:, at_key], cache_ref[:, at_value], fresh_key, fresh_value, seen, fresh_seen
        )
        mixed = mixed.astype(jnp.bfloat16)
        for h in range(GROUP):
            out_ref[:, (g * GROUP + h) * HD : (g * GROUP + h + 1) * HD] = mixed[h * rows : (h + 1) * rows]


def attend_cont(*args):
    return pl.pallas_call(
        attend_cont_kernel,
        out_shape=jax.ShapeDtypeStruct((CTOK, D), jnp.bfloat16),
        in_specs=[SMEM, SMEM] + [VMEM] * 4 + [whole((8, 2 * KV_WIDTH))] + [VMEM] * COL_BLOCKS,
        out_specs=whole((CTOK, D)),
        scratch_shapes=[
            pltpu.VMEM((CTOK, QKV), jnp.float32),
            pltpu.VMEM((COL_BLOCKS,) + args[-1].shape, jnp.bfloat16),
        ],
        compiler_params=kernel_params(),
        cost_estimate=cost(4 * 10**8, 8 * 10**6),
        name="attend_cont",
    )(*args)


def readout_kernel(head_ref, w_hbm, out_ref, w_ref, sem):
    copy = pltpu.make_async_copy(w_hbm.at[0], w_ref, sem)
    copy.start()
    row = head_ref[pl.ds(lax.rem(lax.axis_index("tp"), COL_BLOCKS), 1), :]
    high = row.astype(jnp.bfloat16).astype(jnp.float32)
    middle = (row - high).astype(jnp.bfloat16).astype(jnp.float32)
    low = row - high - middle
    pieces = jnp.concatenate([high, middle, low, jnp.zeros((13, row.shape[1]), jnp.float32)], axis=0)
    copy.wait()
    prod = lax.dot_general(
        pieces.astype(jnp.bfloat16), w_ref[...], (((1,), (1,)), ((), ())), preferred_element_type=jnp.float32
    )
    out_ref[...] = prod[0:1] + prod[1:2] + prod[2:3]


def readout(value_head, blocks):
    return pl.pallas_call(
        readout_kernel,
        out_shape=jax.ShapeDtypeStruct((1, FEATURES), jnp.float32),
        in_specs=[whole(value_head.shape), HBM],
        out_specs=whole((1, FEATURES)),
        scratch_shapes=[pltpu.VMEM((FEATURES, D // COL_BLOCKS), jnp.bfloat16), pltpu.SemaphoreType.DMA],
        compiler_params=kernel_params(),
        cost_estimate=cost(2 * 10**8, 5 * 10**6),
        name="readout",
    )(value_head, in_hbm(blocks))


def out_kernel(tiles, x_ref, read_ref, w_hbm, *refs):
    out_ref, rows_ref, wide_ref, read8_ref, w_ref, sems = refs[-6:]
    n = pl.program_id(0)
    members = x_ref.shape[0]
    lines = members * STEPS
    halves = TILE // 128
    tile = weight_tile(n, tiles, w_hbm, w_ref, sems)

    @pl.when(n == 0)
    def _():
        for j in range(FEATURES // TILE):
            read8_ref[j : j + 1, :] = read_ref[:, j * TILE : (j + 1) * TILE]
        out_ref[:, 8:, :] = jnp.broadcast_to(read8_ref[...][None], (members, 8, TILE))
        packed = x_ref[...].reshape(members * 16, TILE).astype(jnp.float32)
        for k in range(halves):
            wide_ref[k] = packed[:, k * 128 : (k + 1) * 128]
            for j in range(FEATURES // TILE):
                lane = j * TILE + k * 128
                rows_ref[:, lane : lane + 128] = wide_ref[k, pl.ds(j, lines, stride=8), :].astype(jnp.bfloat16)

    tile.wait()
    prod = jnp.dot(rows_ref[...], w_ref[n], preferred_element_type=jnp.float32)
    for k in range(halves):
        wide_ref[k, pl.ds(n, lines, stride=4), :] = prod[:, k * 128 : (k + 1) * 128]

    @pl.when(n == tiles - 1)
    def _():
        for k in range(halves):
            packed = wide_ref[k, : members * 8, :].reshape(members, 8, 128)
            out_ref[:, :8, k * 128 : (k + 1) * 128] = packed


def out_product(rows, read, blocks, after):
    members = rows.shape[0]
    tiles = blocks.shape[2] // TILE
    return pl.pallas_call(
        functools.partial(out_kernel, tiles),
        out_shape=jax.ShapeDtypeStruct((members, 16, TILE), jnp.float32),
        grid=(tiles,),
        in_specs=[whole(rows.shape), whole(read.shape), HBM] + [UNREAD] * len(after),
        out_specs=whole((members, 16, TILE)),
        scratch_shapes=[
            pltpu.VMEM((members * STEPS, FEATURES), jnp.bfloat16),
            pltpu.VMEM((TILE // 128, members * 16, 128), jnp.float32),
            pltpu.VMEM((8, TILE), jnp.float32),
            pltpu.VMEM((tiles, FEATURES, TILE), jnp.bfloat16),
            pltpu.SemaphoreType.DMA((tiles,)),
        ],
        compiler_params=kernel_params(),
        cost_estimate=cost(3 * 10**8, 5 * 10**6),
        name="out_product",
    )(rows, read, in_hbm(blocks), *after)


def finish_kernel(parts_ref, main_ref, cont_ref, head_ref, mixed_ref, out_ref, score_ref, wide_ref):
    cols = D // COL_BLOCKS
    for c in range(COL_BLOCKS):
        total = summed_block(parts_ref, c, slice(0, TILE))
        for j in range(cols // TILE):
            at = slice(c * cols + j * TILE, c * cols + (j + 1) * TILE)
            for s in range(STEPS):
                wide_ref[s : s + 1, at] = total[s * 4 + j : s * 4 + j + 1]
    out_ref[...] = (main_ref[...].astype(jnp.float32) + wide_ref[:STEPS, :]).astype(jnp.bfloat16)
    score = jnp.zeros((CTOK, TILE), jnp.float32)
    direct = jnp.zeros((STEPS, TILE), jnp.float32)
    for r in range(ROW_BLOCKS):
        read = parts_ref[r * COL_BLOCKS, 8:, :]
        for c in range(1, COL_BLOCKS):
            read = read + parts_ref[r * COL_BLOCKS + c, 8:, :]
        for j in range(FEATURES // TILE):
            lanes = slice(r * FEATURES + j * TILE, r * FEATURES + (j + 1) * TILE)
            score = score + mixed_ref[:, lanes].astype(jnp.float32) * read[j : j + 1, :]
            for c in range(CONTS):
                direct = direct + cont_ref[c, :, lanes].astype(jnp.float32) * head_ref[:, lanes]
    total = jnp.sum(score, axis=0, keepdims=True) + jnp.sum(direct, axis=0, keepdims=True)
    score_ref[...] = jnp.broadcast_to(jnp.sum(total, axis=1, keepdims=True) / CONTS, (8, 128))


def finish(parts, main, cont, head, mixed):
    return pl.pallas_call(
        finish_kernel,
        out_shape=(
            jax.ShapeDtypeStruct((STEPS, D), jnp.bfloat16),
            jax.ShapeDtypeStruct((8, 128), jnp.float32),
        ),
        in_specs=[whole(parts.shape), whole(main.shape), whole(cont.shape), whole(head.shape), whole(mixed.shape)],
        out_specs=(whole((STEPS, D)), whole((8, 128))),
        scratch_shapes=[pltpu.VMEM((8, D), jnp.float32)],
        compiler_params=kernel_params(),
        cost_estimate=cost(10**6, 2 * 10**6),
        name="finish",
    )(parts, main, cont, head, mixed)


def rope_tables(positions):
    half = HD // 2
    frequency = THETA ** (-(jnp.arange(half, dtype=jnp.float32) * 2.0) / HD)
    angles = positions.astype(jnp.float32)[:, None] * frequency[None, :]
    cosine = jnp.cos(angles)
    sine = jnp.sin(angles)
    return jnp.concatenate([cosine, cosine], axis=1), jnp.concatenate([-sine, sine], axis=1)


def exchange(rows):
    return lax.all_to_all(rows, "tp", split_axis=0, concat_axis=0, tiled=True)


ALONG = [[z * COL_BLOCKS + c for z in range(ROW_BLOCKS)] for c in range(COL_BLOCKS)]


def from_side(rows, dy, dx):
    route = []
    for to in range(MEMBERS):
        z, y, x = to // 8, to // 4 % 2, to % 4
        route.append((z * 8 + (y + dy) % 2 * 4 + (x + dx) % 4, to))
    return lax.ppermute(rows, "tp", route)


def from_along(rows, dz):
    route = [((to + dz * COL_BLOCKS) % MEMBERS, to) for to in range(MEMBERS)]
    return lax.ppermute(rows, "tp", route)


FIRST_HOMES = ((0, 0), (1, 0), (0, 1), (0, 3))
SECOND_HOMES = ((1, 1), (1, 3), (0, 2), (1, 2))
HOMES = FIRST_HOMES + SECOND_HOMES


def project(rows, blocks, bias):
    near = lax.all_to_all(rows, "tp", split_axis=0, concat_axis=0, tiled=True, axis_index_groups=ALONG)
    over = from_side(near, 1, 0)
    after, before = from_side(near, 0, 1), from_side(near, 0, 3)
    over_after, over_before = from_side(over, 0, 1), from_side(over, 0, 3)
    far = [from_side(before, 0, 3), from_side(over_after, 0, 1)]
    *first, main, weight = block_product([near, over, after, before], blocks)
    first = [first[0]] + [from_along(first[k], -k) for k in range(1, ROW_BLOCKS)]
    *second, main = block_product([over_after, over_before] + far, weight, main, HOMES)
    main, first = lax.optimization_barrier((main, first))
    second = [second[0]] + [from_along(second[k], -k) for k in range(1, ROW_BLOCKS)]
    received = []
    for homes, parts in ((FIRST_HOMES, first), (SECOND_HOMES, second)):
        for (dy, dx), summed in zip(homes, sum_parts(bias, parts)):
            received.append(from_side(summed, -dy, -dx) if dy or dx else summed)
    return received, exchange(main), second[1:] + received[1:4]


def on_device(
    main_inputs, cont_inputs, prefix_cache, prefix_len, boundary, rms_gain, qkv_bias, w_qkv, w_out, value_head
):
    main = main_inputs.reshape(STEPS, D)
    cont = cont_inputs.reshape(CONTS, STEPS, D)
    bias = qkv_bias[None, :]
    cache = prefix_cache[0]
    head = value_head[None, :]
    step = jnp.arange(CTOK, dtype=jnp.int32) % STEPS
    main_tables = rope_tables(prefix_len + step[:8])
    cont_tables = rope_tables(prefix_len + boundary + step)
    read = readout(value_head.reshape(COL_BLOCKS, D // COL_BLOCKS), w_out)
    parts, main_parts, before = project(norm_rows(main, cont, rms_gain[None, :]), w_qkv, bias)
    mixed, main_kv = attend_main(prefix_len, bias, *main_tables, cache, main_parts, before + [read])
    mixed = exchange(mixed)
    cont_mixed = attend_cont(prefix_len, boundary, bias, *cont_tables, cache, main_kv, *parts)
    parts = exchange(out_product(mixed, read, w_out, parts[4:7]))
    main_out, score = finish(parts, main, cont, head, cont_mixed)
    return main_out[None], score[0, :1]


def solution(mesh):
    return jax.shard_map(
        on_device,
        mesh=mesh,
        in_specs=(
            P(("grp", "tp"), None, None),
            P(("grp", "tp"), None, None, None),
            P(("grp", "tp"), None, None),
            P(("grp", "tp")),
            P(("grp", "tp")),
            P(),
            P(),
            P("tp", None, None),
            P("tp", None, None),
            P(),
        ),
        out_specs=(P(("grp", "tp"), None, None), P(("grp", "tp"))),
        check_vma=False,
    )
```

```python
import functools
import math

import jax
import jax.numpy as jnp
from jax import lax
from jax.experimental import pallas as pl
from jax.experimental.pallas import tpu as pltpu
from jax.sharding import PartitionSpec as P

KVH = 8
HD = 128
D = 8192
QKV = 10240
ROW_BLOCKS = 4
COL_BLOCKS = 8
MEMBERS = ROW_BLOCKS * COL_BLOCKS
FEATURES = D // ROW_BLOCKS
CONTS = 8
STEPS = 2
CTOK = CONTS * STEPS
TILE = 256

THETA = 1000000.0
EPS = 1e-06
MASKED_SCORE = -1e30

VMEM_LIMIT = 28 * 1024 * 1024
VMEM = pl.BlockSpec(memory_space=pltpu.VMEM)
SMEM = pl.BlockSpec(memory_space=pltpu.SMEM)
HBM = pl.BlockSpec(memory_space=pltpu.HBM)
UNREAD = pl.BlockSpec(memory_space=pl.ANY)


def whole(shape):
    return pl.BlockSpec(shape, lambda *_: (0,) * len(shape))


def cost(flops, moved):
    return pl.CostEstimate(flops=flops, bytes_accessed=moved, transcendentals=0)


def in_hbm(array):
    return pltpu.with_memory_space_constraint(array, pltpu.HBM)


def kernel_params():
    return pltpu.CompilerParams(vmem_limit_bytes=VMEM_LIMIT)


def norm_kernel(main_hbm, cont_hbm, gain_hbm, out_ref, main_ref, cont_ref, gain_ref, rows_ref, piece_ref, sems):
    pairs = ((main_hbm, main_ref), (cont_hbm, cont_ref), (gain_hbm, gain_ref))
    copies = [pltpu.make_async_copy(src, dst, sems.at[i]) for i, (src, dst) in enumerate(pairs)]
    for copy in copies:
        copy.start()
    for copy in copies:
        copy.wait()

    def normed(wide):
        inv = lax.rsqrt(jnp.mean(wide * wide, axis=-1, keepdims=True) + EPS)
        return wide * inv * gain_ref[...]

    for c in range(CONTS):
        rows_ref[c * STEPS : (c + 1) * STEPS, :] = cont_ref[c].astype(jnp.float32)
    cont = normed(rows_ref[...]).astype(jnp.bfloat16)
    main = normed(main_ref[...].astype(jnp.float32))
    for r in range(ROW_BLOCKS):
        for j in range(FEATURES // TILE):
            lanes = slice(r * FEATURES + j * TILE, r * FEATURES + (j + 1) * TILE)
            for s in range(STEPS):
                piece_ref[r, s * 8 + j : s * 8 + j + 1, :] = main[s : s + 1, lanes]
    for r in range(ROW_BLOCKS):
        piece = piece_ref[r].astype(jnp.bfloat16)
        out_ref[r, :, :FEATURES] = cont[:, r * FEATURES : (r + 1) * FEATURES]
        out_ref[r, :, FEATURES:] = piece


def norm_rows(main, cont, gain):
    return pl.pallas_call(
        norm_kernel,
        out_shape=jax.ShapeDtypeStruct((ROW_BLOCKS, CTOK, FEATURES + TILE), jnp.bfloat16),
        in_specs=[HBM] * 3,
        out_specs=VMEM,
        scratch_shapes=[
            pltpu.VMEM((STEPS, D), jnp.bfloat16),
            pltpu.VMEM((CONTS, STEPS, D), jnp.bfloat16),
            pltpu.VMEM((1, D), jnp.float32),
            pltpu.VMEM((CTOK, D), jnp.float32),
            pltpu.VMEM((ROW_BLOCKS, 16, TILE), jnp.float32),
            pltpu.SemaphoreType.DMA((3,)),
        ],
        compiler_params=kernel_params(),
        cost_estimate=cost(10**6, 4 * 10**6),
        name="norm_rows",
    )(in_hbm(main), in_hbm(cont), in_hbm(gain))


def weight_tile(n, tiles, w_hbm, w_ref, sems):
    def copy(i):
        lanes = pl.ds(pl.multiple_of(i * TILE, TILE), TILE)
        return pltpu.make_async_copy(w_hbm.at[0, :, lanes], w_ref.at[i], sems.at[i])

    @pl.when(n == 0)
    def _():
        for i in range(tiles):
            copy(i).start()

    return copy(n)


REST = 768


def rest_tile(block):
    return jnp.where(block == 6, 2, 0)


def plane_place():
    column = lax.rem(lax.axis_index("tp"), COL_BLOCKS)
    return column // 4, lax.rem(column, 4)


def product_kernel(tiles, counts, places, *refs):
    x_refs, refs = refs[: len(counts)], refs[len(counts) :]
    if places:
        earlier_ref, w_ref, *out_refs = refs[: 2 + ROW_BLOCKS]
        main_ref, rows_ref, wide_ref, part_ref = refs[2 + ROW_BLOCKS :]
    else:
        w_hbm, *out_refs = refs[: 1 + ROW_BLOCKS]
        main_ref, w_ref, rows_ref, wide_ref, part_ref, sems = refs[1 + ROW_BLOCKS :]
    n = pl.program_id(0)
    members = sum(counts)
    count = members * CTOK
    lines = members * STEPS
    halves = TILE // 128
    width = tiles * TILE
    if not places:
        tile = weight_tile(n, tiles, w_hbm, w_ref, sems)

    @pl.when(n == 0)
    def _():
        at = 0
        for x_ref, size in zip(x_refs, counts):
            rows = slice(at * CTOK, (at + size) * CTOK)
            rows_ref[rows, :] = x_ref[:, :, :FEATURES].reshape(size * CTOK, FEATURES)
            packed = x_ref[:, :, FEATURES:].reshape(size * CTOK, TILE).astype(jnp.float32)
            for k in range(halves):
                wide_ref[k, rows, :] = packed[:, k * 128 : (k + 1) * 128]
            at += size
        for k in range(halves):
            for j in range(FEATURES // TILE):
                lane = j * TILE + k * 128
                rows_ref[count:, lane : lane + 128] = wide_ref[k, pl.ds(j, lines, stride=8), :].astype(jnp.bfloat16)

    if not places:
        tile.wait()
    prod = jnp.dot(rows_ref[...], w_ref[n], preferred_element_type=jnp.float32)
    high = prod.astype(jnp.bfloat16)
    part_ref[:, :, pl.ds(pl.multiple_of(n * TILE, TILE), TILE)] = high[:count].reshape(members, CTOK, TILE)
    for k in range(halves):
        wide_ref[k, pl.ds(n, lines, stride=8), :] = prod[count:, k * 128 : (k + 1) * 128]
    start = rest_tile(lax.rem(lax.axis_index("tp"), COL_BLOCKS))

    @pl.when((n >= start) & (n < start + REST // TILE))
    def _():
        low = prod - high.astype(jnp.float32)
        place = n - start
        lane = pl.multiple_of(width + place * TILE, TILE)
        part_ref[:, :, pl.ds(lane, TILE)] = low[:count].astype(jnp.bfloat16).reshape(members, CTOK, TILE)
        for k in range(halves):
            wide_ref[k, pl.ds(tiles + place, lines, stride=8), :] = low[count:, k * 128 : (k + 1) * 128]

    @pl.when(n == tiles - 1)
    def _():
        z = lax.axis_index("tp") // COL_BLOCKS
        done = earlier_ref.shape[0] // ROW_BLOCKS if places else 0
        for k in range(halves):
            lanes = slice(k * 128, (k + 1) * 128)
            packed = wide_ref[k, :count, :].astype(jnp.bfloat16).reshape(members, CTOK, 128)
            if not places:
                main_ref[:, :, lanes] = packed
            for i, (dy, dx) in enumerate(places):
                y, x = plane_place()
                column = lax.rem(y + dy, 2) * 4 + lax.rem(x + dx, 4)
                for r in range(ROW_BLOCKS):
                    if i < done:
                        message = earlier_ref[i * ROW_BLOCKS + r, :, lanes]
                    else:
                        message = packed[(i - done) * ROW_BLOCKS + r]
                    main_ref[r * COL_BLOCKS + column, :, lanes] = message
        for k, out_ref in enumerate(out_refs):
            to = lax.rem(z + k, ROW_BLOCKS)
            for g in range(members // ROW_BLOCKS):
                out_ref[g] = part_ref[g * ROW_BLOCKS + to]


def block_product(messages, weight, earlier=None, places=()):
    tiles = QKV // COL_BLOCKS // TILE
    lanes = tiles * TILE + REST
    counts = tuple(rows.shape[0] for rows in messages)
    members = sum(counts)
    out = [jax.ShapeDtypeStruct((members // ROW_BLOCKS, CTOK, lanes), jnp.bfloat16)] * ROW_BLOCKS
    out.append(jax.ShapeDtypeStruct((MEMBERS if places else members, CTOK, TILE), jnp.bfloat16))
    scratch = [
        pltpu.VMEM((members * (CTOK + STEPS), FEATURES), jnp.bfloat16),
        pltpu.VMEM((TILE // 128, members * CTOK + 8, 128), jnp.float32),
        pltpu.VMEM((members, CTOK, lanes), jnp.bfloat16),
    ]
    if places:
        operands = list(messages) + [earlier, weight]
        in_specs = [VMEM] * len(operands)
    else:
        operands = list(messages) + [in_hbm(weight)]
        in_specs = [VMEM] * len(messages) + [HBM]
        out.append(jax.ShapeDtypeStruct((tiles, FEATURES, TILE), jnp.bfloat16))
        scratch.append(pltpu.SemaphoreType.DMA((tiles,)))
    return pl.pallas_call(
        functools.partial(product_kernel, tiles, counts, places),
        out_shape=out,
        grid=(tiles,),
        in_specs=in_specs,
        out_specs=[VMEM] * len(out),
        scratch_shapes=scratch,
        compiler_params=kernel_params(),
        cost_estimate=cost(2 * members * (CTOK + STEPS) * FEATURES * tiles * TILE, 12 * 10**6),
        name="block_product",
    )(*operands)


def sum_kernel(bias_ref, *refs):
    part_refs, out_refs = refs[:ROW_BLOCKS], refs[ROW_BLOCKS:]
    column = lax.rem(lax.axis_index("tp"), COL_BLOCKS)
    late = column == 6
    last = (column == COL_BLOCKS - 1).astype(jnp.float32)
    cols = QKV // COL_BLOCKS
    tiles = cols // TILE
    kept = REST // TILE
    zero = jnp.zeros((CTOK, TILE), jnp.float32)

    def value_bias(j):
        if j == 0:
            return jnp.zeros((1, TILE), jnp.float32)
        at = QKV - cols + j * TILE
        return bias_ref[:, at : at + TILE] * last

    for g, out_ref in enumerate(out_refs):

        def total(lane):
            value = part_refs[0][g, :, lane : lane + TILE].astype(jnp.float32)
            for ref in part_refs[1:]:
                value = value + ref[g, :, lane : lane + TILE].astype(jnp.float32)
            return value

        rest = [total(cols + i * TILE) for i in range(kept)] + [zero] * (tiles - kept)
        lows = []
        for j in range(tiles):
            shifted = rest[j - tiles + kept] if j >= tiles - kept else zero
            value = total(j * TILE) + jnp.where(late, shifted, rest[j]) + value_bias(j)
            high = value.astype(jnp.bfloat16)
            out_ref[:, j * TILE : (j + 1) * TILE] = high
            lows.append(value - high.astype(jnp.float32))
        for i in range(kept):
            low = jnp.where(late, lows[i + tiles - kept], lows[i])
            out_ref[:, cols + i * TILE : cols + (i + 1) * TILE] = low.astype(jnp.bfloat16)


def sum_parts(bias, parts):
    groups, rows, lanes = parts[0].shape
    return pl.pallas_call(
        sum_kernel,
        out_shape=[jax.ShapeDtypeStruct((rows, lanes), jnp.bfloat16)] * groups,
        in_specs=[VMEM] * (1 + len(parts)),
        out_specs=[VMEM] * groups,
        compiler_params=kernel_params(),
        cost_estimate=cost(10**6, 3 * 10**6),
        name="sum_parts",
    )(bias, *parts)


def load_parts(part_refs, parts_ref):
    y, x = plane_place()
    for ref, (dy, dx) in zip(part_refs, HOMES):
        column = lax.rem(y + dy, 2) * 4 + lax.rem(x + 4 - dx, 4)
        parts_ref[column] = ref[...]


def summed_block(parts_ref, c, lanes):
    total = parts_ref[c, :, lanes].astype(jnp.float32)
    for r in range(1, ROW_BLOCKS):
        total = total + parts_ref[r * COL_BLOCKS + c, :, lanes].astype(jnp.float32)
    return total


def head_attention(query, key, value, fresh_key, fresh_value, seen, fresh_seen):
    inv_root = 1.0 / math.sqrt(HD)
    contract = (((1,), (1,)), ((), ()))
    old = lax.dot_general(query, key, contract, preferred_element_type=jnp.float32) * inv_root
    new = lax.dot_general(query, fresh_key, contract, preferred_element_type=jnp.float32) * inv_root
    old = jnp.where(seen, old, MASKED_SCORE)
    new = jnp.where(fresh_seen, new, MASKED_SCORE)
    highest = jnp.maximum(jnp.max(old, axis=-1, keepdims=True), jnp.max(new, axis=-1, keepdims=True))
    old = jnp.exp(old - highest)
    new = jnp.exp(new - highest)
    mass = jnp.sum(old, axis=-1, keepdims=True) + jnp.sum(new, axis=-1, keepdims=True)
    inv_mass = 1.0 / mass
    mixed = jnp.dot((old * inv_mass).astype(jnp.bfloat16), value, preferred_element_type=jnp.float32)
    return mixed + jnp.dot((new * inv_mass).astype(jnp.bfloat16), fresh_value, preferred_element_type=jnp.float32)


def load_qkv(main, parts_ref, qkv_ref):
    cols = QKV // COL_BLOCKS
    for c in range(COL_BLOCKS):
        first = 2 if c == 6 else 0
        total = summed_block(parts_ref, c, slice(0, TILE)) if main else parts_ref[c].astype(jnp.float32)
        for j in range(cols // TILE):
            lanes = slice(c * cols + j * TILE, c * cols + (j + 1) * TILE)
            rest = j - first
            has_rest = 0 <= rest < REST // TILE
            if main:
                for s in range(STEPS):
                    line = total[s * 8 + j : s * 8 + j + 1]
                    if has_rest:
                        at = s * 8 + cols // TILE + rest
                        line = line + total[at : at + 1]
                    qkv_ref[s : s + 1, lanes] = line
            else:
                value = total[:, j * TILE : (j + 1) * TILE]
                if has_rest:
                    value = value + total[:, cols + rest * TILE : cols + (rest + 1) * TILE]
                qkv_ref[:, lanes] = value


def head_readers(qkv_ref, bias_ref, cos_ref, sin_ref):
    cosine = cos_ref[...]
    sine = sin_ref[...]

    def plain(start):
        return qkv_ref[:, start : start + HD]

    def rotated(start):
        head = plain(start) + bias_ref[:, start : start + HD]
        return head * cosine + pltpu.roll(head, HD // 2, 1) * sine

    return plain, rotated


def fresh_block(pieces):
    rows = sum(piece.shape[0] for piece in pieces)
    pad = jnp.zeros((128 - rows, HD), jnp.float32)
    return jnp.concatenate(list(pieces) + [pad], axis=0).astype(jnp.bfloat16)


GROUP = D // HD // KVH
KV_WIDTH = KVH * HD


def attend_main_kernel(
    len_ref, bias_ref, cos_ref, sin_ref, cache_ref, parts_ref, *refs
):
    out_ref, kv_ref, qkv_ref, piece_ref = refs[-4:]
    rows = qkv_ref.shape[0]
    qkv_ref[...] = jnp.zeros(qkv_ref.shape, jnp.float32)
    load_qkv(True, parts_ref, qkv_ref)
    qkv_ref[:, D + KV_WIDTH :] = qkv_ref[:, D + KV_WIDTH :] + bias_ref[:, D + KV_WIDTH :]
    plain, rotated = head_readers(qkv_ref, bias_ref, cos_ref, sin_ref)
    seen = lax.broadcasted_iota(jnp.int32, (1, cache_ref.shape[0]), 1) < len_ref[0]
    row = lax.broadcasted_iota(jnp.int32, (rows, 128), 0)
    col = lax.broadcasted_iota(jnp.int32, (rows, 128), 1)
    own = ((col <= row) & (col < STEPS)).astype(jnp.int32)
    fresh_seen = jnp.concatenate([own] * GROUP, axis=0) > 0
    for g in range(KVH):
        query = jnp.concatenate([rotated((g * GROUP + h) * HD) for h in range(GROUP)], axis=0).astype(jnp.bfloat16)
        fresh_key = rotated(D + g * HD)
        fresh_value = plain(D + KV_WIDTH + g * HD)
        kv_ref[:, g * HD : (g + 1) * HD] = fresh_key
        kv_ref[:, KV_WIDTH + g * HD : KV_WIDTH + (g + 1) * HD] = fresh_value
        key = cache_ref[:, g * HD : (g + 1) * HD]
        value = cache_ref[:, KV_WIDTH + g * HD : KV_WIDTH + (g + 1) * HD]
        mixed = head_attention(
            query, key, value, fresh_block([fresh_key]), fresh_block([fresh_value]), seen, fresh_seen
        )
        for h in range(GROUP):
            r, place = divmod(g * GROUP + h, FEATURES // HD)
            j, lane = place // 2, (place % 2) * HD
            for s in range(STEPS):
                at = s * 8 + j
                piece_ref[r, at : at + 1, lane : lane + HD] = mixed[h * rows + s : h * rows + s + 1]
    for r in range(ROW_BLOCKS):
        piece = piece_ref[r].astype(jnp.bfloat16)
        for c in range(COL_BLOCKS):
            out_ref[r * COL_BLOCKS + c] = piece


def attend_main(prefix_len, bias, cosine, sine, cache, parts, after):
    return pl.pallas_call(
        attend_main_kernel,
        out_shape=(
            jax.ShapeDtypeStruct((32, 16, TILE), jnp.bfloat16),
            jax.ShapeDtypeStruct((8, 2 * KV_WIDTH), jnp.float32),
        ),
        in_specs=[SMEM] + [VMEM] * 5 + [UNREAD] * len(after),
        out_specs=(whole((32, 16, TILE)), whole((8, 2 * KV_WIDTH))),
        scratch_shapes=[
            pltpu.VMEM((8, QKV), jnp.float32),
            pltpu.VMEM((ROW_BLOCKS, 16, TILE), jnp.float32),
        ],
        compiler_params=kernel_params(),
        cost_estimate=cost(2 * 10**8, 6 * 10**6),
        name="attend_main",
    )(prefix_len, bias, cosine, sine, cache, parts, *after)


def attend_cont_kernel(len_ref, bound_ref, bias_ref, cos_ref, sin_ref, cache_ref, kv_ref, *refs):
    part_refs = refs[:COL_BLOCKS]
    out_ref, qkv_ref, parts_ref = refs[COL_BLOCKS:]
    load_parts(part_refs, parts_ref)
    rows = qkv_ref.shape[0]
    load_qkv(False, parts_ref, qkv_ref)
    plain, rotated = head_readers(qkv_ref, bias_ref, cos_ref, sin_ref)
    seen = lax.broadcasted_iota(jnp.int32, (1, cache_ref.shape[0]), 1) < len_ref[0]
    row = lax.broadcasted_iota(jnp.int32, (rows, 128), 0)
    col = lax.broadcasted_iota(jnp.int32, (rows, 128), 1)
    own = (row // STEPS == col // STEPS) & (col <= row)
    main = (col >= rows) & (col < rows + bound_ref[0])
    fresh_seen = jnp.concatenate([(own | main).astype(jnp.int32)] * GROUP, axis=0) > 0
    for g in range(KVH):
        query = jnp.concatenate([rotated((g * GROUP + h) * HD) for h in range(GROUP)], axis=0).astype(jnp.bfloat16)
        at_key = slice(g * HD, (g + 1) * HD)
        at_value = slice(KV_WIDTH + g * HD, KV_WIDTH + (g + 1) * HD)
        fresh_key = fresh_block([rotated(D + g * HD), kv_ref[:, at_key]])
        fresh_value = fresh_block([plain(D + KV_WIDTH + g * HD), kv_ref[:, at_value]])
        mixed = head_attention(
            query, cache_ref[:, at_key], cache_ref[:, at_value], fresh_key, fresh_value, seen, fresh_seen
        )
        mixed = mixed.astype(jnp.bfloat16)
        for h in range(GROUP):
            out_ref[:, (g * GROUP + h) * HD : (g * GROUP + h + 1) * HD] = mixed[h * rows : (h + 1) * rows]


def attend_cont(*args):
    return pl.pallas_call(
        attend_cont_kernel,
        out_shape=jax.ShapeDtypeStruct((CTOK, D), jnp.bfloat16),
        in_specs=[SMEM, SMEM] + [VMEM] * 4 + [whole((8, 2 * KV_WIDTH))] + [VMEM] * COL_BLOCKS,
        out_specs=whole((CTOK, D)),
        scratch_shapes=[
            pltpu.VMEM((CTOK, QKV), jnp.float32),
            pltpu.VMEM((COL_BLOCKS,) + args[-1].shape, jnp.bfloat16),
        ],
        compiler_params=kernel_params(),
        cost_estimate=cost(4 * 10**8, 8 * 10**6),
        name="attend_cont",
    )(*args)


def readout_kernel(head_ref, w_hbm, out_ref, w_ref, sem):
    copy = pltpu.make_async_copy(w_hbm.at[0], w_ref, sem)
    copy.start()
    row = head_ref[pl.ds(lax.rem(lax.axis_index("tp"), COL_BLOCKS), 1), :]
    high = row.astype(jnp.bfloat16).astype(jnp.float32)
    middle = (row - high).astype(jnp.bfloat16).astype(jnp.float32)
    low = row - high - middle
    pieces = jnp.concatenate([high, middle, low, jnp.zeros((13, row.shape[1]), jnp.float32)], axis=0)
    copy.wait()
    prod = lax.dot_general(
        pieces.astype(jnp.bfloat16), w_ref[...], (((1,), (1,)), ((), ())), preferred_element_type=jnp.float32
    )
    out_ref[...] = prod[0:1] + prod[1:2] + prod[2:3]


def readout(value_head, blocks):
    return pl.pallas_call(
        readout_kernel,
        out_shape=jax.ShapeDtypeStruct((1, FEATURES), jnp.float32),
        in_specs=[whole(value_head.shape), HBM],
        out_specs=whole((1, FEATURES)),
        scratch_shapes=[pltpu.VMEM((FEATURES, D // COL_BLOCKS), jnp.bfloat16), pltpu.SemaphoreType.DMA],
        compiler_params=kernel_params(),
        cost_estimate=cost(2 * 10**8, 5 * 10**6),
        name="readout",
    )(value_head, in_hbm(blocks))


def out_kernel(tiles, x_ref, read_ref, w_hbm, *refs):
    out_ref, rows_ref, wide_ref, read8_ref, w_ref, sems = refs[-6:]
    n = pl.program_id(0)
    members = x_ref.shape[0]
    lines = members * STEPS
    halves = TILE // 128
    tile = weight_tile(n, tiles, w_hbm, w_ref, sems)

    @pl.when(n == 0)
    def _():
        for j in range(FEATURES // TILE):
            read8_ref[j : j + 1, :] = read_ref[:, j * TILE : (j + 1) * TILE]
        out_ref[:, 8:, :] = jnp.broadcast_to(read8_ref[...][None], (members, 8, TILE))
        packed = x_ref[...].reshape(members * 16, TILE).astype(jnp.float32)
        for k in range(halves):
            wide_ref[k, : members * 16, :] = packed[:, k * 128 : (k + 1) * 128]
            for j in range(FEATURES // TILE):
                lane = j * TILE + k * 128
                rows_ref[:, lane : lane + 128] = wide_ref[k, pl.ds(j, lines, stride=8), :].astype(jnp.bfloat16)

    tile.wait()
    prod = jnp.dot(rows_ref[...], w_ref[n], preferred_element_type=jnp.float32)
    for k in range(halves):
        wide_ref[k, pl.ds(n, lines, stride=4), :] = prod[:, k * 128 : (k + 1) * 128]

    @pl.when(n == tiles - 1)
    def _():
        for k in range(halves):
            packed = wide_ref[k, : members * 8, :].reshape(members, 8, 128)
            out_ref[:, :8, k * 128 : (k + 1) * 128] = packed


def out_product(rows, read, blocks, after):
    members = rows.shape[0]
    tiles = blocks.shape[2] // TILE
    return pl.pallas_call(
        functools.partial(out_kernel, tiles),
        out_shape=jax.ShapeDtypeStruct((members, 16, TILE), jnp.float32),
        grid=(tiles,),
        in_specs=[whole(rows.shape), whole(read.shape), HBM] + [UNREAD] * len(after),
        out_specs=whole((members, 16, TILE)),
        scratch_shapes=[
            pltpu.VMEM((members * STEPS, FEATURES), jnp.bfloat16),
            pltpu.VMEM((TILE // 128, members * 16 + 8, 128), jnp.float32),
            pltpu.VMEM((8, TILE), jnp.float32),
            pltpu.VMEM((tiles, FEATURES, TILE), jnp.bfloat16),
            pltpu.SemaphoreType.DMA((tiles,)),
        ],
        compiler_params=kernel_params(),
        cost_estimate=cost(3 * 10**8, 5 * 10**6),
        name="out_product",
    )(rows, read, in_hbm(blocks), *after)


def finish_kernel(parts_ref, main_ref, cont_ref, head_ref, mixed_ref, out_ref, score_ref, wide_ref):
    cols = D // COL_BLOCKS
    for c in range(COL_BLOCKS):
        total = summed_block(parts_ref, c, slice(0, TILE))
        for j in range(cols // TILE):
            at = slice(c * cols + j * TILE, c * cols + (j + 1) * TILE)
            for s in range(STEPS):
                wide_ref[s : s + 1, at] = total[s * 4 + j : s * 4 + j + 1]
    out_ref[...] = (main_ref[...].astype(jnp.float32) + wide_ref[:STEPS, :]).astype(jnp.bfloat16)
    score = jnp.zeros((CTOK, TILE), jnp.float32)
    direct = jnp.zeros((STEPS, TILE), jnp.float32)
    for r in range(ROW_BLOCKS):
        read = parts_ref[r * COL_BLOCKS, 8:, :]
        for c in range(1, COL_BLOCKS):
            read = read + parts_ref[r * COL_BLOCKS + c, 8:, :]
        for j in range(FEATURES // TILE):
            lanes = slice(r * FEATURES + j * TILE, r * FEATURES + (j + 1) * TILE)
            score = score + mixed_ref[:, lanes].astype(jnp.float32) * read[j : j + 1, :]
            for c in range(CONTS):
                direct = direct + cont_ref[c, :, lanes].astype(jnp.float32) * head_ref[:, lanes]
    total = jnp.sum(score, axis=0, keepdims=True) + jnp.sum(direct, axis=0, keepdims=True)
    score_ref[...] = jnp.broadcast_to(jnp.sum(total, axis=1, keepdims=True) / CONTS, (8, 128))


def finish(parts, main, cont, head, mixed):
    return pl.pallas_call(
        finish_kernel,
        out_shape=(
            jax.ShapeDtypeStruct((STEPS, D), jnp.bfloat16),
            jax.ShapeDtypeStruct((8, 128), jnp.float32),
        ),
        in_specs=[whole(parts.shape), whole(main.shape), whole(cont.shape), whole(head.shape), whole(mixed.shape)],
        out_specs=(whole((STEPS, D)), whole((8, 128))),
        scratch_shapes=[pltpu.VMEM((8, D), jnp.float32)],
        compiler_params=kernel_params(),
        cost_estimate=cost(10**6, 2 * 10**6),
        name="finish",
    )(parts, main, cont, head, mixed)


def rope_tables(positions):
    half = HD // 2
    frequency = THETA ** (-(jnp.arange(half, dtype=jnp.float32) * 2.0) / HD)
    angles = positions.astype(jnp.float32)[:, None] * frequency[None, :]
    cosine = jnp.cos(angles)
    sine = jnp.sin(angles)
    return jnp.concatenate([cosine, cosine], axis=1), jnp.concatenate([-sine, sine], axis=1)


def exchange(rows):
    return lax.all_to_all(rows, "tp", split_axis=0, concat_axis=0, tiled=True)


ALONG = [[z * COL_BLOCKS + c for z in range(ROW_BLOCKS)] for c in range(COL_BLOCKS)]


def from_side(rows, dy, dx):
    route = []
    for to in range(MEMBERS):
        z, y, x = to // 8, to // 4 % 2, to % 4
        route.append((z * 8 + (y + dy) % 2 * 4 + (x + dx) % 4, to))
    return lax.ppermute(rows, "tp", route)


def from_along(rows, dz):
    route = [((to + dz * COL_BLOCKS) % MEMBERS, to) for to in range(MEMBERS)]
    return lax.ppermute(rows, "tp", route)


FIRST_HOMES = ((0, 0), (1, 0), (0, 1), (0, 3))
SECOND_HOMES = ((1, 1), (1, 3), (0, 2), (1, 2))
HOMES = FIRST_HOMES + SECOND_HOMES


def project(rows, blocks, bias):
    near = lax.all_to_all(rows, "tp", split_axis=0, concat_axis=0, tiled=True, axis_index_groups=ALONG)
    over = from_side(near, 1, 0)
    after, before = from_side(near, 0, 1), from_side(near, 0, 3)
    over_after, over_before = from_side(over, 0, 1), from_side(over, 0, 3)
    far = [from_side(before, 0, 3), from_side(over_after, 0, 1)]
    *first, main, weight = block_product([near, over, after, before], blocks)
    first = [first[0]] + [from_along(first[k], -k) for k in range(1, ROW_BLOCKS)]
    *second, main = block_product([over_after, over_before] + far, weight, main, HOMES)
    main, first = lax.optimization_barrier((main, first))
    second = [second[0]] + [from_along(second[k], -k) for k in range(1, ROW_BLOCKS)]
    received = []
    for homes, parts in ((FIRST_HOMES, first), (SECOND_HOMES, second)):
        for (dy, dx), summed in zip(homes, sum_parts(bias, parts)):
            received.append(from_side(summed, -dy, -dx) if dy or dx else summed)
    return received, exchange(main), second[1:] + received[1:4]


def on_device(
    main_inputs, cont_inputs, prefix_cache, prefix_len, boundary, rms_gain, qkv_bias, w_qkv, w_out, value_head
):
    main = main_inputs.reshape(STEPS, D)
    cont = cont_inputs.reshape(CONTS, STEPS, D)
    bias = qkv_bias[None, :]
    cache = prefix_cache[0]
    head = value_head[None, :]
    step = jnp.arange(CTOK, dtype=jnp.int32) % STEPS
    main_tables = rope_tables(prefix_len + step[:8])
    cont_tables = rope_tables(prefix_len + boundary + step)
    read = readout(value_head.reshape(COL_BLOCKS, D // COL_BLOCKS), w_out)
    parts, main_parts, before = project(norm_rows(main, cont, rms_gain[None, :]), w_qkv, bias)
    mixed, main_kv = attend_main(prefix_len, bias, *main_tables, cache, main_parts, before + [read])
    mixed = exchange(mixed)
    cont_mixed = attend_cont(prefix_len, boundary, bias, *cont_tables, cache, main_kv, *parts)
    parts = exchange(out_product(mixed, read, w_out, parts[4:6]))
    main_out, score = finish(parts, main, cont, head, cont_mixed)
    return main_out[None], score[0, :1]


def solution(mesh):
    return jax.shard_map(
        on_device,
        mesh=mesh,
        in_specs=(
            P(("grp", "tp"), None, None),
            P(("grp", "tp"), None, None, None),
            P(("grp", "tp"), None, None),
            P(("grp", "tp")),
            P(("grp", "tp")),
            P(),
            P(),
            P("tp", None, None),
            P("tp", None, None),
            P(),
        ),
        out_specs=(P(("grp", "tp"), None, None), P(("grp", "tp"))),
        check_vma=False,
    )
```

```python
import functools
import math

import jax
import jax.numpy as jnp
from jax import lax
from jax.experimental import pallas as pl
from jax.experimental.pallas import tpu as pltpu
from jax.sharding import PartitionSpec as P

KVH = 8
HD = 128
D = 8192
QKV = 10240
ROW_BLOCKS = 4
COL_BLOCKS = 8
MEMBERS = ROW_BLOCKS * COL_BLOCKS
FEATURES = D // ROW_BLOCKS
CONTS = 8
STEPS = 2
CTOK = CONTS * STEPS
TILE = 256

THETA = 1000000.0
EPS = 1e-06
MASKED_SCORE = -1e30

VMEM_LIMIT = 28 * 1024 * 1024
VMEM = pl.BlockSpec(memory_space=pltpu.VMEM)
SMEM = pl.BlockSpec(memory_space=pltpu.SMEM)
HBM = pl.BlockSpec(memory_space=pltpu.HBM)
UNREAD = pl.BlockSpec(memory_space=pl.ANY)


def whole(shape):
    return pl.BlockSpec(shape, lambda *_: (0,) * len(shape))


def cost(flops, moved):
    return pl.CostEstimate(flops=flops, bytes_accessed=moved, transcendentals=0)


def in_hbm(array):
    return pltpu.with_memory_space_constraint(array, pltpu.HBM)


def kernel_params():
    return pltpu.CompilerParams(vmem_limit_bytes=VMEM_LIMIT)


def norm_kernel(main_hbm, cont_hbm, gain_hbm, out_ref, main_ref, cont_ref, gain_ref, rows_ref, piece_ref, sems):
    pairs = ((main_hbm, main_ref), (cont_hbm, cont_ref), (gain_hbm, gain_ref))
    copies = [pltpu.make_async_copy(src, dst, sems.at[i]) for i, (src, dst) in enumerate(pairs)]
    for copy in copies:
        copy.start()
    for copy in copies:
        copy.wait()

    def normed(wide):
        inv = lax.rsqrt(jnp.mean(wide * wide, axis=-1, keepdims=True) + EPS)
        return wide * inv * gain_ref[...]

    for c in range(CONTS):
        rows_ref[c * STEPS : (c + 1) * STEPS, :] = cont_ref[c].astype(jnp.float32)
    cont = normed(rows_ref[...]).astype(jnp.bfloat16)
    main = normed(main_ref[...].astype(jnp.float32))
    for r in range(ROW_BLOCKS):
        for j in range(FEATURES // TILE):
            lanes = slice(r * FEATURES + j * TILE, r * FEATURES + (j + 1) * TILE)
            for s in range(STEPS):
                piece_ref[r, s * 8 + j : s * 8 + j + 1, :] = main[s : s + 1, lanes]
    for r in range(ROW_BLOCKS):
        piece = piece_ref[r].astype(jnp.bfloat16)
        out_ref[r, :, :FEATURES] = cont[:, r * FEATURES : (r + 1) * FEATURES]
        out_ref[r, :, FEATURES:] = piece


def norm_rows(main, cont, gain):
    return pl.pallas_call(
        norm_kernel,
        out_shape=jax.ShapeDtypeStruct((ROW_BLOCKS, CTOK, FEATURES + TILE), jnp.bfloat16),
        in_specs=[HBM] * 3,
        out_specs=VMEM,
        scratch_shapes=[
            pltpu.VMEM((STEPS, D), jnp.bfloat16),
            pltpu.VMEM((CONTS, STEPS, D), jnp.bfloat16),
            pltpu.VMEM((1, D), jnp.float32),
            pltpu.VMEM((CTOK, D), jnp.float32),
            pltpu.VMEM((ROW_BLOCKS, 16, TILE), jnp.float32),
            pltpu.SemaphoreType.DMA((3,)),
        ],
        compiler_params=kernel_params(),
        cost_estimate=cost(10**6, 4 * 10**6),
        name="norm_rows",
    )(in_hbm(main), in_hbm(cont), in_hbm(gain))


def weight_tile(n, tiles, w_hbm, w_ref, sems):
    def copy(i):
        lanes = pl.ds(pl.multiple_of(i * TILE, TILE), TILE)
        return pltpu.make_async_copy(w_hbm.at[0, :, lanes], w_ref.at[i], sems.at[i])

    @pl.when(n == 0)
    def _():
        for i in range(tiles):
            copy(i).start()

    return copy(n)


REST = 768


def rest_tile(block):
    return jnp.where(block == 6, 2, 0)


def plane_place():
    column = lax.rem(lax.axis_index("tp"), COL_BLOCKS)
    return column // 4, lax.rem(column, 4)


def product_kernel(tiles, counts, places, *refs):
    x_refs, refs = refs[: len(counts)], refs[len(counts) :]
    if places:
        earlier_ref, w_ref, *out_refs = refs[: 2 + ROW_BLOCKS]
        main_ref, rows_ref, wide_ref, part_ref = refs[2 + ROW_BLOCKS :]
    else:
        w_hbm, *out_refs = refs[: 1 + ROW_BLOCKS]
        main_ref, w_ref, rows_ref, wide_ref, part_ref, sems = refs[1 + ROW_BLOCKS :]
    n = pl.program_id(0)
    members = sum(counts)
    count = members * CTOK
    lines = members * STEPS
    halves = TILE // 128
    width = tiles * TILE
    if not places:
        tile = weight_tile(n, tiles, w_hbm, w_ref, sems)

    @pl.when(n == 0)
    def _():
        at = 0
        for x_ref, size in zip(x_refs, counts):
            rows = slice(at * CTOK, (at + size) * CTOK)
            rows_ref[rows, :] = x_ref[:, :, :FEATURES].reshape(size * CTOK, FEATURES)
            packed = x_ref[:, :, FEATURES:].reshape(size * CTOK, TILE).astype(jnp.float32)
            for k in range(halves):
                wide_ref[k, rows, :] = packed[:, k * 128 : (k + 1) * 128]
            at += size
        for k in range(halves):
            for j in range(FEATURES // TILE):
                lane = j * TILE + k * 128
                rows_ref[count:, lane : lane + 128] = wide_ref[k, pl.ds(j, lines, stride=8), :].astype(jnp.bfloat16)

    if not places:
        tile.wait()
    prod = jnp.dot(rows_ref[...], w_ref[n], preferred_element_type=jnp.float32)
    high = prod.astype(jnp.bfloat16)
    part_ref[:, :, pl.ds(pl.multiple_of(n * TILE, TILE), TILE)] = high[:count].reshape(members, CTOK, TILE)
    for k in range(halves):
        wide_ref[k, pl.ds(n, lines, stride=8), :] = prod[count:, k * 128 : (k + 1) * 128]
    start = rest_tile(lax.rem(lax.axis_index("tp"), COL_BLOCKS))

    @pl.when((n >= start) & (n < start + REST // TILE))
    def _():
        low = prod - high.astype(jnp.float32)
        place = n - start
        lane = pl.multiple_of(width + place * TILE, TILE)
        part_ref[:, :, pl.ds(lane, TILE)] = low[:count].astype(jnp.bfloat16).reshape(members, CTOK, TILE)
        for k in range(halves):
            wide_ref[k, pl.ds(tiles + place, lines, stride=8), :] = low[count:, k * 128 : (k + 1) * 128]

    @pl.when(n == tiles - 1)
    def _():
        z = lax.axis_index("tp") // COL_BLOCKS
        done = earlier_ref.shape[0] // ROW_BLOCKS if places else 0
        for k in range(halves):
            lanes = slice(k * 128, (k + 1) * 128)
            packed = wide_ref[k, :count, :].astype(jnp.bfloat16).reshape(members, CTOK, 128)
            if not places:
                main_ref[:, :, lanes] = packed
            for i, (dy, dx) in enumerate(places):
                y, x = plane_place()
                column = lax.rem(y + dy, 2) * 4 + lax.rem(x + dx, 4)
                for r in range(ROW_BLOCKS):
                    if i < done:
                        message = earlier_ref[i * ROW_BLOCKS + r, :, lanes]
                    else:
                        message = packed[(i - done) * ROW_BLOCKS + r]
                    main_ref[r * COL_BLOCKS + column, :, lanes] = message
        for k, out_ref in enumerate(out_refs):
            to = lax.rem(z + k, ROW_BLOCKS)
            for g in range(members // ROW_BLOCKS):
                out_ref[g] = part_ref[g * ROW_BLOCKS + to]


def block_product(messages, weight, earlier=None, places=()):
    tiles = QKV // COL_BLOCKS // TILE
    lanes = tiles * TILE + REST
    counts = tuple(rows.shape[0] for rows in messages)
    members = sum(counts)
    out = [jax.ShapeDtypeStruct((members // ROW_BLOCKS, CTOK, lanes), jnp.bfloat16)] * ROW_BLOCKS
    out.append(jax.ShapeDtypeStruct((MEMBERS if places else members, CTOK, TILE), jnp.bfloat16))
    scratch = [
        pltpu.VMEM((members * (CTOK + STEPS), FEATURES), jnp.bfloat16),
        pltpu.VMEM((TILE // 128, members * CTOK + 8, 128), jnp.float32),
        pltpu.VMEM((members, CTOK, lanes), jnp.bfloat16),
    ]
    if places:
        operands = list(messages) + [earlier, weight]
        in_specs = [VMEM] * len(operands)
    else:
        operands = list(messages) + [in_hbm(weight)]
        in_specs = [VMEM] * len(messages) + [HBM]
        out.append(jax.ShapeDtypeStruct((tiles, FEATURES, TILE), jnp.bfloat16))
        scratch.append(pltpu.SemaphoreType.DMA((tiles,)))
    return pl.pallas_call(
        functools.partial(product_kernel, tiles, counts, places),
        out_shape=out,
        grid=(tiles,),
        in_specs=in_specs,
        out_specs=[VMEM] * len(out),
        scratch_shapes=scratch,
        compiler_params=kernel_params(),
        cost_estimate=cost(2 * members * (CTOK + STEPS) * FEATURES * tiles * TILE, 12 * 10**6),
        name="block_product",
    )(*operands)


def sum_kernel(bias_ref, *refs):
    part_refs, out_refs = refs[:ROW_BLOCKS], refs[ROW_BLOCKS:]
    column = lax.rem(lax.axis_index("tp"), COL_BLOCKS)
    late = column == 6
    last = (column == COL_BLOCKS - 1).astype(jnp.float32)
    cols = QKV // COL_BLOCKS
    tiles = cols // TILE
    kept = REST // TILE
    zero = jnp.zeros((CTOK, TILE), jnp.float32)

    def value_bias(j):
        if j == 0:
            return jnp.zeros((1, TILE), jnp.float32)
        at = QKV - cols + j * TILE
        return bias_ref[:, at : at + TILE] * last

    for g, out_ref in enumerate(out_refs):

        def total(lane):
            value = part_refs[0][g, :, lane : lane + TILE].astype(jnp.float32)
            for ref in part_refs[1:]:
                value = value + ref[g, :, lane : lane + TILE].astype(jnp.float32)
            return value

        rest = [total(cols + i * TILE) for i in range(kept)] + [zero] * (tiles - kept)
        lows = []
        for j in range(tiles):
            shifted = rest[j - tiles + kept] if j >= tiles - kept else zero
            value = total(j * TILE) + jnp.where(late, shifted, rest[j]) + value_bias(j)
            high = value.astype(jnp.bfloat16)
            out_ref[:, j * TILE : (j + 1) * TILE] = high
            lows.append(value - high.astype(jnp.float32))
        for i in range(kept):
            low = jnp.where(late, lows[i + tiles - kept], lows[i])
            out_ref[:, cols + i * TILE : cols + (i + 1) * TILE] = low.astype(jnp.bfloat16)


def sum_parts(bias, parts):
    groups, rows, lanes = parts[0].shape
    return pl.pallas_call(
        sum_kernel,
        out_shape=[jax.ShapeDtypeStruct((rows, lanes), jnp.bfloat16)] * groups,
        in_specs=[VMEM] * (1 + len(parts)),
        out_specs=[VMEM] * groups,
        compiler_params=kernel_params(),
        cost_estimate=cost(10**6, 3 * 10**6),
        name="sum_parts",
    )(bias, *parts)


def load_parts(part_refs, parts_ref):
    y, x = plane_place()
    for ref, (dy, dx) in zip(part_refs, HOMES):
        column = lax.rem(y + dy, 2) * 4 + lax.rem(x + 4 - dx, 4)
        parts_ref[column] = ref[...]


def summed_block(parts_ref, c, lanes):
    total = parts_ref[c, :, lanes].astype(jnp.float32)
    for r in range(1, ROW_BLOCKS):
        total = total + parts_ref[r * COL_BLOCKS + c, :, lanes].astype(jnp.float32)
    return total


def head_attention(query, key, value, fresh_key, fresh_value, seen, fresh_seen):
    inv_root = 1.0 / math.sqrt(HD)
    contract = (((1,), (1,)), ((), ()))
    old = lax.dot_general(query, key, contract, preferred_element_type=jnp.float32) * inv_root
    new = lax.dot_general(query, fresh_key, contract, preferred_element_type=jnp.float32) * inv_root
    old = jnp.where(seen, old, MASKED_SCORE)
    new = jnp.where(fresh_seen, new, MASKED_SCORE)
    highest = jnp.maximum(jnp.max(old, axis=-1, keepdims=True), jnp.max(new, axis=-1, keepdims=True))
    old = jnp.exp(old - highest)
    new = jnp.exp(new - highest)
    mass = jnp.sum(old, axis=-1, keepdims=True) + jnp.sum(new, axis=-1, keepdims=True)
    inv_mass = 1.0 / mass
    mixed = jnp.dot((old * inv_mass).astype(jnp.bfloat16), value, preferred_element_type=jnp.float32)
    return mixed + jnp.dot((new * inv_mass).astype(jnp.bfloat16), fresh_value, preferred_element_type=jnp.float32)


def load_qkv(main, parts_ref, qkv_ref):
    cols = QKV // COL_BLOCKS
    for c in range(COL_BLOCKS):
        first = 2 if c == 6 else 0
        total = summed_block(parts_ref, c, slice(0, TILE)) if main else parts_ref[c].astype(jnp.float32)
        for j in range(cols // TILE):
            lanes = slice(c * cols + j * TILE, c * cols + (j + 1) * TILE)
            rest = j - first
            has_rest = 0 <= rest < REST // TILE
            if main:
                for s in range(STEPS):
                    line = total[s * 8 + j : s * 8 + j + 1]
                    if has_rest:
                        at = s * 8 + cols // TILE + rest
                        line = line + total[at : at + 1]
                    qkv_ref[s : s + 1, lanes] = line
            else:
                value = total[:, j * TILE : (j + 1) * TILE]
                if has_rest:
                    value = value + total[:, cols + rest * TILE : cols + (rest + 1) * TILE]
                qkv_ref[:, lanes] = value


def head_readers(qkv_ref, bias_ref, cos_ref, sin_ref):
    cosine = cos_ref[...]
    sine = sin_ref[...]

    def plain(start):
        return qkv_ref[:, start : start + HD]

    def rotated(start):
        head = plain(start) + bias_ref[:, start : start + HD]
        return head * cosine + pltpu.roll(head, HD // 2, 1) * sine

    return plain, rotated


def fresh_block(pieces):
    rows = sum(piece.shape[0] for piece in pieces)
    pad = jnp.zeros((128 - rows, HD), jnp.float32)
    return jnp.concatenate(list(pieces) + [pad], axis=0).astype(jnp.bfloat16)


GROUP = D // HD // KVH
KV_WIDTH = KVH * HD


def attend_main_kernel(
    len_ref, bias_ref, cos_ref, sin_ref, cache_ref, parts_ref, *refs
):
    out_ref, kv_ref, qkv_ref, piece_ref = refs[-4:]
    rows = qkv_ref.shape[0]
    qkv_ref[...] = jnp.zeros(qkv_ref.shape, jnp.float32)
    load_qkv(True, parts_ref, qkv_ref)
    qkv_ref[:, D + KV_WIDTH :] = qkv_ref[:, D + KV_WIDTH :] + bias_ref[:, D + KV_WIDTH :]
    plain, rotated = head_readers(qkv_ref, bias_ref, cos_ref, sin_ref)
    seen = lax.broadcasted_iota(jnp.int32, (1, cache_ref.shape[0]), 1) < len_ref[0]
    row = lax.broadcasted_iota(jnp.int32, (rows, 128), 0)
    col = lax.broadcasted_iota(jnp.int32, (rows, 128), 1)
    own = ((col <= row) & (col < STEPS)).astype(jnp.int32)
    fresh_seen = jnp.concatenate([own] * GROUP, axis=0) > 0
    for g in range(KVH):
        query = jnp.concatenate([rotated((g * GROUP + h) * HD) for h in range(GROUP)], axis=0).astype(jnp.bfloat16)
        fresh_key = rotated(D + g * HD)
        fresh_value = plain(D + KV_WIDTH + g * HD)
        kv_ref[:, g * HD : (g + 1) * HD] = fresh_key
        kv_ref[:, KV_WIDTH + g * HD : KV_WIDTH + (g + 1) * HD] = fresh_value
        key = cache_ref[:, g * HD : (g + 1) * HD]
        value = cache_ref[:, KV_WIDTH + g * HD : KV_WIDTH + (g + 1) * HD]
        mixed = head_attention(
            query, key, value, fresh_block([fresh_key]), fresh_block([fresh_value]), seen, fresh_seen
        )
        for h in range(GROUP):
            r, place = divmod(g * GROUP + h, FEATURES // HD)
            j, lane = place // 2, (place % 2) * HD
            for s in range(STEPS):
                at = s * 8 + j
                piece_ref[r, at : at + 1, lane : lane + HD] = mixed[h * rows + s : h * rows + s + 1]
    for r in range(ROW_BLOCKS):
        piece = piece_ref[r].astype(jnp.bfloat16)
        for c in range(COL_BLOCKS):
            out_ref[r * COL_BLOCKS + c] = piece


def attend_main(prefix_len, bias, cosine, sine, cache, parts, after):
    return pl.pallas_call(
        attend_main_kernel,
        out_shape=(
            jax.ShapeDtypeStruct((32, 16, TILE), jnp.bfloat16),
            jax.ShapeDtypeStruct((8, 2 * KV_WIDTH), jnp.float32),
        ),
        in_specs=[SMEM] + [VMEM] * 5 + [UNREAD] * len(after),
        out_specs=(whole((32, 16, TILE)), whole((8, 2 * KV_WIDTH))),
        scratch_shapes=[
            pltpu.VMEM((8, QKV), jnp.float32),
            pltpu.VMEM((ROW_BLOCKS, 16, TILE), jnp.float32),
        ],
        compiler_params=kernel_params(),
        cost_estimate=cost(2 * 10**8, 6 * 10**6),
        name="attend_main",
    )(prefix_len, bias, cosine, sine, cache, parts, *after)


def attend_cont_kernel(len_ref, bound_ref, bias_ref, cos_ref, sin_ref, cache_ref, kv_ref, *refs):
    part_refs = refs[:COL_BLOCKS]
    out_ref, qkv_ref, parts_ref = refs[COL_BLOCKS:]
    load_parts(part_refs, parts_ref)
    rows = qkv_ref.shape[0]
    load_qkv(False, parts_ref, qkv_ref)
    plain, rotated = head_readers(qkv_ref, bias_ref, cos_ref, sin_ref)
    seen = lax.broadcasted_iota(jnp.int32, (1, cache_ref.shape[0]), 1) < len_ref[0]
    row = lax.broadcasted_iota(jnp.int32, (rows, 128), 0)
    col = lax.broadcasted_iota(jnp.int32, (rows, 128), 1)
    own = (row // STEPS == col // STEPS) & (col <= row)
    main = (col >= rows) & (col < rows + bound_ref[0])
    fresh_seen = jnp.concatenate([(own | main).astype(jnp.int32)] * GROUP, axis=0) > 0
    for g in range(KVH):
        query = jnp.concatenate([rotated((g * GROUP + h) * HD) for h in range(GROUP)], axis=0).astype(jnp.bfloat16)
        at_key = slice(g * HD, (g + 1) * HD)
        at_value = slice(KV_WIDTH + g * HD, KV_WIDTH + (g + 1) * HD)
        fresh_key = fresh_block([rotated(D + g * HD), kv_ref[:, at_key]])
        fresh_value = fresh_block([plain(D + KV_WIDTH + g * HD), kv_ref[:, at_value]])
        mixed = head_attention(
            query, cache_ref[:, at_key], cache_ref[:, at_value], fresh_key, fresh_value, seen, fresh_seen
        )
        mixed = mixed.astype(jnp.bfloat16)
        for h in range(GROUP):
            out_ref[:, (g * GROUP + h) * HD : (g * GROUP + h + 1) * HD] = mixed[h * rows : (h + 1) * rows]


def attend_cont(*args):
    return pl.pallas_call(
        attend_cont_kernel,
        out_shape=jax.ShapeDtypeStruct((CTOK, D), jnp.bfloat16),
        in_specs=[SMEM, SMEM] + [VMEM] * 4 + [whole((8, 2 * KV_WIDTH))] + [VMEM] * COL_BLOCKS,
        out_specs=whole((CTOK, D)),
        scratch_shapes=[
            pltpu.VMEM((CTOK, QKV), jnp.float32),
            pltpu.VMEM((COL_BLOCKS,) + args[-1].shape, jnp.bfloat16),
        ],
        compiler_params=kernel_params(),
        cost_estimate=cost(4 * 10**8, 8 * 10**6),
        name="attend_cont",
    )(*args)


def readout_kernel(head_ref, w_hbm, out_ref, w_ref, sem):
    copy = pltpu.make_async_copy(w_hbm.at[0], w_ref, sem)
    copy.start()
    row = head_ref[pl.ds(lax.rem(lax.axis_index("tp"), COL_BLOCKS), 1), :]
    high = row.astype(jnp.bfloat16).astype(jnp.float32)
    middle = (row - high).astype(jnp.bfloat16).astype(jnp.float32)
    low = row - high - middle
    pieces = jnp.concatenate([high, middle, low, jnp.zeros((13, row.shape[1]), jnp.float32)], axis=0)
    copy.wait()
    prod = lax.dot_general(
        pieces.astype(jnp.bfloat16), w_ref[...], (((1,), (1,)), ((), ())), preferred_element_type=jnp.float32
    )
    out_ref[...] = prod[0:1] + prod[1:2] + prod[2:3]


def readout(value_head, blocks):
    return pl.pallas_call(
        readout_kernel,
        out_shape=jax.ShapeDtypeStruct((1, FEATURES), jnp.float32),
        in_specs=[whole(value_head.shape), HBM],
        out_specs=whole((1, FEATURES)),
        scratch_shapes=[pltpu.VMEM((FEATURES, D // COL_BLOCKS), jnp.bfloat16), pltpu.SemaphoreType.DMA],
        compiler_params=kernel_params(),
        cost_estimate=cost(2 * 10**8, 5 * 10**6),
        name="readout",
    )(value_head, in_hbm(blocks))


def out_kernel(tiles, x_ref, read_ref, w_hbm, *refs):
    out_ref, rows_ref, wide_ref, read8_ref, w_ref, sems = refs[-6:]
    n = pl.program_id(0)
    members = x_ref.shape[0]
    lines = members * STEPS
    halves = TILE // 128
    tile = weight_tile(n, tiles, w_hbm, w_ref, sems)

    @pl.when(n == 0)
    def _():
        for j in range(FEATURES // TILE):
            read8_ref[j : j + 1, :] = read_ref[:, j * TILE : (j + 1) * TILE]
        out_ref[:, 8:, :] = jnp.broadcast_to(read8_ref[...][None], (members, 8, TILE))
        packed = x_ref[...].reshape(members * 16, TILE).astype(jnp.float32)
        for k in range(halves):
            wide_ref[k, : members * 16, :] = packed[:, k * 128 : (k + 1) * 128]
            for j in range(FEATURES // TILE):
                lane = j * TILE + k * 128
                rows_ref[:, lane : lane + 128] = wide_ref[k, pl.ds(j, lines, stride=8), :].astype(jnp.bfloat16)

    tile.wait()
    prod = jnp.dot(rows_ref[...], w_ref[n], preferred_element_type=jnp.float32)
    for k in range(halves):
        wide_ref[k, pl.ds(n, lines, stride=4), :] = prod[:, k * 128 : (k + 1) * 128]

    @pl.when(n == tiles - 1)
    def _():
        for k in range(halves):
            packed = wide_ref[k, : members * 8, :].reshape(members, 8, 128)
            out_ref[:, :8, k * 128 : (k + 1) * 128] = packed


def out_product(rows, read, blocks, after):
    members = rows.shape[0]
    tiles = blocks.shape[2] // TILE
    return pl.pallas_call(
        functools.partial(out_kernel, tiles),
        out_shape=jax.ShapeDtypeStruct((members, 16, TILE), jnp.float32),
        grid=(tiles,),
        in_specs=[whole(rows.shape), whole(read.shape), HBM] + [UNREAD] * len(after),
        out_specs=whole((members, 16, TILE)),
        scratch_shapes=[
            pltpu.VMEM((members * STEPS, FEATURES), jnp.bfloat16),
            pltpu.VMEM((TILE // 128, members * 16 + 8, 128), jnp.float32),
            pltpu.VMEM((8, TILE), jnp.float32),
            pltpu.VMEM((tiles, FEATURES, TILE), jnp.bfloat16),
            pltpu.SemaphoreType.DMA((tiles,)),
        ],
        compiler_params=kernel_params(),
        cost_estimate=cost(3 * 10**8, 5 * 10**6),
        name="out_product",
    )(rows, read, in_hbm(blocks), *after)


def finish_kernel(parts_ref, main_ref, cont_ref, head_ref, mixed_ref, out_ref, score_ref, wide_ref):
    cols = D // COL_BLOCKS
    for c in range(COL_BLOCKS):
        total = summed_block(parts_ref, c, slice(0, TILE))
        for j in range(cols // TILE):
            at = slice(c * cols + j * TILE, c * cols + (j + 1) * TILE)
            for s in range(STEPS):
                wide_ref[s : s + 1, at] = total[s * 4 + j : s * 4 + j + 1]
    out_ref[...] = (main_ref[...].astype(jnp.float32) + wide_ref[:STEPS, :]).astype(jnp.bfloat16)
    score = jnp.zeros((CTOK, TILE), jnp.float32)
    direct = jnp.zeros((STEPS, TILE), jnp.float32)
    for r in range(ROW_BLOCKS):
        read = parts_ref[r * COL_BLOCKS, 8:, :]
        for c in range(1, COL_BLOCKS):
            read = read + parts_ref[r * COL_BLOCKS + c, 8:, :]
        for j in range(FEATURES // TILE):
            lanes = slice(r * FEATURES + j * TILE, r * FEATURES + (j + 1) * TILE)
            score = score + mixed_ref[:, lanes].astype(jnp.float32) * read[j : j + 1, :]
            for c in range(CONTS):
                direct = direct + cont_ref[c, :, lanes].astype(jnp.float32) * head_ref[:, lanes]
    total = jnp.sum(score, axis=0, keepdims=True) + jnp.sum(direct, axis=0, keepdims=True)
    score_ref[0] = jnp.sum(total) / CONTS


def finish(parts, main, cont, head, mixed):
    return pl.pallas_call(
        finish_kernel,
        out_shape=(
            jax.ShapeDtypeStruct((STEPS, D), jnp.bfloat16),
            jax.ShapeDtypeStruct((1,), jnp.float32),
        ),
        in_specs=[whole(parts.shape), whole(main.shape), whole(cont.shape), whole(head.shape), whole(mixed.shape)],
        out_specs=(whole((STEPS, D)), SMEM),
        scratch_shapes=[pltpu.VMEM((8, D), jnp.float32)],
        compiler_params=kernel_params(),
        cost_estimate=cost(10**6, 2 * 10**6),
        name="finish",
    )(parts, main, cont, head, mixed)


def rope_tables(positions):
    half = HD // 2
    frequency = THETA ** (-(jnp.arange(half, dtype=jnp.float32) * 2.0) / HD)
    angles = positions.astype(jnp.float32)[:, None] * frequency[None, :]
    cosine = jnp.cos(angles)
    sine = jnp.sin(angles)
    return jnp.concatenate([cosine, cosine], axis=1), jnp.concatenate([-sine, sine], axis=1)


def exchange(rows):
    return lax.all_to_all(rows, "tp", split_axis=0, concat_axis=0, tiled=True)


ALONG = [[z * COL_BLOCKS + c for z in range(ROW_BLOCKS)] for c in range(COL_BLOCKS)]


def from_side(rows, dy, dx):
    route = []
    for to in range(MEMBERS):
        z, y, x = to // 8, to // 4 % 2, to % 4
        route.append((z * 8 + (y + dy) % 2 * 4 + (x + dx) % 4, to))
    return lax.ppermute(rows, "tp", route)


def from_along(rows, dz):
    route = [((to + dz * COL_BLOCKS) % MEMBERS, to) for to in range(MEMBERS)]
    return lax.ppermute(rows, "tp", route)


FIRST_HOMES = ((0, 0), (1, 0), (0, 1), (0, 3))
SECOND_HOMES = ((1, 1), (1, 3), (0, 2), (1, 2))
HOMES = FIRST_HOMES + SECOND_HOMES


def project(rows, blocks, bias):
    near = lax.all_to_all(rows, "tp", split_axis=0, concat_axis=0, tiled=True, axis_index_groups=ALONG)
    over = from_side(near, 1, 0)
    after, before = from_side(near, 0, 1), from_side(near, 0, 3)
    over_after, over_before = from_side(over, 0, 1), from_side(over, 0, 3)
    far = [from_side(before, 0, 3), from_side(over_after, 0, 1)]
    *first, main, weight = block_product([near, over, after, before], blocks)
    first = [first[0]] + [from_along(first[k], -k) for k in range(1, ROW_BLOCKS)]
    *second, main = block_product([over_after, over_before] + far, weight, main, HOMES)
    main, first = lax.optimization_barrier((main, first))
    second = [second[0]] + [from_along(second[k], -k) for k in range(1, ROW_BLOCKS)]
    received = []
    for homes, parts in ((FIRST_HOMES, first), (SECOND_HOMES, second)):
        for (dy, dx), summed in zip(homes, sum_parts(bias, parts)):
            received.append(from_side(summed, -dy, -dx) if dy or dx else summed)
    return received, exchange(main), second[1:] + received[1:4]


def on_device(
    main_inputs, cont_inputs, prefix_cache, prefix_len, boundary, rms_gain, qkv_bias, w_qkv, w_out, value_head
):
    main = main_inputs.reshape(STEPS, D)
    cont = cont_inputs.reshape(CONTS, STEPS, D)
    bias = qkv_bias[None, :]
    cache = prefix_cache[0]
    head = value_head[None, :]
    step = jnp.arange(CTOK, dtype=jnp.int32) % STEPS
    main_tables = rope_tables(prefix_len + step[:8])
    cont_tables = rope_tables(prefix_len + boundary + step)
    read = readout(value_head.reshape(COL_BLOCKS, D // COL_BLOCKS), w_out)
    parts, main_parts, before = project(norm_rows(main, cont, rms_gain[None, :]), w_qkv, bias)
    mixed, main_kv = attend_main(prefix_len, bias, *main_tables, cache, main_parts, before + [read])
    mixed = exchange(mixed)
    cont_mixed = attend_cont(prefix_len, boundary, bias, *cont_tables, cache, main_kv, *parts)
    parts = exchange(out_product(mixed, read, w_out, parts[6:]))
    main_out, score = finish(parts, main, cont, head, cont_mixed)
    return main_out[None], score


def solution(mesh):
    return jax.shard_map(
        on_device,
        mesh=mesh,
        in_specs=(
            P(("grp", "tp"), None, None),
            P(("grp", "tp"), None, None, None),
            P(("grp", "tp"), None, None),
            P(("grp", "tp")),
            P(("grp", "tp")),
            P(),
            P(),
            P("tp", None, None),
            P("tp", None, None),
            P(),
        ),
        out_specs=(P(("grp", "tp"), None, None), P(("grp", "tp"))),
        check_vma=False,
    )
```

```python
import functools
import math

import jax
import jax.numpy as jnp
from jax import lax
from jax.experimental import pallas as pl
from jax.experimental.pallas import tpu as pltpu
from jax.sharding import PartitionSpec as P

KVH = 8
HD = 128
D = 8192
QKV = 10240
ROW_BLOCKS = 4
COL_BLOCKS = 8
MEMBERS = ROW_BLOCKS * COL_BLOCKS
FEATURES = D // ROW_BLOCKS
CONTS = 8
STEPS = 2
CTOK = CONTS * STEPS
TILE = 256

THETA = 1000000.0
EPS = 1e-06
MASKED_SCORE = -1e30

VMEM_LIMIT = 28 * 1024 * 1024
VMEM = pl.BlockSpec(memory_space=pltpu.VMEM)
SMEM = pl.BlockSpec(memory_space=pltpu.SMEM)
HBM = pl.BlockSpec(memory_space=pltpu.HBM)
UNREAD = pl.BlockSpec(memory_space=pl.ANY)


def whole(shape):
    return pl.BlockSpec(shape, lambda *_: (0,) * len(shape))


def cost(flops, moved):
    return pl.CostEstimate(flops=flops, bytes_accessed=moved, transcendentals=0)


def in_hbm(array):
    return pltpu.with_memory_space_constraint(array, pltpu.HBM)


def kernel_params():
    return pltpu.CompilerParams(vmem_limit_bytes=VMEM_LIMIT)


def norm_kernel(main_hbm, cont_hbm, gain_hbm, out_ref, main_ref, cont_ref, gain_ref, rows_ref, piece_ref, sems):
    pairs = ((main_hbm, main_ref), (cont_hbm, cont_ref), (gain_hbm, gain_ref))
    copies = [pltpu.make_async_copy(src, dst, sems.at[i]) for i, (src, dst) in enumerate(pairs)]
    for copy in copies:
        copy.start()
    for copy in copies:
        copy.wait()

    def normed(wide):
        inv = lax.rsqrt(jnp.mean(wide * wide, axis=-1, keepdims=True) + EPS)
        return wide * inv * gain_ref[...]

    for c in range(CONTS):
        rows_ref[c * STEPS : (c + 1) * STEPS, :] = cont_ref[c].astype(jnp.float32)
    cont = normed(rows_ref[...]).astype(jnp.bfloat16)
    main = normed(main_ref[...].astype(jnp.float32))
    for r in range(ROW_BLOCKS):
        for j in range(FEATURES // TILE):
            lanes = slice(r * FEATURES + j * TILE, r * FEATURES + (j + 1) * TILE)
            for s in range(STEPS):
                piece_ref[r, s * 8 + j : s * 8 + j + 1, :] = main[s : s + 1, lanes]
    for r in range(ROW_BLOCKS):
        piece = piece_ref[r].astype(jnp.bfloat16)
        out_ref[r, :, :FEATURES] = cont[:, r * FEATURES : (r + 1) * FEATURES]
        out_ref[r, :, FEATURES:] = piece


def norm_rows(main, cont, gain):
    return pl.pallas_call(
        norm_kernel,
        out_shape=jax.ShapeDtypeStruct((ROW_BLOCKS, CTOK, FEATURES + TILE), jnp.bfloat16),
        in_specs=[HBM] * 3,
        out_specs=VMEM,
        scratch_shapes=[
            pltpu.VMEM((STEPS, D), jnp.bfloat16),
            pltpu.VMEM((CONTS, STEPS, D), jnp.bfloat16),
            pltpu.VMEM((1, D), jnp.float32),
            pltpu.VMEM((CTOK, D), jnp.float32),
            pltpu.VMEM((ROW_BLOCKS, 16, TILE), jnp.float32),
            pltpu.SemaphoreType.DMA((3,)),
        ],
        compiler_params=kernel_params(),
        cost_estimate=cost(10**6, 4 * 10**6),
        name="norm_rows",
    )(in_hbm(main), in_hbm(cont), in_hbm(gain))


def weight_tile(n, tiles, w_hbm, w_ref, sems):
    def copy(i):
        lanes = pl.ds(pl.multiple_of(i * TILE, TILE), TILE)
        return pltpu.make_async_copy(w_hbm.at[0, :, lanes], w_ref.at[i], sems.at[i])

    @pl.when(n == 0)
    def _():
        for i in range(tiles):
            copy(i).start()

    return copy(n)


REST = 768


def rest_tile(block):
    return jnp.where(block == 6, 2, 0)


def plane_place():
    column = lax.rem(lax.axis_index("tp"), COL_BLOCKS)
    return column // 4, lax.rem(column, 4)


def product_kernel(tiles, counts, places, *refs):
    x_refs, refs = refs[: len(counts)], refs[len(counts) :]
    if places:
        earlier_ref, w_ref, *out_refs = refs[: 2 + ROW_BLOCKS]
        main_ref, rows_ref, wide_ref, part_ref = refs[2 + ROW_BLOCKS :]
    else:
        w_hbm, *out_refs = refs[: 1 + ROW_BLOCKS]
        main_ref, w_ref, rows_ref, wide_ref, part_ref, sems = refs[1 + ROW_BLOCKS :]
    n = pl.program_id(0)
    members = sum(counts)
    count = members * CTOK
    lines = members * STEPS
    halves = TILE // 128
    width = tiles * TILE
    if not places:
        tile = weight_tile(n, tiles, w_hbm, w_ref, sems)

    @pl.when(n == 0)
    def _():
        at = 0
        for x_ref, size in zip(x_refs, counts):
            rows = slice(at * CTOK, (at + size) * CTOK)
            rows_ref[rows, :] = x_ref[:, :, :FEATURES].reshape(size * CTOK, FEATURES)
            packed = x_ref[:, :, FEATURES:].reshape(size * CTOK, TILE).astype(jnp.float32)
            for k in range(halves):
                wide_ref[k, rows, :] = packed[:, k * 128 : (k + 1) * 128]
            at += size
        for k in range(halves):
            for j in range(FEATURES // TILE):
                lane = j * TILE + k * 128
                rows_ref[count:, lane : lane + 128] = wide_ref[k, pl.ds(j, lines, stride=8), :].astype(jnp.bfloat16)

    if not places:
        tile.wait()
    prod = jnp.dot(rows_ref[...], w_ref[n], preferred_element_type=jnp.float32)
    high = prod.astype(jnp.bfloat16)
    part_ref[:, :, pl.ds(pl.multiple_of(n * TILE, TILE), TILE)] = high[:count].reshape(members, CTOK, TILE)
    for k in range(halves):
        wide_ref[k, pl.ds(n, lines, stride=8), :] = prod[count:, k * 128 : (k + 1) * 128]
    start = rest_tile(lax.rem(lax.axis_index("tp"), COL_BLOCKS))

    @pl.when((n >= start) & (n < start + REST // TILE))
    def _():
        low = prod - high.astype(jnp.float32)
        place = n - start
        lane = pl.multiple_of(width + place * TILE, TILE)
        part_ref[:, :, pl.ds(lane, TILE)] = low[:count].astype(jnp.bfloat16).reshape(members, CTOK, TILE)
        for k in range(halves):
            wide_ref[k, pl.ds(tiles + place, lines, stride=8), :] = low[count:, k * 128 : (k + 1) * 128]

    @pl.when(n == tiles - 1)
    def _():
        z = lax.axis_index("tp") // COL_BLOCKS
        done = earlier_ref.shape[0] // ROW_BLOCKS if places else 0
        for k in range(halves):
            lanes = slice(k * 128, (k + 1) * 128)
            packed = wide_ref[k, :count, :].astype(jnp.bfloat16).reshape(members, CTOK, 128)
            if not places:
                main_ref[:, :, lanes] = packed
            for i, (dy, dx) in enumerate(places):
                y, x = plane_place()
                column = lax.rem(y + dy, 2) * 4 + lax.rem(x + dx, 4)
                for r in range(ROW_BLOCKS):
                    if i < done:
                        message = earlier_ref[i * ROW_BLOCKS + r, :, lanes]
                    else:
                        message = packed[(i - done) * ROW_BLOCKS + r]
                    main_ref[r * COL_BLOCKS + column, :, lanes] = message
        for k, out_ref in enumerate(out_refs):
            to = lax.rem(z + k, ROW_BLOCKS)
            for g in range(members // ROW_BLOCKS):
                out_ref[g] = part_ref[g * ROW_BLOCKS + to]


def block_product(messages, weight, earlier=None, places=()):
    tiles = QKV // COL_BLOCKS // TILE
    lanes = tiles * TILE + REST
    counts = tuple(rows.shape[0] for rows in messages)
    members = sum(counts)
    out = [jax.ShapeDtypeStruct((members // ROW_BLOCKS, CTOK, lanes), jnp.bfloat16)] * ROW_BLOCKS
    out.append(jax.ShapeDtypeStruct((MEMBERS if places else members, CTOK, TILE), jnp.bfloat16))
    scratch = [
        pltpu.VMEM((members * (CTOK + STEPS), FEATURES), jnp.bfloat16),
        pltpu.VMEM((TILE // 128, members * CTOK + 8, 128), jnp.float32),
        pltpu.VMEM((members, CTOK, lanes), jnp.bfloat16),
    ]
    if places:
        operands = list(messages) + [earlier, weight]
        in_specs = [VMEM] * len(operands)
    else:
        operands = list(messages) + [in_hbm(weight)]
        in_specs = [VMEM] * len(messages) + [HBM]
        out.append(jax.ShapeDtypeStruct((tiles, FEATURES, TILE), jnp.bfloat16))
        scratch.append(pltpu.SemaphoreType.DMA((tiles,)))
    return pl.pallas_call(
        functools.partial(product_kernel, tiles, counts, places),
        out_shape=out,
        grid=(tiles,),
        in_specs=in_specs,
        out_specs=[VMEM] * len(out),
        scratch_shapes=scratch,
        compiler_params=kernel_params(),
        cost_estimate=cost(2 * members * (CTOK + STEPS) * FEATURES * tiles * TILE, 12 * 10**6),
        name="block_product",
    )(*operands)


def sum_kernel(bias_ref, *refs):
    part_refs, out_refs = refs[:ROW_BLOCKS], refs[ROW_BLOCKS:]
    column = lax.rem(lax.axis_index("tp"), COL_BLOCKS)
    late = column == 6
    last = (column == COL_BLOCKS - 1).astype(jnp.float32)
    cols = QKV // COL_BLOCKS
    tiles = cols // TILE
    kept = REST // TILE
    zero = jnp.zeros((CTOK, TILE), jnp.float32)

    def value_bias(j):
        if j == 0:
            return jnp.zeros((1, TILE), jnp.float32)
        at = QKV - cols + j * TILE
        return bias_ref[:, at : at + TILE] * last

    for g, out_ref in enumerate(out_refs):

        def total(lane):
            value = part_refs[0][g, :, lane : lane + TILE].astype(jnp.float32)
            for ref in part_refs[1:]:
                value = value + ref[g, :, lane : lane + TILE].astype(jnp.float32)
            return value

        rest = [total(cols + i * TILE) for i in range(kept)] + [zero] * (tiles - kept)
        lows = []
        for j in range(tiles):
            shifted = rest[j - tiles + kept] if j >= tiles - kept else zero
            value = total(j * TILE) + jnp.where(late, shifted, rest[j]) + value_bias(j)
            high = value.astype(jnp.bfloat16)
            out_ref[:, j * TILE : (j + 1) * TILE] = high
            lows.append(value - high.astype(jnp.float32))
        for i in range(kept):
            low = jnp.where(late, lows[i + tiles - kept], lows[i])
            out_ref[:, cols + i * TILE : cols + (i + 1) * TILE] = low.astype(jnp.bfloat16)


def sum_parts(bias, parts):
    groups, rows, lanes = parts[0].shape
    return pl.pallas_call(
        sum_kernel,
        out_shape=[jax.ShapeDtypeStruct((rows, lanes), jnp.bfloat16)] * groups,
        in_specs=[VMEM] * (1 + len(parts)),
        out_specs=[VMEM] * groups,
        compiler_params=kernel_params(),
        cost_estimate=cost(10**6, 3 * 10**6),
        name="sum_parts",
    )(bias, *parts)


def load_parts(part_refs, parts_ref):
    y, x = plane_place()
    for ref, (dy, dx) in zip(part_refs, HOMES):
        column = lax.rem(y + dy, 2) * 4 + lax.rem(x + 4 - dx, 4)
        parts_ref[column] = ref[...]


def summed_block(parts_ref, c, lanes):
    total = parts_ref[c, :, lanes].astype(jnp.float32)
    for r in range(1, ROW_BLOCKS):
        total = total + parts_ref[r * COL_BLOCKS + c, :, lanes].astype(jnp.float32)
    return total


def head_attention(query, key, value, fresh_key, fresh_value, seen, fresh_seen):
    inv_root = 1.0 / math.sqrt(HD)
    contract = (((1,), (1,)), ((), ()))
    old = lax.dot_general(query, key, contract, preferred_element_type=jnp.float32) * inv_root
    new = lax.dot_general(query, fresh_key, contract, preferred_element_type=jnp.float32) * inv_root
    old = jnp.where(seen, old, MASKED_SCORE)
    new = jnp.where(fresh_seen, new, MASKED_SCORE)
    highest = jnp.maximum(jnp.max(old, axis=-1, keepdims=True), jnp.max(new, axis=-1, keepdims=True))
    old = jnp.exp(old - highest)
    new = jnp.exp(new - highest)
    mass = jnp.sum(old, axis=-1, keepdims=True) + jnp.sum(new, axis=-1, keepdims=True)
    inv_mass = 1.0 / mass
    mixed = jnp.dot((old * inv_mass).astype(jnp.bfloat16), value, preferred_element_type=jnp.float32)
    return mixed + jnp.dot((new * inv_mass).astype(jnp.bfloat16), fresh_value, preferred_element_type=jnp.float32)


def load_qkv(main, parts_ref, qkv_ref):
    cols = QKV // COL_BLOCKS
    for c in range(COL_BLOCKS):
        first = 2 if c == 6 else 0
        total = summed_block(parts_ref, c, slice(0, TILE)) if main else parts_ref[c].astype(jnp.float32)
        for j in range(cols // TILE):
            lanes = slice(c * cols + j * TILE, c * cols + (j + 1) * TILE)
            rest = j - first
            has_rest = 0 <= rest < REST // TILE
            if main:
                for s in range(STEPS):
                    line = total[s * 8 + j : s * 8 + j + 1]
                    if has_rest:
                        at = s * 8 + cols // TILE + rest
                        line = line + total[at : at + 1]
                    qkv_ref[s : s + 1, lanes] = line
            else:
                value = total[:, j * TILE : (j + 1) * TILE]
                if has_rest:
                    value = value + total[:, cols + rest * TILE : cols + (rest + 1) * TILE]
                qkv_ref[:, lanes] = value


def head_readers(qkv_ref, bias_ref, cos_ref, sin_ref):
    cosine = cos_ref[...]
    sine = sin_ref[...]

    def plain(start):
        return qkv_ref[:, start : start + HD]

    def rotated(start):
        head = plain(start) + bias_ref[:, start : start + HD]
        return head * cosine + pltpu.roll(head, HD // 2, 1) * sine

    return plain, rotated


def fresh_block(pieces):
    rows = sum(piece.shape[0] for piece in pieces)
    pad = jnp.zeros((128 - rows, HD), jnp.float32)
    return jnp.concatenate(list(pieces) + [pad], axis=0).astype(jnp.bfloat16)


GROUP = D // HD // KVH
KV_WIDTH = KVH * HD


def attend_main_kernel(
    len_ref, bias_ref, cos_ref, sin_ref, cache_ref, parts_ref, *refs
):
    out_ref, kv_ref, qkv_ref, piece_ref = refs[-4:]
    rows = qkv_ref.shape[0]
    qkv_ref[...] = jnp.zeros(qkv_ref.shape, jnp.float32)
    load_qkv(True, parts_ref, qkv_ref)
    qkv_ref[:, D + KV_WIDTH :] = qkv_ref[:, D + KV_WIDTH :] + bias_ref[:, D + KV_WIDTH :]
    plain, rotated = head_readers(qkv_ref, bias_ref, cos_ref, sin_ref)
    seen = lax.broadcasted_iota(jnp.int32, (1, cache_ref.shape[0]), 1) < len_ref[0]
    row = lax.broadcasted_iota(jnp.int32, (rows, 128), 0)
    col = lax.broadcasted_iota(jnp.int32, (rows, 128), 1)
    own = ((col <= row) & (col < STEPS)).astype(jnp.int32)
    fresh_seen = jnp.concatenate([own] * GROUP, axis=0) > 0
    for g in range(KVH):
        query = jnp.concatenate([rotated((g * GROUP + h) * HD) for h in range(GROUP)], axis=0).astype(jnp.bfloat16)
        fresh_key = rotated(D + g * HD)
        fresh_value = plain(D + KV_WIDTH + g * HD)
        kv_ref[:, g * HD : (g + 1) * HD] = fresh_key
        kv_ref[:, KV_WIDTH + g * HD : KV_WIDTH + (g + 1) * HD] = fresh_value
        key = cache_ref[:, g * HD : (g + 1) * HD]
        value = cache_ref[:, KV_WIDTH + g * HD : KV_WIDTH + (g + 1) * HD]
        mixed = head_attention(
            query, key, value, fresh_block([fresh_key]), fresh_block([fresh_value]), seen, fresh_seen
        )
        for h in range(GROUP):
            r, place = divmod(g * GROUP + h, FEATURES // HD)
            j, lane = place // 2, (place % 2) * HD
            for s in range(STEPS):
                at = s * 8 + j
                piece_ref[r, at : at + 1, lane : lane + HD] = mixed[h * rows + s : h * rows + s + 1]
    for r in range(ROW_BLOCKS):
        piece = piece_ref[r].astype(jnp.bfloat16)
        for c in range(COL_BLOCKS):
            out_ref[r * COL_BLOCKS + c] = piece


def attend_main(prefix_len, bias, cosine, sine, cache, parts, after):
    return pl.pallas_call(
        attend_main_kernel,
        out_shape=(
            jax.ShapeDtypeStruct((32, 16, TILE), jnp.bfloat16),
            jax.ShapeDtypeStruct((8, 2 * KV_WIDTH), jnp.float32),
        ),
        in_specs=[SMEM] + [VMEM] * 5 + [UNREAD] * len(after),
        out_specs=(VMEM, VMEM),
        scratch_shapes=[
            pltpu.VMEM((8, QKV), jnp.float32),
            pltpu.VMEM((ROW_BLOCKS, 16, TILE), jnp.float32),
        ],
        compiler_params=kernel_params(),
        cost_estimate=cost(2 * 10**8, 6 * 10**6),
        name="attend_main",
    )(prefix_len, bias, cosine, sine, cache, parts, *after)


def attend_cont_kernel(len_ref, bound_ref, bias_ref, cos_ref, sin_ref, cache_ref, kv_ref, *refs):
    part_refs = refs[:COL_BLOCKS]
    out_ref, qkv_ref, parts_ref = refs[COL_BLOCKS:]
    load_parts(part_refs, parts_ref)
    rows = qkv_ref.shape[0]
    load_qkv(False, parts_ref, qkv_ref)
    plain, rotated = head_readers(qkv_ref, bias_ref, cos_ref, sin_ref)
    seen = lax.broadcasted_iota(jnp.int32, (1, cache_ref.shape[0]), 1) < len_ref[0]
    row = lax.broadcasted_iota(jnp.int32, (rows, 128), 0)
    col = lax.broadcasted_iota(jnp.int32, (rows, 128), 1)
    own = (row // STEPS == col // STEPS) & (col <= row)
    main = (col >= rows) & (col < rows + bound_ref[0])
    fresh_seen = jnp.concatenate([(own | main).astype(jnp.int32)] * GROUP, axis=0) > 0
    for g in range(KVH):
        query = jnp.concatenate([rotated((g * GROUP + h) * HD) for h in range(GROUP)], axis=0).astype(jnp.bfloat16)
        at_key = slice(g * HD, (g + 1) * HD)
        at_value = slice(KV_WIDTH + g * HD, KV_WIDTH + (g + 1) * HD)
        fresh_key = fresh_block([rotated(D + g * HD), kv_ref[:, at_key]])
        fresh_value = fresh_block([plain(D + KV_WIDTH + g * HD), kv_ref[:, at_value]])
        mixed = head_attention(
            query, cache_ref[:, at_key], cache_ref[:, at_value], fresh_key, fresh_value, seen, fresh_seen
        )
        mixed = mixed.astype(jnp.bfloat16)
        for h in range(GROUP):
            out_ref[:, (g * GROUP + h) * HD : (g * GROUP + h + 1) * HD] = mixed[h * rows : (h + 1) * rows]


def attend_cont(*args):
    return pl.pallas_call(
        attend_cont_kernel,
        out_shape=jax.ShapeDtypeStruct((CTOK, D), jnp.bfloat16),
        in_specs=[SMEM, SMEM] + [VMEM] * 4 + [whole((8, 2 * KV_WIDTH))] + [VMEM] * COL_BLOCKS,
        out_specs=VMEM,
        scratch_shapes=[
            pltpu.VMEM((CTOK, QKV), jnp.float32),
            pltpu.VMEM((COL_BLOCKS,) + args[-1].shape, jnp.bfloat16),
        ],
        compiler_params=kernel_params(),
        cost_estimate=cost(4 * 10**8, 8 * 10**6),
        name="attend_cont",
    )(*args)


def readout_kernel(head_ref, w_hbm, out_ref, w_ref, sem):
    copy = pltpu.make_async_copy(w_hbm.at[0], w_ref, sem)
    copy.start()
    row = head_ref[pl.ds(lax.rem(lax.axis_index("tp"), COL_BLOCKS), 1), :]
    high = row.astype(jnp.bfloat16).astype(jnp.float32)
    middle = (row - high).astype(jnp.bfloat16).astype(jnp.float32)
    low = row - high - middle
    pieces = jnp.concatenate([high, middle, low, jnp.zeros((13, row.shape[1]), jnp.float32)], axis=0)
    copy.wait()
    prod = lax.dot_general(
        pieces.astype(jnp.bfloat16), w_ref[...], (((1,), (1,)), ((), ())), preferred_element_type=jnp.float32
    )
    out_ref[...] = prod[0:1] + prod[1:2] + prod[2:3]


def readout(value_head, blocks):
    return pl.pallas_call(
        readout_kernel,
        out_shape=jax.ShapeDtypeStruct((1, FEATURES), jnp.float32),
        in_specs=[whole(value_head.shape), HBM],
        out_specs=whole((1, FEATURES)),
        scratch_shapes=[pltpu.VMEM((FEATURES, D // COL_BLOCKS), jnp.bfloat16), pltpu.SemaphoreType.DMA],
        compiler_params=kernel_params(),
        cost_estimate=cost(2 * 10**8, 5 * 10**6),
        name="readout",
    )(value_head, in_hbm(blocks))


def out_kernel(tiles, x_ref, read_ref, w_hbm, *refs):
    out_ref, rows_ref, wide_ref, read8_ref, w_ref, sems = refs[-6:]
    n = pl.program_id(0)
    members = x_ref.shape[0]
    lines = members * STEPS
    halves = TILE // 128
    tile = weight_tile(n, tiles, w_hbm, w_ref, sems)

    @pl.when(n == 0)
    def _():
        for j in range(FEATURES // TILE):
            read8_ref[j : j + 1, :] = read_ref[:, j * TILE : (j + 1) * TILE]
        out_ref[:, 8:, :] = jnp.broadcast_to(read8_ref[...][None], (members, 8, TILE))
        packed = x_ref[...].reshape(members * 16, TILE).astype(jnp.float32)
        for k in range(halves):
            wide_ref[k, : members * 16, :] = packed[:, k * 128 : (k + 1) * 128]
            for j in range(FEATURES // TILE):
                lane = j * TILE + k * 128
                rows_ref[:, lane : lane + 128] = wide_ref[k, pl.ds(j, lines, stride=8), :].astype(jnp.bfloat16)

    tile.wait()
    prod = jnp.dot(rows_ref[...], w_ref[n], preferred_element_type=jnp.float32)
    for k in range(halves):
        wide_ref[k, pl.ds(n, lines, stride=4), :] = prod[:, k * 128 : (k + 1) * 128]

    @pl.when(n == tiles - 1)
    def _():
        for k in range(halves):
            packed = wide_ref[k, : members * 8, :].reshape(members, 8, 128)
            out_ref[:, :8, k * 128 : (k + 1) * 128] = packed


def out_product(rows, read, blocks, after):
    members = rows.shape[0]
    tiles = blocks.shape[2] // TILE
    return pl.pallas_call(
        functools.partial(out_kernel, tiles),
        out_shape=jax.ShapeDtypeStruct((members, 16, TILE), jnp.float32),
        grid=(tiles,),
        in_specs=[VMEM, VMEM, HBM] + [UNREAD] * len(after),
        out_specs=VMEM,
        scratch_shapes=[
            pltpu.VMEM((members * STEPS, FEATURES), jnp.bfloat16),
            pltpu.VMEM((TILE // 128, members * 16 + 8, 128), jnp.float32),
            pltpu.VMEM((8, TILE), jnp.float32),
            pltpu.VMEM((tiles, FEATURES, TILE), jnp.bfloat16),
            pltpu.SemaphoreType.DMA((tiles,)),
        ],
        compiler_params=kernel_params(),
        cost_estimate=cost(3 * 10**8, 5 * 10**6),
        name="out_product",
    )(rows, read, in_hbm(blocks), *after)


def finish_kernel(parts_ref, main_ref, cont_ref, head_ref, mixed_ref, out_ref, score_ref, wide_ref):
    cols = D // COL_BLOCKS
    for c in range(COL_BLOCKS):
        total = summed_block(parts_ref, c, slice(0, TILE))
        for j in range(cols // TILE):
            at = slice(c * cols + j * TILE, c * cols + (j + 1) * TILE)
            for s in range(STEPS):
                wide_ref[s : s + 1, at] = total[s * 4 + j : s * 4 + j + 1]
    out_ref[...] = (main_ref[...].astype(jnp.float32) + wide_ref[:STEPS, :]).astype(jnp.bfloat16)
    score = jnp.zeros((CTOK, TILE), jnp.float32)
    direct = jnp.zeros((STEPS, TILE), jnp.float32)
    for r in range(ROW_BLOCKS):
        read = parts_ref[r * COL_BLOCKS, 8:, :]
        for c in range(1, COL_BLOCKS):
            read = read + parts_ref[r * COL_BLOCKS + c, 8:, :]
        for j in range(FEATURES // TILE):
            lanes = slice(r * FEATURES + j * TILE, r * FEATURES + (j + 1) * TILE)
            score = score + mixed_ref[:, lanes].astype(jnp.float32) * read[j : j + 1, :]
            for c in range(CONTS):
                direct = direct + cont_ref[c, :, lanes].astype(jnp.float32) * head_ref[:, lanes]
    total = jnp.sum(score, axis=0, keepdims=True) + jnp.sum(direct, axis=0, keepdims=True)
    score_ref[0] = jnp.sum(total) / CONTS


def finish(parts, main, cont, head, mixed):
    return pl.pallas_call(
        finish_kernel,
        out_shape=(
            jax.ShapeDtypeStruct((STEPS, D), jnp.bfloat16),
            jax.ShapeDtypeStruct((1,), jnp.float32),
        ),
        in_specs=[VMEM] * 5,
        out_specs=(whole((STEPS, D)), SMEM),
        scratch_shapes=[pltpu.VMEM((8, D), jnp.float32)],
        compiler_params=kernel_params(),
        cost_estimate=cost(10**6, 2 * 10**6),
        name="finish",
    )(parts, main, cont, head, mixed)


def rope_tables(positions):
    half = HD // 2
    frequency = THETA ** (-(jnp.arange(half, dtype=jnp.float32) * 2.0) / HD)
    angles = positions.astype(jnp.float32)[:, None] * frequency[None, :]
    cosine = jnp.cos(angles)
    sine = jnp.sin(angles)
    return jnp.concatenate([cosine, cosine], axis=1), jnp.concatenate([-sine, sine], axis=1)


def exchange(rows):
    return lax.all_to_all(rows, "tp", split_axis=0, concat_axis=0, tiled=True)


ALONG = [[z * COL_BLOCKS + c for z in range(ROW_BLOCKS)] for c in range(COL_BLOCKS)]


def from_side(rows, dy, dx):
    route = []
    for to in range(MEMBERS):
        z, y, x = to // 8, to // 4 % 2, to % 4
        route.append((z * 8 + (y + dy) % 2 * 4 + (x + dx) % 4, to))
    return lax.ppermute(rows, "tp", route)


def from_along(rows, dz):
    route = [((to + dz * COL_BLOCKS) % MEMBERS, to) for to in range(MEMBERS)]
    return lax.ppermute(rows, "tp", route)


FIRST_HOMES = ((0, 0), (1, 0), (0, 1), (0, 3))
SECOND_HOMES = ((1, 1), (1, 3), (0, 2), (1, 2))
HOMES = FIRST_HOMES + SECOND_HOMES


def project(rows, blocks, bias):
    near = lax.all_to_all(rows, "tp", split_axis=0, concat_axis=0, tiled=True, axis_index_groups=ALONG)
    over = from_side(near, 1, 0)
    after, before = from_side(near, 0, 1), from_side(near, 0, 3)
    over_after, over_before = from_side(over, 0, 1), from_side(over, 0, 3)
    far = [from_side(before, 0, 3), from_side(over_after, 0, 1)]
    *first, main, weight = block_product([near, over, after, before], blocks)
    first = [first[0]] + [from_along(first[k], -k) for k in range(1, ROW_BLOCKS)]
    *second, main = block_product([over_after, over_before] + far, weight, main, HOMES)
    main, first = lax.optimization_barrier((main, first))
    second = [second[0]] + [from_along(second[k], -k) for k in range(1, ROW_BLOCKS)]
    received = []
    for homes, parts in ((FIRST_HOMES, first), (SECOND_HOMES, second)):
        for (dy, dx), summed in zip(homes, sum_parts(bias, parts)):
            received.append(from_side(summed, -dy, -dx) if dy or dx else summed)
    return received, exchange(main), second[1:] + received[1:4]


def on_device(
    main_inputs, cont_inputs, prefix_cache, prefix_len, boundary, rms_gain, qkv_bias, w_qkv, w_out, value_head
):
    main = main_inputs.reshape(STEPS, D)
    cont = cont_inputs.reshape(CONTS, STEPS, D)
    bias = qkv_bias[None, :]
    cache = prefix_cache[0]
    head = value_head[None, :]
    step = jnp.arange(CTOK, dtype=jnp.int32) % STEPS
    main_tables = rope_tables(prefix_len + step[:8])
    cont_tables = rope_tables(prefix_len + boundary + step)
    read = readout(value_head.reshape(COL_BLOCKS, D // COL_BLOCKS), w_out)
    parts, main_parts, before = project(norm_rows(main, cont, rms_gain[None, :]), w_qkv, bias)
    mixed, main_kv = attend_main(prefix_len, bias, *main_tables, cache, main_parts, before + [read])
    mixed = exchange(mixed)
    cont_mixed = attend_cont(prefix_len, boundary, bias, *cont_tables, cache, main_kv, *parts)
    parts = exchange(out_product(mixed, read, w_out, parts[6:]))
    main_out, score = finish(parts, main, cont, head, cont_mixed)
    return main_out[None], score


def solution(mesh):
    return jax.shard_map(
        on_device,
        mesh=mesh,
        in_specs=(
            P(("grp", "tp"), None, None),
            P(("grp", "tp"), None, None, None),
            P(("grp", "tp"), None, None),
            P(("grp", "tp")),
            P(("grp", "tp")),
            P(),
            P(),
            P("tp", None, None),
            P("tp", None, None),
            P(),
        ),
        out_specs=(P(("grp", "tp"), None, None), P(("grp", "tp"))),
        check_vma=False,
    )
```

```python
import functools
import math

import jax
import jax.numpy as jnp
from jax import lax
from jax.experimental import pallas as pl
from jax.experimental.pallas import tpu as pltpu
from jax.sharding import PartitionSpec as P

KVH = 8
HD = 128
D = 8192
QKV = 10240
ROW_BLOCKS = 4
COL_BLOCKS = 8
MEMBERS = ROW_BLOCKS * COL_BLOCKS
FEATURES = D // ROW_BLOCKS
CONTS = 8
STEPS = 2
CTOK = CONTS * STEPS
TILE = 256

THETA = 1000000.0
EPS = 1e-06
MASKED_SCORE = -1e30

VMEM_LIMIT = 28 * 1024 * 1024
VMEM = pl.BlockSpec(memory_space=pltpu.VMEM)
SMEM = pl.BlockSpec(memory_space=pltpu.SMEM)
HBM = pl.BlockSpec(memory_space=pltpu.HBM)
UNREAD = pl.BlockSpec(memory_space=pl.ANY)


def whole(shape):
    return pl.BlockSpec(shape, lambda *_: (0,) * len(shape))


def cost(flops, moved):
    return pl.CostEstimate(flops=flops, bytes_accessed=moved, transcendentals=0)


def in_hbm(array):
    return pltpu.with_memory_space_constraint(array, pltpu.HBM)


def kernel_params():
    return pltpu.CompilerParams(vmem_limit_bytes=VMEM_LIMIT)


def norm_kernel(main_hbm, cont_hbm, gain_hbm, out_ref, main_ref, cont_ref, gain_ref, rows_ref, piece_ref, sems):
    pairs = ((main_hbm, main_ref), (cont_hbm, cont_ref), (gain_hbm, gain_ref))
    copies = [pltpu.make_async_copy(src, dst, sems.at[i]) for i, (src, dst) in enumerate(pairs)]
    for copy in copies:
        copy.start()
    for copy in copies:
        copy.wait()

    def normed(wide):
        inv = lax.rsqrt(jnp.mean(wide * wide, axis=-1, keepdims=True) + EPS)
        return wide * inv * gain_ref[...]

    for c in range(CONTS):
        rows_ref[c * STEPS : (c + 1) * STEPS, :] = cont_ref[c].astype(jnp.float32)
    cont = normed(rows_ref[...]).astype(jnp.bfloat16)
    main = normed(main_ref[...].astype(jnp.float32))
    for r in range(ROW_BLOCKS):
        for j in range(FEATURES // TILE):
            lanes = slice(r * FEATURES + j * TILE, r * FEATURES + (j + 1) * TILE)
            for s in range(STEPS):
                piece_ref[r, s * 8 + j : s * 8 + j + 1, :] = main[s : s + 1, lanes]
    for r in range(ROW_BLOCKS):
        piece = piece_ref[r].astype(jnp.bfloat16)
        out_ref[r, :, :FEATURES] = cont[:, r * FEATURES : (r + 1) * FEATURES]
        out_ref[r, :, FEATURES:] = piece


def norm_rows(main, cont, gain):
    return pl.pallas_call(
        norm_kernel,
        out_shape=jax.ShapeDtypeStruct((ROW_BLOCKS, CTOK, FEATURES + TILE), jnp.bfloat16),
        in_specs=[HBM] * 3,
        out_specs=VMEM,
        scratch_shapes=[
            pltpu.VMEM((STEPS, D), jnp.bfloat16),
            pltpu.VMEM((CONTS, STEPS, D), jnp.bfloat16),
            pltpu.VMEM((1, D), jnp.float32),
            pltpu.VMEM((CTOK, D), jnp.float32),
            pltpu.VMEM((ROW_BLOCKS, 16, TILE), jnp.float32),
            pltpu.SemaphoreType.DMA((3,)),
        ],
        compiler_params=kernel_params(),
        cost_estimate=cost(10**6, 4 * 10**6),
        name="norm_rows",
    )(in_hbm(main), in_hbm(cont), in_hbm(gain))


def weight_tile(n, tiles, w_hbm, w_ref, sems):
    def copy(i):
        lanes = pl.ds(pl.multiple_of(i * TILE, TILE), TILE)
        return pltpu.make_async_copy(w_hbm.at[0, :, lanes], w_ref.at[i], sems.at[i])

    @pl.when(n == 0)
    def _():
        for i in range(tiles):
            copy(i).start()

    return copy(n)


REST = 768


def rest_tile(block):
    return jnp.where(block == 6, 2, 0)


def plane_place():
    column = lax.rem(lax.axis_index("tp"), COL_BLOCKS)
    return column // 4, lax.rem(column, 4)


def product_kernel(tiles, counts, places, *refs):
    x_refs, refs = refs[: len(counts)], refs[len(counts) :]
    if places:
        earlier_ref, w_ref, *out_refs = refs[: 2 + ROW_BLOCKS]
        main_ref, rows_ref, wide_ref, part_ref = refs[2 + ROW_BLOCKS :]
    else:
        w_hbm, *out_refs = refs[: 1 + ROW_BLOCKS]
        main_ref, w_ref, rows_ref, wide_ref, part_ref, sems = refs[1 + ROW_BLOCKS :]
    n = pl.program_id(0)
    members = sum(counts)
    count = members * CTOK
    lines = members * STEPS
    halves = TILE // 128
    width = tiles * TILE
    if not places:
        tile = weight_tile(n, tiles, w_hbm, w_ref, sems)

    @pl.when(n == 0)
    def _():
        at = 0
        for x_ref, size in zip(x_refs, counts):
            rows = slice(at * CTOK, (at + size) * CTOK)
            rows_ref[rows, :] = x_ref[:, :, :FEATURES].reshape(size * CTOK, FEATURES)
            packed = x_ref[:, :, FEATURES:].reshape(size * CTOK, TILE).astype(jnp.float32)
            for k in range(halves):
                wide_ref[k, rows, :] = packed[:, k * 128 : (k + 1) * 128]
            at += size
        for k in range(halves):
            for j in range(FEATURES // TILE):
                lane = j * TILE + k * 128
                rows_ref[count:, lane : lane + 128] = wide_ref[k, pl.ds(j, lines, stride=8), :].astype(jnp.bfloat16)

    if not places:
        tile.wait()
    prod = jnp.dot(rows_ref[...], w_ref[n], preferred_element_type=jnp.float32)
    high = prod.astype(jnp.bfloat16)
    part_ref[:, :, pl.ds(pl.multiple_of(n * TILE, TILE), TILE)] = high[:count].reshape(members, CTOK, TILE)
    for k in range(halves):
        wide_ref[k, pl.ds(n, lines, stride=8), :] = prod[count:, k * 128 : (k + 1) * 128]
    start = rest_tile(lax.rem(lax.axis_index("tp"), COL_BLOCKS))

    @pl.when((n >= start) & (n < start + REST // TILE))
    def _():
        low = prod - high.astype(jnp.float32)
        place = n - start
        lane = pl.multiple_of(width + place * TILE, TILE)
        part_ref[:, :, pl.ds(lane, TILE)] = low[:count].astype(jnp.bfloat16).reshape(members, CTOK, TILE)
        for k in range(halves):
            wide_ref[k, pl.ds(tiles + place, lines, stride=8), :] = low[count:, k * 128 : (k + 1) * 128]

    @pl.when(n == tiles - 1)
    def _():
        z = lax.axis_index("tp") // COL_BLOCKS
        done = earlier_ref.shape[0] // ROW_BLOCKS if places else 0
        for k in range(halves):
            lanes = slice(k * 128, (k + 1) * 128)
            packed = wide_ref[k, :count, :].astype(jnp.bfloat16).reshape(members, CTOK, 128)
            if not places:
                main_ref[:, :, lanes] = packed
            for i, (dy, dx) in enumerate(places):
                y, x = plane_place()
                column = lax.rem(y + dy, 2) * 4 + lax.rem(x + dx, 4)
                for r in range(ROW_BLOCKS):
                    if i < done:
                        message = earlier_ref[i * ROW_BLOCKS + r, :, lanes]
                    else:
                        message = packed[(i - done) * ROW_BLOCKS + r]
                    main_ref[r * COL_BLOCKS + column, :, lanes] = message
        for k, out_ref in enumerate(out_refs):
            to = lax.rem(z + k, ROW_BLOCKS)
            for g in range(members // ROW_BLOCKS):
                out_ref[g] = part_ref[g * ROW_BLOCKS + to]


def block_product(messages, weight, earlier=None, places=()):
    tiles = QKV // COL_BLOCKS // TILE
    lanes = tiles * TILE + REST
    counts = tuple(rows.shape[0] for rows in messages)
    members = sum(counts)
    out = [jax.ShapeDtypeStruct((members // ROW_BLOCKS, CTOK, lanes), jnp.bfloat16)] * ROW_BLOCKS
    out.append(jax.ShapeDtypeStruct((MEMBERS if places else members, CTOK, TILE), jnp.bfloat16))
    scratch = [
        pltpu.VMEM((members * (CTOK + STEPS), FEATURES), jnp.bfloat16),
        pltpu.VMEM((TILE // 128, members * CTOK + 8, 128), jnp.float32),
        pltpu.VMEM((members, CTOK, lanes), jnp.bfloat16),
    ]
    if places:
        operands = list(messages) + [earlier, weight]
        in_specs = [VMEM] * len(operands)
    else:
        operands = list(messages) + [in_hbm(weight)]
        in_specs = [VMEM] * len(messages) + [HBM]
        out.append(jax.ShapeDtypeStruct((tiles, FEATURES, TILE), jnp.bfloat16))
        scratch.append(pltpu.SemaphoreType.DMA((tiles,)))
    return pl.pallas_call(
        functools.partial(product_kernel, tiles, counts, places),
        out_shape=out,
        grid=(tiles,),
        in_specs=in_specs,
        out_specs=[VMEM] * len(out),
        scratch_shapes=scratch,
        compiler_params=kernel_params(),
        cost_estimate=cost(2 * members * (CTOK + STEPS) * FEATURES * tiles * TILE, 12 * 10**6),
        name="block_product",
    )(*operands)


def sum_kernel(bias_ref, *refs):
    part_refs, out_refs = refs[:ROW_BLOCKS], refs[ROW_BLOCKS:]
    column = lax.rem(lax.axis_index("tp"), COL_BLOCKS)
    late = column == 6
    last = (column == COL_BLOCKS - 1).astype(jnp.float32)
    cols = QKV // COL_BLOCKS
    tiles = cols // TILE
    kept = REST // TILE
    zero = jnp.zeros((CTOK, TILE), jnp.float32)

    def value_bias(j):
        if j == 0:
            return jnp.zeros((1, TILE), jnp.float32)
        at = QKV - cols + j * TILE
        return bias_ref[:, at : at + TILE] * last

    for g, out_ref in enumerate(out_refs):

        def total(lane):
            value = part_refs[0][g, :, lane : lane + TILE].astype(jnp.float32)
            for ref in part_refs[1:]:
                value = value + ref[g, :, lane : lane + TILE].astype(jnp.float32)
            return value

        rest = [total(cols + i * TILE) for i in range(kept)] + [zero] * (tiles - kept)
        lows = []
        for j in range(tiles):
            shifted = rest[j - tiles + kept] if j >= tiles - kept else zero
            value = total(j * TILE) + jnp.where(late, shifted, rest[j]) + value_bias(j)
            high = value.astype(jnp.bfloat16)
            out_ref[:, j * TILE : (j + 1) * TILE] = high
            lows.append(value - high.astype(jnp.float32))
        for i in range(kept):
            low = jnp.where(late, lows[i + tiles - kept], lows[i])
            out_ref[:, cols + i * TILE : cols + (i + 1) * TILE] = low.astype(jnp.bfloat16)


def sum_parts(bias, parts):
    groups, rows, lanes = parts[0].shape
    return pl.pallas_call(
        sum_kernel,
        out_shape=[jax.ShapeDtypeStruct((rows, lanes), jnp.bfloat16)] * groups,
        in_specs=[VMEM] * (1 + len(parts)),
        out_specs=[VMEM] * groups,
        compiler_params=kernel_params(),
        cost_estimate=cost(10**6, 3 * 10**6),
        name="sum_parts",
    )(bias, *parts)


def load_parts(part_refs, parts_ref):
    y, x = plane_place()
    for ref, (dy, dx) in zip(part_refs, HOMES):
        column = lax.rem(y + dy, 2) * 4 + lax.rem(x + 4 - dx, 4)
        parts_ref[column] = ref[...]


def summed_block(parts_ref, c, lanes):
    total = parts_ref[c, :, lanes].astype(jnp.float32)
    for r in range(1, ROW_BLOCKS):
        total = total + parts_ref[r * COL_BLOCKS + c, :, lanes].astype(jnp.float32)
    return total


def head_attention(query, key, value, fresh_key, fresh_value, seen, fresh_seen):
    inv_root = 1.0 / math.sqrt(HD)
    contract = (((1,), (1,)), ((), ()))
    old = lax.dot_general(query, key, contract, preferred_element_type=jnp.float32) * inv_root
    new = lax.dot_general(query, fresh_key, contract, preferred_element_type=jnp.float32) * inv_root
    old = jnp.where(seen, old, MASKED_SCORE)
    new = jnp.where(fresh_seen, new, MASKED_SCORE)
    highest = jnp.maximum(jnp.max(old, axis=-1, keepdims=True), jnp.max(new, axis=-1, keepdims=True))
    old = jnp.exp(old - highest)
    new = jnp.exp(new - highest)
    mass = jnp.sum(old, axis=-1, keepdims=True) + jnp.sum(new, axis=-1, keepdims=True)
    inv_mass = 1.0 / mass
    mixed = jnp.dot((old * inv_mass).astype(jnp.bfloat16), value, preferred_element_type=jnp.float32)
    return mixed + jnp.dot((new * inv_mass).astype(jnp.bfloat16), fresh_value, preferred_element_type=jnp.float32)


def load_qkv(main, parts_ref, qkv_ref):
    cols = QKV // COL_BLOCKS
    for c in range(COL_BLOCKS):
        first = 2 if c == 6 else 0
        total = summed_block(parts_ref, c, slice(0, TILE)) if main else parts_ref[c].astype(jnp.float32)
        for j in range(cols // TILE):
            lanes = slice(c * cols + j * TILE, c * cols + (j + 1) * TILE)
            rest = j - first
            has_rest = 0 <= rest < REST // TILE
            if main:
                for s in range(STEPS):
                    line = total[s * 8 + j : s * 8 + j + 1]
                    if has_rest:
                        at = s * 8 + cols // TILE + rest
                        line = line + total[at : at + 1]
                    qkv_ref[s : s + 1, lanes] = line
            else:
                value = total[:, j * TILE : (j + 1) * TILE]
                if has_rest:
                    value = value + total[:, cols + rest * TILE : cols + (rest + 1) * TILE]
                qkv_ref[:, lanes] = value


def head_readers(qkv_ref, bias_ref, cos_ref, sin_ref):
    cosine = cos_ref[...]
    sine = sin_ref[...]

    def plain(start):
        return qkv_ref[:, start : start + HD]

    def rotated(start):
        head = plain(start) + bias_ref[:, start : start + HD]
        return head * cosine + pltpu.roll(head, HD // 2, 1) * sine

    return plain, rotated


def fresh_block(pieces):
    rows = sum(piece.shape[0] for piece in pieces)
    pad = jnp.zeros((128 - rows, HD), jnp.float32)
    return jnp.concatenate(list(pieces) + [pad], axis=0).astype(jnp.bfloat16)


GROUP = D // HD // KVH
KV_WIDTH = KVH * HD


def attend_main_kernel(
    len_ref, bias_ref, cos_ref, sin_ref, cache_ref, parts_ref, *refs
):
    out_ref, kv_ref, qkv_ref, piece_ref = refs[-4:]
    rows = qkv_ref.shape[0]
    qkv_ref[...] = jnp.zeros(qkv_ref.shape, jnp.float32)
    load_qkv(True, parts_ref, qkv_ref)
    qkv_ref[:, D + KV_WIDTH :] = qkv_ref[:, D + KV_WIDTH :] + bias_ref[:, D + KV_WIDTH :]
    plain, rotated = head_readers(qkv_ref, bias_ref, cos_ref, sin_ref)
    seen = lax.broadcasted_iota(jnp.int32, (1, cache_ref.shape[0]), 1) < len_ref[0]
    row = lax.broadcasted_iota(jnp.int32, (rows, 128), 0)
    col = lax.broadcasted_iota(jnp.int32, (rows, 128), 1)
    own = ((col <= row) & (col < STEPS)).astype(jnp.int32)
    fresh_seen = jnp.concatenate([own] * GROUP, axis=0) > 0
    for g in range(KVH):
        query = jnp.concatenate([rotated((g * GROUP + h) * HD) for h in range(GROUP)], axis=0).astype(jnp.bfloat16)
        fresh_key = rotated(D + g * HD)
        fresh_value = plain(D + KV_WIDTH + g * HD)
        kv_ref[:, g * HD : (g + 1) * HD] = fresh_key
        kv_ref[:, KV_WIDTH + g * HD : KV_WIDTH + (g + 1) * HD] = fresh_value
        key = cache_ref[:, g * HD : (g + 1) * HD]
        value = cache_ref[:, KV_WIDTH + g * HD : KV_WIDTH + (g + 1) * HD]
        mixed = head_attention(
            query, key, value, fresh_block([fresh_key]), fresh_block([fresh_value]), seen, fresh_seen
        )
        for h in range(GROUP):
            r, place = divmod(g * GROUP + h, FEATURES // HD)
            j, lane = place // 2, (place % 2) * HD
            for s in range(STEPS):
                at = s * 8 + j
                piece_ref[r, at : at + 1, lane : lane + HD] = mixed[h * rows + s : h * rows + s + 1]
    for r in range(ROW_BLOCKS):
        piece = piece_ref[r].astype(jnp.bfloat16)
        for c in range(COL_BLOCKS):
            out_ref[r * COL_BLOCKS + c] = piece


def attend_main(prefix_len, bias, cosine, sine, cache, parts, after):
    return pl.pallas_call(
        attend_main_kernel,
        out_shape=(
            jax.ShapeDtypeStruct((32, 16, TILE), jnp.bfloat16),
            jax.ShapeDtypeStruct((8, 2 * KV_WIDTH), jnp.float32),
        ),
        in_specs=[SMEM] + [VMEM] * 5 + [UNREAD] * len(after),
        out_specs=(whole((32, 16, TILE)), whole((8, 2 * KV_WIDTH))),
        scratch_shapes=[
            pltpu.VMEM((8, QKV), jnp.float32),
            pltpu.VMEM((ROW_BLOCKS, 16, TILE), jnp.float32),
        ],
        compiler_params=kernel_params(),
        cost_estimate=cost(2 * 10**8, 6 * 10**6),
        name="attend_main",
    )(prefix_len, bias, cosine, sine, cache, parts, *after)


def attend_cont_kernel(len_ref, bound_ref, bias_ref, cos_ref, sin_ref, cache_ref, kv_ref, *refs):
    part_refs = refs[:COL_BLOCKS]
    out_ref, qkv_ref, parts_ref = refs[COL_BLOCKS:]
    load_parts(part_refs, parts_ref)
    rows = qkv_ref.shape[0]
    load_qkv(False, parts_ref, qkv_ref)
    plain, rotated = head_readers(qkv_ref, bias_ref, cos_ref, sin_ref)
    seen = lax.broadcasted_iota(jnp.int32, (1, cache_ref.shape[0]), 1) < len_ref[0]
    row = lax.broadcasted_iota(jnp.int32, (rows, 128), 0)
    col = lax.broadcasted_iota(jnp.int32, (rows, 128), 1)
    own = (row // STEPS == col // STEPS) & (col <= row)
    main = (col >= rows) & (col < rows + bound_ref[0])
    fresh_seen = jnp.concatenate([(own | main).astype(jnp.int32)] * GROUP, axis=0) > 0
    for g in range(KVH):
        query = jnp.concatenate([rotated((g * GROUP + h) * HD) for h in range(GROUP)], axis=0).astype(jnp.bfloat16)
        at_key = slice(g * HD, (g + 1) * HD)
        at_value = slice(KV_WIDTH + g * HD, KV_WIDTH + (g + 1) * HD)
        fresh_key = fresh_block([rotated(D + g * HD), kv_ref[:, at_key]])
        fresh_value = fresh_block([plain(D + KV_WIDTH + g * HD), kv_ref[:, at_value]])
        mixed = head_attention(
            query, cache_ref[:, at_key], cache_ref[:, at_value], fresh_key, fresh_value, seen, fresh_seen
        )
        mixed = mixed.astype(jnp.bfloat16)
        for h in range(GROUP):
            out_ref[:, (g * GROUP + h) * HD : (g * GROUP + h + 1) * HD] = mixed[h * rows : (h + 1) * rows]


def attend_cont(*args):
    return pl.pallas_call(
        attend_cont_kernel,
        out_shape=jax.ShapeDtypeStruct((CTOK, D), jnp.bfloat16),
        in_specs=[SMEM, SMEM] + [VMEM] * 4 + [whole((8, 2 * KV_WIDTH))] + [VMEM] * COL_BLOCKS,
        out_specs=whole((CTOK, D)),
        scratch_shapes=[
            pltpu.VMEM((CTOK, QKV), jnp.float32),
            pltpu.VMEM((COL_BLOCKS,) + args[-1].shape, jnp.bfloat16),
        ],
        compiler_params=kernel_params(),
        cost_estimate=cost(4 * 10**8, 8 * 10**6),
        name="attend_cont",
    )(*args)


def readout_kernel(head_ref, w_hbm, out_ref, w_ref, sem):
    copy = pltpu.make_async_copy(w_hbm.at[0], w_ref, sem)
    copy.start()
    row = head_ref[pl.ds(lax.rem(lax.axis_index("tp"), COL_BLOCKS), 1), :]
    high = row.astype(jnp.bfloat16).astype(jnp.float32)
    middle = (row - high).astype(jnp.bfloat16).astype(jnp.float32)
    low = row - high - middle
    pieces = jnp.concatenate([high, middle, low, jnp.zeros((13, row.shape[1]), jnp.float32)], axis=0)
    copy.wait()
    prod = lax.dot_general(
        pieces.astype(jnp.bfloat16), w_ref[...], (((1,), (1,)), ((), ())), preferred_element_type=jnp.float32
    )
    out_ref[...] = prod[0:1] + prod[1:2] + prod[2:3]


def readout(value_head, blocks):
    return pl.pallas_call(
        readout_kernel,
        out_shape=jax.ShapeDtypeStruct((1, FEATURES), jnp.float32),
        in_specs=[whole(value_head.shape), HBM],
        out_specs=whole((1, FEATURES)),
        scratch_shapes=[pltpu.VMEM((FEATURES, D // COL_BLOCKS), jnp.bfloat16), pltpu.SemaphoreType.DMA],
        compiler_params=kernel_params(),
        cost_estimate=cost(2 * 10**8, 5 * 10**6),
        name="readout",
    )(value_head, in_hbm(blocks))


def out_kernel(tiles, x_ref, read_ref, w_hbm, *refs):
    out_ref, rows_ref, wide_ref, read8_ref, w_ref, sems = refs[-6:]
    n = pl.program_id(0)
    members = x_ref.shape[0]
    lines = members * STEPS
    halves = TILE // 128
    tile = weight_tile(n, tiles, w_hbm, w_ref, sems)

    @pl.when(n == 0)
    def _():
        for j in range(FEATURES // TILE):
            read8_ref[j : j + 1, :] = read_ref[:, j * TILE : (j + 1) * TILE]
        out_ref[:, 8:, :] = jnp.broadcast_to(read8_ref[...][None], (members, 8, TILE))
        packed = x_ref[...].reshape(members * 16, TILE).astype(jnp.float32)
        for k in range(halves):
            wide_ref[k, : members * 16, :] = packed[:, k * 128 : (k + 1) * 128]
            for j in range(FEATURES // TILE):
                lane = j * TILE + k * 128
                rows_ref[:, lane : lane + 128] = wide_ref[k, pl.ds(j, lines, stride=8), :].astype(jnp.bfloat16)

    tile.wait()
    prod = jnp.dot(rows_ref[...], w_ref[n], preferred_element_type=jnp.float32)
    for k in range(halves):
        wide_ref[k, pl.ds(n, lines, stride=4), :] = prod[:, k * 128 : (k + 1) * 128]

    @pl.when(n == tiles - 1)
    def _():
        for k in range(halves):
            packed = wide_ref[k, : members * 8, :].reshape(members, 8, 128)
            out_ref[:, :8, k * 128 : (k + 1) * 128] = packed


def out_product(rows, read, blocks, after):
    members = rows.shape[0]
    tiles = blocks.shape[2] // TILE
    return pl.pallas_call(
        functools.partial(out_kernel, tiles),
        out_shape=jax.ShapeDtypeStruct((members, 16, TILE), jnp.float32),
        grid=(tiles,),
        in_specs=[whole(rows.shape), whole(read.shape), HBM] + [UNREAD] * len(after),
        out_specs=whole((members, 16, TILE)),
        scratch_shapes=[
            pltpu.VMEM((members * STEPS, FEATURES), jnp.bfloat16),
            pltpu.VMEM((TILE // 128, members * 16 + 8, 128), jnp.float32),
            pltpu.VMEM((8, TILE), jnp.float32),
            pltpu.VMEM((tiles, FEATURES, TILE), jnp.bfloat16),
            pltpu.SemaphoreType.DMA((tiles,)),
        ],
        compiler_params=kernel_params(),
        cost_estimate=cost(3 * 10**8, 5 * 10**6),
        name="out_product",
    )(rows, read, in_hbm(blocks), *after)


def finish_kernel(parts_ref, main_ref, cont_ref, head_ref, mixed_ref, out_ref, score_ref, wide_ref):
    cols = D // COL_BLOCKS
    for c in range(COL_BLOCKS):
        total = summed_block(parts_ref, c, slice(0, TILE))
        for j in range(cols // TILE):
            at = slice(c * cols + j * TILE, c * cols + (j + 1) * TILE)
            for s in range(STEPS):
                wide_ref[s : s + 1, at] = total[s * 4 + j : s * 4 + j + 1]
    out_ref[...] = (main_ref[...].astype(jnp.float32) + wide_ref[:STEPS, :]).astype(jnp.bfloat16)
    score = jnp.zeros((CTOK, TILE), jnp.float32)
    direct = jnp.zeros((STEPS, TILE), jnp.float32)
    for r in range(ROW_BLOCKS):
        read = parts_ref[r * COL_BLOCKS, 8:, :]
        for c in range(1, COL_BLOCKS):
            read = read + parts_ref[r * COL_BLOCKS + c, 8:, :]
        for j in range(FEATURES // TILE):
            lanes = slice(r * FEATURES + j * TILE, r * FEATURES + (j + 1) * TILE)
            score = score + mixed_ref[:, lanes].astype(jnp.float32) * read[j : j + 1, :]
            for c in range(CONTS):
                direct = direct + cont_ref[c, :, lanes].astype(jnp.float32) * head_ref[:, lanes]
    total = jnp.sum(score, axis=0, keepdims=True) + jnp.sum(direct, axis=0, keepdims=True)
    score_ref[0] = jnp.sum(total) / CONTS


def finish(parts, main, cont, head, mixed):
    return pl.pallas_call(
        finish_kernel,
        out_shape=(
            jax.ShapeDtypeStruct((STEPS, D), jnp.bfloat16),
            jax.ShapeDtypeStruct((1,), jnp.float32),
        ),
        in_specs=[whole(parts.shape), whole(main.shape), whole(cont.shape), whole(head.shape), whole(mixed.shape)],
        out_specs=(whole((STEPS, D)), SMEM),
        scratch_shapes=[pltpu.VMEM((8, D), jnp.float32)],
        compiler_params=kernel_params(),
        cost_estimate=cost(10**6, 2 * 10**6),
        name="finish",
    )(parts, main, cont, head, mixed)


def rope_tables(positions):
    half = HD // 2
    frequency = THETA ** (-(jnp.arange(half, dtype=jnp.float32) * 2.0) / HD)
    angles = positions.astype(jnp.float32)[:, None] * frequency[None, :]
    cosine = jnp.cos(angles)
    sine = jnp.sin(angles)
    return jnp.concatenate([cosine, cosine], axis=1), jnp.concatenate([-sine, sine], axis=1)


def exchange(rows):
    return lax.all_to_all(rows, "tp", split_axis=0, concat_axis=0, tiled=True)


ALONG = [[z * COL_BLOCKS + c for z in range(ROW_BLOCKS)] for c in range(COL_BLOCKS)]


def from_side(rows, dy, dx):
    route = []
    for to in range(MEMBERS):
        z, y, x = to // 8, to // 4 % 2, to % 4
        route.append((z * 8 + (y + dy) % 2 * 4 + (x + dx) % 4, to))
    return lax.ppermute(rows, "tp", route)


def from_along(rows, dz):
    route = [((to + dz * COL_BLOCKS) % MEMBERS, to) for to in range(MEMBERS)]
    return lax.ppermute(rows, "tp", route)


FIRST_HOMES = ((0, 0), (1, 0), (0, 1), (0, 3), (1, 1))
SECOND_HOMES = ((1, 3), (0, 2), (1, 2))
HOMES = FIRST_HOMES + SECOND_HOMES


def project(rows, blocks, bias):
    near = lax.all_to_all(rows, "tp", split_axis=0, concat_axis=0, tiled=True, axis_index_groups=ALONG)
    over = from_side(near, 1, 0)
    after, before = from_side(near, 0, 1), from_side(near, 0, 3)
    over_after, over_before = from_side(over, 0, 1), from_side(over, 0, 3)
    far = [from_side(before, 0, 3), from_side(over_after, 0, 1)]
    *first, main, weight = block_product([near, over, after, before, over_after], blocks)
    first = [first[0]] + [from_along(first[k], -k) for k in range(1, ROW_BLOCKS)]
    *second, main = block_product([over_before] + far, weight, main, HOMES)
    main, first = lax.optimization_barrier((main, first))
    second = [second[0]] + [from_along(second[k], -k) for k in range(1, ROW_BLOCKS)]
    received = []
    for homes, parts in ((FIRST_HOMES, first), (SECOND_HOMES, second)):
        for (dy, dx), summed in zip(homes, sum_parts(bias, parts)):
            received.append(from_side(summed, -dy, -dx) if dy or dx else summed)
    return received, exchange(main), second[1:] + received[1:5]


def on_device(
    main_inputs, cont_inputs, prefix_cache, prefix_len, boundary, rms_gain, qkv_bias, w_qkv, w_out, value_head
):
    main = main_inputs.reshape(STEPS, D)
    cont = cont_inputs.reshape(CONTS, STEPS, D)
    bias = qkv_bias[None, :]
    cache = prefix_cache[0]
    head = value_head[None, :]
    step = jnp.arange(CTOK, dtype=jnp.int32) % STEPS
    main_tables = rope_tables(prefix_len + step[:8])
    cont_tables = rope_tables(prefix_len + boundary + step)
    read = readout(value_head.reshape(COL_BLOCKS, D // COL_BLOCKS), w_out)
    parts, main_parts, before = project(norm_rows(main, cont, rms_gain[None, :]), w_qkv, bias)
    mixed, main_kv = attend_main(prefix_len, bias, *main_tables, cache, main_parts, before + [read])
    mixed = exchange(mixed)
    cont_mixed = attend_cont(prefix_len, boundary, bias, *cont_tables, cache, main_kv, *parts)
    parts = exchange(out_product(mixed, read, w_out, parts[6:]))
    main_out, score = finish(parts, main, cont, head, cont_mixed)
    return main_out[None], score


def solution(mesh):
    return jax.shard_map(
        on_device,
        mesh=mesh,
        in_specs=(
            P(("grp", "tp"), None, None),
            P(("grp", "tp"), None, None, None),
            P(("grp", "tp"), None, None),
            P(("grp", "tp")),
            P(("grp", "tp")),
            P(),
            P(),
            P("tp", None, None),
            P("tp", None, None),
            P(),
        ),
        out_specs=(P(("grp", "tp"), None, None), P(("grp", "tp"))),
        check_vma=False,
    )
```
